32 devices in a mesh: dp: 8 (over z, y), ctx: 4 (over x, core).
Axes of the slice: x: 2, y: 2, z: 4, core: 2. Of those that a mesh axis runs over, the one named last changes fastest.
Arguments:
- block_input: bfloat16 [8, 2048, 896], P('dp', 'ctx'), may hold values from -6 to 6
- cotangent: bfloat16 [8, 2048, 896], P('dp', 'ctx'), may hold values from -6 to 6
- lengths: int32 [8], P('dp'), may hold values from 1537 to 2048, as said below
- doc_starts: int32 [8], P('dp'), may hold values from 128 to 511
- master: float32 [32, 465920], P(('dp', 'ctx'))
- momentum: float32 [32, 465920], P(('dp', 'ctx'))
- vectors: float32 [32, 92], P(('dp', 'ctx'))
- vector_first: float32 [32, 92], P(('dp', 'ctx'))
- vector_second: float32 [32, 92], P(('dp', 'ctx'))
Outputs:
- layer_out: bfloat16 [8, 2048, 896], P('dp', 'ctx')
- input_grad: bfloat16 [8, 2048, 896], P('dp', 'ctx')
- new_master: float32 [32, 465920], P(('dp', 'ctx'))
- new_momentum: float32 [32, 465920], P(('dp', 'ctx'))
- master_copy: bfloat16 [32, 465920], P(('dp', 'ctx'))
- new_vectors: float32 [32, 92], P(('dp', 'ctx'))
- first_moment: float32 [32, 92], P(('dp', 'ctx'))
- second_moment: float32 [32, 92], P(('dp', 'ctx'))
The draws below stay inside these ranges and needn't reach their ends.
Inputs may be any that keep to these rules, and one draw needn't show every extreme that they name: `lengths`: in every draw some slot is used to its end.
All inputs are finite; a program needn't handle non-finite values.
Results may differ from the reference program's by a relative error of at most 0.014.
Values may be sent and summed in bfloat16 or wider, within the bound.
No kernel may reach another device: no remote copies, remote signals or barrier semaphores. Data moves between devices by JAX's collectives and lax.ppermute only.
A program may use at most 384 MiB of HBM per device.

```python
import math
import jax
import jax.numpy as jnp
from jax import lax

D = 896
HEADS = 14
KVH = 2
HD = 64
FF = 4864
SLOT = 2048
NS_STEPS = 3
STEP = 10
QD = 896
KVD = 128
SLOTS = 8
N_DP = 8
N_CTX = 4


def matrix_shapes_drawn():
    return [(D, QD), (D, KVD), (D, KVD), (QD, D), (D, FF), (D, FF), (FF, D)]


def vector_sizes_drawn():
    return [D, D, QD, KVD, KVD]


def gradient_size():
    return math.sqrt(SLOTS * SLOT)


def vector_scale(devices):
    factors = [1.0, 1.5, 0.3, 0.3, 0.3]
    parts = []
    for index, extent in enumerate(vector_sizes_drawn()):
        parts.append(jnp.full((extent,), factors[index] * gradient_size(), jnp.float32).reshape(devices, -1))
    return jnp.concatenate(parts, axis=1)


def draw_master(key, part):
    key = jax.random.fold_in(key, 11)
    devices = N_DP * N_CTX
    fans = [D, D, D, QD // 8, D, D, FF]
    pieces = []
    for index, shape_pair in enumerate(matrix_shapes_drawn()):
        sample = jax.random.normal(jax.random.fold_in(key, index), shape_pair, jnp.float32)
        pieces.append((sample * fans[index] ** (-0.5)).reshape(devices, -1))
    return jnp.concatenate(pieces, axis=1)


def draw_momentum(key, part):
    key = jax.random.fold_in(key, 12)
    devices = N_DP * N_CTX
    factors = [1.0, 1.0, 1.0, 0.3, 0.5, 0.5, 0.4]
    pieces = []
    for index, shape_pair in enumerate(matrix_shapes_drawn()):
        sample = jax.random.normal(jax.random.fold_in(key, index), shape_pair, jnp.float32)
        pieces.append((sample * factors[index] * gradient_size()).reshape(devices, -1))
    return jnp.concatenate(pieces, axis=1)


def draw_vectors(key, part):
    key = jax.random.fold_in(key, 13)
    devices = N_DP * N_CTX
    pieces = []
    for index, extent in enumerate(vector_sizes_drawn()):
        inner = jax.random.fold_in(key, index)
        if index < 2:
            sample = 1.0 + 0.3 * jax.random.uniform(inner, (extent,), jnp.float32, -1.0, 1.0)
        else:
            sample = 0.5 * jax.random.normal(inner, (extent,), jnp.float32)
        pieces.append(sample.reshape(devices, -1))
    return jnp.concatenate(pieces, axis=1)


def draw_vector_first(key, part):
    key = jax.random.fold_in(key, 14)
    devices = N_DP * N_CTX
    scale = vector_scale(devices)
    return 0.11 * scale * jax.random.normal(key, scale.shape, jnp.float32)


def draw_vector_second(key, part):
    key = jax.random.fold_in(key, 15)
    devices = N_DP * N_CTX
    scale = vector_scale(devices)
    factor = jnp.exp(jax.random.uniform(key, scale.shape, jnp.float32, math.log(0.5), math.log(2.0)))
    return 0.105 * scale * scale * factor


def draw_lengths(key, part):
    key = jax.random.fold_in(key, 16)
    drawn = jax.random.randint(jax.random.fold_in(key, 1), (SLOTS,), 3 * SLOT // 4 + 1, SLOT + 1)
    chosen = jax.random.randint(jax.random.fold_in(key, 2), (), 0, SLOTS)
    return drawn.at[chosen].set(SLOT).astype(jnp.int32)


def draw_doc_starts(key, part):
    key = jax.random.fold_in(key, 17)
    return jax.random.randint(key, (SLOTS,), SLOT // 16, SLOT // 4).astype(jnp.int32)


def shard_levels(stream_key, shape, shards, smallest, top_value):
    factor_of, own = 1.0, jax.random.fold_in(stream_key, 6)
    for dim, blocks in shards:
        steps = jnp.exp(jax.random.uniform(jax.random.fold_in(own, dim), (blocks,), jnp.float32, smallest / len(shards), top_value / len(shards)))
        factor_of = factor_of * jnp.repeat(steps, shape[dim] // blocks).reshape([-1 if axis == dim else 1 for axis in range(len(shape))])
    return factor_of


def scatter_about(rng, shape, width, bound, cuts=(), kind=jnp.bfloat16):
    level = shard_levels(rng, shape, cuts, -0.22, 0.18) if cuts else 1.0
    values = jax.random.normal(rng, shape, jnp.float32) * width * level
    return jnp.minimum(jnp.maximum(values, -bound), bound).astype(kind)


def setup_inputs(seed: int = 0) -> dict:
    streams_of = jax.random.split(jax.random.key(seed), 10)
    return {
        "block_input": scatter_about(streams_of[0], (SLOTS, SLOT, D), 1.0, 6.0, ((0, 8), (1, 4))),
        "cotangent": scatter_about(streams_of[1], (SLOTS, SLOT, D), 1.0, 6.0, ((0, 8), (1, 4))),
        "lengths": draw_lengths(jax.random.fold_in(streams_of[9], 71), 0),
        "doc_starts": draw_doc_starts(jax.random.fold_in(streams_of[9], 71), 0),
        "master": draw_master(jax.random.fold_in(streams_of[9], 71), 0),
        "momentum": draw_momentum(jax.random.fold_in(streams_of[9], 71), 0),
        "vectors": draw_vectors(jax.random.fold_in(streams_of[9], 71), 0),
        "vector_first": draw_vector_first(jax.random.fold_in(streams_of[9], 71), 0),
        "vector_second": draw_vector_second(jax.random.fold_in(streams_of[9], 71), 0),
    }


@jax.custom_vjp
def low(v):
    return lax.optimization_barrier(v.astype(jnp.bfloat16)).astype(jnp.float32)

@jax.custom_vjp
def low_back(v):
    return v

def low_keep(v):
    return (low(v), None)

def low_pass(kept, grad):
    return (grad,)

def back_keep(v):
    return (v, None)

def back_low(kept, grad):
    return (low(grad),)
low.defvjp(low_keep, low_pass)
low_back.defvjp(back_keep, back_low)
NORM_EPS = 1e-06
ROPE_BASE = 1000000.0
NS_LINEAR = 3.4445
NS_SQUARE = -4.775
NS_CUBIC = 2.0315
MOMENTUM_DECAY = 0.5
MUON_RATE = 0.6
MUON_DECAY = 0.1
ADAM_RATE = 0.2
BETA_FIRST = 0.9
BETA_SECOND = 0.95
ADAM_EPS = 1e-08
MASK_FLOOR = -1e+30

def matrix_shapes():
    return [(D, QD), (D, KVD), (D, KVD), (QD, D), (D, FF), (D, FF), (FF, D)]

def vector_sizes():
    return [D, D, QD, KVD, KVD]

def split_matrices(flat, devices):
    result = []
    offset = 0
    for height, breadth in matrix_shapes():
        extent = height // devices * breadth
        result.append(flat[:, offset:offset + extent].reshape(height, breadth))
        offset += extent
    return result

def join_matrices(pieces, devices):
    return jnp.concatenate([piece.reshape(devices, -1) for piece in pieces], axis=1)

def split_vectors(flat, devices):
    result = []
    offset = 0
    for extent_all in vector_sizes():
        extent = extent_all // devices
        result.append(flat[:, offset:offset + extent].reshape(extent_all))
        offset += extent
    return result

def join_vectors(pieces, devices):
    return jnp.concatenate([piece.reshape(devices, -1) for piece in pieces], axis=1)

def slot_layout(lengths, doc_starts):
    places = jnp.arange(SLOT, dtype=jnp.int32)[None, :]
    second = doc_starts[:, None]
    ending = lengths[:, None]
    document = (places >= second).astype(jnp.int32) + (places >= ending).astype(jnp.int32)
    doc_begin = jnp.where(document == 0, 0, jnp.where(document == 1, second, ending))
    position = (places - doc_begin).astype(jnp.float32)
    living = (places < ending).astype(jnp.float32)
    return (document, position, living)

def rotary_tables(position):
    indices = jnp.arange(HD // 2, dtype=jnp.float32)
    inverse = ROPE_BASE ** (-2.0 * indices / HD)
    angles = position[..., None] * inverse
    cosine = jnp.concatenate([jnp.cos(angles), jnp.cos(angles)], axis=-1)
    sine_part = jnp.concatenate([jnp.sin(angles), jnp.sin(angles)], axis=-1)
    return (cosine, sine_part)

def rotate(values, cosine, sine_part):
    midpoint = HD // 2
    turned = jnp.concatenate([-values[..., midpoint:], values[..., :midpoint]], axis=-1)
    return values * cosine[:, None, :] + turned * sine_part[:, None, :]

def orthogonalize(moment):
    tall = moment.shape[0] > moment.shape[1]
    work = moment.T if tall else moment
    work = (work / (jnp.sqrt(jnp.sum(work * work)) + 1e-07)).astype(jnp.bfloat16)
    for _ in range(NS_STEPS):
        gram = jnp.dot(work, work.T, preferred_element_type=jnp.float32).astype(jnp.bfloat16)
        poly = (NS_SQUARE * gram.astype(jnp.float32) + NS_CUBIC * jnp.dot(gram, gram, preferred_element_type=jnp.float32)).astype(jnp.bfloat16)
        work = (NS_LINEAR * work.astype(jnp.float32) + jnp.dot(poly, work, preferred_element_type=jnp.float32)).astype(jnp.bfloat16)
    return work.T if tall else work

def slot_forward(inputs, document, position, living, params):
    w_query, w_key, w_value, w_out, w_gate, w_up, w_down, gain_first, gain_second, bias_query, bias_key, bias_value = params
    exact = lax.Precision.HIGHEST
    group = HEADS // KVH
    block = min(512, SLOT)
    scale_one = lax.rsqrt(lax.optimization_barrier(jnp.mean(inputs * inputs, axis=-1, keepdims=True)) + NORM_EPS)
    normed_one = low(inputs * scale_one * gain_first)
    pre_query = low_back(jnp.dot(normed_one, w_query, precision=exact) + bias_query)
    pre_key = low_back(jnp.dot(normed_one, w_key, precision=exact) + bias_key)
    value_all = low(low_back(jnp.dot(normed_one, w_value, precision=exact) + bias_value)).reshape(SLOT, KVH, HD)
    cosine, sine_part = rotary_tables(position)
    queries = low(rotate(pre_query.reshape(SLOT, HEADS, HD), cosine, sine_part)).reshape(SLOT, KVH, group, HD)
    keys_all = low(rotate(pre_key.reshape(SLOT, KVH, HD), cosine, sine_part))
    key_place = jnp.arange(SLOT, dtype=jnp.int32)

    def query_block(first_row):
        query_part = lax.dynamic_slice_in_dim(queries, first_row, block, 0)
        query_place = first_row + jnp.arange(block, dtype=jnp.int32)
        doc_query = lax.dynamic_slice_in_dim(document, first_row, block, 0)
        raw = low_back(jnp.einsum('tgha,sga->ghts', query_part, keys_all, precision=exact) * HD ** (-0.5))
        allowed = (doc_query[:, None] == document[None, :]) & (key_place[None, :] <= query_place[:, None])
        masked = jnp.where(allowed[None, None], raw, MASK_FLOOR)
        log_total = jax.nn.logsumexp(masked, axis=-1, keepdims=True)
        shares = low(jnp.where(allowed[None, None], jnp.exp(masked - log_total), 0.0))
        return jnp.einsum('ghts,sga->tgha', shares, value_all, precision=exact).reshape(block, QD)
    first_rows = jnp.arange(0, SLOT, block, dtype=jnp.int32)
    attended = lax.map(jax.checkpoint(query_block), first_rows).reshape(SLOT, QD)
    mixed_heads = low(low_back(attended))
    hidden = inputs + low_back(jnp.dot(mixed_heads, w_out, precision=exact))
    scale_two = lax.rsqrt(lax.optimization_barrier(jnp.mean(hidden * hidden, axis=-1, keepdims=True)) + NORM_EPS)
    normed_two = low(hidden * scale_two * gain_second)
    gate_pre = low_back(jnp.dot(normed_two, w_gate, precision=exact))
    up_pre = low_back(jnp.dot(normed_two, w_up, precision=exact))
    activated = low(jax.nn.silu(gate_pre) * up_pre)
    return (hidden + low_back(jnp.dot(activated, w_down, precision=exact))) * living[:, None]

def reference(block_input, cotangent, lengths, doc_starts, master, momentum, vectors, vector_first, vector_second):
    devices = N_DP * N_CTX
    matrices = split_matrices(master, devices)
    vector_list = split_vectors(vectors, devices)
    document, position, living = slot_layout(lengths, doc_starts)

    def forward(params, inputs):
        rounded = [low(param) for param in params]

        def per_slot(carry, item):
            return (carry, jax.checkpoint(slot_forward)(item[0], item[1], item[2], item[3], rounded))
        _, outputs = lax.scan(per_slot, None, (inputs, document, position, living))
        return outputs
    outputs, pullback = jax.vjp(forward, matrices + vector_list, block_input.astype(jnp.float32))
    param_grads, input_grad = pullback(cotangent.astype(jnp.float32))
    moment_list = split_matrices(momentum, devices)
    new_moments = []
    new_weights = []
    for index, (height, breadth) in enumerate(matrix_shapes()):
        renewed = MOMENTUM_DECAY * moment_list[index] + param_grads[index]
        orthogonal = orthogonalize(renewed).astype(jnp.float32)
        factor = math.sqrt(max(1.0, breadth / height))
        new_weights.append(matrices[index] * (1.0 - MUON_RATE * MUON_DECAY) - MUON_RATE * factor * orthogonal)
        new_moments.append(renewed)
    new_master = join_matrices(new_weights, devices)
    new_momentum = join_matrices(new_moments, devices)
    vector_grad = join_vectors(list(param_grads[7:]), devices)
    first_new = BETA_FIRST * vector_first + (1.0 - BETA_FIRST) * vector_grad
    second_new = BETA_SECOND * vector_second + (1.0 - BETA_SECOND) * vector_grad * vector_grad
    adjusted = first_new / (1.0 - BETA_FIRST ** STEP) / (jnp.sqrt(second_new / (1.0 - BETA_SECOND ** STEP)) + ADAM_EPS)
    new_vectors = vectors - ADAM_RATE * adjusted
    return (outputs.astype(jnp.bfloat16), input_grad.astype(jnp.bfloat16), new_master, new_momentum, new_master.astype(jnp.bfloat16), new_vectors, first_new, second_new)
```

```python
import math

import jax
import jax.numpy as jnp
from jax import lax
from jax.sharding import PartitionSpec as P

D = 896
HEADS = 14
KVH = 2
HD = 64
FF = 4864
SLOT = 2048
NS_STEPS = 3
STEP = 10
QD = 896
KVD = 128

NORM_EPS = 1e-06
ROPE_BASE = 1000000.0
NS_LINEAR = 3.4445
NS_SQUARE = -4.775
NS_CUBIC = 2.0315
MOMENTUM_DECAY = 0.5
MUON_RATE = 0.6
MUON_DECAY = 0.1
ADAM_RATE = 0.2
BETA_FIRST = 0.9
BETA_SECOND = 0.95
ADAM_EPS = 1e-08
MASK_FLOOR = -1e30

F32 = jnp.float32
BF16 = jnp.bfloat16
BOTH = ("dp", "ctx")


def matrix_shapes():
    return [(D, QD), (D, KVD), (D, KVD), (QD, D), (D, FF), (D, FF), (FF, D)]


def vector_sizes():
    return [D, D, QD, KVD, KVD]


def mm(left, right, contract=((1,), (0,))):
    return lax.dot_general(left, right, (contract, ((), ())), preferred_element_type=F32)


def split_rows(row, devices):
    result = []
    offset = 0
    for height, breadth in matrix_shapes():
        extent = height // devices * breadth
        result.append(row[offset : offset + extent].reshape(height // devices, breadth))
        offset += extent
    return result


def split_small(flat, devices):
    result = []
    offset = 0
    for extent_all in vector_sizes():
        extent = extent_all // devices
        result.append(flat[:, offset : offset + extent].reshape(extent_all))
        offset += extent
    return result


def join_small(pieces, devices):
    return jnp.concatenate([piece.reshape(devices, -1) for piece in pieces], axis=1)


def slot_layout(lengths, doc_starts):
    places = jnp.arange(SLOT, dtype=jnp.int32)[None, :]
    second = doc_starts[:, None]
    ending = lengths[:, None]
    document = (places >= second).astype(jnp.int32) + (places >= ending).astype(jnp.int32)
    doc_begin = jnp.where(document == 0, 0, jnp.where(document == 1, second, ending))
    position = (places - doc_begin).astype(F32)
    living = (places < ending).astype(F32)
    return (document, position, living)


def rotary_tables(position):
    indices = jnp.arange(HD // 2, dtype=F32)
    inverse = ROPE_BASE ** (-2.0 * indices / HD)
    angles = position[..., None] * inverse
    cosine = jnp.concatenate([jnp.cos(angles), jnp.cos(angles)], axis=-1)
    sine_part = jnp.concatenate([jnp.sin(angles), jnp.sin(angles)], axis=-1)
    return (cosine, sine_part)


def rotate(values, cosine, sine_part):
    midpoint = HD // 2
    turned = jnp.concatenate([-values[..., midpoint:], values[..., :midpoint]], axis=-1)
    return values * cosine[:, None, :] + turned * sine_part[:, None, :]


def rotate_back(gradient, cosine, sine_part):
    midpoint = HD // 2
    scaled = gradient * sine_part[:, None, :]
    turned = jnp.concatenate([scaled[..., midpoint:], -scaled[..., :midpoint]], axis=-1)
    return gradient * cosine[:, None, :] + turned


def norm_backward(source, scale_row, gain, incoming):
    gain_grad = jnp.sum(incoming * source * scale_row, axis=0)
    weighted = incoming * gain
    result = scale_row * weighted - source * scale_row**3 * jnp.mean(
        weighted * source, axis=-1, keepdims=True
    )
    return (result, gain_grad)


def attention_scores(queries, key_block, doc_query, doc_key, query_place, key_place):
    raw = jnp.einsum(
        "cgha,kga->ghck", queries, key_block, preferred_element_type=F32
    ) * HD ** (-0.5)
    allowed = (doc_query[:, None] == doc_key[None, :]) & (
        key_place[None, :] <= query_place[:, None]
    )
    allowed = allowed[None, None, :, :]
    return (jnp.where(allowed, raw, MASK_FLOOR), allowed)


def gram_steps(gram, rows):
    scale = 1.0 / (jnp.sqrt(jnp.trace(gram)) + 1e-07)
    gram = gram * (scale * scale)
    work = (rows * scale).astype(BF16)
    for step in range(NS_STEPS):
        low = gram.astype(BF16)
        poly = (NS_SQUARE * gram + NS_CUBIC * mm(low, low)).astype(BF16)
        work = (NS_LINEAR * work.astype(F32) + mm(work, poly)).astype(BF16)
        if step + 1 < NS_STEPS:
            first = mm(poly, low)
            second = mm(poly, first.astype(BF16))
            gram = NS_LINEAR * NS_LINEAR * gram + (2.0 * NS_LINEAR) * first + second
    return work


def on_device(
    block_input,
    cotangent,
    lengths,
    doc_starts,
    master,
    momentum,
    vectors,
    vector_first,
    vector_second,
):
    n_dp = lax.axis_size("dp")
    n_ctx = lax.axis_size("ctx")
    devices = n_dp * n_ctx
    rows = D // devices
    frows = FF // devices
    fblock = FF // n_ctx
    slots, span, width = block_input.shape
    tokens = slots * span
    group = HEADS // KVH
    block = min(512, SLOT)
    here = lax.axis_index("ctx") * span
    packed = QD + 2 * KVD + D

    master_parts = split_rows(master[0], devices)
    momentum_parts = split_rows(momentum[0], devices)

    small = jnp.pad(vectors, ((0, 0), (0, packed - vectors.shape[1])))
    attn_local = jnp.concatenate(
        [jnp.concatenate(master_parts[:4], axis=1), small], axis=0
    ).astype(BF16)
    attn_full = lax.all_gather(attn_local, BOTH, axis=0)
    attn_mats = attn_full[:, :rows].reshape(D, packed)
    gain_first, gain_second, bias_query, bias_key, bias_value = [
        piece.astype(F32) for piece in split_small(attn_full[:, rows], devices)
    ]
    w_qkv = attn_mats[:, : QD + 2 * KVD]
    w_out = attn_mats[:, QD + 2 * KVD :]

    def by_ctx(part):
        return part.reshape(rows, n_dp, n_ctx, frows).transpose(2, 0, 1, 3).reshape(n_ctx, rows, fblock)

    gate_up = jnp.stack([by_ctx(master_parts[4]), by_ctx(master_parts[5])], axis=1).astype(BF16)
    gate_up = lax.all_to_all(gate_up, "ctx", split_axis=0, concat_axis=0, tiled=True)
    gate_up = gate_up.transpose(1, 0, 2, 3).reshape(2, n_ctx * rows, fblock)
    gate_up = lax.all_gather(gate_up, "dp", axis=1, tiled=True)
    w_gate, w_up = gate_up[0], gate_up[1]
    w_down = lax.all_gather(master_parts[6].astype(BF16), "dp", axis=0, tiled=True)

    def to_columns(gate, up):
        both = jnp.concatenate(
            [gate.reshape(rows, devices, frows), up.reshape(rows, devices, frows)], axis=2
        )
        both = both.transpose(1, 0, 2).astype(BF16)
        both = lax.all_to_all(both, BOTH, split_axis=0, concat_axis=0, tiled=True)
        return both.reshape(D, 2 * frows).T

    def to_rows(pair):
        both = pair.T.reshape(devices, rows, 2 * frows)
        both = lax.all_to_all(both, BOTH, split_axis=0, concat_axis=0, tiled=True)
        both = both.transpose(1, 0, 2)
        return (
            both[:, :, :frows].reshape(rows, FF),
            both[:, :, frows:].reshape(rows, FF),
        )

    momentum_pair = to_columns(momentum_parts[4], momentum_parts[5])

    document, position, living = slot_layout(lengths, doc_starts)
    doc_all = document[0]
    doc_here = lax.dynamic_slice_in_dim(doc_all, here, span, 0)
    place_here = lax.dynamic_slice_in_dim(position[0], here, span, 0)
    live_all = living.reshape(SLOT, 1)
    live_here = lax.dynamic_slice_in_dim(live_all, here, span, 0)
    query_place = here + jnp.arange(span, dtype=jnp.int32)

    cot_all = lax.all_gather(cotangent.reshape(tokens, width), "ctx", axis=0, tiled=True)
    out_grad_all = jnp.where(live_all > 0, cot_all, jnp.zeros_like(cot_all))

    inputs = block_input.astype(F32).reshape(tokens, width)
    scale_one = lax.rsqrt(jnp.mean(inputs * inputs, axis=-1, keepdims=True) + NORM_EPS)
    normed_one = (inputs * scale_one * gain_first).astype(BF16)
    pre_qkv = mm(normed_one, w_qkv) + jnp.concatenate([bias_query, bias_key, bias_value])
    cosine, sine_part = rotary_tables(place_here)
    queries = rotate(pre_qkv[:, :QD].reshape(tokens, HEADS, HD), cosine, sine_part).astype(BF16)
    queries = queries.reshape(span, KVH, group, HD)
    keys_here = rotate(
        pre_qkv[:, QD : QD + KVD].reshape(tokens, KVH, HD), cosine, sine_part
    ).astype(BF16)
    keys_values = jnp.concatenate(
        [keys_here.reshape(span, KVD), pre_qkv[:, QD + KVD :].astype(BF16)], axis=1
    )
    keys_values = lax.all_gather(keys_values, "ctx", axis=0, tiled=True)
    keys_all = keys_values[:, :KVD]
    values_all = keys_values[:, KVD:]

    def key_pieces(begin_at):
        key_block = keys_all[begin_at : begin_at + block].reshape(block, KVH, HD)
        value_block = values_all[begin_at : begin_at + block].reshape(block, KVH, HD)
        doc_key = doc_all[begin_at : begin_at + block]
        key_place = begin_at + jnp.arange(block, dtype=jnp.int32)
        masked, allowed = attention_scores(
            queries, key_block, doc_here, doc_key, query_place, key_place
        )
        return (key_block, value_block, masked, allowed)

    run_max = jnp.full((KVH, group, span), MASK_FLOOR, F32)
    run_total = jnp.zeros((KVH, group, span), F32)
    kept_scores = []
    for begin_at in range(0, SLOT, block):
        key_block, value_block, masked, allowed = key_pieces(begin_at)
        kept_scores.append((value_block, masked, allowed))
        new_max = jnp.maximum(run_max, jnp.max(masked, axis=-1))
        present = jnp.where(allowed, jnp.exp(masked - new_max[..., None]), 0.0)
        run_total = run_total * jnp.exp(run_max - new_max) + jnp.sum(present, axis=-1)
        run_max = new_max
    log_total = run_max + jnp.log(run_total)
    attended = jnp.zeros((span, KVH, group, HD), F32)
    for value_block, masked, allowed in kept_scores:
        shares = jnp.where(allowed, jnp.exp(masked - log_total[..., None]), 0.0).astype(BF16)
        attended = attended + jnp.einsum(
            "ghck,kga->cgha", shares, value_block, preferred_element_type=F32
        )
    mixed_heads = attended.reshape(tokens, QD).astype(BF16)
    hidden = inputs + mm(mixed_heads, w_out)
    scale_two = lax.rsqrt(jnp.mean(hidden * hidden, axis=-1, keepdims=True) + NORM_EPS)
    normed_two = (hidden * scale_two * gain_second).astype(BF16)

    normed_all = lax.all_gather(normed_two, "ctx", axis=0, tiled=True)
    grad_act = mm(out_grad_all, w_down, ((1,), (1,)))
    gate_pre = mm(normed_all, w_gate)
    up_pre = mm(normed_all, w_up)
    sigmoid_gate = jax.nn.sigmoid(gate_pre)
    swish = gate_pre * sigmoid_gate
    activated = (swish * up_pre).astype(BF16)
    slope = sigmoid_gate * (1.0 + gate_pre * (1.0 - sigmoid_gate))
    gate_back = (grad_act * up_pre * slope).astype(BF16)
    up_back = (grad_act * swish).astype(BF16)
    normed_two_part = mm(gate_back, w_gate, ((1,), (1,))) + mm(up_back, w_up, ((1,), (1,)))
    normed_two_grad = lax.psum_scatter(
        normed_two_part.astype(BF16), "ctx", scatter_dimension=0, tiled=True
    ).astype(F32)
    out_part = mm(activated, w_down)
    grad_gate = mm(gate_back, normed_all, ((0,), (0,)))
    grad_upper = mm(up_back, normed_all, ((0,), (0,)))
    grad_down = mm(activated, out_grad_all, ((0,), (0,)))
    out_sum = lax.psum_scatter(out_part.astype(BF16), "ctx", scatter_dimension=0, tiled=True)
    layer_out = (hidden + out_sum.astype(F32)) * live_here
    gate_sum, up_sum, down_sum = [
        lax.psum_scatter(part.astype(BF16), "dp", scatter_dimension=0, tiled=True)
        for part in (grad_gate, grad_upper, grad_down)
    ]

    out_grad = cotangent.astype(F32).reshape(tokens, width) * live_here
    hidden_norm_grad, grad_gain_second = norm_backward(
        hidden, scale_two, gain_second, normed_two_grad
    )
    hidden_grad = out_grad + hidden_norm_grad
    hidden_low = hidden_grad.astype(BF16)
    grad_output = mm(mixed_heads, hidden_low, ((0,), (0,)))
    heads_grad = mm(hidden_low, w_out, ((1,), (1,))).astype(BF16)
    heads_grad = heads_grad.reshape(span, KVH, group, HD)
    delta = jnp.einsum("cgha,cgha->ghc", heads_grad.astype(F32), attended)
    query_acc = jnp.zeros((span, KVH, group, HD), F32)
    key_grads = []
    value_grads = []
    for begin_at in range(0, SLOT, block):
        key_block, value_block, masked, allowed = key_pieces(begin_at)
        shares = jnp.where(allowed, jnp.exp(masked - log_total[..., None]), 0.0)
        value_grads.append(
            jnp.einsum(
                "ghck,cgha->kga", shares.astype(BF16), heads_grad, preferred_element_type=F32
            )
        )
        share_grad = jnp.einsum(
            "cgha,kga->ghck", heads_grad, value_block, preferred_element_type=F32
        )
        score_grad = (shares * (share_grad - delta[..., None])).astype(BF16)
        query_acc = query_acc + jnp.einsum(
            "ghck,kga->cgha", score_grad, key_block, preferred_element_type=F32
        )
        key_grads.append(
            jnp.einsum("ghck,cgha->kga", score_grad, queries, preferred_element_type=F32)
            * HD ** (-0.5)
        )
    key_full = jnp.concatenate(key_grads, axis=0).reshape(SLOT, KVD)
    value_full = jnp.concatenate(value_grads, axis=0).reshape(SLOT, KVD)
    kv_grad = lax.psum_scatter(
        jnp.concatenate([key_full, value_full], axis=1).astype(BF16),
        "ctx",
        scatter_dimension=0,
        tiled=True,
    ).astype(F32)
    query_grad = (query_acc * HD ** (-0.5)).reshape(tokens, HEADS, HD)
    query_back = rotate_back(query_grad, cosine, sine_part).reshape(tokens, QD)
    key_back = rotate_back(kv_grad[:, :KVD].reshape(tokens, KVH, HD), cosine, sine_part).reshape(
        tokens, KVD
    )
    qkv_back = jnp.concatenate([query_back, key_back, kv_grad[:, KVD:]], axis=1).astype(BF16)
    grad_qkv = mm(normed_one, qkv_back, ((0,), (0,)))
    grad_bias = jnp.sum(qkv_back.astype(F32), axis=0)
    normed_one_grad = mm(qkv_back, w_qkv, ((1,), (1,)))
    input_norm_grad, grad_gain_first = norm_backward(inputs, scale_one, gain_first, normed_one_grad)
    input_grad = (hidden_grad + input_norm_grad).astype(BF16).reshape(slots, span, width)

    vector_part = join_small(
        [
            grad_gain_first,
            grad_gain_second,
            grad_bias[:QD],
            grad_bias[QD : QD + KVD],
            grad_bias[QD + KVD :],
        ],
        devices,
    )
    vector_grad = jnp.sum(
        lax.all_to_all(vector_part, BOTH, split_axis=0, concat_axis=0, tiled=True),
        axis=0,
        keepdims=True,
    )
    attn_part = (
        jnp.concatenate([grad_qkv, grad_output], axis=1).reshape(devices, rows, packed).astype(BF16)
    )
    attn_sum = lax.psum_scatter(attn_part, BOTH, scatter_dimension=0, tiled=True)[0].astype(F32)

    momentum_attn = jnp.concatenate(momentum_parts[:4], axis=1)
    moved_attn = MOMENTUM_DECAY * momentum_attn + attn_sum
    moved_down = MOMENTUM_DECAY * momentum_parts[6] + down_sum.astype(F32)
    pair_sum = jnp.concatenate([gate_sum, up_sum], axis=0)
    moved_pair = MOMENTUM_DECAY * momentum_pair.astype(F32) + pair_sum.astype(F32)
    gate_rows, up_rows = to_rows(pair_sum)
    moved_gate = MOMENTUM_DECAY * momentum_parts[4] + gate_rows.astype(F32)
    moved_up = MOMENTUM_DECAY * momentum_parts[5] + up_rows.astype(F32)

    slices = [moved_pair[:frows], moved_pair[frows:], moved_down]
    lows = [piece.astype(BF16) for piece in slices]
    grams = jnp.stack([mm(low, low, ((0,), (0,))) for low in lows]).astype(BF16)
    grams = lax.psum(grams, BOTH).astype(F32)
    wide = [gram_steps(grams[index], slices[index]) for index in range(3)]
    ortho_gate, ortho_up = to_rows(jnp.concatenate(wide[:2], axis=0))
    attn_moved_low = moved_attn.astype(BF16)
    attn_moved_all = lax.all_gather(attn_moved_low, BOTH, axis=0).reshape(D, packed)
    ortho_attn = []
    offset = 0
    for breadth in (QD, KVD, KVD, D):
        whole = attn_moved_all[:, offset : offset + breadth]
        ortho_attn.append(
            gram_steps(mm(whole, whole, ((0,), (0,))), moved_attn[:, offset : offset + breadth])
        )
        offset += breadth
    ortho = ortho_attn + [ortho_gate, ortho_up, wide[2]]

    new_pieces = []
    for index, (height, breadth) in enumerate(matrix_shapes()):
        factor = math.sqrt(max(1.0, breadth / height))
        new_pieces.append(
            (
                master_parts[index] * (1.0 - MUON_RATE * MUON_DECAY)
                - MUON_RATE * factor * ortho[index].astype(F32)
            ).reshape(-1)
        )
    new_master = jnp.concatenate(new_pieces)[None, :]
    new_momentum = jnp.concatenate(
        [
            moved_attn[:, :QD].reshape(-1),
            moved_attn[:, QD : QD + KVD].reshape(-1),
            moved_attn[:, QD + KVD : QD + 2 * KVD].reshape(-1),
            moved_attn[:, QD + 2 * KVD :].reshape(-1),
            moved_gate.reshape(-1),
            moved_up.reshape(-1),
            moved_down.reshape(-1),
        ]
    )[None, :]
    first_new = BETA_FIRST * vector_first + (1.0 - BETA_FIRST) * vector_grad
    second_new = BETA_SECOND * vector_second + (1.0 - BETA_SECOND) * vector_grad * vector_grad
    adjusted = (
        first_new
        / (1.0 - BETA_FIRST**STEP)
        / (jnp.sqrt(second_new / (1.0 - BETA_SECOND**STEP)) + ADAM_EPS)
    )
    new_vectors = vectors - ADAM_RATE * adjusted
    return (
        layer_out.astype(BF16).reshape(slots, span, width),
        input_grad,
        new_master,
        new_momentum,
        new_master.astype(BF16),
        new_vectors,
        first_new,
        second_new,
    )


def solution(mesh):
    return jax.shard_map(
        on_device,
        mesh=mesh,
        in_specs=(
            P("dp", "ctx", None),
            P("dp", "ctx", None),
            P("dp"),
            P("dp"),
            P(BOTH, None),
            P(BOTH, None),
            P(BOTH, None),
            P(BOTH, None),
            P(BOTH, None),
        ),
        out_specs=(
            P("dp", "ctx", None),
            P("dp", "ctx", None),
            P(BOTH, None),
            P(BOTH, None),
            P(BOTH, None),
            P(BOTH, None),
            P(BOTH, None),
            P(BOTH, None),
        ),
        check_vma=False,
    )
```

```python
import math

import jax
import jax.numpy as jnp
from jax import lax
from jax.experimental import pallas as pl
from jax.experimental.pallas import tpu as pltpu
from jax.sharding import PartitionSpec as P

D = 896
HEADS = 14
KVH = 2
HD = 64
FF = 4864
SLOT = 2048
NS_STEPS = 3
STEP = 10
QD = 896
KVD = 128

NORM_EPS = 1e-06
ROPE_BASE = 1000000.0
NS_LINEAR = 3.4445
NS_SQUARE = -4.775
NS_CUBIC = 2.0315
MOMENTUM_DECAY = 0.5
MUON_RATE = 0.6
MUON_DECAY = 0.1
ADAM_RATE = 0.2
BETA_FIRST = 0.9
BETA_SECOND = 0.95
ADAM_EPS = 1e-08
MASK_FLOOR = -1e30

F32 = jnp.float32
BF16 = jnp.bfloat16
BOTH = ("dp", "ctx")


def matrix_shapes():
    return [(D, QD), (D, KVD), (D, KVD), (QD, D), (D, FF), (D, FF), (FF, D)]


def vector_sizes():
    return [D, D, QD, KVD, KVD]


def mm(left, right, contract=((1,), (0,))):
    return lax.dot_general(left, right, (contract, ((), ())), preferred_element_type=F32)


def split_rows(row, devices):
    result = []
    offset = 0
    for height, breadth in matrix_shapes():
        extent = height // devices * breadth
        result.append(row[offset : offset + extent].reshape(height // devices, breadth))
        offset += extent
    return result


def split_small(flat, devices):
    result = []
    offset = 0
    for extent_all in vector_sizes():
        extent = extent_all // devices
        result.append(flat[:, offset : offset + extent].reshape(extent_all))
        offset += extent
    return result


def join_small(pieces, devices):
    return jnp.concatenate([piece.reshape(devices, -1) for piece in pieces], axis=1)


def swap(value, mask, devices):
    return lax.ppermute(value, BOTH, [(index, index ^ mask) for index in range(devices)])


def gather_bits(value, bits, me, devices, total):
    held = value
    done = []
    for bit in bits:
        place = sum(1 for other in done if other > bit)
        got = swap(held, bit, devices)
        mine = (me & bit) != 0
        held = jnp.where(
            mine, jnp.stack([got, held], axis=place), jnp.stack([held, got], axis=place)
        )
        done.append(bit)
    return held


def scatter_sum(value, bits, me, devices):
    left = sorted(bits, reverse=True)
    held = value
    for bit in bits:
        axis = left.index(bit)
        mine = jnp.where((me & bit) != 0, 1, 0)
        sent = lax.dynamic_index_in_dim(held, 1 - mine, axis, keepdims=False).astype(BF16)
        kept = lax.dynamic_index_in_dim(held, mine, axis, keepdims=False)
        got = swap(sent, bit, devices)
        held = (kept.astype(F32) + got.astype(F32)).astype(BF16)
        left.pop(axis)
    return held


def rotate(values, cosine, sine_part):
    midpoint = HD // 2
    turned = jnp.concatenate([-values[:, midpoint:], values[:, :midpoint]], axis=1)
    return values * cosine + turned * sine_part


def rotate_back(gradient, cosine, sine_part):
    midpoint = HD // 2
    scaled = gradient * sine_part
    turned = jnp.concatenate([scaled[:, midpoint:], -scaled[:, :midpoint]], axis=1)
    return gradient * cosine + turned


def norm_backward(source, scale_row, gain, incoming):
    gain_grad = jnp.sum(incoming * source * scale_row, axis=0)
    weighted = incoming * gain
    result = scale_row * weighted - source * scale_row**3 * jnp.mean(
        weighted * source, axis=-1, keepdims=True
    )
    return (result, gain_grad)


def fill_rows(info, kv, offset, groups, target, chunk):
    for group in range(groups):
        begin = offset + group * HD
        target[chunk, group] = kv[chunk, begin : begin + HD, :].astype(F32).T.astype(BF16)


def fill_mask(info, mask, chunk, span):
    key = chunk * span + lax.broadcasted_iota(jnp.int32, (span, span), 0)
    query = info[0] * span + lax.broadcasted_iota(jnp.int32, (span, span), 1)
    key_doc = (key >= info[2]).astype(jnp.int32) + (key >= info[1]).astype(jnp.int32)
    query_doc = (query >= info[2]).astype(jnp.int32) + (query >= info[1]).astype(jnp.int32)
    allowed = jnp.logical_and(key_doc == query_doc, key <= query)
    mask[chunk] = jnp.where(allowed, 0.0, MASK_FLOOR).astype(F32)


def attend_kernel(info, kv, q, out, lse, keys, mask, best, total, acc):
    head = pl.program_id(0)
    span = q.shape[-1]
    mine = info[0]
    chunks = mine + 1

    @pl.when(head == 0)
    def _():
        def fill(chunk, carry):
            slot = jnp.bitwise_xor(chunk, mine)
            for group in range(KVH):
                rows = kv[slot, group * HD : (group + 1) * HD, :]
                keys[chunk, group] = rows.astype(F32).T.astype(BF16)
            fill_mask(info, mask, chunk, span)
            return carry

        lax.fori_loop(0, chunks, fill, 0)

    group = head // (HEADS // KVH)
    best[...] = jnp.full(best.shape, MASK_FLOOR, F32)
    total[...] = jnp.zeros(total.shape, F32)
    acc[...] = jnp.zeros(acc.shape, F32)
    queries = q[0]

    def step(index, carry):
        chunk = mine - index
        slot = jnp.bitwise_xor(chunk, mine)
        scores = jnp.dot(keys[chunk, group], queries, preferred_element_type=F32) + mask[chunk]
        old = best[...]
        new = jnp.maximum(old, jnp.max(scores, axis=0, keepdims=True))
        present = jnp.exp(scores - new)
        shrink = jnp.exp(old - new)
        best[...] = new
        total[...] = total[...] * shrink + jnp.sum(present, axis=0, keepdims=True)
        values = kv[slot, pl.ds(pl.multiple_of(KVD + group * HD, HD), HD), :]
        acc[...] = acc[...] * shrink + jnp.dot(
            values, present.astype(BF16), preferred_element_type=F32
        )
        return carry

    lax.fori_loop(0, chunks, step, 0)
    out[0] = acc[...] / total[...]
    lse[0] = best[...] + jnp.log(total[...])


def attend_back_kernel(
    first_head, info, kv, q, dout, lse, delta, dq, dkv, keys, values, mask, dk, dv, acc
):
    head = pl.program_id(0)
    span = q.shape[-1]
    mine = info[0]
    chunks = mine + 1
    n_ctx = kv.shape[0]

    @pl.when(head == 0)
    def _():
        dk[...] = jnp.zeros(dk.shape, F32)
        dv[...] = jnp.zeros(dv.shape, F32)

        def fill(chunk, carry):
            slot = jnp.bitwise_xor(chunk, mine)
            keys[chunk] = kv[slot, :HD, :].astype(F32).T.astype(BF16)
            values[chunk] = kv[slot, HD:, :].astype(F32).T.astype(BF16)
            fill_mask(info, mask, chunk, span)
            return carry

        lax.fori_loop(0, chunks, fill, 0)

    acc[...] = jnp.zeros(acc.shape, F32)
    queries = q[0]
    douts = dout[0]
    query_rows = queries.astype(F32).T.astype(BF16)
    dout_rows = douts.astype(F32).T.astype(BF16)

    def step(chunk, carry):
        slot = jnp.bitwise_xor(chunk, mine)
        scores = jnp.dot(keys[chunk], queries, preferred_element_type=F32) + mask[chunk]
        shares = jnp.exp(scores - lse[0])
        share_grad = jnp.dot(values[chunk], douts, preferred_element_type=F32)
        score_grad = (shares * (share_grad - delta[0])).astype(BF16)
        dv[chunk] += jnp.dot(shares.astype(BF16), dout_rows, preferred_element_type=F32)
        dk[chunk] += jnp.dot(score_grad, query_rows, preferred_element_type=F32)
        acc[...] += jnp.dot(kv[slot, :HD, :], score_grad, preferred_element_type=F32)
        return carry

    lax.fori_loop(0, chunks, step, 0)
    dq[0] = acc[...] * HD ** (-0.5)

    @pl.when(head == HEADS // KVH - 1)
    def _():
        for chunk in range(n_ctx):
            dkv[chunk, :HD, :] = dk[chunk].T.astype(BF16)
            dkv[chunk, HD:, :] = dv[chunk].T.astype(BF16)


def attend(info, kv, q):
    heads, _, span = q.shape
    n_ctx = kv.shape[0]
    per_head = lambda rows: pl.BlockSpec((1, rows, span), lambda head: (head, 0, 0))
    return pl.pallas_call(
        attend_kernel,
        grid=(heads,),
        in_specs=[
            pl.BlockSpec(memory_space=pltpu.SMEM),
            pl.BlockSpec(kv.shape, lambda head: (0, 0, 0)),
            per_head(HD),
        ],
        out_specs=[per_head(HD), per_head(1)],
        out_shape=[
            jax.ShapeDtypeStruct((heads, HD, span), F32),
            jax.ShapeDtypeStruct((heads, 1, span), F32),
        ],
        scratch_shapes=[
            pltpu.VMEM((n_ctx, KVH, span, HD), BF16),
            pltpu.VMEM((n_ctx, span, span), F32),
            pltpu.VMEM((1, span), F32),
            pltpu.VMEM((1, span), F32),
            pltpu.VMEM((HD, span), F32),
        ],
        compiler_params=pltpu.CompilerParams(vmem_limit_bytes=40 * 1024 * 1024),
        cost_estimate=pl.CostEstimate(
            flops=4 * heads * span * span * n_ctx * HD * 4,
            bytes_accessed=4 * heads * span * HD * 2,
            transcendentals=heads * span * span * n_ctx,
        ),
        name="attend",
    )(info, kv, q)


def attend_back(info, kv, q, dout, lse, delta):
    heads, _, span = q.shape
    n_ctx = kv.shape[0]
    per_head = lambda rows: pl.BlockSpec((1, rows, span), lambda head: (head, 0, 0))
    return pl.pallas_call(
        lambda *refs: attend_back_kernel(0, *refs),
        grid=(heads,),
        in_specs=[
            pl.BlockSpec(memory_space=pltpu.SMEM),
            pl.BlockSpec(kv.shape, lambda head: (0, 0, 0)),
            per_head(HD),
            per_head(HD),
            per_head(1),
            per_head(1),
        ],
        out_specs=[per_head(HD), pl.BlockSpec(kv.shape, lambda head: (0, 0, 0))],
        out_shape=[
            jax.ShapeDtypeStruct((heads, HD, span), F32),
            jax.ShapeDtypeStruct(kv.shape, BF16),
        ],
        scratch_shapes=[
            pltpu.VMEM((n_ctx, span, HD), BF16),
            pltpu.VMEM((n_ctx, span, HD), BF16),
            pltpu.VMEM((n_ctx, span, span), F32),
            pltpu.VMEM((n_ctx, span, HD), F32),
            pltpu.VMEM((n_ctx, span, HD), F32),
            pltpu.VMEM((HD, span), F32),
        ],
        compiler_params=pltpu.CompilerParams(vmem_limit_bytes=40 * 1024 * 1024),
        cost_estimate=pl.CostEstimate(
            flops=10 * heads * span * span * n_ctx * HD * 4,
            bytes_accessed=8 * heads * span * HD * 2,
            transcendentals=heads * span * span * n_ctx,
        ),
        name="attend_back",
    )(info, kv, q, dout, lse, delta)


def gram_steps(gram, rows):
    scale = 1.0 / (jnp.sqrt(jnp.trace(gram)) + 1e-07)
    gram = gram * (scale * scale)
    work = (rows * scale).astype(BF16)
    for step in range(NS_STEPS):
        low = gram.astype(BF16)
        poly = (NS_SQUARE * gram + NS_CUBIC * mm(low, low)).astype(BF16)
        work = (NS_LINEAR * work.astype(F32) + mm(work, poly)).astype(BF16)
        if step + 1 < NS_STEPS:
            first = mm(poly, low)
            second = mm(poly, first.astype(BF16))
            gram = NS_LINEAR * NS_LINEAR * gram + (2.0 * NS_LINEAR) * first + second
    return work


def on_device(
    block_input,
    cotangent,
    lengths,
    doc_starts,
    master,
    momentum,
    vectors,
    vector_first,
    vector_second,
):
    n_dp = lax.axis_size("dp")
    n_ctx = lax.axis_size("ctx")
    devices = n_dp * n_ctx
    rows = D // devices
    frows = FF // devices
    fblock = FF // n_ctx
    slots, span, width = block_input.shape
    tokens = slots * span
    group = HEADS // KVH
    qkv = QD + 2 * KVD
    my_ctx = lax.axis_index("ctx")
    me = lax.axis_index("dp") * n_ctx + my_ctx
    core_bit, x_bit = 1, 2
    ctx_bits = [core_bit, x_bit]
    dp_bits = [n_ctx << index for index in range(n_dp.bit_length() - 1)]
    all_bits = ctx_bits + dp_bits
    many = tuple([2] * len(all_bits))

    master_parts = split_rows(master[0], devices)
    momentum_parts = split_rows(momentum[0], devices)

    small = jnp.pad(vectors, ((0, 0), (0, qkv - vectors.shape[1])))
    qkv_local = jnp.concatenate(
        [jnp.concatenate(master_parts[:3], axis=1), small], axis=0
    ).astype(BF16)
    qkv_full = gather_bits(qkv_local, all_bits[::-1], me, devices, all_bits)
    qkv_full = qkv_full.reshape(devices, rows + 1, qkv)
    gain_first, gain_second, bias_query, bias_key, bias_value = [
        piece.astype(F32) for piece in split_small(qkv_full[:, rows], devices)
    ]
    w_qkv = qkv_full[:, :rows].reshape(D, qkv)
    w_out = lax.all_gather(master_parts[3].astype(BF16), BOTH, axis=0).reshape(QD, D)

    def by_ctx(part):
        return part.reshape(rows, n_dp, n_ctx, frows).transpose(2, 0, 1, 3).reshape(n_ctx, rows, fblock)

    gate_up = jnp.stack([by_ctx(master_parts[4]), by_ctx(master_parts[5])], axis=1).astype(BF16)
    gate_up = lax.all_to_all(gate_up, "ctx", split_axis=0, concat_axis=0, tiled=True)
    gate_up = gate_up.transpose(1, 0, 2, 3).reshape(2, n_ctx * rows, fblock)
    gate_up = lax.all_gather(gate_up, "dp", axis=1, tiled=True)
    w_gate, w_up = gate_up[0], gate_up[1]
    w_down = lax.all_gather(master_parts[6].astype(BF16), "dp", axis=0, tiled=True)

    def to_columns(gate, up):
        both = jnp.concatenate(
            [gate.reshape(rows, devices, frows), up.reshape(rows, devices, frows)], axis=2
        )
        both = both.transpose(1, 0, 2).astype(BF16)
        both = lax.all_to_all(both, BOTH, split_axis=0, concat_axis=0, tiled=True)
        return both.reshape(D, 2 * frows).T

    def to_rows(pair):
        both = pair.T.reshape(devices, rows, 2 * frows)
        both = lax.all_to_all(both, BOTH, split_axis=0, concat_axis=0, tiled=True)
        both = both.transpose(1, 0, 2)
        return (
            both[:, :, :frows].reshape(rows, FF),
            both[:, :, frows:].reshape(rows, FF),
        )

    momentum_pair = to_columns(momentum_parts[4], momentum_parts[5])

    length, second = lengths[0], doc_starts[0]
    places = my_ctx * span + jnp.arange(span, dtype=jnp.int32)
    doc_begin = jnp.where(places >= length, length, jnp.where(places >= second, second, 0))
    position = (places - doc_begin).astype(F32)
    live = (places < length)[:, None]
    info = jnp.stack([my_ctx, length, second]).astype(jnp.int32)
    inverse = ROPE_BASE ** (-2.0 * jnp.arange(HD // 2, dtype=F32) / HD)
    angles = inverse[:, None] * position[None, :]
    cosine, sine_part = jnp.cos(angles), jnp.sin(angles)
    cosine = jnp.concatenate([cosine, cosine], axis=0)[None]
    sine_part = jnp.concatenate([sine_part, sine_part], axis=0)[None]

    def from_ctx(value):
        other_core = swap(value, core_bit, devices)
        other_x = swap(value, x_bit, devices)
        return value, other_core, other_x, swap(other_x, core_bit, devices)

    cot_here = jnp.where(live, cotangent.reshape(tokens, width), jnp.zeros((), BF16))
    cot = from_ctx(cot_here)
    cot_halves = [jnp.concatenate(cot[:2], axis=0), jnp.concatenate(cot[2:], axis=0)]

    inputs = block_input.astype(F32).reshape(tokens, width)
    scale_one = lax.rsqrt(jnp.mean(inputs * inputs, axis=-1, keepdims=True) + NORM_EPS)
    normed_one = (inputs * scale_one * gain_first).astype(BF16)
    bias = jnp.concatenate([bias_query, bias_key, bias_value])
    pre = mm(w_qkv, normed_one, ((0,), (1,))) + bias[:, None]
    turned = rotate(
        pre[: QD + KVD].reshape(HEADS + KVH, HD, tokens), cosine, sine_part
    )
    queries = (turned[:HEADS].astype(BF16).astype(F32) * HD ** (-0.5)).astype(BF16)
    kv_here = jnp.concatenate(
        [turned[HEADS:].astype(BF16).reshape(KVD, tokens), pre[QD + KVD :].astype(BF16)], axis=0
    )
    kv = jnp.stack(from_ctx(kv_here))
    attended, log_total = attend(info, kv, queries)

    mixed_heads = attended.reshape(QD, tokens).astype(BF16)
    hidden = inputs + mm(mixed_heads, w_out, ((0,), (0,)))
    scale_two = lax.rsqrt(jnp.mean(hidden * hidden, axis=-1, keepdims=True) + NORM_EPS)
    normed_two = (hidden * scale_two * gain_second).astype(BF16)

    normed = from_ctx(normed_two)
    normed_halves = [jnp.concatenate(normed[:2], axis=0), jnp.concatenate(normed[2:], axis=0)]
    acts, gate_backs, up_backs, back_parts = [], [], [], []
    for normed_half, cot_half in zip(normed_halves, cot_halves):
        grad_act = mm(cot_half, w_down, ((1,), (1,)))
        gate_pre = mm(normed_half, w_gate)
        up_pre = mm(normed_half, w_up)
        sigmoid_gate = jax.nn.sigmoid(gate_pre)
        swish = gate_pre * sigmoid_gate
        slope = sigmoid_gate * (1.0 + gate_pre * (1.0 - sigmoid_gate))
        acts.append((swish * up_pre).astype(BF16))
        gate_backs.append((grad_act * up_pre * slope).astype(BF16))
        up_backs.append((grad_act * swish).astype(BF16))
        back_parts.append(
            (
                mm(gate_backs[-1], w_gate, ((1,), (1,))) + mm(up_backs[-1], w_up, ((1,), (1,)))
            ).astype(BF16)
        )

    def to_ctx(halves):
        crossed = swap(halves[1][span:], core_bit, devices)
        far = (halves[1][:span].astype(F32) + crossed.astype(F32)).astype(BF16)
        far = swap(far, x_bit, devices)
        near = swap(halves[0][span:], core_bit, devices)
        return halves[0][:span].astype(F32) + near.astype(F32) + far.astype(F32)

    normed_two_grad = to_ctx(back_parts)

    def over_tokens(left, right):
        return mm(left[0], right[0], ((0,), (0,))) + mm(left[1], right[1], ((0,), (0,)))

    dp_shape = tuple([2] * len(dp_bits)) + (frows, D)
    dp_first = [dp_bits, dp_bits, dp_bits[1:] + dp_bits[:1]]
    gate_sum, up_sum, down_sum = [
        scatter_sum(part.astype(BF16).reshape(dp_shape), bits, me, devices)
        for part, bits in zip(
            (
                over_tokens(gate_backs, normed_halves),
                over_tokens(up_backs, normed_halves),
                over_tokens(acts, cot_halves),
            ),
            dp_first,
        )
    ]
    out_sum = to_ctx([mm(act, w_down).astype(BF16) for act in acts])
    layer_out = jnp.where(live, hidden + out_sum, 0.0)

    out_grad = cot_here.astype(F32)
    hidden_norm_grad, grad_gain_second = norm_backward(
        hidden, scale_two, gain_second, normed_two_grad
    )
    hidden_grad = out_grad + hidden_norm_grad
    hidden_low = hidden_grad.astype(BF16)
    heads_grad = mm(w_out, hidden_low, ((1,), (1,))).astype(BF16).reshape(HEADS, HD, tokens)
    delta = jnp.sum(heads_grad.astype(F32) * attended, axis=1, keepdims=True)
    grad_output = mm(mixed_heads, hidden_low)
    query_grads, kv_grads = [], []
    for index in range(KVH):
        chosen = slice(index * group, (index + 1) * group)
        kv_one = jnp.concatenate(
            [kv[:, index * HD : (index + 1) * HD], kv[:, KVD + index * HD : KVD + (index + 1) * HD]],
            axis=1,
        )
        query_grad, kv_grad = attend_back(
            info, kv_one, queries[chosen], heads_grad[chosen], log_total[chosen], delta[chosen]
        )
        query_grads.append(query_grad)
        kv_grads.append(
            scatter_sum(kv_grad.reshape(2, 2, 2 * HD, span), ctx_bits, me, devices)
            .astype(F32)
            .reshape(2, HD, span)
        )
    qk_grad = jnp.concatenate(query_grads + [grad[:1] for grad in kv_grads], axis=0)
    qk_back = rotate_back(qk_grad, cosine, sine_part).reshape(QD + KVD, tokens)
    qkv_back = jnp.concatenate(
        [qk_back] + [grad[1] for grad in kv_grads], axis=0
    ).astype(BF16)
    grad_qkv = mm(normed_one, qkv_back, ((0,), (1,)))
    grad_bias = jnp.sum(qkv_back.astype(F32), axis=1)
    normed_one_grad = mm(qkv_back, w_qkv, ((0,), (1,)))
    input_norm_grad, grad_gain_first = norm_backward(inputs, scale_one, gain_first, normed_one_grad)
    input_grad = (hidden_grad + input_norm_grad).astype(BF16).reshape(slots, span, width)

    vector_part = join_small(
        [
            grad_gain_first,
            grad_gain_second,
            grad_bias[:QD],
            grad_bias[QD : QD + KVD],
            grad_bias[QD + KVD :],
        ],
        devices,
    )
    vector_grad = jnp.sum(
        lax.all_to_all(vector_part, BOTH, split_axis=0, concat_axis=0, tiled=True),
        axis=0,
        keepdims=True,
    )
    out_sum_rows = scatter_sum(
        grad_output.astype(BF16).reshape(many + (rows, D)), all_bits, me, devices
    )
    qkv_sum_rows = scatter_sum(
        grad_qkv.astype(BF16).reshape(many + (rows, qkv)), all_bits, me, devices
    )
    moved_qkv = MOMENTUM_DECAY * jnp.concatenate(momentum_parts[:3], axis=1) + qkv_sum_rows.astype(
        F32
    )
    moved_out = MOMENTUM_DECAY * momentum_parts[3] + out_sum_rows.astype(F32)
    moved_down = MOMENTUM_DECAY * momentum_parts[6] + down_sum.astype(F32)
    pair_sum = jnp.concatenate([gate_sum, up_sum], axis=0)
    moved_pair = MOMENTUM_DECAY * momentum_pair.astype(F32) + pair_sum.astype(F32)
    gate_rows, up_rows = to_rows(pair_sum)
    moved_gate = MOMENTUM_DECAY * momentum_parts[4] + gate_rows.astype(F32)
    moved_up = MOMENTUM_DECAY * momentum_parts[5] + up_rows.astype(F32)

    slices = [moved_pair[:frows], moved_pair[frows:], moved_down]
    dp_turn = len(dp_bits)
    orders = [
        [core_bit, x_bit] + dp_bits,
        [core_bit] + dp_bits[:1] + dp_bits[1:] + [x_bit],
        [core_bit] + dp_bits[1:] + [x_bit] + dp_bits[:1],
    ]
    wide = []
    for piece, order in zip(slices, orders):
        low = piece.astype(BF16)
        gram = mm(low, low, ((0,), (0,))).astype(BF16).reshape(many + (rows, D))
        gram = scatter_sum(gram, order, me, devices)
        gram = gather_bits(gram, order[::-1], me, devices, all_bits).reshape(D, D).astype(F32)
        wide.append(gram_steps(gram, piece))
    ortho_gate, ortho_up = to_rows(jnp.concatenate(wide[:2], axis=0))

    def gathered(part):
        breadth = part.shape[1]
        full = gather_bits(part.astype(BF16), all_bits[::-1], me, devices, all_bits)
        return full.reshape(D, breadth)

    def own_rows(whole, part):
        return gram_steps(mm(whole, whole, ((0,), (0,))), part)

    out_all = gathered(moved_out)
    ortho_out = own_rows(out_all, moved_out)
    qkv_all = gathered(moved_qkv)
    ortho_query = own_rows(qkv_all[:, :QD], moved_qkv[:, :QD])
    ortho_key = own_rows(qkv_all[:, QD : QD + KVD], moved_qkv[:, QD : QD + KVD])
    ortho_value = own_rows(qkv_all[:, QD + KVD :], moved_qkv[:, QD + KVD :])
    ortho = [ortho_query, ortho_key, ortho_value, ortho_out, ortho_gate, ortho_up, wide[2]]

    new_pieces = []
    for index, (height, breadth) in enumerate(matrix_shapes()):
        factor = math.sqrt(max(1.0, breadth / height))
        new_pieces.append(
            (
                master_parts[index] * (1.0 - MUON_RATE * MUON_DECAY)
                - MUON_RATE * factor * ortho[index].astype(F32)
            ).reshape(-1)
        )
    new_master = jnp.concatenate(new_pieces)[None, :]
    new_momentum = jnp.concatenate(
        [
            moved_qkv[:, :QD].reshape(-1),
            moved_qkv[:, QD : QD + KVD].reshape(-1),
            moved_qkv[:, QD + KVD :].reshape(-1),
            moved_out.reshape(-1),
            moved_gate.reshape(-1),
            moved_up.reshape(-1),
            moved_down.reshape(-1),
        ]
    )[None, :]
    first_new = BETA_FIRST * vector_first + (1.0 - BETA_FIRST) * vector_grad
    second_new = BETA_SECOND * vector_second + (1.0 - BETA_SECOND) * vector_grad * vector_grad
    adjusted = (
        first_new
        / (1.0 - BETA_FIRST**STEP)
        / (jnp.sqrt(second_new / (1.0 - BETA_SECOND**STEP)) + ADAM_EPS)
    )
    new_vectors = vectors - ADAM_RATE * adjusted
    return (
        layer_out.astype(BF16).reshape(slots, span, width),
        input_grad,
        new_master,
        new_momentum,
        new_master.astype(BF16),
        new_vectors,
        first_new,
        second_new,
    )


def solution(mesh):
    return jax.shard_map(
        on_device,
        mesh=mesh,
        in_specs=(
            P("dp", "ctx", None),
            P("dp", "ctx", None),
            P("dp"),
            P("dp"),
            P(BOTH, None),
            P(BOTH, None),
            P(BOTH, None),
            P(BOTH, None),
            P(BOTH, None),
        ),
        out_specs=(
            P("dp", "ctx", None),
            P("dp", "ctx", None),
            P(BOTH, None),
            P(BOTH, None),
            P(BOTH, None),
            P(BOTH, None),
            P(BOTH, None),
            P(BOTH, None),
        ),
        check_vma=False,
    )
```

```python
import math

import jax
import jax.numpy as jnp
from jax import lax
from jax.experimental import pallas as pl
from jax.experimental.pallas import tpu as pltpu
from jax.sharding import PartitionSpec as P

D = 896
HEADS = 14
KVH = 2
HD = 64
FF = 4864
SLOT = 2048
NS_STEPS = 3
STEP = 10
QD = 896
KVD = 128

NORM_EPS = 1e-06
ROPE_BASE = 1000000.0
NS_LINEAR = 3.4445
NS_SQUARE = -4.775
NS_CUBIC = 2.0315
MOMENTUM_DECAY = 0.5
MUON_RATE = 0.6
MUON_DECAY = 0.1
ADAM_RATE = 0.2
BETA_FIRST = 0.9
BETA_SECOND = 0.95
ADAM_EPS = 1e-08
MASK_FLOOR = -1e30

F32 = jnp.float32
BF16 = jnp.bfloat16
BOTH = ("dp", "ctx")


def matrix_shapes():
    return [(D, QD), (D, KVD), (D, KVD), (QD, D), (D, FF), (D, FF), (FF, D)]


def vector_sizes():
    return [D, D, QD, KVD, KVD]


def mm(left, right, contract=((1,), (0,))):
    return lax.dot_general(left, right, (contract, ((), ())), preferred_element_type=F32)


def split_rows(row, devices):
    result = []
    offset = 0
    for height, breadth in matrix_shapes():
        extent = height // devices * breadth
        result.append(row[offset : offset + extent].reshape(height // devices, breadth))
        offset += extent
    return result


def split_small(flat, devices):
    result = []
    offset = 0
    for extent_all in vector_sizes():
        extent = extent_all // devices
        result.append(flat[:, offset : offset + extent].reshape(extent_all))
        offset += extent
    return result


def join_small(pieces, devices):
    return jnp.concatenate([piece.reshape(devices, -1) for piece in pieces], axis=1)


def swap(value, mask, devices):
    return lax.ppermute(value, BOTH, [(index, index ^ mask) for index in range(devices)])


def gather_bits(value, bits, me, devices, total):
    held = value
    done = []
    for bit in bits:
        place = sum(1 for other in done if other > bit)
        got = swap(held, bit, devices)
        mine = (me & bit) != 0
        held = jnp.where(
            mine, jnp.stack([got, held], axis=place), jnp.stack([held, got], axis=place)
        )
        done.append(bit)
    return held


def scatter_start(held, left, bit, me, devices):
    left = sorted(left, reverse=True)
    axis = left.index(bit)
    mine = jnp.where((me & bit) != 0, 1, 0)
    sent = lax.dynamic_index_in_dim(held, 1 - mine, axis, keepdims=False).astype(BF16)
    kept = lax.dynamic_index_in_dim(held, mine, axis, keepdims=False)
    return kept, swap(sent, bit, devices)


def scatter_end(parts):
    return (parts[0].astype(F32) + parts[1].astype(F32)).astype(BF16)


def scatter_sum(value, bits, me, devices):
    left = list(bits)
    held = value
    for bit in bits:
        held = scatter_end(scatter_start(held, left, bit, me, devices))
        left.remove(bit)
    return held


def rotate(values, cosine, sine_part):
    midpoint = HD // 2
    turned = jnp.concatenate([-values[:, midpoint:], values[:, :midpoint]], axis=1)
    return values * cosine + turned * sine_part


def rotate_back(gradient, cosine, sine_part):
    midpoint = HD // 2
    scaled = gradient * sine_part
    turned = jnp.concatenate([scaled[:, midpoint:], -scaled[:, :midpoint]], axis=1)
    return gradient * cosine + turned


def norm_backward(source, scale_row, gain, incoming):
    gain_grad = jnp.sum(incoming * source * scale_row, axis=0)
    weighted = incoming * gain
    result = scale_row * weighted - source * scale_row**3 * jnp.mean(
        weighted * source, axis=-1, keepdims=True
    )
    return (result, gain_grad)


def fill_rows(info, kv, offset, groups, target, chunk):
    for group in range(groups):
        begin = offset + group * HD
        target[chunk, group] = kv[chunk, begin : begin + HD, :].astype(F32).T.astype(BF16)


def fill_mask(info, mask, chunk, span):
    key = chunk * span + lax.broadcasted_iota(jnp.int32, (span, span), 0)
    query = info[0] * span + lax.broadcasted_iota(jnp.int32, (span, span), 1)
    key_doc = (key >= info[2]).astype(jnp.int32) + (key >= info[1]).astype(jnp.int32)
    query_doc = (query >= info[2]).astype(jnp.int32) + (query >= info[1]).astype(jnp.int32)
    allowed = jnp.logical_and(key_doc == query_doc, key <= query)
    mask[chunk] = jnp.where(allowed, 0.0, MASK_FLOOR).astype(F32)


def attend_kernel(info, kv, q, out, lse, keys, mask, best, total, acc):
    head = pl.program_id(0)
    span = q.shape[-1]
    mine = info[0]
    chunks = mine + 1

    @pl.when(head == 0)
    def _():
        def fill(chunk, carry):
            slot = jnp.bitwise_xor(chunk, mine)
            for group in range(KVH):
                rows = kv[slot, group * HD : (group + 1) * HD, :]
                keys[chunk, group] = rows.astype(F32).T.astype(BF16)
            fill_mask(info, mask, chunk, span)
            return carry

        lax.fori_loop(0, chunks, fill, 0)

    group = head // (HEADS // KVH)
    best[...] = jnp.full(best.shape, MASK_FLOOR, F32)
    total[...] = jnp.zeros(total.shape, F32)
    acc[...] = jnp.zeros(acc.shape, F32)
    queries = q[0]

    def step(index, carry):
        chunk = mine - index
        slot = jnp.bitwise_xor(chunk, mine)
        scores = jnp.dot(keys[chunk, group], queries, preferred_element_type=F32) + mask[chunk]
        old = best[...]
        new = jnp.maximum(old, jnp.max(scores, axis=0, keepdims=True))
        present = jnp.exp(scores - new)
        shrink = jnp.exp(old - new)
        best[...] = new
        total[...] = total[...] * shrink + jnp.sum(present, axis=0, keepdims=True)
        values = kv[slot, pl.ds(pl.multiple_of(KVD + group * HD, HD), HD), :]
        acc[...] = acc[...] * shrink + jnp.dot(
            values, present.astype(BF16), preferred_element_type=F32
        )
        return carry

    lax.fori_loop(0, chunks, step, 0)
    out[0] = acc[...] / total[...]
    lse[0] = best[...] + jnp.log(total[...])


def attend_back_kernel(
    first_head, info, kv, q, dout, lse, delta, dq, dkv, keys, values, mask, dk, dv, acc
):
    head = pl.program_id(0)
    span = q.shape[-1]
    mine = info[0]
    chunks = mine + 1
    n_ctx = kv.shape[0]

    @pl.when(head == 0)
    def _():
        dk[...] = jnp.zeros(dk.shape, F32)
        dv[...] = jnp.zeros(dv.shape, F32)

        def fill(chunk, carry):
            slot = jnp.bitwise_xor(chunk, mine)
            keys[chunk] = kv[slot, :HD, :].astype(F32).T.astype(BF16)
            values[chunk] = kv[slot, HD:, :].astype(F32).T.astype(BF16)
            fill_mask(info, mask, chunk, span)
            return carry

        lax.fori_loop(0, chunks, fill, 0)

    acc[...] = jnp.zeros(acc.shape, F32)
    queries = q[0]
    douts = dout[0]
    query_rows = queries.astype(F32).T.astype(BF16)
    dout_rows = douts.astype(F32).T.astype(BF16)

    def step(chunk, carry):
        slot = jnp.bitwise_xor(chunk, mine)
        scores = jnp.dot(keys[chunk], queries, preferred_element_type=F32) + mask[chunk]
        shares = jnp.exp(scores - lse[0])
        share_grad = jnp.dot(values[chunk], douts, preferred_element_type=F32)
        score_grad = (shares * (share_grad - delta[0])).astype(BF16)
        dv[chunk] += jnp.dot(shares.astype(BF16), dout_rows, preferred_element_type=F32)
        dk[chunk] += jnp.dot(score_grad, query_rows, preferred_element_type=F32)
        acc[...] += jnp.dot(kv[slot, :HD, :], score_grad, preferred_element_type=F32)
        return carry

    lax.fori_loop(0, chunks, step, 0)
    dq[0] = acc[...] * HD ** (-0.5)

    @pl.when(head == HEADS // KVH - 1)
    def _():
        for chunk in range(n_ctx):
            dkv[chunk, :HD, :] = dk[chunk].T.astype(BF16)
            dkv[chunk, HD:, :] = dv[chunk].T.astype(BF16)


def attend(info, kv, q):
    heads, _, span = q.shape
    n_ctx = kv.shape[0]
    per_head = lambda rows: pl.BlockSpec((1, rows, span), lambda head: (head, 0, 0))
    return pl.pallas_call(
        attend_kernel,
        grid=(heads,),
        in_specs=[
            pl.BlockSpec(memory_space=pltpu.SMEM),
            pl.BlockSpec(kv.shape, lambda head: (0, 0, 0)),
            per_head(HD),
        ],
        out_specs=[per_head(HD), per_head(1)],
        out_shape=[
            jax.ShapeDtypeStruct((heads, HD, span), F32),
            jax.ShapeDtypeStruct((heads, 1, span), F32),
        ],
        scratch_shapes=[
            pltpu.VMEM((n_ctx, KVH, span, HD), BF16),
            pltpu.VMEM((n_ctx, span, span), F32),
            pltpu.VMEM((1, span), F32),
            pltpu.VMEM((1, span), F32),
            pltpu.VMEM((HD, span), F32),
        ],
        compiler_params=pltpu.CompilerParams(vmem_limit_bytes=40 * 1024 * 1024),
        cost_estimate=pl.CostEstimate(
            flops=4 * heads * span * span * n_ctx * HD * 4,
            bytes_accessed=4 * heads * span * HD * 2,
            transcendentals=heads * span * span * n_ctx,
        ),
        name="attend",
    )(info, kv, q)


def attend_back(info, kv, q, dout, lse, delta):
    heads, _, span = q.shape
    n_ctx = kv.shape[0]
    per_head = lambda rows: pl.BlockSpec((1, rows, span), lambda head: (head, 0, 0))
    return pl.pallas_call(
        lambda *refs: attend_back_kernel(0, *refs),
        grid=(heads,),
        in_specs=[
            pl.BlockSpec(memory_space=pltpu.SMEM),
            pl.BlockSpec(kv.shape, lambda head: (0, 0, 0)),
            per_head(HD),
            per_head(HD),
            per_head(1),
            per_head(1),
        ],
        out_specs=[per_head(HD), pl.BlockSpec(kv.shape, lambda head: (0, 0, 0))],
        out_shape=[
            jax.ShapeDtypeStruct((heads, HD, span), F32),
            jax.ShapeDtypeStruct(kv.shape, BF16),
        ],
        scratch_shapes=[
            pltpu.VMEM((n_ctx, span, HD), BF16),
            pltpu.VMEM((n_ctx, span, HD), BF16),
            pltpu.VMEM((n_ctx, span, span), F32),
            pltpu.VMEM((n_ctx, span, HD), F32),
            pltpu.VMEM((n_ctx, span, HD), F32),
            pltpu.VMEM((HD, span), F32),
        ],
        compiler_params=pltpu.CompilerParams(vmem_limit_bytes=40 * 1024 * 1024),
        cost_estimate=pl.CostEstimate(
            flops=10 * heads * span * span * n_ctx * HD * 4,
            bytes_accessed=8 * heads * span * HD * 2,
            transcendentals=heads * span * span * n_ctx,
        ),
        name="attend_back",
    )(info, kv, q, dout, lse, delta)


BLOCK = 128


def block_pairs(count):
    return [(low, high) for low in range(count) for high in range(low, count)]


def gram_kernel(rows, out):
    count = rows.shape[1] // BLOCK
    place = 0
    for low in range(count):
        left = rows[:, low * BLOCK : (low + 1) * BLOCK]
        line = lax.dot_general(
            left, rows[:, low * BLOCK :], (((0,), (0,)), ((), ())), preferred_element_type=F32
        ).astype(BF16)
        for high in range(low, count):
            out[place] = line[:, (high - low) * BLOCK : (high - low + 1) * BLOCK]
            place += 1
    for extra in range(place, out.shape[0]):
        out[extra] = jnp.zeros((BLOCK, BLOCK), BF16)


def gram_blocks(rows, places):
    return pl.pallas_call(
        gram_kernel,
        out_shape=jax.ShapeDtypeStruct((places, BLOCK, BLOCK), BF16),
        compiler_params=pltpu.CompilerParams(vmem_limit_bytes=32 * 1024 * 1024),
        name="gram",
    )(rows)


def newton_schulz(gram, low, poly, mixed, rows):
    size = gram.shape[0]
    part = size // 2 if size % 16 == 0 and size > BLOCK else size
    parts = [pl.ds(begin, part) for begin in range(0, size, part)]
    row_id = lax.broadcasted_iota(jnp.int32, (size, size), 0)
    column_id = lax.broadcasted_iota(jnp.int32, (size, size), 1)
    square = jnp.where(row_id == column_id, gram[...], 0.0)
    square = jnp.sum(jnp.sum(square, axis=0, keepdims=True), axis=1, keepdims=True)
    scale = 1.0 / (jnp.sqrt(square) + 1e-07)
    for place in parts:
        scaled = gram[place, :] * (scale * scale)
        gram[place, :] = scaled
        low[place, :] = scaled.astype(BF16)
    work = (rows * scale).astype(BF16)
    for step in range(NS_STEPS):
        for place in parts:
            second = jnp.dot(low[place, :], low[...], preferred_element_type=F32)
            poly[place, :] = (NS_SQUARE * gram[place, :] + NS_CUBIC * second).astype(BF16)
        moved = jnp.dot(work, poly[...], preferred_element_type=F32)
        work = (NS_LINEAR * work.astype(F32) + moved).astype(BF16)
        if step + 1 < NS_STEPS:
            for place in parts:
                first = jnp.dot(poly[place, :], low[...], preferred_element_type=F32)
                mixed[place, :] = first.astype(BF16)
                gram[place, :] = (
                    NS_LINEAR * NS_LINEAR * gram[place, :] + (2.0 * NS_LINEAR) * first
                )
            for place in parts:
                second = jnp.dot(poly[place, :], mixed[...], preferred_element_type=F32)
                renewed = gram[place, :] + second
                gram[place, :] = renewed
                low[place, :] = renewed.astype(BF16)
    return work


def wide_kernel(blocks, rows, out, gram, low, poly, mixed):
    for place, (first, second) in enumerate(block_pairs(gram.shape[0] // BLOCK)):
        tile = blocks[place].astype(F32)
        gram[first * BLOCK : (first + 1) * BLOCK, second * BLOCK : (second + 1) * BLOCK] = tile
        if first != second:
            gram[second * BLOCK : (second + 1) * BLOCK, first * BLOCK : (first + 1) * BLOCK] = tile.T
    out[...] = newton_schulz(gram, low, poly, mixed, rows[...])


def square_scratch(size):
    return [
        pltpu.VMEM((size, size), F32),
        pltpu.VMEM((size, size), BF16),
        pltpu.VMEM((size, size), BF16),
        pltpu.VMEM((size, size), BF16),
    ]


def orthogonal_wide(blocks, rows):
    return pl.pallas_call(
        wide_kernel,
        out_shape=jax.ShapeDtypeStruct(rows.shape, BF16),
        scratch_shapes=square_scratch(rows.shape[1]),
        compiler_params=pltpu.CompilerParams(vmem_limit_bytes=40 * 1024 * 1024),
        cost_estimate=pl.CostEstimate(
            flops=14 * rows.shape[1] ** 3, bytes_accessed=4 * rows.size, transcendentals=0
        ),
        name="newton_wide",
    )(blocks, rows)


def whole_kernel(widths, whole, rows, out, *scratch):
    begin = 0
    for index, width in enumerate(widths):
        gram, low, poly, mixed = scratch[4 * index : 4 * index + 4]
        for first in range(0, width, BLOCK):
            gram[first : first + BLOCK, :] = lax.dot_general(
                whole[:, begin + first : begin + first + BLOCK],
                whole[:, begin : begin + width],
                (((0,), (0,)), ((), ())),
                preferred_element_type=F32,
            )
        out[:, begin : begin + width] = newton_schulz(
            gram, low, poly, mixed, rows[:, begin : begin + width]
        )
        begin += width


def orthogonal_whole(whole, rows, widths):
    scratch = []
    for width in widths:
        scratch += square_scratch(width)
    return pl.pallas_call(
        lambda *refs: whole_kernel(widths, *refs),
        out_shape=jax.ShapeDtypeStruct(rows.shape, BF16),
        scratch_shapes=scratch,
        compiler_params=pltpu.CompilerParams(vmem_limit_bytes=48 * 1024 * 1024),
        cost_estimate=pl.CostEstimate(
            flops=16 * sum(width**3 for width in widths),
            bytes_accessed=2 * whole.size,
            transcendentals=0,
        ),
        name="newton_whole",
    )(whole, rows)


def on_device(
    block_input,
    cotangent,
    lengths,
    doc_starts,
    master,
    momentum,
    vectors,
    vector_first,
    vector_second,
):
    n_dp = lax.axis_size("dp")
    n_ctx = lax.axis_size("ctx")
    devices = n_dp * n_ctx
    rows = D // devices
    frows = FF // devices
    fblock = FF // n_ctx
    slots, span, width = block_input.shape
    tokens = slots * span
    group = HEADS // KVH
    qkv = QD + 2 * KVD
    my_ctx = lax.axis_index("ctx")
    me = lax.axis_index("dp") * n_ctx + my_ctx
    core_bit, x_bit = 1, 2
    ctx_bits = [core_bit, x_bit]
    dp_bits = [n_ctx << index for index in range(n_dp.bit_length() - 1)]
    all_bits = ctx_bits + dp_bits
    many = tuple([2] * len(all_bits))
    padded = (rows // 16 + 1) * 16

    def padded_rows(part):
        return jnp.pad(part, ((0, padded - rows), (0, 0)))

    def padded_pieces(part):
        part = part.reshape(devices, rows, part.shape[1])
        part = jnp.pad(part, ((0, 0), (0, padded - rows), (0, 0)))
        return part.reshape(many + part.shape[1:])

    master_parts = split_rows(master[0], devices)
    momentum_parts = split_rows(momentum[0], devices)

    small = jnp.pad(vectors, ((0, padded - rows - 1), (0, qkv - vectors.shape[1])))
    qkv_local = jnp.concatenate(
        [jnp.concatenate(master_parts[:3], axis=1), small], axis=0
    ).astype(BF16)
    qkv_full = gather_bits(qkv_local, all_bits[::-1], me, devices, all_bits)
    qkv_full = qkv_full.reshape(devices, padded, qkv)
    gain_first, gain_second, bias_query, bias_key, bias_value = [
        piece.astype(F32) for piece in split_small(qkv_full[:, rows], devices)
    ]
    w_qkv = qkv_full[:, :rows].reshape(D, qkv)
    w_out = gather_bits(
        padded_rows(master_parts[3]).astype(BF16), all_bits[::-1], me, devices, all_bits
    )
    w_out = w_out.reshape(devices, padded, D)[:, :rows].reshape(QD, D)

    def by_ctx(part):
        return part.reshape(rows, n_dp, n_ctx, frows).transpose(2, 0, 1, 3).reshape(n_ctx, rows, fblock)

    gate_up = jnp.stack([by_ctx(master_parts[4]), by_ctx(master_parts[5])], axis=1).astype(BF16)
    gate_up = lax.all_to_all(gate_up, "ctx", split_axis=0, concat_axis=0, tiled=True)
    w_gate, w_up = [
        lax.all_gather(gate_up[:, index].reshape(n_ctx * rows, fblock), "dp", axis=0, tiled=True)
        for index in range(2)
    ]
    w_down = lax.all_gather(master_parts[6].astype(BF16), "dp", axis=0, tiled=True)

    def to_columns(gate, up):
        both = jnp.concatenate(
            [gate.reshape(rows, devices, frows), up.reshape(rows, devices, frows)], axis=2
        )
        both = both.transpose(1, 0, 2).astype(BF16)
        both = lax.all_to_all(both, BOTH, split_axis=0, concat_axis=0, tiled=True)
        return both.reshape(D, 2 * frows).T

    def to_rows(pair):
        both = pair.T.reshape(devices, rows, 2 * frows)
        both = lax.all_to_all(both, BOTH, split_axis=0, concat_axis=0, tiled=True)
        both = both.transpose(1, 0, 2)
        return (
            both[:, :, :frows].reshape(rows, FF),
            both[:, :, frows:].reshape(rows, FF),
        )

    momentum_pair = to_columns(momentum_parts[4], momentum_parts[5])

    length, second = lengths[0], doc_starts[0]
    places = my_ctx * span + jnp.arange(span, dtype=jnp.int32)
    doc_begin = jnp.where(places >= length, length, jnp.where(places >= second, second, 0))
    position = (places - doc_begin).astype(F32)
    live = (places < length)[:, None]
    info = jnp.stack([my_ctx, length, second]).astype(jnp.int32)
    inverse = ROPE_BASE ** (-2.0 * jnp.arange(HD // 2, dtype=F32) / HD)
    angles = inverse[:, None] * position[None, :]
    cosine, sine_part = jnp.cos(angles), jnp.sin(angles)
    cosine = jnp.concatenate([cosine, cosine], axis=0)[None]
    sine_part = jnp.concatenate([sine_part, sine_part], axis=0)[None]

    def from_ctx(value):
        other_core = swap(value, core_bit, devices)
        other_x = swap(value, x_bit, devices)
        return value, other_core, other_x, swap(other_x, core_bit, devices)

    cot_here = jnp.where(live, cotangent.reshape(tokens, width), jnp.zeros((), BF16))
    cot = from_ctx(cot_here)
    cot_halves = [jnp.concatenate(cot[:2], axis=0), jnp.concatenate(cot[2:], axis=0)]

    inputs = block_input.astype(F32).reshape(tokens, width)
    scale_one = lax.rsqrt(jnp.mean(inputs * inputs, axis=-1, keepdims=True) + NORM_EPS)
    normed_one = (inputs * scale_one * gain_first).astype(BF16)
    bias = jnp.concatenate([bias_query, bias_key, bias_value])
    pre = mm(w_qkv, normed_one, ((0,), (1,))) + bias[:, None]
    turned = rotate(
        pre[: QD + KVD].reshape(HEADS + KVH, HD, tokens), cosine, sine_part
    )
    queries = (turned[:HEADS].astype(BF16).astype(F32) * HD ** (-0.5)).astype(BF16)
    kv_here = jnp.concatenate(
        [turned[HEADS:].astype(BF16).reshape(KVD, tokens), pre[QD + KVD :].astype(BF16)], axis=0
    )
    kv = jnp.stack(from_ctx(kv_here))
    attended, log_total = attend(info, kv, queries)

    mixed_heads = attended.reshape(QD, tokens).astype(BF16)
    hidden = inputs + mm(mixed_heads, w_out, ((0,), (0,)))
    scale_two = lax.rsqrt(jnp.mean(hidden * hidden, axis=-1, keepdims=True) + NORM_EPS)
    normed_two = (hidden * scale_two * gain_second).astype(BF16)

    normed = from_ctx(normed_two)
    normed_halves = [jnp.concatenate(normed[:2], axis=0), jnp.concatenate(normed[2:], axis=0)]
    acts, gate_backs, up_backs, back_parts = [], [], [], []
    for normed_half, cot_half in zip(normed_halves, cot_halves):
        grad_act = mm(cot_half, w_down, ((1,), (1,)))
        gate_pre = mm(normed_half, w_gate)
        up_pre = mm(normed_half, w_up)
        sigmoid_gate = jax.nn.sigmoid(gate_pre)
        swish = gate_pre * sigmoid_gate
        slope = sigmoid_gate * (1.0 + gate_pre * (1.0 - sigmoid_gate))
        acts.append((swish * up_pre).astype(BF16))
        gate_backs.append((grad_act * up_pre * slope).astype(BF16))
        up_backs.append((grad_act * swish).astype(BF16))
        back_parts.append(
            (
                mm(gate_backs[-1], w_gate, ((1,), (1,))) + mm(up_backs[-1], w_up, ((1,), (1,)))
            ).astype(BF16)
        )

    def to_ctx(halves):
        crossed = swap(halves[1][span:], core_bit, devices)
        far = (halves[1][:span].astype(F32) + crossed.astype(F32)).astype(BF16)
        near = swap(halves[0][span:], core_bit, devices)
        near = halves[0][:span].astype(F32) + near.astype(F32)
        return near + swap(far, x_bit, devices).astype(F32), far

    normed_two_grad, ready = to_ctx(back_parts)
    (acts, gate_backs, up_backs), ready = lax.optimization_barrier(
        ((acts, gate_backs, up_backs), ready)
    )

    def over_tokens(left, right):
        return mm(left[0], right[0], ((0,), (0,))) + mm(left[1], right[1], ((0,), (0,)))

    dp_shape = tuple([2] * len(dp_bits)) + (frows, D)
    dp_order = dp_bits[1:] + dp_bits[:1]
    down_parts = scatter_start(
        over_tokens(acts, cot_halves).astype(BF16).reshape(dp_shape), dp_bits, dp_order[0], me, devices
    )
    gate_parts = scatter_start(
        over_tokens(gate_backs, normed_halves).astype(BF16).reshape(dp_shape),
        dp_bits,
        dp_bits[0],
        me,
        devices,
    )
    up_parts = scatter_start(
        over_tokens(up_backs, normed_halves).astype(BF16).reshape(dp_shape),
        dp_bits,
        dp_bits[0],
        me,
        devices,
    )
    out_sum, _ = to_ctx([mm(act, w_down).astype(BF16) for act in acts])
    layer_out = jnp.where(live, hidden + out_sum, 0.0)

    out_grad = cot_here.astype(F32)
    hidden_norm_grad, grad_gain_second = norm_backward(
        hidden, scale_two, gain_second, normed_two_grad
    )
    hidden_grad = out_grad + hidden_norm_grad
    hidden_low = hidden_grad.astype(BF16)
    heads_grad = mm(w_out, hidden_low, ((1,), (1,))).astype(BF16).reshape(HEADS, HD, tokens)
    delta = jnp.sum(heads_grad.astype(F32) * attended, axis=1, keepdims=True)
    grad_output = mm(mixed_heads, hidden_low)
    query_grads, kv_parts = [], []
    wide_parts = [gate_parts, up_parts, down_parts]
    wide_orders = [list(dp_bits), list(dp_bits), list(dp_order)]
    for index in range(KVH):
        chosen = slice(index * group, (index + 1) * group)
        kv_one = jnp.concatenate(
            [kv[:, index * HD : (index + 1) * HD], kv[:, KVD + index * HD : KVD + (index + 1) * HD]],
            axis=1,
        )
        query_grad, kv_grad = attend_back(
            info, kv_one, queries[chosen], heads_grad[chosen], log_total[chosen], delta[chosen]
        )
        (query_grad, kv_grad), wide_parts = lax.optimization_barrier(
            ((query_grad, kv_grad), wide_parts)
        )
        query_grads.append(query_grad)
        kv_parts.append(
            scatter_sum(kv_grad.reshape(2, 2, 2 * HD, span), ctx_bits, me, devices)
        )
        for place in range(3):
            wide_orders[place].pop(0)
            if wide_orders[place]:
                wide_parts[place] = scatter_start(
                    scatter_end(wide_parts[place]),
                    wide_orders[place],
                    wide_orders[place][0],
                    me,
                    devices,
                )
    kv_grads = [part.astype(F32).reshape(2, HD, span) for part in kv_parts]
    qk_grad = jnp.concatenate(query_grads + [grad[:1] for grad in kv_grads], axis=0)
    qk_back = rotate_back(qk_grad, cosine, sine_part).reshape(QD + KVD, tokens)
    qkv_back = jnp.concatenate(
        [qk_back] + [grad[1] for grad in kv_grads], axis=0
    ).astype(BF16)
    grad_qkv = mm(normed_one, qkv_back, ((0,), (1,)))
    grad_bias = jnp.sum(qkv_back.astype(F32), axis=1)
    normed_one_grad = mm(qkv_back, w_qkv, ((0,), (1,)))
    input_norm_grad, grad_gain_first = norm_backward(inputs, scale_one, gain_first, normed_one_grad)
    input_grad = (hidden_grad + input_norm_grad).astype(BF16).reshape(slots, span, width)

    vector_part = join_small(
        [
            grad_gain_first,
            grad_gain_second,
            grad_bias[:QD],
            grad_bias[QD : QD + KVD],
            grad_bias[QD + KVD :],
        ],
        devices,
    )
    vector_grad = jnp.sum(
        lax.all_to_all(vector_part, BOTH, split_axis=0, concat_axis=0, tiled=True),
        axis=0,
        keepdims=True,
    )
    grad_qkv, wide_parts = lax.optimization_barrier((grad_qkv, wide_parts))
    gate_sum, up_sum, down_sum = [
        scatter_sum(scatter_end(parts), order[1:], me, devices)
        for parts, order in zip(wide_parts, wide_orders)
    ]
    out_sum_rows = scatter_sum(padded_pieces(grad_output.astype(BF16)), all_bits, me, devices)
    qkv_sum_rows = scatter_sum(padded_pieces(grad_qkv.astype(BF16)), all_bits, me, devices)
    moved_qkv = MOMENTUM_DECAY * padded_rows(
        jnp.concatenate(momentum_parts[:3], axis=1)
    ) + qkv_sum_rows.astype(F32)
    moved_out = MOMENTUM_DECAY * padded_rows(momentum_parts[3]) + out_sum_rows.astype(F32)
    moved_down = MOMENTUM_DECAY * momentum_parts[6] + down_sum.astype(F32)
    pair_sum = jnp.concatenate([gate_sum, up_sum], axis=0)
    moved_pair = MOMENTUM_DECAY * momentum_pair.astype(F32) + pair_sum.astype(F32)
    gate_rows, up_rows = to_rows(pair_sum)
    moved_gate = MOMENTUM_DECAY * momentum_parts[4] + gate_rows.astype(F32)
    moved_up = MOMENTUM_DECAY * momentum_parts[5] + up_rows.astype(F32)

    slices = [moved_pair[:frows], moved_pair[frows:], moved_down]
    places = len(block_pairs(D // BLOCK))
    grams = [gram_blocks(piece.astype(BF16), places) for piece in slices]
    grams = [lax.psum(gram, BOTH) for gram in grams]
    wide = [orthogonal_wide(gram, piece) for gram, piece in zip(grams, slices)]
    ortho_gate, ortho_up = to_rows(jnp.concatenate(wide[:2], axis=0))

    def gathered(part):
        full = gather_bits(part.astype(BF16), all_bits[::-1], me, devices, all_bits)
        return full.reshape(devices * padded, part.shape[1])

    ortho_out = orthogonal_whole(gathered(moved_out), moved_out, (D,))[:rows]
    ortho_qkv = orthogonal_whole(gathered(moved_qkv), moved_qkv, (QD, KVD, KVD))[:rows]
    ortho = [
        ortho_qkv[:, :QD],
        ortho_qkv[:, QD : QD + KVD],
        ortho_qkv[:, QD + KVD :],
        ortho_out,
        ortho_gate,
        ortho_up,
        wide[2],
    ]
    moved_qkv, moved_out = moved_qkv[:rows], moved_out[:rows]

    new_pieces = []
    for index, (height, breadth) in enumerate(matrix_shapes()):
        factor = math.sqrt(max(1.0, breadth / height))
        new_pieces.append(
            (
                master_parts[index] * (1.0 - MUON_RATE * MUON_DECAY)
                - MUON_RATE * factor * ortho[index].astype(F32)
            ).reshape(-1)
        )
    new_master = jnp.concatenate(new_pieces)[None, :]
    new_momentum = jnp.concatenate(
        [
            moved_qkv[:, :QD].reshape(-1),
            moved_qkv[:, QD : QD + KVD].reshape(-1),
            moved_qkv[:, QD + KVD :].reshape(-1),
            moved_out.reshape(-1),
            moved_gate.reshape(-1),
            moved_up.reshape(-1),
            moved_down.reshape(-1),
        ]
    )[None, :]
    first_new = BETA_FIRST * vector_first + (1.0 - BETA_FIRST) * vector_grad
    second_new = BETA_SECOND * vector_second + (1.0 - BETA_SECOND) * vector_grad * vector_grad
    adjusted = (
        first_new
        / (1.0 - BETA_FIRST**STEP)
        / (jnp.sqrt(second_new / (1.0 - BETA_SECOND**STEP)) + ADAM_EPS)
    )
    new_vectors = vectors - ADAM_RATE * adjusted
    return (
        layer_out.astype(BF16).reshape(slots, span, width),
        input_grad,
        new_master,
        new_momentum,
        new_master.astype(BF16),
        new_vectors,
        first_new,
        second_new,
    )


def solution(mesh):
    return jax.shard_map(
        on_device,
        mesh=mesh,
        in_specs=(
            P("dp", "ctx", None),
            P("dp", "ctx", None),
            P("dp"),
            P("dp"),
            P(BOTH, None),
            P(BOTH, None),
            P(BOTH, None),
            P(BOTH, None),
            P(BOTH, None),
        ),
        out_specs=(
            P("dp", "ctx", None),
            P("dp", "ctx", None),
            P(BOTH, None),
            P(BOTH, None),
            P(BOTH, None),
            P(BOTH, None),
            P(BOTH, None),
            P(BOTH, None),
        ),
        check_vma=False,
    )
```

```python
import math

import jax
import jax.numpy as jnp
from jax import lax
from jax.experimental import pallas as pl
from jax.experimental.pallas import tpu as pltpu
from jax.sharding import PartitionSpec as P

D = 896
HEADS = 14
KVH = 2
HD = 64
FF = 4864
SLOT = 2048
NS_STEPS = 3
STEP = 10
QD = 896
KVD = 128

NORM_EPS = 1e-06
ROPE_BASE = 1000000.0
NS_LINEAR = 3.4445
NS_SQUARE = -4.775
NS_CUBIC = 2.0315
MOMENTUM_DECAY = 0.5
MUON_RATE = 0.6
MUON_DECAY = 0.1
ADAM_RATE = 0.2
BETA_FIRST = 0.9
BETA_SECOND = 0.95
ADAM_EPS = 1e-08
MASK_FLOOR = -1e30

F32 = jnp.float32
BF16 = jnp.bfloat16
BOTH = ("dp", "ctx")
LANES = 128


def matrix_shapes():
    return [(D, QD), (D, KVD), (D, KVD), (QD, D), (D, FF), (D, FF), (FF, D)]


def vector_sizes():
    return [D, D, QD, KVD, KVD]


def mm(left, right, contract=((1,), (0,))):
    return lax.dot_general(left, right, (contract, ((), ())), preferred_element_type=F32)


def split_small(flat, devices):
    result = []
    offset = 0
    for extent_all in vector_sizes():
        extent = extent_all // devices
        result.append(flat[:, offset : offset + extent].reshape(extent_all))
        offset += extent
    return result


def join_small(pieces, devices):
    return jnp.concatenate([piece.reshape(devices, -1) for piece in pieces], axis=1)


def swap(value, mask, devices):
    return lax.ppermute(value, BOTH, [(index, index ^ mask) for index in range(devices)])


def gather_bits(value, bits, me, devices, total):
    held = value
    done = []
    for bit in bits:
        place = sum(1 for other in done if other > bit)
        got = swap(held, bit, devices)
        mine = (me & bit) != 0
        held = jnp.where(
            mine, jnp.stack([got, held], axis=place), jnp.stack([held, got], axis=place)
        )
        done.append(bit)
    return held


def scatter_start(held, left, bit, me, devices):
    left = sorted(left, reverse=True)
    axis = left.index(bit)
    mine = jnp.where((me & bit) != 0, 1, 0)
    sent = lax.dynamic_index_in_dim(held, 1 - mine, axis, keepdims=False).astype(BF16)
    kept = lax.dynamic_index_in_dim(held, mine, axis, keepdims=False)
    return kept, swap(sent, bit, devices)


def scatter_end(parts):
    return (parts[0].astype(F32) + parts[1].astype(F32)).astype(BF16)


def scatter_sum(value, bits, me, devices):
    left = list(bits)
    held = value
    for bit in bits:
        held = scatter_end(scatter_start(held, left, bit, me, devices))
        left.remove(bit)
    return held


def rotate(values, cosine, sine_part):
    midpoint = HD // 2
    turned = jnp.concatenate([-values[:, midpoint:], values[:, :midpoint]], axis=1)
    return values * cosine + turned * sine_part


def rotate_back(gradient, cosine, sine_part):
    midpoint = HD // 2
    scaled = gradient * sine_part
    turned = jnp.concatenate([scaled[:, midpoint:], -scaled[:, :midpoint]], axis=1)
    return gradient * cosine + turned


def norm_backward(source, scale_row, gain, incoming):
    gain_grad = jnp.sum(incoming * source * scale_row, axis=0)
    weighted = incoming * gain
    result = scale_row * weighted - source * scale_row**3 * jnp.mean(
        weighted * source, axis=-1, keepdims=True
    )
    return (result, gain_grad)


def fill_rows(info, kv, offset, groups, target, chunk):
    for group in range(groups):
        begin = offset + group * HD
        target[chunk, group] = kv[chunk, begin : begin + HD, :].astype(F32).T.astype(BF16)


def fill_mask(info, mask, chunk, span):
    key = chunk * span + lax.broadcasted_iota(jnp.int32, (span, span), 0)
    query = info[0] * span + lax.broadcasted_iota(jnp.int32, (span, span), 1)
    key_doc = (key >= info[2]).astype(jnp.int32) + (key >= info[1]).astype(jnp.int32)
    query_doc = (query >= info[2]).astype(jnp.int32) + (query >= info[1]).astype(jnp.int32)
    allowed = jnp.logical_and(key_doc == query_doc, key <= query)
    mask[chunk] = jnp.where(allowed, 0.0, MASK_FLOOR).astype(F32)


def attend_kernel(info, kv, q, out, lse, keys, mask, best, total, acc):
    head = pl.program_id(0)
    span = q.shape[-1]
    mine = info[0]
    chunks = mine + 1

    @pl.when(head == 0)
    def _():
        def fill(chunk, carry):
            slot = jnp.bitwise_xor(chunk, mine)
            for group in range(KVH):
                rows = kv[slot, group * HD : (group + 1) * HD, :]
                keys[chunk, group] = rows.astype(F32).T.astype(BF16)
            fill_mask(info, mask, chunk, span)
            return carry

        lax.fori_loop(0, chunks, fill, 0)

    group = head // (HEADS // KVH)
    best[...] = jnp.full(best.shape, MASK_FLOOR, F32)
    total[...] = jnp.zeros(total.shape, F32)
    acc[...] = jnp.zeros(acc.shape, F32)
    queries = q[0]

    def step(index, carry):
        chunk = mine - index
        slot = jnp.bitwise_xor(chunk, mine)
        scores = jnp.dot(keys[chunk, group], queries, preferred_element_type=F32) + mask[chunk]
        old = best[...]
        new = jnp.maximum(old, jnp.max(scores, axis=0, keepdims=True))
        present = jnp.exp(scores - new)
        shrink = jnp.exp(old - new)
        best[...] = new
        total[...] = total[...] * shrink + jnp.sum(present, axis=0, keepdims=True)
        values = kv[slot, pl.ds(pl.multiple_of(KVD + group * HD, HD), HD), :]
        acc[...] = acc[...] * shrink + jnp.dot(
            values, present.astype(BF16), preferred_element_type=F32
        )
        return carry

    lax.fori_loop(0, chunks, step, 0)
    out[0] = acc[...] / total[...]
    lse[0] = best[...] + jnp.log(total[...])


def attend_back_kernel(
    first_head, info, kv, q, dout, lse, delta, dq, dkv, keys, values, mask, dk, dv, acc
):
    head = pl.program_id(0)
    span = q.shape[-1]
    mine = info[0]
    chunks = mine + 1
    n_ctx = kv.shape[0]

    @pl.when(head == 0)
    def _():
        dk[...] = jnp.zeros(dk.shape, F32)
        dv[...] = jnp.zeros(dv.shape, F32)

        def fill(chunk, carry):
            slot = jnp.bitwise_xor(chunk, mine)
            keys[chunk] = kv[slot, :HD, :].astype(F32).T.astype(BF16)
            values[chunk] = kv[slot, HD:, :].astype(F32).T.astype(BF16)
            fill_mask(info, mask, chunk, span)
            return carry

        lax.fori_loop(0, chunks, fill, 0)

    acc[...] = jnp.zeros(acc.shape, F32)
    queries = q[0]
    douts = dout[0]
    query_rows = queries.astype(F32).T.astype(BF16)
    dout_rows = douts.astype(F32).T.astype(BF16)

    def step(chunk, carry):
        slot = jnp.bitwise_xor(chunk, mine)
        scores = jnp.dot(keys[chunk], queries, preferred_element_type=F32) + mask[chunk]
        shares = jnp.exp(scores - lse[0])
        share_grad = jnp.dot(values[chunk], douts, preferred_element_type=F32)
        score_grad = (shares * (share_grad - delta[0])).astype(BF16)
        dv[chunk] += jnp.dot(shares.astype(BF16), dout_rows, preferred_element_type=F32)
        dk[chunk] += jnp.dot(score_grad, query_rows, preferred_element_type=F32)
        acc[...] += jnp.dot(kv[slot, :HD, :], score_grad, preferred_element_type=F32)
        return carry

    lax.fori_loop(0, chunks, step, 0)
    dq[0] = acc[...] * HD ** (-0.5)

    @pl.when(head == HEADS // KVH - 1)
    def _():
        for chunk in range(n_ctx):
            dkv[chunk, :HD, :] = dk[chunk].T.astype(BF16)
            dkv[chunk, HD:, :] = dv[chunk].T.astype(BF16)


def attend(info, kv, q):
    heads, _, span = q.shape
    n_ctx = kv.shape[0]
    per_head = lambda rows: pl.BlockSpec((1, rows, span), lambda head: (head, 0, 0))
    return pl.pallas_call(
        attend_kernel,
        grid=(heads,),
        in_specs=[
            pl.BlockSpec(memory_space=pltpu.SMEM),
            pl.BlockSpec(kv.shape, lambda head: (0, 0, 0)),
            per_head(HD),
        ],
        out_specs=[per_head(HD), per_head(1)],
        out_shape=[
            jax.ShapeDtypeStruct((heads, HD, span), F32),
            jax.ShapeDtypeStruct((heads, 1, span), F32),
        ],
        scratch_shapes=[
            pltpu.VMEM((n_ctx, KVH, span, HD), BF16),
            pltpu.VMEM((n_ctx, span, span), F32),
            pltpu.VMEM((1, span), F32),
            pltpu.VMEM((1, span), F32),
            pltpu.VMEM((HD, span), F32),
        ],
        compiler_params=pltpu.CompilerParams(vmem_limit_bytes=40 * 1024 * 1024),
        cost_estimate=pl.CostEstimate(
            flops=4 * heads * span * span * n_ctx * HD * 4,
            bytes_accessed=4 * heads * span * HD * 2,
            transcendentals=heads * span * span * n_ctx,
        ),
        name="attend",
    )(info, kv, q)


def attend_back(info, kv, q, dout, lse, delta):
    heads, _, span = q.shape
    n_ctx = kv.shape[0]
    per_head = lambda rows: pl.BlockSpec((1, rows, span), lambda head: (head, 0, 0))
    return pl.pallas_call(
        lambda *refs: attend_back_kernel(0, *refs),
        grid=(heads,),
        in_specs=[
            pl.BlockSpec(memory_space=pltpu.SMEM),
            pl.BlockSpec(kv.shape, lambda head: (0, 0, 0)),
            per_head(HD),
            per_head(HD),
            per_head(1),
            per_head(1),
        ],
        out_specs=[per_head(HD), pl.BlockSpec(kv.shape, lambda head: (0, 0, 0))],
        out_shape=[
            jax.ShapeDtypeStruct((heads, HD, span), F32),
            jax.ShapeDtypeStruct(kv.shape, BF16),
        ],
        scratch_shapes=[
            pltpu.VMEM((n_ctx, span, HD), BF16),
            pltpu.VMEM((n_ctx, span, HD), BF16),
            pltpu.VMEM((n_ctx, span, span), F32),
            pltpu.VMEM((n_ctx, span, HD), F32),
            pltpu.VMEM((n_ctx, span, HD), F32),
            pltpu.VMEM((HD, span), F32),
        ],
        compiler_params=pltpu.CompilerParams(vmem_limit_bytes=40 * 1024 * 1024),
        cost_estimate=pl.CostEstimate(
            flops=10 * heads * span * span * n_ctx * HD * 4,
            bytes_accessed=8 * heads * span * HD * 2,
            transcendentals=heads * span * span * n_ctx,
        ),
        name="attend_back",
    )(info, kv, q, dout, lse, delta)


BLOCK = 128


def block_pairs(count):
    return [(low, high) for low in range(count) for high in range(low, count)]


def gram_kernel(rows, out):
    count = rows.shape[2] // BLOCK
    for which in range(rows.shape[0]):
        place = 0
        for low in range(count):
            line = lax.dot_general(
                rows[which, :, low * BLOCK : (low + 1) * BLOCK],
                rows[which, :, low * BLOCK :],
                (((0,), (0,)), ((), ())),
                preferred_element_type=F32,
            ).astype(BF16)
            for high in range(low, count):
                out[place, which] = line[:, (high - low) * BLOCK : (high - low + 1) * BLOCK]
                place += 1
        for extra in range(place, out.shape[0]):
            out[extra, which] = jnp.zeros((BLOCK, BLOCK), BF16)


def gram_blocks(rows, places):
    return pl.pallas_call(
        gram_kernel,
        out_shape=jax.ShapeDtypeStruct((places, rows.shape[0], BLOCK, BLOCK), BF16),
        compiler_params=pltpu.CompilerParams(vmem_limit_bytes=32 * 1024 * 1024),
        name="gram",
    )(rows)


def newton_schulz(gram, low, poly, mixed, rows):
    size = gram.shape[0]
    part = size // 2 if size % 16 == 0 and size > BLOCK else size
    parts = [pl.ds(begin, part) for begin in range(0, size, part)]
    row_id = lax.broadcasted_iota(jnp.int32, (size, size), 0)
    column_id = lax.broadcasted_iota(jnp.int32, (size, size), 1)
    square = jnp.where(row_id == column_id, gram[...], 0.0)
    square = jnp.sum(jnp.sum(square, axis=0, keepdims=True), axis=1, keepdims=True)
    scale = 1.0 / (jnp.sqrt(square) + 1e-07)
    for place in parts:
        scaled = gram[place, :] * (scale * scale)
        gram[place, :] = scaled
        low[place, :] = scaled.astype(BF16)
    work = (rows * scale).astype(BF16)
    for step in range(NS_STEPS):
        for place in parts:
            second = jnp.dot(low[place, :], low[...], preferred_element_type=F32)
            poly[place, :] = (NS_SQUARE * gram[place, :] + NS_CUBIC * second).astype(BF16)
        moved = jnp.dot(work, poly[...], preferred_element_type=F32)
        work = (NS_LINEAR * work.astype(F32) + moved).astype(BF16)
        if step + 1 < NS_STEPS:
            for place in parts:
                first = jnp.dot(poly[place, :], low[...], preferred_element_type=F32)
                mixed[place, :] = first.astype(BF16)
                gram[place, :] = (
                    NS_LINEAR * NS_LINEAR * gram[place, :] + (2.0 * NS_LINEAR) * first
                )
            for place in parts:
                second = jnp.dot(poly[place, :], mixed[...], preferred_element_type=F32)
                renewed = gram[place, :] + second
                gram[place, :] = renewed
                low[place, :] = renewed.astype(BF16)
    return work


def wide_kernel(blocks, rows, out, gram, low, poly, mixed):
    for place, (first, second) in enumerate(block_pairs(gram.shape[0] // BLOCK)):
        tile = blocks[place].astype(F32)
        gram[first * BLOCK : (first + 1) * BLOCK, second * BLOCK : (second + 1) * BLOCK] = tile
        if first != second:
            gram[second * BLOCK : (second + 1) * BLOCK, first * BLOCK : (first + 1) * BLOCK] = tile.T
    out[...] = newton_schulz(gram, low, poly, mixed, rows[...])


def square_scratch(size):
    return [
        pltpu.VMEM((size, size), F32),
        pltpu.VMEM((size, size), BF16),
        pltpu.VMEM((size, size), BF16),
        pltpu.VMEM((size, size), BF16),
    ]


def orthogonal_wide(blocks, rows):
    return pl.pallas_call(
        wide_kernel,
        out_shape=jax.ShapeDtypeStruct(rows.shape, BF16),
        scratch_shapes=square_scratch(rows.shape[1]),
        compiler_params=pltpu.CompilerParams(vmem_limit_bytes=40 * 1024 * 1024),
        cost_estimate=pl.CostEstimate(
            flops=14 * rows.shape[1] ** 3, bytes_accessed=4 * rows.size, transcendentals=0
        ),
        name="newton_wide",
    )(blocks, rows)


def whole_kernel(widths, whole, rows, out, *scratch):
    begin = 0
    for index, width in enumerate(widths):
        gram, low, poly, mixed = scratch[4 * index : 4 * index + 4]
        for first in range(0, width, BLOCK):
            gram[first : first + BLOCK, :] = lax.dot_general(
                whole[:, begin + first : begin + first + BLOCK],
                whole[:, begin : begin + width],
                (((0,), (0,)), ((), ())),
                preferred_element_type=F32,
            )
        out[:, begin : begin + width] = newton_schulz(
            gram, low, poly, mixed, rows[:, begin : begin + width]
        )
        begin += width


def orthogonal_whole(whole, rows, widths):
    scratch = []
    for width in widths:
        scratch += square_scratch(width)
    return pl.pallas_call(
        lambda *refs: whole_kernel(widths, *refs),
        out_shape=jax.ShapeDtypeStruct(rows.shape, BF16),
        scratch_shapes=scratch,
        compiler_params=pltpu.CompilerParams(vmem_limit_bytes=48 * 1024 * 1024),
        cost_estimate=pl.CostEstimate(
            flops=16 * sum(width**3 for width in widths),
            bytes_accessed=2 * whole.size,
            transcendentals=0,
        ),
        name="newton_whole",
    )(whole, rows)


def from_flat(flat, base, target, height, breadth):
    lines = breadth // LANES
    for begin in range(0, height, 8):
        count = min(8, height - begin)
        for index in range(lines):
            start = base + begin * lines + index
            if lines == 1:
                tile = flat[start : start + count, :]
            else:
                tile = flat[pl.ds(start, count, stride=lines), :]
            target[begin : begin + count, index * LANES : (index + 1) * LANES] = tile


def to_flat(flat, base, value, height, breadth):
    lines = breadth // LANES
    for begin in range(0, height, 8):
        count = min(8, height - begin)
        for index in range(lines):
            start = base + begin * lines + index
            tile = value(slice(begin, begin + count), slice(index * LANES, (index + 1) * LANES))
            if lines == 1:
                flat[start : start + count, :] = tile
            else:
                flat[pl.ds(start, count, stride=lines), :] = tile


def section_bases(devices):
    bases = []
    base = 0
    for height, breadth in matrix_shapes():
        bases.append(base)
        base += height // devices * breadth // LANES
    return bases


def pack_kernel(devices, group, flat, extra, qkv_out, out_out, wide_out, down_out, qkv, out, wide, down):
    rows = D // devices
    frows = FF // devices
    bases = section_bases(devices)
    qkv[...] = jnp.zeros(qkv.shape, F32)
    out[...] = jnp.zeros(out.shape, F32)
    from_flat(flat, bases[0], qkv.at[:, :QD], rows, QD)
    from_flat(flat, bases[1], qkv.at[:, QD : QD + KVD], rows, KVD)
    from_flat(flat, bases[2], qkv.at[:, QD + KVD :], rows, KVD)
    if extra is not None:
        qkv[rows : rows + 1, :LANES] = extra[...]
    from_flat(flat, bases[3], out, rows, D)
    from_flat(flat, bases[6], down, FF // devices, D)
    qkv_out[...] = qkv[...].astype(qkv_out.dtype)
    out_out[...] = out[...].astype(out_out.dtype)
    down_out[...] = down[...].astype(down_out.dtype)
    for which in range(2):
        from_flat(flat, bases[4 + which], wide, rows, FF)
        targets = devices // group
        for target in range(targets):
            piece = jnp.concatenate(
                [
                    wide[:, (turn * targets + target) * frows : (turn * targets + target + 1) * frows]
                    for turn in range(group)
                ],
                axis=1,
            )
            if group == 1:
                wide_out[target, :, which * frows : (which + 1) * frows] = piece.astype(wide_out.dtype)
            else:
                wide_out[target, which] = piece.astype(wide_out.dtype)


def pack(flat, extra, devices, group, dtype):
    rows = D // devices
    frows = FF // devices
    padded = (rows // 16 + 1) * 16
    targets = devices // group
    wide = (targets, rows, 2 * frows) if group == 1 else (targets, 2, rows, group * frows)
    shapes = [(padded, QD + 2 * KVD), (padded, D), wide, (frows, D)]
    types = [dtype, dtype, BF16, dtype]
    if extra is None:
        body = lambda flat_ref, *refs: pack_kernel(devices, group, flat_ref, None, *refs)
        operands = [flat]
    else:
        body = lambda *refs: pack_kernel(devices, group, *refs)
        operands = [flat, extra]
    return pl.pallas_call(
        body,
        out_shape=[jax.ShapeDtypeStruct(shape, kind) for shape, kind in zip(shapes, types)],
        scratch_shapes=[
            pltpu.VMEM((padded, QD + 2 * KVD), F32),
            pltpu.VMEM((padded, D), F32),
            pltpu.VMEM((rows, FF), F32),
            pltpu.VMEM((frows, D), F32),
        ],
        compiler_params=pltpu.CompilerParams(vmem_limit_bytes=32 * 1024 * 1024),
        cost_estimate=pl.CostEstimate(flops=0, bytes_accessed=6 * flat.size, transcendentals=0),
        name="pack",
    )(*operands)


def update_kernel(devices, decay, factors, flat, qkv, out, wide, down, result, moved, rows_wide):
    rows = D // devices
    frows = FF // devices
    bases = section_bases(devices)
    whole = qkv[...].astype(F32)
    out_whole = out[...].astype(F32)
    down_whole = down[...].astype(F32)
    parts = [
        lambda r, c: whole[r, c],
        lambda r, c: whole[r, slice(QD + c.start, QD + c.stop)],
        lambda r, c: whole[r, slice(QD + KVD + c.start, QD + KVD + c.stop)],
        lambda r, c: out_whole[r, c],
    ]
    shapes = matrix_shapes()
    for index, part in enumerate(parts):
        to_flat(
            moved, bases[index], lambda r, c: part(r, c) * factors[index], rows, shapes[index][1]
        )
    to_flat(moved, bases[6], lambda r, c: down_whole[r, c] * factors[6], frows, D)
    for which in range(2):
        for source in range(devices):
            rows_wide[:, source * frows : (source + 1) * frows] = wide[
                source, :, which * frows : (which + 1) * frows
            ].astype(F32)
        to_flat(
            moved, bases[4 + which], lambda r, c: rows_wide[r, c] * factors[4 + which], rows, FF
        )
    result[...] = decay * flat[...] + moved[...]


def update(flat, qkv, out, wide, down, devices, decay, factors):
    return pl.pallas_call(
        lambda *refs: update_kernel(devices, decay, factors, *refs),
        out_shape=jax.ShapeDtypeStruct(flat.shape, F32),
        scratch_shapes=[
            pltpu.VMEM(flat.shape, F32),
            pltpu.VMEM((D // devices, FF), F32),
        ],
        compiler_params=pltpu.CompilerParams(vmem_limit_bytes=32 * 1024 * 1024),
        cost_estimate=pl.CostEstimate(flops=0, bytes_accessed=10 * flat.size, transcendentals=0),
        name="update",
    )(flat, qkv, out, wide, down)


def on_device(
    block_input,
    cotangent,
    lengths,
    doc_starts,
    master,
    momentum,
    vectors,
    vector_first,
    vector_second,
):
    n_dp = lax.axis_size("dp")
    n_ctx = lax.axis_size("ctx")
    devices = n_dp * n_ctx
    rows = D // devices
    frows = FF // devices
    fblock = FF // n_ctx
    slots, span, width = block_input.shape
    tokens = slots * span
    group = HEADS // KVH
    qkv = QD + 2 * KVD
    my_ctx = lax.axis_index("ctx")
    me = lax.axis_index("dp") * n_ctx + my_ctx
    core_bit, x_bit = 1, 2
    ctx_bits = [core_bit, x_bit]
    dp_bits = [n_ctx << index for index in range(n_dp.bit_length() - 1)]
    all_bits = ctx_bits + dp_bits
    many = tuple([2] * len(all_bits))
    padded = (rows // 16 + 1) * 16

    def padded_pieces(part):
        part = part.reshape(devices, rows, part.shape[1])
        part = jnp.pad(part, ((0, 0), (0, padded - rows), (0, 0)))
        return part.reshape(many + part.shape[1:])

    master_flat = master.reshape(-1, LANES)
    momentum_flat = momentum.reshape(-1, LANES)
    small = jnp.pad(vectors, ((0, 0), (0, LANES - vectors.shape[1])))
    qkv_local, out_local, gate_up, down_local = pack(master_flat, small, devices, n_dp, BF16)
    old_qkv, old_out, old_pair, old_down = pack(momentum_flat, None, devices, 1, F32)

    qkv_full = gather_bits(qkv_local, all_bits[::-1], me, devices, all_bits)
    qkv_full = qkv_full.reshape(devices, padded, qkv)
    gain_first, gain_second, bias_query, bias_key, bias_value = [
        piece.astype(F32) for piece in split_small(qkv_full[:, rows], devices)
    ]
    w_qkv = qkv_full[:, :rows].reshape(D, qkv)
    w_out = gather_bits(out_local, all_bits[::-1], me, devices, all_bits)
    w_out = w_out.reshape(devices, padded, D)[:, :rows].reshape(QD, D)

    gate_up = lax.all_to_all(gate_up, "ctx", split_axis=0, concat_axis=0, tiled=True)
    w_gate, w_up = [
        lax.all_gather(gate_up[:, index].reshape(n_ctx * rows, fblock), "dp", axis=0, tiled=True)
        for index in range(2)
    ]
    w_down = lax.all_gather(down_local, "dp", axis=0, tiled=True)

    old_pair = lax.all_to_all(old_pair, BOTH, split_axis=0, concat_axis=0, tiled=True)
    old_pair = old_pair.reshape(D, 2 * frows).T

    def to_rows(pair):
        both = pair.T.reshape(devices, rows, 2 * frows)
        return lax.all_to_all(both, BOTH, split_axis=0, concat_axis=0, tiled=True)

    length, second = lengths[0], doc_starts[0]
    places = my_ctx * span + jnp.arange(span, dtype=jnp.int32)
    doc_begin = jnp.where(places >= length, length, jnp.where(places >= second, second, 0))
    position = (places - doc_begin).astype(F32)
    live = (places < length)[:, None]
    info = jnp.stack([my_ctx, length, second]).astype(jnp.int32)
    inverse = ROPE_BASE ** (-2.0 * jnp.arange(HD // 2, dtype=F32) / HD)
    angles = inverse[:, None] * position[None, :]
    cosine, sine_part = jnp.cos(angles), jnp.sin(angles)
    cosine = jnp.concatenate([cosine, cosine], axis=0)[None]
    sine_part = jnp.concatenate([sine_part, sine_part], axis=0)[None]

    def from_ctx(value):
        other_core = swap(value, core_bit, devices)
        other_x = swap(value, x_bit, devices)
        return value, other_core, other_x, swap(other_x, core_bit, devices)

    cot_here = jnp.where(live, cotangent.reshape(tokens, width), jnp.zeros((), BF16))
    cot = from_ctx(cot_here)
    cot_halves = [jnp.concatenate(cot[:2], axis=0), jnp.concatenate(cot[2:], axis=0)]

    inputs = block_input.astype(F32).reshape(tokens, width)
    scale_one = lax.rsqrt(jnp.mean(inputs * inputs, axis=-1, keepdims=True) + NORM_EPS)
    normed_one = (inputs * scale_one * gain_first).astype(BF16)
    bias = jnp.concatenate([bias_query, bias_key, bias_value])
    pre = mm(w_qkv, normed_one, ((0,), (1,))) + bias[:, None]
    turned = rotate(
        pre[: QD + KVD].reshape(HEADS + KVH, HD, tokens), cosine, sine_part
    )
    queries = (turned[:HEADS].astype(BF16).astype(F32) * HD ** (-0.5)).astype(BF16)
    kv_here = jnp.concatenate(
        [turned[HEADS:].astype(BF16).reshape(KVD, tokens), pre[QD + KVD :].astype(BF16)], axis=0
    )
    kv = jnp.stack(from_ctx(kv_here))
    attended, log_total = attend(info, kv, queries)

    mixed_heads = attended.reshape(QD, tokens).astype(BF16)
    hidden = inputs + mm(mixed_heads, w_out, ((0,), (0,)))
    scale_two = lax.rsqrt(jnp.mean(hidden * hidden, axis=-1, keepdims=True) + NORM_EPS)
    normed_two = (hidden * scale_two * gain_second).astype(BF16)

    normed = from_ctx(normed_two)
    normed_halves = [jnp.concatenate(normed[:2], axis=0), jnp.concatenate(normed[2:], axis=0)]
    acts, gate_backs, up_backs, back_parts = [], [], [], []
    for normed_half, cot_half in zip(normed_halves, cot_halves):
        grad_act = mm(cot_half, w_down, ((1,), (1,)))
        gate_pre = mm(normed_half, w_gate)
        up_pre = mm(normed_half, w_up)
        sigmoid_gate = jax.nn.sigmoid(gate_pre)
        swish = gate_pre * sigmoid_gate
        slope = sigmoid_gate * (1.0 + gate_pre * (1.0 - sigmoid_gate))
        acts.append((swish * up_pre).astype(BF16))
        gate_backs.append((grad_act * up_pre * slope).astype(BF16))
        up_backs.append((grad_act * swish).astype(BF16))
        back_parts.append(
            (
                mm(gate_backs[-1], w_gate, ((1,), (1,))) + mm(up_backs[-1], w_up, ((1,), (1,)))
            ).astype(BF16)
        )

    def to_ctx(halves):
        crossed = swap(halves[1][span:], core_bit, devices)
        far = (halves[1][:span].astype(F32) + crossed.astype(F32)).astype(BF16)
        near = swap(halves[0][span:], core_bit, devices)
        near = halves[0][:span].astype(F32) + near.astype(F32)
        return near + swap(far, x_bit, devices).astype(F32), far

    normed_two_grad, ready = to_ctx(back_parts)
    (acts, gate_backs, up_backs), ready = lax.optimization_barrier(
        ((acts, gate_backs, up_backs), ready)
    )

    def over_tokens(left, right):
        return mm(left[0], right[0], ((0,), (0,))) + mm(left[1], right[1], ((0,), (0,)))

    dp_shape = tuple([2] * len(dp_bits)) + (frows, D)
    dp_order = dp_bits[1:] + dp_bits[:1]
    down_parts = scatter_start(
        over_tokens(acts, cot_halves).astype(BF16).reshape(dp_shape), dp_bits, dp_order[0], me, devices
    )
    gate_parts = scatter_start(
        over_tokens(gate_backs, normed_halves).astype(BF16).reshape(dp_shape),
        dp_bits,
        dp_bits[0],
        me,
        devices,
    )
    up_parts = scatter_start(
        over_tokens(up_backs, normed_halves).astype(BF16).reshape(dp_shape),
        dp_bits,
        dp_bits[0],
        me,
        devices,
    )
    out_sum, _ = to_ctx([mm(act, w_down).astype(BF16) for act in acts])
    layer_out = jnp.where(live, hidden + out_sum, 0.0)

    out_grad = cot_here.astype(F32)
    hidden_norm_grad, grad_gain_second = norm_backward(
        hidden, scale_two, gain_second, normed_two_grad
    )
    hidden_grad = out_grad + hidden_norm_grad
    hidden_low = hidden_grad.astype(BF16)
    heads_grad = mm(w_out, hidden_low, ((1,), (1,))).astype(BF16).reshape(HEADS, HD, tokens)
    delta = jnp.sum(heads_grad.astype(F32) * attended, axis=1, keepdims=True)
    grad_output = mm(mixed_heads, hidden_low)
    query_grads, kv_parts = [], []
    wide_parts = [gate_parts, up_parts, down_parts]
    wide_orders = [list(dp_bits), list(dp_bits), list(dp_order)]
    for index in range(KVH):
        chosen = slice(index * group, (index + 1) * group)
        kv_one = jnp.concatenate(
            [kv[:, index * HD : (index + 1) * HD], kv[:, KVD + index * HD : KVD + (index + 1) * HD]],
            axis=1,
        )
        query_grad, kv_grad = attend_back(
            info, kv_one, queries[chosen], heads_grad[chosen], log_total[chosen], delta[chosen]
        )
        (query_grad, kv_grad), wide_parts = lax.optimization_barrier(
            ((query_grad, kv_grad), wide_parts)
        )
        query_grads.append(query_grad)
        kv_parts.append(
            scatter_sum(kv_grad.reshape(2, 2, 2 * HD, span), ctx_bits, me, devices)
        )
        for place in range(3):
            wide_orders[place].pop(0)
            if wide_orders[place]:
                wide_parts[place] = scatter_start(
                    scatter_end(wide_parts[place]),
                    wide_orders[place],
                    wide_orders[place][0],
                    me,
                    devices,
                )
    kv_grads = [part.astype(F32).reshape(2, HD, span) for part in kv_parts]
    qk_grad = jnp.concatenate(query_grads + [grad[:1] for grad in kv_grads], axis=0)
    qk_back = rotate_back(qk_grad, cosine, sine_part).reshape(QD + KVD, tokens)
    qkv_back = jnp.concatenate(
        [qk_back] + [grad[1] for grad in kv_grads], axis=0
    ).astype(BF16)
    grad_qkv = mm(normed_one, qkv_back, ((0,), (1,)))
    grad_bias = jnp.sum(qkv_back.astype(F32), axis=1)
    normed_one_grad = mm(qkv_back, w_qkv, ((0,), (1,)))
    input_norm_grad, grad_gain_first = norm_backward(inputs, scale_one, gain_first, normed_one_grad)
    input_grad = (hidden_grad + input_norm_grad).astype(BF16).reshape(slots, span, width)

    vector_part = join_small(
        [
            grad_gain_first,
            grad_gain_second,
            grad_bias[:QD],
            grad_bias[QD : QD + KVD],
            grad_bias[QD + KVD :],
        ],
        devices,
    )
    vector_grad = jnp.sum(
        lax.all_to_all(vector_part, BOTH, split_axis=0, concat_axis=0, tiled=True),
        axis=0,
        keepdims=True,
    )
    grad_qkv, wide_parts = lax.optimization_barrier((grad_qkv, wide_parts))
    gate_sum, up_sum, down_sum = [
        scatter_sum(scatter_end(parts), order[1:], me, devices)
        for parts, order in zip(wide_parts, wide_orders)
    ]
    out_sum_rows = scatter_sum(padded_pieces(grad_output.astype(BF16)), all_bits, me, devices)
    qkv_sum_rows = scatter_sum(padded_pieces(grad_qkv.astype(BF16)), all_bits, me, devices)
    moved_qkv = MOMENTUM_DECAY * old_qkv + qkv_sum_rows.astype(F32)
    moved_out = MOMENTUM_DECAY * old_out + out_sum_rows.astype(F32)
    moved_down = MOMENTUM_DECAY * old_down + down_sum.astype(F32)
    pair_sum = jnp.concatenate([gate_sum, up_sum], axis=0)
    moved_pair = MOMENTUM_DECAY * old_pair.astype(F32) + pair_sum.astype(F32)
    new_momentum = update(
        momentum_flat,
        qkv_sum_rows,
        out_sum_rows,
        to_rows(pair_sum),
        down_sum,
        devices,
        MOMENTUM_DECAY,
        [1.0] * 7,
    ).reshape(momentum.shape)

    slices = jnp.stack([moved_pair[:frows], moved_pair[frows:], moved_down])
    grams = gram_blocks(slices.astype(BF16), devices).reshape(many + (3, BLOCK, BLOCK))
    grams = scatter_sum(grams, all_bits, me, devices)
    grams = gather_bits(grams, all_bits[::-1], me, devices, all_bits)
    grams = grams.reshape(devices, 3, BLOCK, BLOCK)
    wide = [orthogonal_wide(grams[:, index], slices[index]) for index in range(3)]
    ortho_pair = to_rows(jnp.concatenate(wide[:2], axis=0))

    def gathered(part):
        full = gather_bits(part.astype(BF16), all_bits[::-1], me, devices, all_bits)
        return full.reshape(devices * padded, part.shape[1])

    ortho_out = orthogonal_whole(gathered(moved_out), moved_out, (D,))
    ortho_qkv = orthogonal_whole(gathered(moved_qkv), moved_qkv, (QD, KVD, KVD))
    factors = [
        -MUON_RATE * math.sqrt(max(1.0, breadth / height)) for height, breadth in matrix_shapes()
    ]
    new_master = update(
        master_flat,
        ortho_qkv,
        ortho_out,
        ortho_pair,
        wide[2],
        devices,
        1.0 - MUON_RATE * MUON_DECAY,
        factors,
    ).reshape(master.shape)
    first_new = BETA_FIRST * vector_first + (1.0 - BETA_FIRST) * vector_grad
    second_new = BETA_SECOND * vector_second + (1.0 - BETA_SECOND) * vector_grad * vector_grad
    adjusted = (
        first_new
        / (1.0 - BETA_FIRST**STEP)
        / (jnp.sqrt(second_new / (1.0 - BETA_SECOND**STEP)) + ADAM_EPS)
    )
    new_vectors = vectors - ADAM_RATE * adjusted
    return (
        layer_out.astype(BF16).reshape(slots, span, width),
        input_grad,
        new_master,
        new_momentum,
        new_master.astype(BF16),
        new_vectors,
        first_new,
        second_new,
    )


def solution(mesh):
    return jax.shard_map(
        on_device,
        mesh=mesh,
        in_specs=(
            P("dp", "ctx", None),
            P("dp", "ctx", None),
            P("dp"),
            P("dp"),
            P(BOTH, None),
            P(BOTH, None),
            P(BOTH, None),
            P(BOTH, None),
            P(BOTH, None),
        ),
        out_specs=(
            P("dp", "ctx", None),
            P("dp", "ctx", None),
            P(BOTH, None),
            P(BOTH, None),
            P(BOTH, None),
            P(BOTH, None),
            P(BOTH, None),
            P(BOTH, None),
        ),
        check_vma=False,
    )
```

```python
import math

import jax
import jax.numpy as jnp
from jax import lax
from jax.experimental import pallas as pl
from jax.experimental.pallas import tpu as pltpu
from jax.sharding import PartitionSpec as P

D = 896
HEADS = 14
KVH = 2
HD = 64
FF = 4864
SLOT = 2048
NS_STEPS = 3
STEP = 10
QD = 896
KVD = 128

NORM_EPS = 1e-06
ROPE_BASE = 1000000.0
NS_LINEAR = 3.4445
NS_SQUARE = -4.775
NS_CUBIC = 2.0315
MOMENTUM_DECAY = 0.5
MUON_RATE = 0.6
MUON_DECAY = 0.1
ADAM_RATE = 0.2
BETA_FIRST = 0.9
BETA_SECOND = 0.95
ADAM_EPS = 1e-08
MASK_FLOOR = -1e30

F32 = jnp.float32
BF16 = jnp.bfloat16
BOTH = ("dp", "ctx")
LANES = 128


def matrix_shapes():
    return [(D, QD), (D, KVD), (D, KVD), (QD, D), (D, FF), (D, FF), (FF, D)]


def vector_sizes():
    return [D, D, QD, KVD, KVD]


def mm(left, right, contract=((1,), (0,))):
    return lax.dot_general(left, right, (contract, ((), ())), preferred_element_type=F32)


def split_small(flat, devices):
    result = []
    offset = 0
    for extent_all in vector_sizes():
        extent = extent_all // devices
        result.append(flat[:, offset : offset + extent].reshape(extent_all))
        offset += extent
    return result


def join_small(pieces, devices):
    return jnp.concatenate([piece.reshape(devices, -1) for piece in pieces], axis=1)


def swap(value, mask, devices):
    return lax.ppermute(value, BOTH, [(index, index ^ mask) for index in range(devices)])


def gather_bits(value, bits, me, devices, before=()):
    held = value
    done = list(before)
    for bit in bits:
        place = sum(1 for other in done if other > bit)
        got = swap(held, bit, devices)
        mine = (me & bit) != 0
        held = jnp.where(
            mine, jnp.stack([got, held], axis=place), jnp.stack([held, got], axis=place)
        )
        done.append(bit)
    return held


def scatter_start(held, left, bit, me, devices):
    left = sorted(left, reverse=True)
    axis = left.index(bit)
    mine = jnp.where((me & bit) != 0, 1, 0)
    sent = lax.dynamic_index_in_dim(held, 1 - mine, axis, keepdims=False).astype(BF16)
    kept = lax.dynamic_index_in_dim(held, mine, axis, keepdims=False)
    return kept, swap(sent, bit, devices)


def scatter_end(parts):
    return (parts[0].astype(F32) + parts[1].astype(F32)).astype(BF16)


def scatter_sum(value, bits, me, devices):
    left = list(bits)
    held = value
    for bit in bits:
        held = scatter_end(scatter_start(held, left, bit, me, devices))
        left.remove(bit)
    return held


def choose(value, mine, axis):
    return lax.dynamic_index_in_dim(value, mine, axis, keepdims=False)


def to_owner(value, core_bit, x_bit, me, devices):
    core = jnp.where((me & core_bit) != 0, 1, 0)
    across = jnp.where((me & x_bit) != 0, 1, 0)
    got = swap(choose(value, 1 - core, 1), core_bit, devices)
    value = jnp.stack([choose(value, core, 1), got], axis=1)
    got = swap(choose(value, 1 - across, 0), x_bit, devices)
    return jnp.stack([choose(value, across, 0), got])


def from_owner(value, core_bit, x_bit, me, devices):
    got = swap(value[1], x_bit, devices)
    value = jnp.where(
        (me & x_bit) != 0, jnp.stack([got, value[0]]), jnp.stack([value[0], got])
    )
    got = swap(value[:, 1], core_bit, devices)
    return jnp.where(
        (me & core_bit) != 0,
        jnp.stack([got, value[:, 0]], axis=1),
        jnp.stack([value[:, 0], got], axis=1),
    )


def rotate(values, cosine, sine_part):
    midpoint = HD // 2
    turned = jnp.concatenate([-values[:, midpoint:], values[:, :midpoint]], axis=1)
    return values * cosine + turned * sine_part


def rotate_back(gradient, cosine, sine_part):
    midpoint = HD // 2
    scaled = gradient * sine_part
    turned = jnp.concatenate([scaled[:, midpoint:], -scaled[:, :midpoint]], axis=1)
    return gradient * cosine + turned


def norm_backward(source, scale_row, gain, incoming):
    gain_grad = jnp.sum(incoming * source * scale_row, axis=0)
    weighted = incoming * gain
    result = scale_row * weighted - source * scale_row**3 * jnp.mean(
        weighted * source, axis=-1, keepdims=True
    )
    return (result, gain_grad)


def fill_mask(info, mask, chunk, span):
    key = chunk * span + lax.broadcasted_iota(jnp.int32, (span, span), 0)
    query = info[0] * span + lax.broadcasted_iota(jnp.int32, (span, span), 1)
    key_doc = (key >= info[2]).astype(jnp.int32) + (key >= info[1]).astype(jnp.int32)
    query_doc = (query >= info[2]).astype(jnp.int32) + (query >= info[1]).astype(jnp.int32)
    allowed = jnp.logical_and(key_doc == query_doc, key <= query)
    mask[chunk] = jnp.where(allowed, 0.0, MASK_FLOOR).astype(F32)


def attend_kernel(info, kv, q, out, lse, keys, mask, best, total, acc):
    head = pl.program_id(0)
    span = q.shape[-1]
    mine = info[0]
    chunks = mine + 1

    @pl.when(head == 0)
    def _():
        def fill(chunk, carry):
            slot = jnp.bitwise_xor(chunk, mine)
            keys[chunk] = kv[slot, :HD, :].astype(F32).T.astype(BF16)
            fill_mask(info, mask, chunk, span)
            return carry

        lax.fori_loop(0, chunks, fill, 0)

    best[...] = jnp.full(best.shape, MASK_FLOOR, F32)
    total[...] = jnp.zeros(total.shape, F32)
    acc[...] = jnp.zeros(acc.shape, F32)
    queries = q[0]

    def step(index, carry):
        chunk = mine - index
        slot = jnp.bitwise_xor(chunk, mine)
        scores = jnp.dot(keys[chunk], queries, preferred_element_type=F32) + mask[chunk]
        old = best[...]
        new = jnp.maximum(old, jnp.max(scores, axis=0, keepdims=True))
        present = jnp.exp(scores - new)
        shrink = jnp.exp(old - new)
        best[...] = new
        total[...] = total[...] * shrink + jnp.sum(present, axis=0, keepdims=True)
        acc[...] = acc[...] * shrink + jnp.dot(
            kv[slot, HD:, :], present.astype(BF16), preferred_element_type=F32
        )
        return carry

    lax.fori_loop(0, chunks, step, 0)
    out[0] = acc[...] / total[...]
    lse[0] = best[...] + jnp.log(total[...])


def attend_back_kernel(
    info, kv, q, dout, lse, delta, dq, dkv, keys, values, mask, dk, dv, acc
):
    head = pl.program_id(0)
    span = q.shape[-1]
    mine = info[0]
    chunks = mine + 1
    n_ctx = kv.shape[0]

    @pl.when(head == 0)
    def _():
        dk[...] = jnp.zeros(dk.shape, F32)
        dv[...] = jnp.zeros(dv.shape, F32)

        def fill(chunk, carry):
            slot = jnp.bitwise_xor(chunk, mine)
            keys[chunk] = kv[slot, :HD, :].astype(F32).T.astype(BF16)
            values[chunk] = kv[slot, HD:, :].astype(F32).T.astype(BF16)
            fill_mask(info, mask, chunk, span)
            return carry

        lax.fori_loop(0, chunks, fill, 0)

    acc[...] = jnp.zeros(acc.shape, F32)
    queries = q[0]
    douts = dout[0]
    query_rows = queries.astype(F32).T.astype(BF16)
    dout_rows = douts.astype(F32).T.astype(BF16)

    def step(chunk, carry):
        slot = jnp.bitwise_xor(chunk, mine)
        scores = jnp.dot(keys[chunk], queries, preferred_element_type=F32) + mask[chunk]
        shares = jnp.exp(scores - lse[0])
        share_grad = jnp.dot(values[chunk], douts, preferred_element_type=F32)
        score_grad = (shares * (share_grad - delta[0])).astype(BF16)
        dv[chunk] += jnp.dot(shares.astype(BF16), dout_rows, preferred_element_type=F32)
        dk[chunk] += jnp.dot(score_grad, query_rows, preferred_element_type=F32)
        acc[...] += jnp.dot(kv[slot, :HD, :], score_grad, preferred_element_type=F32)
        return carry

    lax.fori_loop(0, chunks, step, 0)
    dq[0] = acc[...] * HD ** (-0.5)

    @pl.when(head == HEADS // KVH - 1)
    def _():
        for chunk in range(n_ctx):
            dkv[chunk, :HD, :] = dk[chunk].T.astype(BF16)
            dkv[chunk, HD:, :] = dv[chunk].T.astype(BF16)


def attend(info, kv, q):
    heads, _, span = q.shape
    n_ctx = kv.shape[0]
    per_head = lambda rows: pl.BlockSpec((1, rows, span), lambda head: (head, 0, 0))
    return pl.pallas_call(
        attend_kernel,
        grid=(heads,),
        in_specs=[
            pl.BlockSpec(memory_space=pltpu.SMEM),
            pl.BlockSpec(kv.shape, lambda head: (0, 0, 0)),
            per_head(HD),
        ],
        out_specs=[per_head(HD), per_head(1)],
        out_shape=[
            jax.ShapeDtypeStruct((heads, HD, span), F32),
            jax.ShapeDtypeStruct((heads, 1, span), F32),
        ],
        scratch_shapes=[
            pltpu.VMEM((n_ctx, span, HD), BF16),
            pltpu.VMEM((n_ctx, span, span), F32),
            pltpu.VMEM((1, span), F32),
            pltpu.VMEM((1, span), F32),
            pltpu.VMEM((HD, span), F32),
        ],
        compiler_params=pltpu.CompilerParams(vmem_limit_bytes=40 * 1024 * 1024),
        cost_estimate=pl.CostEstimate(
            flops=4 * heads * span * span * n_ctx * HD * 4,
            bytes_accessed=4 * heads * span * HD * 2,
            transcendentals=heads * span * span * n_ctx,
        ),
        name="attend",
    )(info, kv, q)


def attend_back(info, kv, q, dout, lse, delta):
    heads, _, span = q.shape
    n_ctx = kv.shape[0]
    per_head = lambda rows: pl.BlockSpec((1, rows, span), lambda head: (head, 0, 0))
    return pl.pallas_call(
        attend_back_kernel,
        grid=(heads,),
        in_specs=[
            pl.BlockSpec(memory_space=pltpu.SMEM),
            pl.BlockSpec(kv.shape, lambda head: (0, 0, 0)),
            per_head(HD),
            per_head(HD),
            per_head(1),
            per_head(1),
        ],
        out_specs=[per_head(HD), pl.BlockSpec(kv.shape, lambda head: (0, 0, 0))],
        out_shape=[
            jax.ShapeDtypeStruct((heads, HD, span), F32),
            jax.ShapeDtypeStruct(kv.shape, BF16),
        ],
        scratch_shapes=[
            pltpu.VMEM((n_ctx, span, HD), BF16),
            pltpu.VMEM((n_ctx, span, HD), BF16),
            pltpu.VMEM((n_ctx, span, span), F32),
            pltpu.VMEM((n_ctx, span, HD), F32),
            pltpu.VMEM((n_ctx, span, HD), F32),
            pltpu.VMEM((HD, span), F32),
        ],
        compiler_params=pltpu.CompilerParams(vmem_limit_bytes=40 * 1024 * 1024),
        cost_estimate=pl.CostEstimate(
            flops=10 * heads * span * span * n_ctx * HD * 4,
            bytes_accessed=8 * heads * span * HD * 2,
            transcendentals=heads * span * span * n_ctx,
        ),
        name="attend_back",
    )(info, kv, q, dout, lse, delta)


BLOCK = 128


def block_pairs(count):
    return [(low, high) for low in range(count) for high in range(low, count)]


def gram_kernel(rows, out):
    count = rows.shape[1] // BLOCK
    place = 0
    for low in range(count):
        line = lax.dot_general(
            rows[:, low * BLOCK : (low + 1) * BLOCK],
            rows[:, low * BLOCK :],
            (((0,), (0,)), ((), ())),
            preferred_element_type=F32,
        ).astype(BF16)
        for high in range(low, count):
            out[place] = line[:, (high - low) * BLOCK : (high - low + 1) * BLOCK]
            place += 1
    for extra in range(place, out.shape[0]):
        out[extra] = jnp.zeros((BLOCK, BLOCK), BF16)


def gram_blocks(rows, places):
    return pl.pallas_call(
        gram_kernel,
        out_shape=jax.ShapeDtypeStruct((places, BLOCK, BLOCK), BF16),
        compiler_params=pltpu.CompilerParams(vmem_limit_bytes=32 * 1024 * 1024),
        name="gram",
    )(rows)


def newton_schulz(gram, low, poly, mixed, rows):
    size = gram.shape[0]
    part = size // 2 if size % 16 == 0 and size > BLOCK else size
    parts = [pl.ds(begin, part) for begin in range(0, size, part)]
    row_id = lax.broadcasted_iota(jnp.int32, (size, size), 0)
    column_id = lax.broadcasted_iota(jnp.int32, (size, size), 1)
    square = jnp.where(row_id == column_id, gram[...], 0.0)
    square = jnp.sum(jnp.sum(square, axis=0, keepdims=True), axis=1, keepdims=True)
    scale = 1.0 / (jnp.sqrt(square) + 1e-07)
    for place in parts:
        scaled = gram[place, :] * (scale * scale)
        gram[place, :] = scaled
        low[place, :] = scaled.astype(BF16)
    work = (rows * scale).astype(BF16)
    for step in range(NS_STEPS):
        for place in parts:
            second = jnp.dot(low[place, :], low[...], preferred_element_type=F32)
            poly[place, :] = (NS_SQUARE * gram[place, :] + NS_CUBIC * second).astype(BF16)
        moved = jnp.dot(work, poly[...], preferred_element_type=F32)
        work = (NS_LINEAR * work.astype(F32) + moved).astype(BF16)
        if step + 1 < NS_STEPS:
            for place in parts:
                first = jnp.dot(poly[place, :], low[...], preferred_element_type=F32)
                mixed[place, :] = first.astype(BF16)
                gram[place, :] = (
                    NS_LINEAR * NS_LINEAR * gram[place, :] + (2.0 * NS_LINEAR) * first
                )
            for place in parts:
                second = jnp.dot(poly[place, :], mixed[...], preferred_element_type=F32)
                renewed = gram[place, :] + second
                gram[place, :] = renewed
                low[place, :] = renewed.astype(BF16)
    return work


def wide_kernel(blocks, rows, out, gram, low, poly, mixed):
    for place, (first, second) in enumerate(block_pairs(gram.shape[0] // BLOCK)):
        tile = blocks[place].astype(F32)
        gram[first * BLOCK : (first + 1) * BLOCK, second * BLOCK : (second + 1) * BLOCK] = tile
        if first != second:
            gram[second * BLOCK : (second + 1) * BLOCK, first * BLOCK : (first + 1) * BLOCK] = tile.T
    out[...] = newton_schulz(gram, low, poly, mixed, rows[...].astype(F32))


def square_scratch(size):
    return [
        pltpu.VMEM((size, size), F32),
        pltpu.VMEM((size, size), BF16),
        pltpu.VMEM((size, size), BF16),
        pltpu.VMEM((size, size), BF16),
    ]


def orthogonal_wide(blocks, rows):
    return pl.pallas_call(
        wide_kernel,
        out_shape=jax.ShapeDtypeStruct(rows.shape, BF16),
        scratch_shapes=square_scratch(rows.shape[1]),
        compiler_params=pltpu.CompilerParams(vmem_limit_bytes=40 * 1024 * 1024),
        cost_estimate=pl.CostEstimate(
            flops=14 * rows.shape[1] ** 3, bytes_accessed=4 * rows.size, transcendentals=0
        ),
        name="newton_wide",
    )(blocks, rows)


def whole_kernel(widths, whole, rows, out, *scratch):
    begin = 0
    for index, width in enumerate(widths):
        gram, low, poly, mixed = scratch[4 * index : 4 * index + 4]
        for first in range(0, width, BLOCK):
            gram[first : first + BLOCK, :] = lax.dot_general(
                whole[:, begin + first : begin + first + BLOCK],
                whole[:, begin : begin + width],
                (((0,), (0,)), ((), ())),
                preferred_element_type=F32,
            )
        out[:, begin : begin + width] = newton_schulz(
            gram, low, poly, mixed, rows[:, begin : begin + width]
        )
        begin += width


def orthogonal_whole(whole, rows, widths):
    scratch = []
    for width in widths:
        scratch += square_scratch(width)
    return pl.pallas_call(
        lambda *refs: whole_kernel(widths, *refs),
        out_shape=jax.ShapeDtypeStruct(rows.shape, BF16),
        scratch_shapes=scratch,
        compiler_params=pltpu.CompilerParams(vmem_limit_bytes=48 * 1024 * 1024),
        cost_estimate=pl.CostEstimate(
            flops=16 * sum(width**3 for width in widths),
            bytes_accessed=2 * whole.size,
            transcendentals=0,
        ),
        name="newton_whole",
    )(whole, rows)


def from_flat(flat, base, target, height, breadth):
    lines = breadth // LANES
    for begin in range(0, height, 8):
        count = min(8, height - begin)
        for index in range(lines):
            start = base + begin * lines + index
            if lines == 1:
                tile = flat[start : start + count, :]
            else:
                tile = flat[pl.ds(start, count, stride=lines), :]
            target[begin : begin + count, index * LANES : (index + 1) * LANES] = tile


def to_flat(flat, base, value, height, breadth):
    lines = breadth // LANES
    for begin in range(0, height, 8):
        count = min(8, height - begin)
        for index in range(lines):
            start = base + begin * lines + index
            tile = value(slice(begin, begin + count), slice(index * LANES, (index + 1) * LANES))
            if lines == 1:
                flat[start : start + count, :] = tile
            else:
                flat[pl.ds(start, count, stride=lines), :] = tile


def section_bases(devices):
    bases = []
    base = 0
    for height, breadth in matrix_shapes():
        bases.append(base)
        base += height // devices * breadth // LANES
    return bases


def pack_kernel(devices, group, flat, extra, qkv_out, out_out, wide_out, down_out, qkv, out, wide, down):
    rows = D // devices
    frows = FF // devices
    bases = section_bases(devices)
    qkv[...] = jnp.zeros(qkv.shape, F32)
    out[...] = jnp.zeros(out.shape, F32)
    from_flat(flat, bases[0], qkv.at[:, :QD], rows, QD)
    from_flat(flat, bases[1], qkv.at[:, QD : QD + KVD], rows, KVD)
    from_flat(flat, bases[2], qkv.at[:, QD + KVD :], rows, KVD)
    if extra is not None:
        qkv[rows : rows + 1, :LANES] = extra[...]
    from_flat(flat, bases[3], out, rows, D)
    from_flat(flat, bases[6], down, FF // devices, D)
    qkv_out[...] = qkv[...].astype(qkv_out.dtype)
    out_out[...] = out[...].astype(out_out.dtype)
    down_out[...] = down[...].astype(down_out.dtype)
    for which in range(2):
        from_flat(flat, bases[4 + which], wide, rows, FF)
        targets = devices // group
        for target in range(targets):
            piece = jnp.concatenate(
                [
                    wide[:, (turn * targets + target) * frows : (turn * targets + target + 1) * frows]
                    for turn in range(group)
                ],
                axis=1,
            )
            if group == 1:
                wide_out[target, :, which * frows : (which + 1) * frows] = piece.astype(wide_out.dtype)
            else:
                wide_out[target, which] = piece.astype(wide_out.dtype)


def pack(flat, extra, devices, group, dtype):
    rows = D // devices
    frows = FF // devices
    padded = (rows // 16 + 1) * 16
    targets = devices // group
    wide = (targets, rows, 2 * frows) if group == 1 else (targets, 2, rows, group * frows)
    shapes = [(padded, QD + 2 * KVD), (padded, D), wide, (frows, D)]
    types = [dtype, dtype, BF16, dtype]
    if extra is None:
        body = lambda flat_ref, *refs: pack_kernel(devices, group, flat_ref, None, *refs)
        operands = [flat]
    else:
        body = lambda *refs: pack_kernel(devices, group, *refs)
        operands = [flat, extra]
    return pl.pallas_call(
        body,
        out_shape=[jax.ShapeDtypeStruct(shape, kind) for shape, kind in zip(shapes, types)],
        scratch_shapes=[
            pltpu.VMEM((padded, QD + 2 * KVD), F32),
            pltpu.VMEM((padded, D), F32),
            pltpu.VMEM((rows, FF), F32),
            pltpu.VMEM((frows, D), F32),
        ],
        compiler_params=pltpu.CompilerParams(vmem_limit_bytes=32 * 1024 * 1024),
        cost_estimate=pl.CostEstimate(flops=0, bytes_accessed=6 * flat.size, transcendentals=0),
        name="pack",
    )(*operands)


def update_kernel(devices, decay, factors, flat, qkv, out, wide, down, result, moved, rows_wide):
    rows = D // devices
    frows = FF // devices
    bases = section_bases(devices)
    whole = qkv[...].astype(F32)
    out_whole = out[...].astype(F32)
    down_whole = down[...].astype(F32)
    parts = [
        lambda r, c: whole[r, c],
        lambda r, c: whole[r, slice(QD + c.start, QD + c.stop)],
        lambda r, c: whole[r, slice(QD + KVD + c.start, QD + KVD + c.stop)],
        lambda r, c: out_whole[r, c],
    ]
    shapes = matrix_shapes()
    for index, part in enumerate(parts):
        to_flat(
            moved, bases[index], lambda r, c: part(r, c) * factors[index], rows, shapes[index][1]
        )
    to_flat(moved, bases[6], lambda r, c: down_whole[r, c] * factors[6], frows, D)
    for which in range(2):
        for source in range(devices):
            rows_wide[:, source * frows : (source + 1) * frows] = wide[
                source, :, which * frows : (which + 1) * frows
            ].astype(F32)
        to_flat(
            moved, bases[4 + which], lambda r, c: rows_wide[r, c] * factors[4 + which], rows, FF
        )
    result[...] = decay * flat[...] + moved[...]


def update(flat, qkv, out, wide, down, devices, decay, factors):
    return pl.pallas_call(
        lambda *refs: update_kernel(devices, decay, factors, *refs),
        out_shape=jax.ShapeDtypeStruct(flat.shape, F32),
        scratch_shapes=[
            pltpu.VMEM(flat.shape, F32),
            pltpu.VMEM((D // devices, FF), F32),
        ],
        compiler_params=pltpu.CompilerParams(vmem_limit_bytes=32 * 1024 * 1024),
        cost_estimate=pl.CostEstimate(flops=0, bytes_accessed=10 * flat.size, transcendentals=0),
        name="update",
    )(flat, qkv, out, wide, down)


def on_device(
    block_input,
    cotangent,
    lengths,
    doc_starts,
    master,
    momentum,
    vectors,
    vector_first,
    vector_second,
):
    n_dp = lax.axis_size("dp")
    n_ctx = lax.axis_size("ctx")
    devices = n_dp * n_ctx
    rows = D // devices
    frows = FF // devices
    fblock = FF // n_ctx
    slots, span, width = block_input.shape
    tokens = slots * span
    group = HEADS // KVH
    qkv = QD + 2 * KVD
    my_ctx = lax.axis_index("ctx")
    me = lax.axis_index("dp") * n_ctx + my_ctx
    core_bit, x_bit = 1, 2
    ctx_bits = [core_bit, x_bit]
    dp_bits = [n_ctx << index for index in range(n_dp.bit_length() - 1)]
    all_bits = ctx_bits + dp_bits
    many = tuple([2] * len(all_bits))
    padded = (rows // 16 + 1) * 16

    def padded_pieces(part):
        part = part.reshape(devices, rows, part.shape[1])
        part = jnp.pad(part, ((0, 0), (0, padded - rows), (0, 0)))
        return part.reshape(many + part.shape[1:])

    master_flat = master.reshape(-1, LANES)
    momentum_flat = momentum.reshape(-1, LANES)
    small = jnp.pad(vectors, ((0, 0), (0, LANES - vectors.shape[1])))
    qkv_local, out_local, gate_up, down_local = pack(master_flat, small, devices, n_dp, BF16)

    attn_full = gather_bits(
        jnp.concatenate([qkv_local, out_local], axis=1), dp_bits[::-1], me, devices
    )
    qkv_full = gather_bits(attn_full[..., :qkv], ctx_bits[::-1], me, devices, dp_bits)
    qkv_full = qkv_full.reshape(devices, padded, qkv)
    gain_first, gain_second, bias_query, bias_key, bias_value = [
        piece.astype(F32) for piece in split_small(qkv_full[:, rows], devices)
    ]
    w_qkv = qkv_full[:, :rows].reshape(D, qkv)

    w_down = lax.all_gather(down_local, "dp", axis=0, tiled=True)
    came = [choose(gate_up, my_ctx, 0)] + [
        swap(choose(gate_up, my_ctx ^ mask, 0), mask, devices) for mask in range(1, n_ctx)
    ]
    ordered = []
    for source in range(n_ctx):
        piece = came[0]
        for mask in range(1, n_ctx):
            piece = jnp.where(my_ctx ^ mask == source, came[mask], piece)
        ordered.append(piece)
    gate_up = jnp.concatenate(ordered, axis=1)
    w_gate, w_up = [lax.all_gather(gate_up[index], "dp", axis=0, tiled=True) for index in range(2)]

    def to_rows(pair):
        both = pair.T.reshape(devices, rows, 2 * frows)
        return lax.all_to_all(both, BOTH, split_axis=0, concat_axis=0, tiled=True)

    length, second = lengths[0], doc_starts[0]
    places = my_ctx * span + jnp.arange(span, dtype=jnp.int32)
    doc_begin = jnp.where(places >= length, length, jnp.where(places >= second, second, 0))
    position = (places - doc_begin).astype(F32)
    live = (places < length)[:, None]
    info = jnp.stack([my_ctx, length, second]).astype(jnp.int32)
    inverse = ROPE_BASE ** (-2.0 * jnp.arange(HD // 2, dtype=F32) / HD)
    angles = inverse[:, None] * position[None, :]
    cosine, sine_part = jnp.cos(angles), jnp.sin(angles)
    cosine = jnp.concatenate([cosine, cosine], axis=0)[None]
    sine_part = jnp.concatenate([sine_part, sine_part], axis=0)[None]

    def from_ctx(value):
        other_core = swap(value, core_bit, devices)
        other_x = swap(value, x_bit, devices)
        return value, other_core, other_x, swap(other_x, core_bit, devices)

    cot_here = jnp.where(live, cotangent.reshape(tokens, width), jnp.zeros((), BF16))
    cot = from_ctx(cot_here)
    cot_halves = [jnp.concatenate(cot[:2], axis=0), jnp.concatenate(cot[2:], axis=0)]

    def pair_of_heads(kv, index):
        begin = index * HD
        return jnp.concatenate(
            [kv[:, begin : begin + HD], kv[:, KVD + begin : KVD + begin + HD]], axis=1
        )

    inputs = block_input.astype(F32).reshape(tokens, width)
    scale_one = lax.rsqrt(jnp.mean(inputs * inputs, axis=-1, keepdims=True) + NORM_EPS)
    normed_one = (inputs * scale_one * gain_first).astype(BF16)
    bias = jnp.concatenate([bias_query, bias_key, bias_value])
    pre = mm(w_qkv, normed_one, ((0,), (1,))) + bias[:, None]
    turned = rotate(
        pre[: QD + KVD].reshape(HEADS + KVH, HD, tokens), cosine, sine_part
    )
    queries = (turned[:HEADS].astype(BF16).astype(F32) * HD ** (-0.5)).astype(BF16)
    kv_here = jnp.concatenate(
        [turned[HEADS:].astype(BF16).reshape(KVD, tokens), pre[QD + KVD :].astype(BF16)], axis=0
    )
    kv = jnp.stack(from_ctx(kv_here))
    out_full, kv = lax.optimization_barrier((attn_full[..., qkv:], kv))
    halves = []
    for index in range(KVH):
        if index == 1:
            out_full, halves = lax.optimization_barrier((out_full, halves))
        out_full = gather_bits(
            out_full, ctx_bits[::-1][index : index + 1], me, devices, dp_bits + ctx_bits[::-1][:index]
        )
        kv_one = pair_of_heads(kv, index)
        halves.append(attend(info, kv_one, queries[index * group : (index + 1) * group]))
    attended = jnp.concatenate([half[0] for half in halves], axis=0)
    log_total = jnp.concatenate([half[1] for half in halves], axis=0)
    w_out = out_full.reshape(devices, padded, D)[:, :rows].reshape(QD, D)

    mixed_heads = attended.reshape(QD, tokens).astype(BF16)
    hidden = inputs + mm(mixed_heads, w_out, ((0,), (0,)))
    scale_two = lax.rsqrt(jnp.mean(hidden * hidden, axis=-1, keepdims=True) + NORM_EPS)
    normed_two = (hidden * scale_two * gain_second).astype(BF16)

    momentum_flat, normed_two = lax.optimization_barrier((momentum_flat, normed_two))
    old_qkv, old_out, old_pair, old_down = pack(momentum_flat, None, devices, 1, F32)
    old_pair = lax.all_to_all(old_pair, BOTH, split_axis=0, concat_axis=0, tiled=True)
    old_pair = old_pair.reshape(D, 2 * frows).T

    normed = from_ctx(normed_two)
    normed_halves = [jnp.concatenate(normed[:2], axis=0), jnp.concatenate(normed[2:], axis=0)]
    acts, gate_backs, up_backs, back_parts = [], [], [], []
    for normed_half, cot_half in zip(normed_halves, cot_halves):
        grad_act = mm(cot_half, w_down, ((1,), (1,)))
        gate_pre = mm(normed_half, w_gate)
        up_pre = mm(normed_half, w_up)
        sigmoid_gate = jax.nn.sigmoid(gate_pre)
        swish = gate_pre * sigmoid_gate
        slope = sigmoid_gate * (1.0 + gate_pre * (1.0 - sigmoid_gate))
        acts.append((swish * up_pre).astype(BF16))
        gate_backs.append((grad_act * up_pre * slope).astype(BF16))
        up_backs.append((grad_act * swish).astype(BF16))
        back_parts.append(
            (
                mm(gate_backs[-1], w_gate, ((1,), (1,))) + mm(up_backs[-1], w_up, ((1,), (1,)))
            ).astype(BF16)
        )

    def to_ctx(halves):
        crossed = swap(halves[1][span:], core_bit, devices)
        far = (halves[1][:span].astype(F32) + crossed.astype(F32)).astype(BF16)
        near = swap(halves[0][span:], core_bit, devices)
        near = halves[0][:span].astype(F32) + near.astype(F32)
        return near + swap(far, x_bit, devices).astype(F32), far

    normed_two_grad, ready = to_ctx(back_parts)
    (acts, gate_backs, up_backs), ready = lax.optimization_barrier(
        ((acts, gate_backs, up_backs), ready)
    )

    def over_tokens(left, right):
        return mm(left[0], right[0], ((0,), (0,))) + mm(left[1], right[1], ((0,), (0,)))

    dp_shape = tuple([2] * len(dp_bits)) + (frows, D)
    dp_order = dp_bits[1:] + dp_bits[:1]
    down_parts = scatter_start(
        over_tokens(acts, cot_halves).astype(BF16).reshape(dp_shape), dp_bits, dp_order[0], me, devices
    )
    gate_parts = scatter_start(
        over_tokens(gate_backs, normed_halves).astype(BF16).reshape(dp_shape),
        dp_bits,
        dp_bits[0],
        me,
        devices,
    )
    up_parts = scatter_start(
        over_tokens(up_backs, normed_halves).astype(BF16).reshape(dp_shape),
        dp_bits,
        dp_bits[0],
        me,
        devices,
    )
    out_sum, _ = to_ctx([mm(act, w_down).astype(BF16) for act in acts])
    layer_out = jnp.where(live, hidden + out_sum, 0.0)

    out_grad = cot_here.astype(F32)
    hidden_norm_grad, grad_gain_second = norm_backward(
        hidden, scale_two, gain_second, normed_two_grad
    )
    hidden_grad = out_grad + hidden_norm_grad
    hidden_low = hidden_grad.astype(BF16)
    heads_grad = mm(w_out, hidden_low, ((1,), (1,))).astype(BF16).reshape(HEADS, HD, tokens)
    delta = jnp.sum(heads_grad.astype(F32) * attended, axis=1, keepdims=True)
    grad_output = mm(mixed_heads, hidden_low)
    query_grads, kv_parts = [], []
    wide_parts = [gate_parts, up_parts, down_parts]
    wide_orders = [list(dp_bits), list(dp_bits), list(dp_order)]
    for index in range(KVH):
        chosen = slice(index * group, (index + 1) * group)
        kv_one = pair_of_heads(kv, index)
        query_grad, kv_grad = attend_back(
            info, kv_one, queries[chosen], heads_grad[chosen], log_total[chosen], delta[chosen]
        )
        (query_grad, kv_grad), wide_parts = lax.optimization_barrier(
            ((query_grad, kv_grad), wide_parts)
        )
        query_grads.append(query_grad)
        kv_parts.append(
            scatter_sum(kv_grad.reshape(2, 2, 2 * HD, span), ctx_bits, me, devices)
        )
        for place in range(3):
            wide_orders[place].pop(0)
            if wide_orders[place]:
                wide_parts[place] = scatter_start(
                    scatter_end(wide_parts[place]),
                    wide_orders[place],
                    wide_orders[place][0],
                    me,
                    devices,
                )
    kv_grads = [part.astype(F32).reshape(2, HD, span) for part in kv_parts]
    qk_grad = jnp.concatenate(query_grads + [grad[:1] for grad in kv_grads], axis=0)
    qk_back = rotate_back(qk_grad, cosine, sine_part).reshape(QD + KVD, tokens)
    qkv_back = jnp.concatenate(
        [qk_back] + [grad[1] for grad in kv_grads], axis=0
    ).astype(BF16)
    grad_qkv = mm(normed_one, qkv_back, ((0,), (1,)))
    grad_bias = jnp.sum(qkv_back.astype(F32), axis=1)
    normed_one_grad = mm(qkv_back, w_qkv, ((0,), (1,)))
    input_norm_grad, grad_gain_first = norm_backward(inputs, scale_one, gain_first, normed_one_grad)
    input_grad = (hidden_grad + input_norm_grad).astype(BF16).reshape(slots, span, width)

    vector_part = join_small(
        [
            grad_gain_first,
            grad_gain_second,
            grad_bias[:QD],
            grad_bias[QD : QD + KVD],
            grad_bias[QD + KVD :],
        ],
        devices,
    )
    vector_grad = jnp.sum(
        lax.all_to_all(vector_part, BOTH, split_axis=0, concat_axis=0, tiled=True),
        axis=0,
        keepdims=True,
    )
    grad_qkv, wide_parts = lax.optimization_barrier((grad_qkv, wide_parts))
    gate_sum, up_sum, down_sum = [
        scatter_sum(scatter_end(parts), order[1:], me, devices)
        for parts, order in zip(wide_parts, wide_orders)
    ]
    out_sum_rows = scatter_sum(padded_pieces(grad_output.astype(BF16)), all_bits, me, devices)
    qkv_sum_rows = scatter_sum(padded_pieces(grad_qkv.astype(BF16)), all_bits, me, devices)
    moved_qkv = MOMENTUM_DECAY * old_qkv + qkv_sum_rows.astype(F32)
    moved_out = MOMENTUM_DECAY * old_out + out_sum_rows.astype(F32)
    moved_down = MOMENTUM_DECAY * old_down + down_sum.astype(F32)
    pair_sum = jnp.concatenate([gate_sum, up_sum], axis=0)
    moved_pair = MOMENTUM_DECAY * old_pair.astype(F32) + pair_sum.astype(F32)
    new_momentum = update(
        momentum_flat,
        qkv_sum_rows,
        out_sum_rows,
        to_rows(pair_sum),
        down_sum,
        devices,
        MOMENTUM_DECAY,
        [1.0] * 7,
    ).reshape(momentum.shape)

    mats = jnp.stack(
        [
            moved_pair[:frows],
            moved_pair[frows:],
            moved_down,
            jnp.pad(moved_out, ((0, frows - padded), (0, 0))),
        ]
    ).astype(BF16)
    owned = to_owner(mats.reshape(2, 2, frows, D), core_bit, x_bit, me, devices)
    owned = owned.reshape(n_ctx * frows, D)
    count = len(block_pairs(D // BLOCK))
    places = (count + n_dp - 1) // n_dp * n_dp
    dp_many = tuple([2] * len(dp_bits))
    gram = gram_blocks(owned, places).reshape(dp_many + (places // n_dp, BLOCK, BLOCK))
    gram = scatter_sum(gram, dp_bits, me, devices)
    gram = gather_bits(gram, dp_bits[::-1], me, devices).reshape(places, BLOCK, BLOCK)
    ortho = orthogonal_wide(gram, owned).reshape(2, 2, frows, D)
    ortho = from_owner(ortho, core_bit, x_bit, me, devices).reshape(n_ctx, frows, D)
    ortho_pair = to_rows(ortho[:2].reshape(2 * frows, D))

    def gathered(part):
        full = gather_bits(part.astype(BF16), all_bits[::-1], me, devices)
        return full.reshape(devices * padded, part.shape[1])

    ortho_qkv = orthogonal_whole(gathered(moved_qkv), moved_qkv, (QD, KVD, KVD))
    factors = [
        -MUON_RATE * math.sqrt(max(1.0, breadth / height)) for height, breadth in matrix_shapes()
    ]
    new_master = update(
        master_flat,
        ortho_qkv,
        ortho[3, :padded],
        ortho_pair,
        ortho[2],
        devices,
        1.0 - MUON_RATE * MUON_DECAY,
        factors,
    ).reshape(master.shape)
    first_new = BETA_FIRST * vector_first + (1.0 - BETA_FIRST) * vector_grad
    second_new = BETA_SECOND * vector_second + (1.0 - BETA_SECOND) * vector_grad * vector_grad
    adjusted = (
        first_new
        / (1.0 - BETA_FIRST**STEP)
        / (jnp.sqrt(second_new / (1.0 - BETA_SECOND**STEP)) + ADAM_EPS)
    )
    new_vectors = vectors - ADAM_RATE * adjusted
    return (
        layer_out.astype(BF16).reshape(slots, span, width),
        input_grad,
        new_master,
        new_momentum,
        new_master.astype(BF16),
        new_vectors,
        first_new,
        second_new,
    )


def solution(mesh):
    return jax.shard_map(
        on_device,
        mesh=mesh,
        in_specs=(
            P("dp", "ctx", None),
            P("dp", "ctx", None),
            P("dp"),
            P("dp"),
            P(BOTH, None),
            P(BOTH, None),
            P(BOTH, None),
            P(BOTH, None),
            P(BOTH, None),
        ),
        out_specs=(
            P("dp", "ctx", None),
            P("dp", "ctx", None),
            P(BOTH, None),
            P(BOTH, None),
            P(BOTH, None),
            P(BOTH, None),
            P(BOTH, None),
            P(BOTH, None),
        ),
        check_vma=False,
    )
```

```python
import math

import jax
import jax.numpy as jnp
from jax import lax
from jax.experimental import pallas as pl
from jax.experimental.pallas import tpu as pltpu
from jax.sharding import PartitionSpec as P

D = 896
HEADS = 14
KVH = 2
HD = 64
FF = 4864
SLOT = 2048
NS_STEPS = 3
STEP = 10
QD = 896
KVD = 128

NORM_EPS = 1e-06
ROPE_BASE = 1000000.0
NS_LINEAR = 3.4445
NS_SQUARE = -4.775
NS_CUBIC = 2.0315
MOMENTUM_DECAY = 0.5
MUON_RATE = 0.6
MUON_DECAY = 0.1
ADAM_RATE = 0.2
BETA_FIRST = 0.9
BETA_SECOND = 0.95
ADAM_EPS = 1e-08
MASK_FLOOR = -1e30

F32 = jnp.float32
BF16 = jnp.bfloat16
BOTH = ("dp", "ctx")
LANES = 128


def matrix_shapes():
    return [(D, QD), (D, KVD), (D, KVD), (QD, D), (D, FF), (D, FF), (FF, D)]


def vector_sizes():
    return [D, D, QD, KVD, KVD]


def mm(left, right, contract=((1,), (0,))):
    return lax.dot_general(left, right, (contract, ((), ())), preferred_element_type=F32)


def split_small(flat, devices):
    result = []
    offset = 0
    for extent_all in vector_sizes():
        extent = extent_all // devices
        result.append(flat[:, offset : offset + extent].reshape(extent_all))
        offset += extent
    return result


def join_small(pieces, devices):
    return jnp.concatenate([piece.reshape(devices, -1) for piece in pieces], axis=1)


def swap(value, mask, devices):
    return lax.ppermute(value, BOTH, [(index, index ^ mask) for index in range(devices)])


def gather_bits(value, bits, me, devices, before=()):
    held = value
    done = list(before)
    for bit in bits:
        place = sum(1 for other in done if other > bit)
        got = swap(held, bit, devices)
        mine = (me & bit) != 0
        held = jnp.where(
            mine, jnp.stack([got, held], axis=place), jnp.stack([held, got], axis=place)
        )
        done.append(bit)
    return held


def scatter_start(held, left, bit, me, devices):
    left = sorted(left, reverse=True)
    axis = left.index(bit)
    mine = jnp.where((me & bit) != 0, 1, 0)
    sent = lax.dynamic_index_in_dim(held, 1 - mine, axis, keepdims=False).astype(BF16)
    kept = lax.dynamic_index_in_dim(held, mine, axis, keepdims=False)
    return kept, swap(sent, bit, devices)


def scatter_end(parts):
    return (parts[0].astype(F32) + parts[1].astype(F32)).astype(BF16)


def scatter_sum(value, bits, me, devices):
    left = list(bits)
    held = value
    for bit in bits:
        held = scatter_end(scatter_start(held, left, bit, me, devices))
        left.remove(bit)
    return held


def choose(value, mine, axis):
    return lax.dynamic_index_in_dim(value, mine, axis, keepdims=False)


def to_owner(value, core_bit, x_bit, me, devices):
    core = jnp.where((me & core_bit) != 0, 1, 0)
    across = jnp.where((me & x_bit) != 0, 1, 0)
    got = swap(choose(value, 1 - core, 1), core_bit, devices)
    value = jnp.stack([choose(value, core, 1), got], axis=1)
    got = swap(choose(value, 1 - across, 0), x_bit, devices)
    return jnp.stack([choose(value, across, 0), got])


def from_owner(value, core_bit, x_bit, me, devices):
    got = swap(value[1], x_bit, devices)
    value = jnp.where(
        (me & x_bit) != 0, jnp.stack([got, value[0]]), jnp.stack([value[0], got])
    )
    got = swap(value[:, 1], core_bit, devices)
    return jnp.where(
        (me & core_bit) != 0,
        jnp.stack([got, value[:, 0]], axis=1),
        jnp.stack([value[:, 0], got], axis=1),
    )


def rotate(values, cosine, sine_part):
    midpoint = HD // 2
    turned = jnp.concatenate([-values[:, midpoint:], values[:, :midpoint]], axis=1)
    return values * cosine + turned * sine_part


def rotate_back(gradient, cosine, sine_part):
    midpoint = HD // 2
    scaled = gradient * sine_part
    turned = jnp.concatenate([scaled[:, midpoint:], -scaled[:, :midpoint]], axis=1)
    return gradient * cosine + turned


def norm_backward(source, scale_row, gain, incoming):
    gain_grad = jnp.sum(incoming * source * scale_row, axis=0)
    weighted = incoming * gain
    result = scale_row * weighted - source * scale_row**3 * jnp.mean(
        weighted * source, axis=-1, keepdims=True
    )
    return (result, gain_grad)


def halves_of(span):
    return [slice(0, span // 2), slice(span // 2, span)]


def fill_mask(info, mask, chunk, span):
    key = chunk * span + lax.broadcasted_iota(jnp.int32, (span, span), 0)
    query = info[0] * span + lax.broadcasted_iota(jnp.int32, (span, span), 1)
    key_doc = (key >= info[2]).astype(jnp.int32) + (key >= info[1]).astype(jnp.int32)
    query_doc = (query >= info[2]).astype(jnp.int32) + (query >= info[1]).astype(jnp.int32)
    allowed = jnp.logical_and(key_doc == query_doc, key <= query)
    mask[chunk] = jnp.where(allowed, 0.0, MASK_FLOOR).astype(F32)


def attend_kernel(info, kv, q, out, lse, keys, mask, best, total, acc):
    head = pl.program_id(0)
    span = q.shape[-1]
    mine = info[0]
    chunks = mine + 1

    @pl.when(head == 0)
    def _():
        def fill(chunk, carry):
            slot = jnp.bitwise_xor(chunk, mine)
            keys[chunk] = kv[slot, :HD, :].astype(F32).T.astype(BF16)
            fill_mask(info, mask, chunk, span)
            return carry

        lax.fori_loop(0, chunks, fill, 0)

    best[...] = jnp.full(best.shape, MASK_FLOOR, F32)
    total[...] = jnp.zeros(total.shape, F32)
    acc[...] = jnp.zeros(acc.shape, F32)
    queries = q[0]

    def step(index, carry):
        chunk = mine - index
        slot = jnp.bitwise_xor(chunk, mine)
        for lanes in halves_of(span):
            scores = (
                jnp.dot(keys[chunk], queries[:, lanes], preferred_element_type=F32)
                + mask[chunk, :, lanes]
            )
            old = best[:, lanes]
            new = jnp.maximum(old, jnp.max(scores, axis=0, keepdims=True))
            present = jnp.exp(scores - new)
            shrink = jnp.exp(old - new)
            best[:, lanes] = new
            total[:, lanes] = total[:, lanes] * shrink + jnp.sum(present, axis=0, keepdims=True)
            acc[:, lanes] = acc[:, lanes] * shrink + jnp.dot(
                kv[slot, HD:, :], present.astype(BF16), preferred_element_type=F32
            )
        return carry

    lax.fori_loop(0, chunks, step, 0)
    out[0] = acc[...] / total[...]
    lse[0] = best[...] + jnp.log(total[...])


def attend_back_kernel(
    info, kv, q, dout, lse, delta, dq, dkv, keys, values, mask, dk, dv, acc
):
    head = pl.program_id(0)
    span = q.shape[-1]
    mine = info[0]
    chunks = mine + 1
    n_ctx = kv.shape[0]

    @pl.when(head == 0)
    def _():
        dk[...] = jnp.zeros(dk.shape, F32)
        dv[...] = jnp.zeros(dv.shape, F32)

        def fill(chunk, carry):
            slot = jnp.bitwise_xor(chunk, mine)
            keys[chunk] = kv[slot, :HD, :].astype(F32).T.astype(BF16)
            values[chunk] = kv[slot, HD:, :].astype(F32).T.astype(BF16)
            fill_mask(info, mask, chunk, span)
            return carry

        lax.fori_loop(0, chunks, fill, 0)

    acc[...] = jnp.zeros(acc.shape, F32)
    queries = q[0]
    douts = dout[0]
    query_rows = queries.astype(F32).T.astype(BF16)
    dout_rows = douts.astype(F32).T.astype(BF16)

    def step(chunk, carry):
        slot = jnp.bitwise_xor(chunk, mine)
        value_sum, key_sum = dv[chunk], dk[chunk]
        for lanes in halves_of(span):
            scores = (
                jnp.dot(keys[chunk], queries[:, lanes], preferred_element_type=F32)
                + mask[chunk, :, lanes]
            )
            shares = jnp.exp(scores - lse[0, :, lanes])
            share_grad = jnp.dot(values[chunk], douts[:, lanes], preferred_element_type=F32)
            score_grad = (shares * (share_grad - delta[0, :, lanes])).astype(BF16)
            value_sum += jnp.dot(
                shares.astype(BF16), dout_rows[lanes, :], preferred_element_type=F32
            )
            key_sum += jnp.dot(score_grad, query_rows[lanes, :], preferred_element_type=F32)
            acc[:, lanes] += jnp.dot(kv[slot, :HD, :], score_grad, preferred_element_type=F32)
        dv[chunk], dk[chunk] = value_sum, key_sum
        return carry

    lax.fori_loop(0, chunks, step, 0)
    dq[0] = acc[...] * HD ** (-0.5)

    @pl.when(head == HEADS // KVH - 1)
    def _():
        for chunk in range(n_ctx):
            dkv[chunk, :HD, :] = dk[chunk].T.astype(BF16)
            dkv[chunk, HD:, :] = dv[chunk].T.astype(BF16)


def attend(info, kv, q):
    heads, _, span = q.shape
    n_ctx = kv.shape[0]
    per_head = lambda rows: pl.BlockSpec((1, rows, span), lambda head: (head, 0, 0))
    return pl.pallas_call(
        attend_kernel,
        grid=(heads,),
        in_specs=[
            pl.BlockSpec(memory_space=pltpu.SMEM),
            pl.BlockSpec(kv.shape, lambda head: (0, 0, 0)),
            per_head(HD),
        ],
        out_specs=[per_head(HD), per_head(1)],
        out_shape=[
            jax.ShapeDtypeStruct((heads, HD, span), F32),
            jax.ShapeDtypeStruct((heads, 1, span), F32),
        ],
        scratch_shapes=[
            pltpu.VMEM((n_ctx, span, HD), BF16),
            pltpu.VMEM((n_ctx, span, span), F32),
            pltpu.VMEM((1, span), F32),
            pltpu.VMEM((1, span), F32),
            pltpu.VMEM((HD, span), F32),
        ],
        compiler_params=pltpu.CompilerParams(vmem_limit_bytes=40 * 1024 * 1024),
        cost_estimate=pl.CostEstimate(
            flops=4 * heads * span * span * n_ctx * HD * 4,
            bytes_accessed=4 * heads * span * HD * 2,
            transcendentals=heads * span * span * n_ctx,
        ),
        name="attend",
    )(info, kv, q)


def attend_back(info, kv, q, dout, lse, delta):
    heads, _, span = q.shape
    n_ctx = kv.shape[0]
    per_head = lambda rows: pl.BlockSpec((1, rows, span), lambda head: (head, 0, 0))
    return pl.pallas_call(
        attend_back_kernel,
        grid=(heads,),
        in_specs=[
            pl.BlockSpec(memory_space=pltpu.SMEM),
            pl.BlockSpec(kv.shape, lambda head: (0, 0, 0)),
            per_head(HD),
            per_head(HD),
            per_head(1),
            per_head(1),
        ],
        out_specs=[per_head(HD), pl.BlockSpec(kv.shape, lambda head: (0, 0, 0))],
        out_shape=[
            jax.ShapeDtypeStruct((heads, HD, span), F32),
            jax.ShapeDtypeStruct(kv.shape, BF16),
        ],
        scratch_shapes=[
            pltpu.VMEM((n_ctx, span, HD), BF16),
            pltpu.VMEM((n_ctx, span, HD), BF16),
            pltpu.VMEM((n_ctx, span, span), F32),
            pltpu.VMEM((n_ctx, span, HD), F32),
            pltpu.VMEM((n_ctx, span, HD), F32),
            pltpu.VMEM((HD, span), F32),
        ],
        compiler_params=pltpu.CompilerParams(vmem_limit_bytes=40 * 1024 * 1024),
        cost_estimate=pl.CostEstimate(
            flops=10 * heads * span * span * n_ctx * HD * 4,
            bytes_accessed=8 * heads * span * HD * 2,
            transcendentals=heads * span * span * n_ctx,
        ),
        name="attend_back",
    )(info, kv, q, dout, lse, delta)


def forward_backward_kernel(
    x0, x1, dy0, dy1, gate, up, down, act_out, gate_back_out, up_back_out, back_out, x_out, dy_out
):
    first = pl.program_id(0) == 0
    x = jnp.where(first, x0[...], x1[...])
    dy = jnp.where(first, dy0[...], dy1[...])
    x_out[...] = x
    dy_out[...] = dy
    gate_pre = jnp.dot(x, gate[...], preferred_element_type=F32)
    up_pre = jnp.dot(x, up[...], preferred_element_type=F32)
    grad_act = mm(dy, down[...], ((1,), (1,)))
    sigmoid_gate = jax.nn.sigmoid(gate_pre)
    swish = gate_pre * sigmoid_gate
    slope = sigmoid_gate * (1.0 + gate_pre * (1.0 - sigmoid_gate))
    act_out[...] = (swish * up_pre).astype(BF16)
    gate_back = (grad_act * up_pre * slope).astype(BF16)
    up_back = (grad_act * swish).astype(BF16)
    gate_back_out[...] = gate_back
    up_back_out[...] = up_back
    back_out[...] = (
        mm(gate_back, gate[...], ((1,), (1,))) + mm(up_back, up[...], ((1,), (1,)))
    ).astype(BF16)


def feed_forward(x, dy, gate, up, down):
    span, width = x[0].shape
    units = gate.shape[1]
    whole = lambda shape: pl.BlockSpec(shape, lambda block: (0, 0))
    line = lambda columns: pl.BlockSpec((span, columns), lambda block: (block, 0))
    columns = [units, units, units, width, width, width]
    return pl.pallas_call(
        forward_backward_kernel,
        grid=(2,),
        in_specs=[whole((span, width))] * 4
        + [whole((width, units))] * 2
        + [whole((units, width))],
        out_specs=[line(count) for count in columns],
        out_shape=[jax.ShapeDtypeStruct((2 * span, count), BF16) for count in columns],
        compiler_params=pltpu.CompilerParams(vmem_limit_bytes=58 * 1024 * 1024),
        cost_estimate=pl.CostEstimate(
            flops=20 * span * width * units,
            bytes_accessed=6 * width * units + 2 * span * 10 * width,
            transcendentals=2 * span * units,
        ),
        name="feed_forward",
    )(*x, *dy, gate, up, down)


BLOCK = 128


def block_pairs(count):
    return [(low, high) for low in range(count) for high in range(low, count)]


def gram_kernel(rows, out):
    count = rows.shape[1] // BLOCK
    place = 0
    for low in range(count):
        line = lax.dot_general(
            rows[:, low * BLOCK : (low + 1) * BLOCK],
            rows[:, low * BLOCK :],
            (((0,), (0,)), ((), ())),
            preferred_element_type=F32,
        ).astype(BF16)
        for high in range(low, count):
            out[place] = line[:, (high - low) * BLOCK : (high - low + 1) * BLOCK]
            place += 1
    for extra in range(place, out.shape[0]):
        out[extra] = jnp.zeros((BLOCK, BLOCK), BF16)


def gram_blocks(rows, places):
    return pl.pallas_call(
        gram_kernel,
        out_shape=jax.ShapeDtypeStruct((places, BLOCK, BLOCK), BF16),
        compiler_params=pltpu.CompilerParams(vmem_limit_bytes=32 * 1024 * 1024),
        name="gram",
    )(rows)


def newton_schulz(gram, low, poly, mixed, rows):
    size = gram.shape[0]
    part = size // 2 if size % 16 == 0 and size > BLOCK else size
    parts = [pl.ds(begin, part) for begin in range(0, size, part)]
    row_id = lax.broadcasted_iota(jnp.int32, (size, size), 0)
    column_id = lax.broadcasted_iota(jnp.int32, (size, size), 1)
    square = jnp.where(row_id == column_id, gram[...], 0.0)
    square = jnp.sum(jnp.sum(square, axis=0, keepdims=True), axis=1, keepdims=True)
    scale = 1.0 / (jnp.sqrt(square) + 1e-07)
    for place in parts:
        scaled = gram[place, :] * (scale * scale)
        gram[place, :] = scaled
        low[place, :] = scaled.astype(BF16)
    work = (rows * scale).astype(BF16)
    for step in range(NS_STEPS):
        for place in parts:
            second = jnp.dot(low[place, :], low[...], preferred_element_type=F32)
            poly[place, :] = (NS_SQUARE * gram[place, :] + NS_CUBIC * second).astype(BF16)
        moved = jnp.dot(work, poly[...], preferred_element_type=F32)
        work = (NS_LINEAR * work.astype(F32) + moved).astype(BF16)
        if step + 1 < NS_STEPS:
            for place in parts:
                first = jnp.dot(poly[place, :], low[...], preferred_element_type=F32)
                mixed[place, :] = first.astype(BF16)
                gram[place, :] = (
                    NS_LINEAR * NS_LINEAR * gram[place, :] + (2.0 * NS_LINEAR) * first
                )
            for place in parts:
                second = jnp.dot(poly[place, :], mixed[...], preferred_element_type=F32)
                renewed = gram[place, :] + second
                gram[place, :] = renewed
                low[place, :] = renewed.astype(BF16)
    return work


def wide_kernel(blocks, rows, out, gram, low, poly, mixed):
    for place, (first, second) in enumerate(block_pairs(gram.shape[0] // BLOCK)):
        tile = blocks[place].astype(F32)
        gram[first * BLOCK : (first + 1) * BLOCK, second * BLOCK : (second + 1) * BLOCK] = tile
        if first != second:
            gram[second * BLOCK : (second + 1) * BLOCK, first * BLOCK : (first + 1) * BLOCK] = tile.T
    out[...] = newton_schulz(gram, low, poly, mixed, rows[...].astype(F32))


def square_scratch(size):
    return [
        pltpu.VMEM((size, size), F32),
        pltpu.VMEM((size, size), BF16),
        pltpu.VMEM((size, size), BF16),
        pltpu.VMEM((size, size), BF16),
    ]


def orthogonal_wide(blocks, rows):
    return pl.pallas_call(
        wide_kernel,
        out_shape=jax.ShapeDtypeStruct(rows.shape, BF16),
        scratch_shapes=square_scratch(rows.shape[1]),
        compiler_params=pltpu.CompilerParams(vmem_limit_bytes=40 * 1024 * 1024),
        cost_estimate=pl.CostEstimate(
            flops=14 * rows.shape[1] ** 3, bytes_accessed=4 * rows.size, transcendentals=0
        ),
        name="newton_wide",
    )(blocks, rows)


def whole_kernel(widths, whole, rows, out, *scratch):
    begin = 0
    for index, width in enumerate(widths):
        gram, low, poly, mixed = scratch[4 * index : 4 * index + 4]
        for first in range(0, width, BLOCK):
            gram[first : first + BLOCK, :] = lax.dot_general(
                whole[:, begin + first : begin + first + BLOCK],
                whole[:, begin : begin + width],
                (((0,), (0,)), ((), ())),
                preferred_element_type=F32,
            )
        out[:, begin : begin + width] = newton_schulz(
            gram, low, poly, mixed, rows[:, begin : begin + width]
        )
        begin += width


def orthogonal_whole(whole, rows, widths):
    scratch = []
    for width in widths:
        scratch += square_scratch(width)
    return pl.pallas_call(
        lambda *refs: whole_kernel(widths, *refs),
        out_shape=jax.ShapeDtypeStruct(rows.shape, BF16),
        scratch_shapes=scratch,
        compiler_params=pltpu.CompilerParams(vmem_limit_bytes=48 * 1024 * 1024),
        cost_estimate=pl.CostEstimate(
            flops=16 * sum(width**3 for width in widths),
            bytes_accessed=2 * whole.size,
            transcendentals=0,
        ),
        name="newton_whole",
    )(whole, rows)


def from_flat(flat, base, target, height, breadth):
    lines = breadth // LANES
    for begin in range(0, height, 8):
        count = min(8, height - begin)
        for index in range(lines):
            start = base + begin * lines + index
            if lines == 1:
                tile = flat[start : start + count, :]
            else:
                tile = flat[pl.ds(start, count, stride=lines), :]
            target[begin : begin + count, index * LANES : (index + 1) * LANES] = tile


def to_flat(flat, base, value, height, breadth):
    lines = breadth // LANES
    for begin in range(0, height, 8):
        count = min(8, height - begin)
        for index in range(lines):
            start = base + begin * lines + index
            tile = value(slice(begin, begin + count), slice(index * LANES, (index + 1) * LANES))
            if lines == 1:
                flat[start : start + count, :] = tile
            else:
                flat[pl.ds(start, count, stride=lines), :] = tile


def section_bases(devices):
    bases = []
    base = 0
    for height, breadth in matrix_shapes():
        bases.append(base)
        base += height // devices * breadth // LANES
    return bases


def pack_kernel(devices, group, flat, extra, qkv_out, out_out, wide_out, down_out, qkv, out, wide, down):
    rows = D // devices
    frows = FF // devices
    bases = section_bases(devices)
    qkv[...] = jnp.zeros(qkv.shape, F32)
    out[...] = jnp.zeros(out.shape, F32)
    from_flat(flat, bases[0], qkv.at[:, :QD], rows, QD)
    from_flat(flat, bases[1], qkv.at[:, QD : QD + KVD], rows, KVD)
    from_flat(flat, bases[2], qkv.at[:, QD + KVD :], rows, KVD)
    if extra is not None:
        qkv[rows : rows + 1, :LANES] = extra[...]
    from_flat(flat, bases[3], out, rows, D)
    from_flat(flat, bases[6], down, FF // devices, D)
    qkv_out[...] = qkv[...].astype(qkv_out.dtype)
    out_out[...] = out[...].astype(out_out.dtype)
    down_out[...] = down[...].astype(down_out.dtype)
    for which in range(2):
        from_flat(flat, bases[4 + which], wide, rows, FF)
        targets = devices // group
        for target in range(targets):
            piece = jnp.concatenate(
                [
                    wide[:, (turn * targets + target) * frows : (turn * targets + target + 1) * frows]
                    for turn in range(group)
                ],
                axis=1,
            )
            if group == 1:
                wide_out[target, :, which * frows : (which + 1) * frows] = piece.astype(wide_out.dtype)
            else:
                wide_out[target, which] = piece.astype(wide_out.dtype)


def pack(flat, extra, devices, group, dtype):
    rows = D // devices
    frows = FF // devices
    padded = (rows // 16 + 1) * 16
    targets = devices // group
    wide = (targets, rows, 2 * frows) if group == 1 else (targets, 2, rows, group * frows)
    shapes = [(padded, QD + 2 * KVD), (padded, D), wide, (frows, D)]
    types = [dtype, dtype, BF16, dtype]
    if extra is None:
        body = lambda flat_ref, *refs: pack_kernel(devices, group, flat_ref, None, *refs)
        operands = [flat]
    else:
        body = lambda *refs: pack_kernel(devices, group, *refs)
        operands = [flat, extra]
    return pl.pallas_call(
        body,
        out_shape=[jax.ShapeDtypeStruct(shape, kind) for shape, kind in zip(shapes, types)],
        scratch_shapes=[
            pltpu.VMEM((padded, QD + 2 * KVD), F32),
            pltpu.VMEM((padded, D), F32),
            pltpu.VMEM((rows, FF), F32),
            pltpu.VMEM((frows, D), F32),
        ],
        compiler_params=pltpu.CompilerParams(vmem_limit_bytes=32 * 1024 * 1024),
        cost_estimate=pl.CostEstimate(flops=0, bytes_accessed=6 * flat.size, transcendentals=0),
        name="pack",
    )(*operands)


def update_kernel(devices, decay, factors, flat, qkv, out, wide, down, result, moved, rows_wide):
    rows = D // devices
    frows = FF // devices
    bases = section_bases(devices)
    whole = qkv[...].astype(F32)
    out_whole = out[...].astype(F32)
    down_whole = down[...].astype(F32)
    parts = [
        lambda r, c: whole[r, c],
        lambda r, c: whole[r, slice(QD + c.start, QD + c.stop)],
        lambda r, c: whole[r, slice(QD + KVD + c.start, QD + KVD + c.stop)],
        lambda r, c: out_whole[r, c],
    ]
    shapes = matrix_shapes()
    for index, part in enumerate(parts):
        to_flat(
            moved, bases[index], lambda r, c: part(r, c) * factors[index], rows, shapes[index][1]
        )
    to_flat(moved, bases[6], lambda r, c: down_whole[r, c] * factors[6], frows, D)
    for which in range(2):
        for source in range(devices):
            rows_wide[:, source * frows : (source + 1) * frows] = wide[
                source, :, which * frows : (which + 1) * frows
            ].astype(F32)
        to_flat(
            moved, bases[4 + which], lambda r, c: rows_wide[r, c] * factors[4 + which], rows, FF
        )
    result[...] = decay * flat[...] + moved[...]


def update(flat, qkv, out, wide, down, devices, decay, factors):
    return pl.pallas_call(
        lambda *refs: update_kernel(devices, decay, factors, *refs),
        out_shape=jax.ShapeDtypeStruct(flat.shape, F32),
        scratch_shapes=[
            pltpu.VMEM(flat.shape, F32),
            pltpu.VMEM((D // devices, FF), F32),
        ],
        compiler_params=pltpu.CompilerParams(vmem_limit_bytes=32 * 1024 * 1024),
        cost_estimate=pl.CostEstimate(flops=0, bytes_accessed=10 * flat.size, transcendentals=0),
        name="update",
    )(flat, qkv, out, wide, down)


def on_device(
    block_input,
    cotangent,
    lengths,
    doc_starts,
    master,
    momentum,
    vectors,
    vector_first,
    vector_second,
):
    n_dp = lax.axis_size("dp")
    n_ctx = lax.axis_size("ctx")
    devices = n_dp * n_ctx
    rows = D // devices
    frows = FF // devices
    fblock = FF // n_ctx
    slots, span, width = block_input.shape
    tokens = slots * span
    group = HEADS // KVH
    qkv = QD + 2 * KVD
    my_ctx = lax.axis_index("ctx")
    me = lax.axis_index("dp") * n_ctx + my_ctx
    core_bit, x_bit = 1, 2
    ctx_bits = [core_bit, x_bit]
    dp_bits = [n_ctx << index for index in range(n_dp.bit_length() - 1)]
    all_bits = ctx_bits + dp_bits
    many = tuple([2] * len(all_bits))
    padded = (rows // 16 + 1) * 16

    def padded_pieces(part):
        part = part.reshape(devices, rows, part.shape[1])
        part = jnp.pad(part, ((0, 0), (0, padded - rows), (0, 0)))
        return part.reshape(many + part.shape[1:])

    master_flat = master.reshape(-1, LANES)
    momentum_flat = momentum.reshape(-1, LANES)
    small = jnp.pad(vectors, ((0, 0), (0, LANES - vectors.shape[1])))
    qkv_local, out_local, gate_up, down_local = pack(master_flat, small, devices, n_dp, BF16)

    attn_full = gather_bits(
        jnp.concatenate([qkv_local, out_local], axis=1), dp_bits[::-1], me, devices
    )
    qkv_full = gather_bits(attn_full[..., :qkv], ctx_bits[::-1], me, devices, dp_bits)
    qkv_full = qkv_full.reshape(devices, padded, qkv)
    gain_first, gain_second, bias_query, bias_key, bias_value = [
        piece.astype(F32) for piece in split_small(qkv_full[:, rows], devices)
    ]
    w_qkv = qkv_full[:, :rows].reshape(D, qkv)

    gate_up, attn_full = lax.optimization_barrier((gate_up, attn_full))
    came = [choose(gate_up, my_ctx, 0)] + [
        swap(choose(gate_up, my_ctx ^ mask, 0), mask, devices) for mask in range(1, n_ctx)
    ]
    ordered = []
    for source in range(n_ctx):
        piece = came[0]
        for mask in range(1, n_ctx):
            piece = jnp.where(my_ctx ^ mask == source, came[mask], piece)
        ordered.append(piece)
    gate_up = jnp.concatenate(ordered, axis=1)
    w_gate, w_up = [lax.all_gather(gate_up[index], "dp", axis=0, tiled=True) for index in range(2)]

    def to_rows(pair):
        both = pair.T.reshape(devices, rows, 2 * frows)
        return lax.all_to_all(both, BOTH, split_axis=0, concat_axis=0, tiled=True)

    length, second = lengths[0], doc_starts[0]
    places = my_ctx * span + jnp.arange(span, dtype=jnp.int32)
    doc_begin = jnp.where(places >= length, length, jnp.where(places >= second, second, 0))
    position = (places - doc_begin).astype(F32)
    live = (places < length)[:, None]
    info = jnp.stack([my_ctx, length, second]).astype(jnp.int32)
    inverse = ROPE_BASE ** (-2.0 * jnp.arange(HD // 2, dtype=F32) / HD)
    angles = inverse[:, None] * position[None, :]
    cosine, sine_part = jnp.cos(angles), jnp.sin(angles)
    cosine = jnp.concatenate([cosine, cosine], axis=0)[None]
    sine_part = jnp.concatenate([sine_part, sine_part], axis=0)[None]

    def from_ctx(value):
        other_core = swap(value, core_bit, devices)
        other_x = swap(value, x_bit, devices)
        return value, other_core, other_x, swap(other_x, core_bit, devices)

    cot_here = jnp.where(live, cotangent.reshape(tokens, width), jnp.zeros((), BF16))

    def pair_of_heads(kv, index):
        begin = index * HD
        return jnp.concatenate(
            [kv[:, begin : begin + HD], kv[:, KVD + begin : KVD + begin + HD]], axis=1
        )

    inputs = block_input.astype(F32).reshape(tokens, width)
    scale_one = lax.rsqrt(jnp.mean(inputs * inputs, axis=-1, keepdims=True) + NORM_EPS)
    normed_one = (inputs * scale_one * gain_first).astype(BF16)
    bias = jnp.concatenate([bias_query, bias_key, bias_value])
    pre = mm(w_qkv, normed_one, ((0,), (1,))) + bias[:, None]
    turned = rotate(
        pre[: QD + KVD].reshape(HEADS + KVH, HD, tokens), cosine, sine_part
    )
    queries = (turned[:HEADS].astype(BF16).astype(F32) * HD ** (-0.5)).astype(BF16)
    kv_here = jnp.concatenate(
        [turned[HEADS:].astype(BF16).reshape(KVD, tokens), pre[QD + KVD :].astype(BF16)], axis=0
    )
    kv = jnp.stack(from_ctx(kv_here))
    down_bits = dp_bits[::-1]
    down_local, kv_here = lax.optimization_barrier((down_local, kv_here))
    down_part = gather_bits(down_local, down_bits[:1], me, devices)
    out_full, down_part, cot_here, kv = lax.optimization_barrier(
        (attn_full[..., qkv:], down_part, cot_here, kv)
    )
    halves = []
    for index in range(KVH):
        if index == 1:
            out_full, down_part, halves = lax.optimization_barrier((out_full, down_part, halves))
        out_full = gather_bits(
            out_full, ctx_bits[::-1][index : index + 1], me, devices, dp_bits + ctx_bits[::-1][:index]
        )
        down_part = gather_bits(
            down_part, down_bits[index + 1 : index + 2], me, devices, down_bits[: index + 1]
        )
        kv_one = pair_of_heads(kv, index)
        halves.append(attend(info, kv_one, queries[index * group : (index + 1) * group]))
    attended = jnp.concatenate([half[0] for half in halves], axis=0)
    log_total = jnp.concatenate([half[1] for half in halves], axis=0)
    w_out = out_full.reshape(devices, padded, D)[:, :rows].reshape(QD, D)
    w_down = gather_bits(down_part, down_bits[KVH + 1 :], me, devices, down_bits[: KVH + 1])
    w_down = w_down.reshape(fblock, D)

    mixed_heads = attended.reshape(QD, tokens).astype(BF16)
    hidden = inputs + mm(mixed_heads, w_out, ((0,), (0,)))
    scale_two = lax.rsqrt(jnp.mean(hidden * hidden, axis=-1, keepdims=True) + NORM_EPS)
    normed_two = (hidden * scale_two * gain_second).astype(BF16)

    normed = from_ctx(normed_two)
    cot = from_ctx(cot_here)
    results = [
        feed_forward(normed[begin : begin + 2], cot[begin : begin + 2], w_gate, w_up, w_down)
        for begin in (0, 2)
    ]
    acts, gate_backs, up_backs, back_parts, normed_halves, cot_halves = zip(*results)

    def to_ctx(halves):
        crossed = swap(halves[1][span:], core_bit, devices)
        far = (halves[1][:span].astype(F32) + crossed.astype(F32)).astype(BF16)
        near = swap(halves[0][span:], core_bit, devices)
        near = halves[0][:span].astype(F32) + near.astype(F32)
        return near + swap(far, x_bit, devices).astype(F32), far

    normed_two_grad, ready = to_ctx(back_parts)
    (acts, gate_backs, up_backs), ready = lax.optimization_barrier(
        ((acts, gate_backs, up_backs), ready)
    )

    def over_tokens(left, right):
        return mm(left[0], right[0], ((0,), (0,))) + mm(left[1], right[1], ((0,), (0,)))

    dp_shape = tuple([2] * len(dp_bits)) + (frows, D)
    dp_order = dp_bits[1:] + dp_bits[:1]
    down_parts = scatter_start(
        over_tokens(acts, cot_halves).astype(BF16).reshape(dp_shape), dp_bits, dp_order[0], me, devices
    )
    gate_parts = scatter_start(
        over_tokens(gate_backs, normed_halves).astype(BF16).reshape(dp_shape),
        dp_bits,
        dp_bits[0],
        me,
        devices,
    )
    up_parts = scatter_start(
        over_tokens(up_backs, normed_halves).astype(BF16).reshape(dp_shape),
        dp_bits,
        dp_bits[0],
        me,
        devices,
    )
    momentum_flat, up_parts = lax.optimization_barrier((momentum_flat, up_parts))
    old_qkv, old_out, old_pair, old_down = pack(momentum_flat, None, devices, 1, F32)
    old_pair = lax.all_to_all(old_pair, BOTH, split_axis=0, concat_axis=0, tiled=True)
    old_pair = old_pair.reshape(D, 2 * frows).T

    out_sum, _ = to_ctx([mm(act, w_down).astype(BF16) for act in acts])
    layer_out = jnp.where(live, hidden + out_sum, 0.0)

    out_grad = cot_here.astype(F32)
    hidden_norm_grad, grad_gain_second = norm_backward(
        hidden, scale_two, gain_second, normed_two_grad
    )
    hidden_grad = out_grad + hidden_norm_grad
    hidden_low = hidden_grad.astype(BF16)
    heads_grad = mm(w_out, hidden_low, ((1,), (1,))).astype(BF16).reshape(HEADS, HD, tokens)
    delta = jnp.sum(heads_grad.astype(F32) * attended, axis=1, keepdims=True)
    grad_output = mm(mixed_heads, hidden_low)
    query_grads, kv_parts = [], []
    wide_parts = [gate_parts, up_parts, down_parts]
    wide_orders = [list(dp_bits), list(dp_bits), list(dp_order)]
    for index in range(KVH):
        chosen = slice(index * group, (index + 1) * group)
        kv_one = pair_of_heads(kv, index)
        query_grad, kv_grad = attend_back(
            info, kv_one, queries[chosen], heads_grad[chosen], log_total[chosen], delta[chosen]
        )
        (query_grad, kv_grad), wide_parts = lax.optimization_barrier(
            ((query_grad, kv_grad), wide_parts)
        )
        query_grads.append(query_grad)
        kv_parts.append(
            scatter_sum(kv_grad.reshape(2, 2, 2 * HD, span), ctx_bits, me, devices)
        )
        for place in range(3):
            wide_orders[place].pop(0)
            if wide_orders[place]:
                wide_parts[place] = scatter_start(
                    scatter_end(wide_parts[place]),
                    wide_orders[place],
                    wide_orders[place][0],
                    me,
                    devices,
                )
    kv_grads = [part.astype(F32).reshape(2, HD, span) for part in kv_parts]
    qk_grad = jnp.concatenate(query_grads + [grad[:1] for grad in kv_grads], axis=0)
    qk_back = rotate_back(qk_grad, cosine, sine_part).reshape(QD + KVD, tokens)
    qkv_back = jnp.concatenate(
        [qk_back] + [grad[1] for grad in kv_grads], axis=0
    ).astype(BF16)
    grad_qkv = mm(normed_one, qkv_back, ((0,), (1,)))
    grad_bias = jnp.sum(qkv_back.astype(F32), axis=1)
    normed_one_grad = mm(qkv_back, w_qkv, ((0,), (1,)))
    input_norm_grad, grad_gain_first = norm_backward(inputs, scale_one, gain_first, normed_one_grad)
    input_grad = (hidden_grad + input_norm_grad).astype(BF16).reshape(slots, span, width)

    vector_part = join_small(
        [
            grad_gain_first,
            grad_gain_second,
            grad_bias[:QD],
            grad_bias[QD : QD + KVD],
            grad_bias[QD + KVD :],
        ],
        devices,
    )
    vector_grad = jnp.sum(
        lax.all_to_all(vector_part, BOTH, split_axis=0, concat_axis=0, tiled=True),
        axis=0,
        keepdims=True,
    )
    grad_qkv, wide_parts = lax.optimization_barrier((grad_qkv, wide_parts))
    gate_sum, up_sum, down_sum = [
        scatter_sum(scatter_end(parts), order[1:], me, devices)
        for parts, order in zip(wide_parts, wide_orders)
    ]
    out_sum_rows = scatter_sum(padded_pieces(grad_output.astype(BF16)), all_bits, me, devices)
    qkv_sum_rows = scatter_sum(padded_pieces(grad_qkv.astype(BF16)), all_bits, me, devices)
    moved_qkv = MOMENTUM_DECAY * old_qkv + qkv_sum_rows.astype(F32)
    moved_out = MOMENTUM_DECAY * old_out + out_sum_rows.astype(F32)
    moved_down = MOMENTUM_DECAY * old_down + down_sum.astype(F32)
    pair_sum = jnp.concatenate([gate_sum, up_sum], axis=0)
    moved_pair = MOMENTUM_DECAY * old_pair.astype(F32) + pair_sum.astype(F32)
    new_momentum = update(
        momentum_flat,
        qkv_sum_rows,
        out_sum_rows,
        to_rows(pair_sum),
        down_sum,
        devices,
        MOMENTUM_DECAY,
        [1.0] * 7,
    ).reshape(momentum.shape)

    mats = jnp.stack(
        [
            moved_pair[:frows],
            moved_pair[frows:],
            moved_down,
            jnp.pad(moved_out, ((0, frows - padded), (0, 0))),
        ]
    ).astype(BF16)
    owned = to_owner(mats.reshape(2, 2, frows, D), core_bit, x_bit, me, devices)
    owned = owned.reshape(n_ctx * frows, D)
    count = len(block_pairs(D // BLOCK))
    places = (count + n_dp - 1) // n_dp * n_dp
    dp_many = tuple([2] * len(dp_bits))
    gram = gram_blocks(owned, places).reshape(dp_many + (places // n_dp, BLOCK, BLOCK))
    gram = scatter_sum(gram, dp_bits, me, devices)
    gram = gather_bits(gram, dp_bits[::-1], me, devices).reshape(places, BLOCK, BLOCK)
    ortho = orthogonal_wide(gram, owned).reshape(2, 2, frows, D)
    ortho = from_owner(ortho, core_bit, x_bit, me, devices).reshape(n_ctx, frows, D)
    ortho_pair = to_rows(ortho[:2].reshape(2 * frows, D))

    def gathered(part):
        full = gather_bits(part.astype(BF16), all_bits[::-1], me, devices)
        return full.reshape(devices * padded, part.shape[1])

    ortho_qkv = orthogonal_whole(gathered(moved_qkv), moved_qkv, (QD, KVD, KVD))
    factors = [
        -MUON_RATE * math.sqrt(max(1.0, breadth / height)) for height, breadth in matrix_shapes()
    ]
    new_master = update(
        master_flat,
        ortho_qkv,
        ortho[3, :padded],
        ortho_pair,
        ortho[2],
        devices,
        1.0 - MUON_RATE * MUON_DECAY,
        factors,
    ).reshape(master.shape)
    first_new = BETA_FIRST * vector_first + (1.0 - BETA_FIRST) * vector_grad
    second_new = BETA_SECOND * vector_second + (1.0 - BETA_SECOND) * vector_grad * vector_grad
    adjusted = (
        first_new
        / (1.0 - BETA_FIRST**STEP)
        / (jnp.sqrt(second_new / (1.0 - BETA_SECOND**STEP)) + ADAM_EPS)
    )
    new_vectors = vectors - ADAM_RATE * adjusted
    return (
        layer_out.astype(BF16).reshape(slots, span, width),
        input_grad,
        new_master,
        new_momentum,
        new_master.astype(BF16),
        new_vectors,
        first_new,
        second_new,
    )


def solution(mesh):
    return jax.shard_map(
        on_device,
        mesh=mesh,
        in_specs=(
            P("dp", "ctx", None),
            P("dp", "ctx", None),
            P("dp"),
            P("dp"),
            P(BOTH, None),
            P(BOTH, None),
            P(BOTH, None),
            P(BOTH, None),
            P(BOTH, None),
        ),
        out_specs=(
            P("dp", "ctx", None),
            P("dp", "ctx", None),
            P(BOTH, None),
            P(BOTH, None),
            P(BOTH, None),
            P(BOTH, None),
            P(BOTH, None),
            P(BOTH, None),
        ),
        check_vma=False,
    )
```

```python
import math

import jax
import jax.numpy as jnp
from jax import lax
from jax.experimental import pallas as pl
from jax.experimental.pallas import tpu as pltpu
from jax.sharding import PartitionSpec as P

D = 896
HEADS = 14
KVH = 2
HD = 64
FF = 4864
SLOT = 2048
NS_STEPS = 3
STEP = 10
QD = 896
KVD = 128

NORM_EPS = 1e-06
ROPE_BASE = 1000000.0
NS_LINEAR = 3.4445
NS_SQUARE = -4.775
NS_CUBIC = 2.0315
MOMENTUM_DECAY = 0.5
MUON_RATE = 0.6
MUON_DECAY = 0.1
ADAM_RATE = 0.2
BETA_FIRST = 0.9
BETA_SECOND = 0.95
ADAM_EPS = 1e-08
MASK_FLOOR = -1e30

F32 = jnp.float32
BF16 = jnp.bfloat16
BOTH = ("dp", "ctx")
LANES = 128


def matrix_shapes():
    return [(D, QD), (D, KVD), (D, KVD), (QD, D), (D, FF), (D, FF), (FF, D)]


def vector_sizes():
    return [D, D, QD, KVD, KVD]


def mm(left, right, contract=((1,), (0,))):
    return lax.dot_general(left, right, (contract, ((), ())), preferred_element_type=F32)


def split_small(flat, devices):
    result = []
    offset = 0
    for extent_all in vector_sizes():
        extent = extent_all // devices
        result.append(flat[:, offset : offset + extent].reshape(extent_all))
        offset += extent
    return result


def join_small(pieces, devices):
    return jnp.concatenate([piece.reshape(devices, -1) for piece in pieces], axis=1)


def swap(value, mask, devices):
    return lax.ppermute(value, BOTH, [(index, index ^ mask) for index in range(devices)])


def gather_bits(value, bits, me, devices, before=()):
    held = value
    done = list(before)
    for bit in bits:
        place = sum(1 for other in done if other > bit)
        got = swap(held, bit, devices)
        mine = (me & bit) != 0
        held = jnp.where(
            mine, jnp.stack([got, held], axis=place), jnp.stack([held, got], axis=place)
        )
        done.append(bit)
    return held


def scatter_split(held, left, bit, me):
    axis = sorted(left, reverse=True).index(bit)
    mine = jnp.where((me & bit) != 0, 1, 0)
    return choose(held, 1 - mine, axis).astype(BF16), choose(held, mine, axis)


def scatter_start(held, left, bit, me, devices):
    sent, kept = scatter_split(held, left, bit, me)
    return kept, swap(sent, bit, devices)


def scatter_end(parts):
    return (parts[0].astype(F32) + parts[1].astype(F32)).astype(BF16)


def scatter_sum(value, bits, me, devices):
    left = list(bits)
    held = value
    for bit in bits:
        held = scatter_end(scatter_start(held, left, bit, me, devices))
        left.remove(bit)
    return held


def choose(value, mine, axis):
    return lax.dynamic_index_in_dim(value, mine, axis, keepdims=False)


def to_owner(value, core_bit, x_bit, me, devices):
    core = jnp.where((me & core_bit) != 0, 1, 0)
    across = jnp.where((me & x_bit) != 0, 1, 0)
    got = swap(choose(value, 1 - core, 1), core_bit, devices)
    value = jnp.stack([choose(value, core, 1), got], axis=1)
    got = swap(choose(value, 1 - across, 0), x_bit, devices)
    return jnp.stack([choose(value, across, 0), got])


def from_owner(value, core_bit, x_bit, me, devices):
    got = swap(value[1], x_bit, devices)
    value = jnp.where(
        (me & x_bit) != 0, jnp.stack([got, value[0]]), jnp.stack([value[0], got])
    )
    got = swap(value[:, 1], core_bit, devices)
    return jnp.where(
        (me & core_bit) != 0,
        jnp.stack([got, value[:, 0]], axis=1),
        jnp.stack([value[:, 0], got], axis=1),
    )


def rotate(values, cosine, sine_part):
    midpoint = HD // 2
    turned = jnp.concatenate([-values[:, midpoint:], values[:, :midpoint]], axis=1)
    return values * cosine + turned * sine_part


def rotate_back(gradient, cosine, sine_part):
    midpoint = HD // 2
    scaled = gradient * sine_part
    turned = jnp.concatenate([scaled[:, midpoint:], -scaled[:, :midpoint]], axis=1)
    return gradient * cosine + turned


def norm_backward(source, scale_row, gain, incoming):
    gain_grad = jnp.sum(incoming * source * scale_row, axis=0)
    weighted = incoming * gain
    result = scale_row * weighted - source * scale_row**3 * jnp.mean(
        weighted * source, axis=-1, keepdims=True
    )
    return (result, gain_grad)


def halves_of(span):
    return [slice(0, span // 2), slice(span // 2, span)]


def fill_mask(info, mask, chunk, span):
    key = chunk * span + lax.broadcasted_iota(jnp.int32, (span, span), 0)
    query = info[0] * span + lax.broadcasted_iota(jnp.int32, (span, span), 1)
    key_doc = (key >= info[2]).astype(jnp.int32) + (key >= info[1]).astype(jnp.int32)
    query_doc = (query >= info[2]).astype(jnp.int32) + (query >= info[1]).astype(jnp.int32)
    allowed = jnp.logical_and(key_doc == query_doc, key <= query)
    mask[chunk] = jnp.where(allowed, 0.0, MASK_FLOOR).astype(F32)


def attend_kernel(info, kv, q, out, lse, keys, mask, best, total, acc):
    head = pl.program_id(0)
    span = q.shape[-1]
    mine = info[0]
    chunks = mine + 1

    @pl.when(head == 0)
    def _():
        def fill(chunk, carry):
            slot = jnp.bitwise_xor(chunk, mine)
            keys[chunk] = kv[slot, :HD, :].astype(F32).T.astype(BF16)
            fill_mask(info, mask, chunk, span)
            return carry

        lax.fori_loop(0, chunks, fill, 0)

    best[...] = jnp.full(best.shape, MASK_FLOOR, F32)
    total[...] = jnp.zeros(total.shape, F32)
    acc[...] = jnp.zeros(acc.shape, F32)
    queries = q[0]

    def step(index, carry):
        chunk = mine - index
        slot = jnp.bitwise_xor(chunk, mine)
        scores = jnp.dot(keys[chunk], queries, preferred_element_type=F32) + mask[chunk]
        old = best[...]
        new = jnp.maximum(old, jnp.max(scores, axis=0, keepdims=True))
        present = jnp.exp(scores - new)
        shrink = jnp.exp(old - new)
        best[...] = new
        total[...] = total[...] * shrink + jnp.sum(present, axis=0, keepdims=True)
        acc[...] = acc[...] * shrink + jnp.dot(
            kv[slot, HD:, :], present.astype(BF16), preferred_element_type=F32
        )
        return carry

    lax.fori_loop(0, chunks, step, 0)
    out[0] = acc[...] / total[...]
    lse[0] = best[...] + jnp.log(total[...])


def attend_back_kernel(
    info, kv, q, dout, lse, delta, before, dq, dkv, keys, values, mask, dk, dv, acc
):
    head = pl.program_id(0)
    span = q.shape[-1]
    mine = info[0]
    chunks = mine + 1
    n_ctx = kv.shape[0]

    @pl.when(head == 0)
    def _():
        dk[...] = jnp.zeros(dk.shape, F32)
        dv[...] = jnp.zeros(dv.shape, F32)

        def fill(chunk, carry):
            slot = jnp.bitwise_xor(chunk, mine)
            keys[chunk] = kv[slot, :HD, :].astype(F32).T.astype(BF16)
            values[chunk] = kv[slot, HD:, :].astype(F32).T.astype(BF16)
            fill_mask(info, mask, chunk, span)
            return carry

        lax.fori_loop(0, chunks, fill, 0)

    acc[...] = jnp.zeros(acc.shape, F32)
    queries = q[0]
    douts = dout[0]
    query_rows = queries.astype(F32).T.astype(BF16)
    dout_rows = douts.astype(F32).T.astype(BF16)

    def step(chunk, carry):
        slot = jnp.bitwise_xor(chunk, mine)
        value_sum, key_sum = dv[chunk], dk[chunk]
        for lanes in halves_of(span):
            scores = (
                jnp.dot(keys[chunk], queries[:, lanes], preferred_element_type=F32)
                + mask[chunk, :, lanes]
            )
            shares = jnp.exp(scores - lse[0, :, lanes])
            share_grad = jnp.dot(values[chunk], douts[:, lanes], preferred_element_type=F32)
            score_grad = (shares * (share_grad - delta[0, :, lanes])).astype(BF16)
            value_sum += jnp.dot(
                shares.astype(BF16), dout_rows[lanes, :], preferred_element_type=F32
            )
            key_sum += jnp.dot(score_grad, query_rows[lanes, :], preferred_element_type=F32)
            acc[:, lanes] += jnp.dot(kv[slot, :HD, :], score_grad, preferred_element_type=F32)
        dv[chunk], dk[chunk] = value_sum, key_sum
        return carry

    lax.fori_loop(0, chunks, step, 0)
    dq[0] = acc[...] * HD ** (-0.5)

    @pl.when(head == pl.num_programs(0) - 1)
    def _():
        for chunk in range(n_ctx):
            sums = jnp.concatenate([dk[chunk].T, dv[chunk].T], axis=0)
            if before is not None:
                sums += before[chunk].astype(F32)
            dkv[chunk] = sums.astype(BF16)


def attend(info, kv, q):
    heads, _, span = q.shape
    n_ctx = kv.shape[0]
    per_head = lambda rows: pl.BlockSpec((1, rows, span), lambda head: (head, 0, 0))
    return pl.pallas_call(
        attend_kernel,
        grid=(heads,),
        in_specs=[
            pl.BlockSpec(memory_space=pltpu.SMEM),
            pl.BlockSpec(kv.shape, lambda head: (0, 0, 0)),
            per_head(HD),
        ],
        out_specs=[per_head(HD), per_head(1)],
        out_shape=[
            jax.ShapeDtypeStruct((heads, HD, span), F32),
            jax.ShapeDtypeStruct((heads, 1, span), F32),
        ],
        scratch_shapes=[
            pltpu.VMEM((n_ctx, span, HD), BF16),
            pltpu.VMEM((n_ctx, span, span), F32),
            pltpu.VMEM((1, span), F32),
            pltpu.VMEM((1, span), F32),
            pltpu.VMEM((HD, span), F32),
        ],
        compiler_params=pltpu.CompilerParams(vmem_limit_bytes=40 * 1024 * 1024),
        cost_estimate=pl.CostEstimate(
            flops=4 * heads * span * span * n_ctx * HD * 4,
            bytes_accessed=4 * heads * span * HD * 2,
            transcendentals=heads * span * span * n_ctx,
        ),
        name="attend",
    )(info, kv, q)


def attend_back(info, kv, q, dout, lse, delta, before):
    heads, _, span = q.shape
    n_ctx = kv.shape[0]
    per_head = lambda rows: pl.BlockSpec((1, rows, span), lambda head: (head, 0, 0))
    whole = pl.BlockSpec(kv.shape, lambda head: (0, 0, 0))
    if before is None:
        body = lambda *refs: attend_back_kernel(*refs[:6], None, *refs[6:])
    else:
        body = attend_back_kernel
    return pl.pallas_call(
        body,
        grid=(heads,),
        in_specs=[
            pl.BlockSpec(memory_space=pltpu.SMEM),
            whole,
            per_head(HD),
            per_head(HD),
            per_head(1),
            per_head(1),
        ]
        + [whole] * (before is not None),
        out_specs=[per_head(HD), whole],
        out_shape=[
            jax.ShapeDtypeStruct((heads, HD, span), F32),
            jax.ShapeDtypeStruct(kv.shape, BF16),
        ],
        scratch_shapes=[
            pltpu.VMEM((n_ctx, span, HD), BF16),
            pltpu.VMEM((n_ctx, span, HD), BF16),
            pltpu.VMEM((n_ctx, span, span), F32),
            pltpu.VMEM((n_ctx, span, HD), F32),
            pltpu.VMEM((n_ctx, span, HD), F32),
            pltpu.VMEM((HD, span), F32),
        ],
        compiler_params=pltpu.CompilerParams(vmem_limit_bytes=40 * 1024 * 1024),
        cost_estimate=pl.CostEstimate(
            flops=10 * heads * span * span * n_ctx * HD * 4,
            bytes_accessed=8 * heads * span * HD * 2,
            transcendentals=heads * span * span * n_ctx,
        ),
        name="attend_back",
    )(*[info, kv, q, dout, lse, delta] + [before] * (before is not None))


def forward_backward_kernel(
    x0, x1, dy0, dy1, gate, up, down, act_out, gate_back_out, up_back_out, back_out, x_out, dy_out
):
    first = pl.program_id(0) == 0
    x = jnp.where(first, x0[...], x1[...])
    dy = jnp.where(first, dy0[...], dy1[...])
    x_out[...] = x
    dy_out[...] = dy
    gate_pre = jnp.dot(x, gate[...], preferred_element_type=F32)
    up_pre = jnp.dot(x, up[...], preferred_element_type=F32)
    grad_act = mm(dy, down[...], ((1,), (1,)))
    sigmoid_gate = jax.nn.sigmoid(gate_pre)
    swish = gate_pre * sigmoid_gate
    slope = sigmoid_gate * (1.0 + gate_pre * (1.0 - sigmoid_gate))
    act_out[...] = (swish * up_pre).astype(BF16)
    gate_back = (grad_act * up_pre * slope).astype(BF16)
    up_back = (grad_act * swish).astype(BF16)
    gate_back_out[...] = gate_back
    up_back_out[...] = up_back
    back_out[...] = (
        mm(gate_back, gate[...], ((1,), (1,))) + mm(up_back, up[...], ((1,), (1,)))
    ).astype(BF16)


def feed_forward(x, dy, gate, up, down):
    span, width = x[0].shape
    units = gate.shape[1]
    whole = lambda shape: pl.BlockSpec(shape, lambda block: (0, 0))
    line = lambda columns: pl.BlockSpec((span, columns), lambda block: (block, 0))
    columns = [units, units, units, width, width, width]
    return pl.pallas_call(
        forward_backward_kernel,
        grid=(2,),
        in_specs=[whole((span, width))] * 4
        + [whole((width, units))] * 2
        + [whole((units, width))],
        out_specs=[line(count) for count in columns],
        out_shape=[jax.ShapeDtypeStruct((2 * span, count), BF16) for count in columns],
        compiler_params=pltpu.CompilerParams(vmem_limit_bytes=58 * 1024 * 1024),
        cost_estimate=pl.CostEstimate(
            flops=20 * span * width * units,
            bytes_accessed=6 * width * units + 2 * span * 10 * width,
            transcendentals=2 * span * units,
        ),
        name="feed_forward",
    )(*x, *dy, gate, up, down)


BLOCK = 128


def block_pairs(count):
    return [(low, high) for low in range(count) for high in range(low, count)]


def gram_kernel(rows, out):
    count = rows.shape[1] // BLOCK
    place = 0
    for low in range(count):
        line = lax.dot_general(
            rows[:, low * BLOCK : (low + 1) * BLOCK],
            rows[:, low * BLOCK :],
            (((0,), (0,)), ((), ())),
            preferred_element_type=F32,
        ).astype(BF16)
        for high in range(low, count):
            out[place] = line[:, (high - low) * BLOCK : (high - low + 1) * BLOCK]
            place += 1
    for extra in range(place, out.shape[0]):
        out[extra] = jnp.zeros((BLOCK, BLOCK), BF16)


def gram_blocks(rows, places):
    return pl.pallas_call(
        gram_kernel,
        out_shape=jax.ShapeDtypeStruct((places, BLOCK, BLOCK), BF16),
        compiler_params=pltpu.CompilerParams(vmem_limit_bytes=32 * 1024 * 1024),
        name="gram",
    )(rows)


def newton_schulz(gram, low, poly, mixed, rows):
    size = gram.shape[0]
    part = size // 2 if size % 16 == 0 and size > BLOCK else size
    parts = [pl.ds(begin, part) for begin in range(0, size, part)]
    row_id = lax.broadcasted_iota(jnp.int32, (size, size), 0)
    column_id = lax.broadcasted_iota(jnp.int32, (size, size), 1)
    square = jnp.where(row_id == column_id, gram[...], 0.0)
    square = jnp.sum(jnp.sum(square, axis=0, keepdims=True), axis=1, keepdims=True)
    scale = 1.0 / (jnp.sqrt(square) + 1e-07)
    for place in parts:
        scaled = gram[place, :] * (scale * scale)
        gram[place, :] = scaled
        low[place, :] = scaled.astype(BF16)
    work = (rows * scale).astype(BF16)
    for step in range(NS_STEPS):
        for place in parts:
            second = jnp.dot(low[place, :], low[...], preferred_element_type=F32)
            poly[place, :] = (NS_SQUARE * gram[place, :] + NS_CUBIC * second).astype(BF16)
        moved = jnp.dot(work, poly[...], preferred_element_type=F32)
        work = (NS_LINEAR * work.astype(F32) + moved).astype(BF16)
        if step + 1 < NS_STEPS:
            for place in parts:
                first = jnp.dot(poly[place, :], low[...], preferred_element_type=F32)
                mixed[place, :] = first.astype(BF16)
                gram[place, :] = (
                    NS_LINEAR * NS_LINEAR * gram[place, :] + (2.0 * NS_LINEAR) * first
                )
            for place in parts:
                second = jnp.dot(poly[place, :], mixed[...], preferred_element_type=F32)
                renewed = gram[place, :] + second
                gram[place, :] = renewed
                low[place, :] = renewed.astype(BF16)
    return work


def wide_kernel(blocks, rows, out, gram, low, poly, mixed):
    for place, (first, second) in enumerate(block_pairs(gram.shape[0] // BLOCK)):
        tile = blocks[place].astype(F32)
        gram[first * BLOCK : (first + 1) * BLOCK, second * BLOCK : (second + 1) * BLOCK] = tile
        if first != second:
            gram[second * BLOCK : (second + 1) * BLOCK, first * BLOCK : (first + 1) * BLOCK] = tile.T
    out[...] = newton_schulz(gram, low, poly, mixed, rows[...].astype(F32))


def square_scratch(size):
    return [
        pltpu.VMEM((size, size), F32),
        pltpu.VMEM((size, size), BF16),
        pltpu.VMEM((size, size), BF16),
        pltpu.VMEM((size, size), BF16),
    ]


def orthogonal_wide(blocks, rows):
    return pl.pallas_call(
        wide_kernel,
        out_shape=jax.ShapeDtypeStruct(rows.shape, BF16),
        scratch_shapes=square_scratch(rows.shape[1]),
        compiler_params=pltpu.CompilerParams(vmem_limit_bytes=40 * 1024 * 1024),
        cost_estimate=pl.CostEstimate(
            flops=14 * rows.shape[1] ** 3, bytes_accessed=4 * rows.size, transcendentals=0
        ),
        name="newton_wide",
    )(blocks, rows)


def whole_kernel(widths, whole, rows, out, *scratch):
    begin = 0
    for index, width in enumerate(widths):
        gram, low, poly, mixed = scratch[4 * index : 4 * index + 4]
        for first in range(0, width, BLOCK):
            gram[first : first + BLOCK, :] = lax.dot_general(
                whole[:, begin + first : begin + first + BLOCK],
                whole[:, begin : begin + width],
                (((0,), (0,)), ((), ())),
                preferred_element_type=F32,
            )
        out[:, begin : begin + width] = newton_schulz(
            gram, low, poly, mixed, rows[:, begin : begin + width]
        )
        begin += width


def orthogonal_whole(whole, rows, widths):
    scratch = []
    for width in widths:
        scratch += square_scratch(width)
    return pl.pallas_call(
        lambda *refs: whole_kernel(widths, *refs),
        out_shape=jax.ShapeDtypeStruct(rows.shape, BF16),
        scratch_shapes=scratch,
        compiler_params=pltpu.CompilerParams(vmem_limit_bytes=48 * 1024 * 1024),
        cost_estimate=pl.CostEstimate(
            flops=16 * sum(width**3 for width in widths),
            bytes_accessed=2 * whole.size,
            transcendentals=0,
        ),
        name="newton_whole",
    )(whole, rows)


def from_flat(flat, base, target, height, breadth):
    lines = breadth // LANES
    for begin in range(0, height, 8):
        count = min(8, height - begin)
        for index in range(lines):
            start = base + begin * lines + index
            if lines == 1:
                tile = flat[start : start + count, :]
            else:
                tile = flat[pl.ds(start, count, stride=lines), :]
            target[begin : begin + count, index * LANES : (index + 1) * LANES] = tile


def to_flat(flat, base, value, height, breadth):
    lines = breadth // LANES
    for begin in range(0, height, 8):
        count = min(8, height - begin)
        for index in range(lines):
            start = base + begin * lines + index
            tile = value(slice(begin, begin + count), slice(index * LANES, (index + 1) * LANES))
            if lines == 1:
                flat[start : start + count, :] = tile
            else:
                flat[pl.ds(start, count, stride=lines), :] = tile


def section_bases(devices):
    bases = []
    base = 0
    for height, breadth in matrix_shapes():
        bases.append(base)
        base += height // devices * breadth // LANES
    return bases


def pack_kernel(devices, group, flat, extra, qkv_out, out_out, wide_out, down_out, qkv, out, wide, down):
    rows = D // devices
    frows = FF // devices
    bases = section_bases(devices)
    qkv[...] = jnp.zeros(qkv.shape, F32)
    out[...] = jnp.zeros(out.shape, F32)
    from_flat(flat, bases[0], qkv.at[:, :QD], rows, QD)
    from_flat(flat, bases[1], qkv.at[:, QD : QD + KVD], rows, KVD)
    from_flat(flat, bases[2], qkv.at[:, QD + KVD :], rows, KVD)
    if extra is not None:
        qkv[rows : rows + 1, :LANES] = extra[...]
    from_flat(flat, bases[3], out, rows, D)
    from_flat(flat, bases[6], down, FF // devices, D)
    qkv_out[...] = qkv[...].astype(qkv_out.dtype)
    out_out[...] = out[...].astype(out_out.dtype)
    down_out[...] = down[...].astype(down_out.dtype)
    for which in range(2):
        from_flat(flat, bases[4 + which], wide, rows, FF)
        targets = devices // group
        for target in range(targets):
            piece = jnp.concatenate(
                [
                    wide[:, (turn * targets + target) * frows : (turn * targets + target + 1) * frows]
                    for turn in range(group)
                ],
                axis=1,
            )
            if group == 1:
                wide_out[target, :, which * frows : (which + 1) * frows] = piece.astype(wide_out.dtype)
            else:
                wide_out[target, which] = piece.astype(wide_out.dtype)


def pack(flat, extra, devices, group, dtype):
    rows = D // devices
    frows = FF // devices
    padded = (rows // 16 + 1) * 16
    targets = devices // group
    wide = (targets, rows, 2 * frows) if group == 1 else (targets, 2, rows, group * frows)
    shapes = [(padded, QD + 2 * KVD), (padded, D), wide, (frows, D)]
    types = [dtype, dtype, BF16, dtype]
    if extra is None:
        body = lambda flat_ref, *refs: pack_kernel(devices, group, flat_ref, None, *refs)
        operands = [flat]
    else:
        body = lambda *refs: pack_kernel(devices, group, *refs)
        operands = [flat, extra]
    return pl.pallas_call(
        body,
        out_shape=[jax.ShapeDtypeStruct(shape, kind) for shape, kind in zip(shapes, types)],
        scratch_shapes=[
            pltpu.VMEM((padded, QD + 2 * KVD), F32),
            pltpu.VMEM((padded, D), F32),
            pltpu.VMEM((rows, FF), F32),
            pltpu.VMEM((frows, D), F32),
        ],
        compiler_params=pltpu.CompilerParams(vmem_limit_bytes=32 * 1024 * 1024),
        cost_estimate=pl.CostEstimate(flops=0, bytes_accessed=6 * flat.size, transcendentals=0),
        name="pack",
    )(*operands)


def update_kernel(devices, decay, factors, flat, qkv, out, wide, down, result, moved, rows_wide):
    rows = D // devices
    frows = FF // devices
    bases = section_bases(devices)
    whole = qkv[...].astype(F32)
    out_whole = out[...].astype(F32)
    down_whole = down[...].astype(F32)
    parts = [
        lambda r, c: whole[r, c],
        lambda r, c: whole[r, slice(QD + c.start, QD + c.stop)],
        lambda r, c: whole[r, slice(QD + KVD + c.start, QD + KVD + c.stop)],
        lambda r, c: out_whole[r, c],
    ]
    shapes = matrix_shapes()
    for index, part in enumerate(parts):
        to_flat(
            moved, bases[index], lambda r, c: part(r, c) * factors[index], rows, shapes[index][1]
        )
    to_flat(moved, bases[6], lambda r, c: down_whole[r, c] * factors[6], frows, D)
    for which in range(2):
        for source in range(devices):
            rows_wide[:, source * frows : (source + 1) * frows] = wide[
                source, :, which * frows : (which + 1) * frows
            ].astype(F32)
        to_flat(
            moved, bases[4 + which], lambda r, c: rows_wide[r, c] * factors[4 + which], rows, FF
        )
    result[...] = decay * flat[...] + moved[...]


def update(flat, qkv, out, wide, down, devices, decay, factors):
    return pl.pallas_call(
        lambda *refs: update_kernel(devices, decay, factors, *refs),
        out_shape=jax.ShapeDtypeStruct(flat.shape, F32),
        scratch_shapes=[
            pltpu.VMEM(flat.shape, F32),
            pltpu.VMEM((D // devices, FF), F32),
        ],
        compiler_params=pltpu.CompilerParams(vmem_limit_bytes=32 * 1024 * 1024),
        cost_estimate=pl.CostEstimate(flops=0, bytes_accessed=10 * flat.size, transcendentals=0),
        name="update",
    )(flat, qkv, out, wide, down)


def on_device(
    block_input,
    cotangent,
    lengths,
    doc_starts,
    master,
    momentum,
    vectors,
    vector_first,
    vector_second,
):
    n_dp = lax.axis_size("dp")
    n_ctx = lax.axis_size("ctx")
    devices = n_dp * n_ctx
    rows = D // devices
    frows = FF // devices
    fblock = FF // n_ctx
    slots, span, width = block_input.shape
    tokens = slots * span
    group = HEADS // KVH
    qkv = QD + 2 * KVD
    my_ctx = lax.axis_index("ctx")
    me = lax.axis_index("dp") * n_ctx + my_ctx
    core_bit, x_bit = 1, 2
    ctx_bits = [core_bit, x_bit]
    dp_bits = [n_ctx << index for index in range(n_dp.bit_length() - 1)]
    all_bits = ctx_bits + dp_bits
    many = tuple([2] * len(all_bits))
    padded = (rows // 16 + 1) * 16

    master_flat = master.reshape(-1, LANES)
    momentum_flat = momentum.reshape(-1, LANES)
    small = jnp.pad(vectors, ((0, 0), (0, LANES - vectors.shape[1])))
    qkv_local, out_local, gate_up, down_local = pack(master_flat, small, devices, n_dp, BF16)

    attn_full = gather_bits(
        jnp.concatenate([qkv_local, out_local], axis=1), dp_bits[::-1], me, devices
    )
    down_bits = dp_bits[::-1]
    down_part, _ = lax.optimization_barrier((down_local, attn_full))
    down_part = gather_bits(down_part, down_bits[:1], me, devices)
    qkv_full = gather_bits(attn_full[..., :qkv], ctx_bits[::-1], me, devices, dp_bits)
    qkv_full = qkv_full.reshape(devices, padded, qkv)
    gain_first, gain_second, bias_query, bias_key, bias_value = [
        piece.astype(F32) for piece in split_small(qkv_full[:, rows], devices)
    ]
    w_qkv = qkv_full[:, :rows].reshape(D, qkv)

    came = [choose(gate_up, my_ctx, 0)] + [
        swap(choose(gate_up, my_ctx ^ mask, 0), mask, devices) for mask in range(1, n_ctx)
    ]
    came, _ = lax.optimization_barrier((came, attn_full))
    ordered = []
    for source in range(n_ctx):
        piece = came[0]
        for mask in range(1, n_ctx):
            piece = jnp.where(my_ctx ^ mask == source, came[mask], piece)
        ordered.append(piece)
    gate_up = jnp.concatenate(ordered, axis=1)
    w_gate, w_up = [lax.all_gather(gate_up[index], "dp", axis=0, tiled=True) for index in range(2)]

    def to_rows(pair):
        both = pair.T.reshape(devices, rows, 2 * frows)
        return lax.all_to_all(both, BOTH, split_axis=0, concat_axis=0, tiled=True)

    length, second = lengths[0], doc_starts[0]
    places = my_ctx * span + jnp.arange(span, dtype=jnp.int32)
    doc_begin = jnp.where(places >= length, length, jnp.where(places >= second, second, 0))
    position = (places - doc_begin).astype(F32)
    live = (places < length)[:, None]
    info = jnp.stack([my_ctx, length, second]).astype(jnp.int32)
    inverse = ROPE_BASE ** (-2.0 * jnp.arange(HD // 2, dtype=F32) / HD)
    angles = inverse[:, None] * position[None, :]
    cosine, sine_part = jnp.cos(angles), jnp.sin(angles)
    cosine = jnp.concatenate([cosine, cosine], axis=0)[None]
    sine_part = jnp.concatenate([sine_part, sine_part], axis=0)[None]

    def from_ctx(value, other_x=None):
        other_core = swap(value, core_bit, devices)
        if other_x is None:
            other_x = swap(value, x_bit, devices)
        return value, other_core, other_x, swap(other_x, core_bit, devices)

    cot_here = jnp.where(live, cotangent.reshape(tokens, width), jnp.zeros((), BF16))

    def pair_of_heads(kv, index):
        begin = index * HD
        return jnp.concatenate(
            [kv[:, begin : begin + HD], kv[:, KVD + begin : KVD + begin + HD]], axis=1
        )

    inputs = block_input.astype(F32).reshape(tokens, width)
    scale_one = lax.rsqrt(jnp.mean(inputs * inputs, axis=-1, keepdims=True) + NORM_EPS)
    normed_one = (inputs * scale_one * gain_first).astype(BF16)
    bias = jnp.concatenate([bias_query, bias_key, bias_value])
    pre = mm(w_qkv, normed_one, ((0,), (1,))) + bias[:, None]
    turned = rotate(
        pre[: QD + KVD].reshape(HEADS + KVH, HD, tokens), cosine, sine_part
    )
    queries = (turned[:HEADS].astype(BF16).astype(F32) * HD ** (-0.5)).astype(BF16)
    kv_here = jnp.concatenate(
        [turned[HEADS:].astype(BF16).reshape(KVD, tokens), pre[QD + KVD :].astype(BF16)], axis=0
    )
    kv = jnp.stack(from_ctx(kv_here))
    down_part, _ = lax.optimization_barrier((down_part, kv_here))
    down_part = gather_bits(down_part, down_bits[1:2], me, devices, down_bits[:1])
    back_one = jnp.pad(
        normed_one.T.reshape(devices, rows, tokens), ((0, 0), (0, padded - rows), (0, 0))
    ).reshape(devices * padded, tokens)
    back_one, kv = lax.optimization_barrier((back_one, kv))
    out_full, _ = lax.optimization_barrier((attn_full[..., qkv:], kv))
    halves = []
    for index in range(KVH):
        if index == 1:
            out_full, down_part, cot_here, _ = lax.optimization_barrier(
                (out_full, down_part, cot_here, halves)
            )
            cot_far = swap(cot_here, x_bit, devices)
            down_part = gather_bits(down_part, down_bits[2:3], me, devices, down_bits[:2])
        out_full = gather_bits(
            out_full, ctx_bits[::-1][index : index + 1], me, devices, dp_bits + ctx_bits[::-1][:index]
        )
        kv_one = pair_of_heads(kv, index)
        halves.append(attend(info, kv_one, queries[index * group : (index + 1) * group]))
    halves, cot_far, down_part = lax.optimization_barrier((halves, cot_far, down_part))
    attended = jnp.concatenate([half[0] for half in halves], axis=0)
    log_total = jnp.concatenate([half[1] for half in halves], axis=0)
    w_out = out_full.reshape(devices, padded, D)[:, :rows].reshape(QD, D)
    w_down = gather_bits(down_part, down_bits[3:], me, devices, down_bits[:3])
    w_down = w_down.reshape(fblock, D)

    mixed_heads = attended.reshape(QD, tokens).astype(BF16)
    hidden = inputs + mm(mixed_heads, w_out, ((0,), (0,)))
    scale_two = lax.rsqrt(jnp.mean(hidden * hidden, axis=-1, keepdims=True) + NORM_EPS)
    normed_two = (hidden * scale_two * gain_second).astype(BF16)

    normed = from_ctx(normed_two)
    cot = from_ctx(cot_here, cot_far)
    results = [feed_forward(normed[:2], cot[:2], w_gate, w_up, w_down)]
    (w_gate, w_up, w_down), results = lax.optimization_barrier(((w_gate, w_up, w_down), results))
    results.append(feed_forward(normed[2:], cot[2:], w_gate, w_up, w_down))
    acts, gate_backs, up_backs, back_parts, normed_halves, cot_halves = zip(*results)

    def to_ctx(halves):
        crossed = swap(halves[1][span:], core_bit, devices)
        far = (halves[1][:span].astype(F32) + crossed.astype(F32)).astype(BF16)
        near = swap(halves[0][span:], core_bit, devices)
        near = halves[0][:span].astype(F32) + near.astype(F32)
        return near + swap(far, x_bit, devices).astype(F32), far

    normed_two_grad, ready = to_ctx(back_parts)
    (acts, gate_backs, up_backs), ready = lax.optimization_barrier(
        ((acts, gate_backs, up_backs), ready)
    )

    def over_tokens(left, right):
        return mm(left[0], right[0], ((0,), (0,))) + mm(left[1], right[1], ((0,), (0,)))

    dp_shape = tuple([2] * len(dp_bits)) + (frows, D)
    dp_order = dp_bits[1:] + dp_bits[:1]
    down_value = over_tokens(acts, cot_halves).astype(BF16)
    gate_value = over_tokens(gate_backs, normed_halves).astype(BF16)
    up_value = over_tokens(up_backs, normed_halves).astype(BF16)
    down_parts, gate_parts, up_parts = [
        scatter_start(value.reshape(dp_shape), dp_bits, bit, me, devices)
        for value, bit in (
            (down_value, dp_order[0]),
            (gate_value, dp_bits[0]),
            (up_value, dp_bits[0]),
        )
    ]
    momentum_flat, acts, _ = lax.optimization_barrier((momentum_flat, acts, (down_value, gate_value, up_value)))
    old_qkv, old_out, old_pair, old_down = pack(momentum_flat, None, devices, 1, F32)
    old_pair = lax.all_to_all(old_pair, BOTH, split_axis=0, concat_axis=0, tiled=True)
    old_pair = old_pair.reshape(D, 2 * frows).T

    out_grad = cot_here.astype(F32)
    hidden_norm_grad, grad_gain_second = norm_backward(
        hidden, scale_two, gain_second, normed_two_grad
    )
    hidden_grad = out_grad + hidden_norm_grad
    hidden_low = hidden_grad.astype(BF16)
    heads_grad = mm(w_out, hidden_low, ((1,), (1,))).astype(BF16).reshape(HEADS, HD, tokens)
    delta = jnp.sum(heads_grad.astype(F32) * attended, axis=1, keepdims=True)
    mixed_pieces = jnp.pad(
        mixed_heads.reshape(devices, rows, tokens), ((0, 0), (0, padded - rows), (0, 0))
    ).reshape(devices * padded, tokens)
    grad_output = mm(mixed_pieces, hidden_low)
    query_grads, kv_parts = [], []
    sent, kept = scatter_split(
        grad_output.astype(BF16).reshape(many + (padded, D)), all_bits, all_bits[0], me
    )
    wide_parts = [gate_parts, up_parts, down_parts, (kept, swap(sent, all_bits[0], devices))]
    wide_orders = [list(dp_bits), list(dp_bits), list(dp_order), list(all_bits)]
    steps = [[2, 3], [3], [0, 3], [1, 2, 3], [0], [1]]
    shares = [3, 2, 2]
    ready = [sent]
    for index in range(KVH):
        kv_one = pair_of_heads(kv, index)
        kv_grad = None
        begin = index * group
        for count in shares:
            chosen = slice(begin, begin + count)
            begin += count
            query_part, ready = lax.optimization_barrier((queries[chosen], ready))
            query_grad, kv_grad = attend_back(
                info, kv_one, query_part, heads_grad[chosen], log_total[chosen], delta[chosen], kv_grad
            )
            query_grads.append(query_grad)
            ready = []
            for which in steps.pop(0):
                order = wide_orders[which]
                parts, _ = lax.optimization_barrier((wide_parts[which], query_grad))
                order.pop(0)
                sent, kept = scatter_split(scatter_end(parts), order, order[0], me)
                ready.append(sent)
                wide_parts[which] = (kept, swap(sent, order[0], devices))
        kv_parts.append(
            scatter_sum(kv_grad.reshape(2, 2, 2 * HD, span), ctx_bits, me, devices)
        )
    kv_grads = [part.astype(F32).reshape(2, HD, span) for part in kv_parts]
    acts, _ = lax.optimization_barrier((acts, query_grads[3]))
    out_sum, _ = to_ctx([mm(act, w_down).astype(BF16) for act in acts])
    layer_out = jnp.where(live, hidden + out_sum, 0.0)
    qk_grad = jnp.concatenate(query_grads + [grad[:1] for grad in kv_grads], axis=0)
    qk_back = rotate_back(qk_grad, cosine, sine_part).reshape(QD + KVD, tokens)
    qkv_back = jnp.concatenate(
        [qk_back] + [grad[1] for grad in kv_grads], axis=0
    ).astype(BF16)
    grad_qkv = mm(back_one, qkv_back, ((1,), (1,)))
    grad_bias = jnp.sum(qkv_back.astype(F32), axis=1)
    normed_one_grad = mm(qkv_back, w_qkv, ((0,), (1,)))
    input_norm_grad, grad_gain_first = norm_backward(inputs, scale_one, gain_first, normed_one_grad)
    input_grad = (hidden_grad + input_norm_grad).astype(BF16).reshape(slots, span, width)

    vector_part = join_small(
        [
            grad_gain_first,
            grad_gain_second,
            grad_bias[:QD],
            grad_bias[QD : QD + KVD],
            grad_bias[QD + KVD :],
        ],
        devices,
    )
    vector_grad = jnp.sum(
        lax.all_to_all(vector_part, BOTH, split_axis=0, concat_axis=0, tiled=True),
        axis=0,
        keepdims=True,
    )
    sent, kept = scatter_split(
        grad_qkv.astype(BF16).reshape(many + (padded, qkv)), all_bits, all_bits[0], me
    )
    wide_parts, sent = lax.optimization_barrier((wide_parts, sent))
    qkv_parts = (kept, swap(sent, all_bits[0], devices))
    gate_sum, up_sum, down_sum, out_sum_rows = [
        scatter_sum(scatter_end(parts), order[1:], me, devices)
        for parts, order in zip(wide_parts, wide_orders)
    ]
    qkv_sum_rows = scatter_sum(scatter_end(qkv_parts), all_bits[1:], me, devices)
    moved_qkv = MOMENTUM_DECAY * old_qkv + qkv_sum_rows.astype(F32)
    moved_out = MOMENTUM_DECAY * old_out + out_sum_rows.astype(F32)
    moved_down = MOMENTUM_DECAY * old_down + down_sum.astype(F32)
    pair_sum = jnp.concatenate([gate_sum, up_sum], axis=0)
    moved_pair = MOMENTUM_DECAY * old_pair.astype(F32) + pair_sum.astype(F32)
    mats = jnp.stack(
        [
            moved_pair[:frows],
            moved_pair[frows:],
            moved_down,
            jnp.pad(moved_out, ((0, frows - padded), (0, 0))),
        ]
    ).astype(BF16)
    owned = to_owner(mats.reshape(2, 2, frows, D), core_bit, x_bit, me, devices)
    owned = owned.reshape(n_ctx * frows, D)
    count = len(block_pairs(D // BLOCK))
    places = (count + n_dp - 1) // n_dp * n_dp
    dp_many = tuple([2] * len(dp_bits))
    gram = gram_blocks(owned, places).reshape(dp_many + (places // n_dp, BLOCK, BLOCK))
    pair_sum, _ = lax.optimization_barrier((pair_sum, gram))
    new_momentum = update(
        momentum_flat,
        qkv_sum_rows,
        out_sum_rows,
        to_rows(pair_sum),
        down_sum,
        devices,
        MOMENTUM_DECAY,
        [1.0] * 7,
    ).reshape(momentum.shape)
    gram = scatter_sum(gram, dp_bits, me, devices)
    gram = gather_bits(gram, dp_bits[::-1], me, devices).reshape(places, BLOCK, BLOCK)
    ortho = orthogonal_wide(gram, owned).reshape(2, 2, frows, D)
    ortho = from_owner(ortho, core_bit, x_bit, me, devices).reshape(n_ctx, frows, D)
    ortho_pair = to_rows(ortho[:2].reshape(2 * frows, D))

    def gathered(part):
        full = gather_bits(part.astype(BF16), all_bits[::-1], me, devices)
        return full.reshape(devices * padded, part.shape[1])

    ortho_qkv = orthogonal_whole(gathered(moved_qkv), moved_qkv, (QD, KVD, KVD))
    factors = [
        -MUON_RATE * math.sqrt(max(1.0, breadth / height)) for height, breadth in matrix_shapes()
    ]
    new_master = update(
        master_flat,
        ortho_qkv,
        ortho[3, :padded],
        ortho_pair,
        ortho[2],
        devices,
        1.0 - MUON_RATE * MUON_DECAY,
        factors,
    ).reshape(master.shape)
    first_new = BETA_FIRST * vector_first + (1.0 - BETA_FIRST) * vector_grad
    second_new = BETA_SECOND * vector_second + (1.0 - BETA_SECOND) * vector_grad * vector_grad
    adjusted = (
        first_new
        / (1.0 - BETA_FIRST**STEP)
        / (jnp.sqrt(second_new / (1.0 - BETA_SECOND**STEP)) + ADAM_EPS)
    )
    new_vectors = vectors - ADAM_RATE * adjusted
    return (
        layer_out.astype(BF16).reshape(slots, span, width),
        input_grad,
        new_master,
        new_momentum,
        new_master.astype(BF16),
        new_vectors,
        first_new,
        second_new,
    )


def solution(mesh):
    return jax.shard_map(
        on_device,
        mesh=mesh,
        in_specs=(
            P("dp", "ctx", None),
            P("dp", "ctx", None),
            P("dp"),
            P("dp"),
            P(BOTH, None),
            P(BOTH, None),
            P(BOTH, None),
            P(BOTH, None),
            P(BOTH, None),
        ),
        out_specs=(
            P("dp", "ctx", None),
            P("dp", "ctx", None),
            P(BOTH, None),
            P(BOTH, None),
            P(BOTH, None),
            P(BOTH, None),
            P(BOTH, None),
            P(BOTH, None),
        ),
        check_vma=False,
    )
```

```python
import math

import jax
import jax.numpy as jnp
from jax import lax
from jax.experimental import pallas as pl
from jax.experimental.pallas import tpu as pltpu
from jax.sharding import PartitionSpec as P

D = 896
HEADS = 14
KVH = 2
HD = 64
FF = 4864
SLOT = 2048
NS_STEPS = 3
STEP = 10
QD = 896
KVD = 128

NORM_EPS = 1e-06
ROPE_BASE = 1000000.0
NS_LINEAR = 3.4445
NS_SQUARE = -4.775
NS_CUBIC = 2.0315
MOMENTUM_DECAY = 0.5
MUON_RATE = 0.6
MUON_DECAY = 0.1
ADAM_RATE = 0.2
BETA_FIRST = 0.9
BETA_SECOND = 0.95
ADAM_EPS = 1e-08
MASK_FLOOR = -1e30

F32 = jnp.float32
BF16 = jnp.bfloat16
BOTH = ("dp", "ctx")
LANES = 128


def matrix_shapes():
    return [(D, QD), (D, KVD), (D, KVD), (QD, D), (D, FF), (D, FF), (FF, D)]


def vector_sizes():
    return [D, D, QD, KVD, KVD]


def mm(left, right, contract=((1,), (0,))):
    return lax.dot_general(left, right, (contract, ((), ())), preferred_element_type=F32)


def split_small(flat, devices):
    result = []
    offset = 0
    for extent_all in vector_sizes():
        extent = extent_all // devices
        result.append(flat[:, offset : offset + extent].reshape(extent_all))
        offset += extent
    return result


def join_small(pieces, devices):
    return jnp.concatenate([piece.reshape(devices, -1) for piece in pieces], axis=1)


def swap(value, mask, devices):
    return lax.ppermute(value, BOTH, [(index, index ^ mask) for index in range(devices)])


def gather_bits(value, bits, me, devices, before=()):
    held = value
    done = list(before)
    for bit in bits:
        place = sum(1 for other in done if other > bit)
        got = swap(held, bit, devices)
        mine = (me & bit) != 0
        held = jnp.where(
            mine, jnp.stack([got, held], axis=place), jnp.stack([held, got], axis=place)
        )
        done.append(bit)
    return held


def scatter_split(held, left, bit, me):
    axis = sorted(left, reverse=True).index(bit)
    mine = jnp.where((me & bit) != 0, 1, 0)
    return choose(held, 1 - mine, axis).astype(BF16), choose(held, mine, axis)


def scatter_start(held, left, bit, me, devices):
    sent, kept = scatter_split(held, left, bit, me)
    return kept, swap(sent, bit, devices)


def scatter_end(parts):
    return (parts[0].astype(F32) + parts[1].astype(F32)).astype(BF16)


def scatter_sum(value, bits, me, devices):
    left = list(bits)
    held = value
    for bit in bits:
        held = scatter_end(scatter_start(held, left, bit, me, devices))
        left.remove(bit)
    return held


def choose(value, mine, axis):
    return lax.dynamic_index_in_dim(value, mine, axis, keepdims=False)


def to_owner(value, core_bit, x_bit, me, devices):
    core = jnp.where((me & core_bit) != 0, 1, 0)
    across = jnp.where((me & x_bit) != 0, 1, 0)
    got = swap(choose(value, 1 - core, 1), core_bit, devices)
    value = jnp.stack([choose(value, core, 1), got], axis=1)
    got = swap(choose(value, 1 - across, 0), x_bit, devices)
    return jnp.stack([choose(value, across, 0), got])


def from_owner(value, core_bit, x_bit, me, devices):
    got = swap(value[1], x_bit, devices)
    value = jnp.where(
        (me & x_bit) != 0, jnp.stack([got, value[0]]), jnp.stack([value[0], got])
    )
    got = swap(value[:, 1], core_bit, devices)
    return jnp.where(
        (me & core_bit) != 0,
        jnp.stack([got, value[:, 0]], axis=1),
        jnp.stack([value[:, 0], got], axis=1),
    )


def rotate(values, cosine, sine_part):
    midpoint = HD // 2
    turned = jnp.concatenate([-values[:, midpoint:], values[:, :midpoint]], axis=1)
    return values * cosine + turned * sine_part


def rotate_back(gradient, cosine, sine_part):
    midpoint = HD // 2
    scaled = gradient * sine_part
    turned = jnp.concatenate([scaled[:, midpoint:], -scaled[:, :midpoint]], axis=1)
    return gradient * cosine + turned


def norm_backward(source, scale_row, gain, incoming):
    gain_grad = jnp.sum(incoming * source * scale_row, axis=0)
    weighted = incoming * gain
    result = scale_row * weighted - source * scale_row**3 * jnp.mean(
        weighted * source, axis=-1, keepdims=True
    )
    return (result, gain_grad)


def halves_of(span):
    return [slice(0, span // 2), slice(span // 2, span)]


def fill_mask(info, mask, chunk, span):
    key = chunk * span + lax.broadcasted_iota(jnp.int32, (span, span), 0)
    query = info[0] * span + lax.broadcasted_iota(jnp.int32, (span, span), 1)
    key_doc = (key >= info[2]).astype(jnp.int32) + (key >= info[1]).astype(jnp.int32)
    query_doc = (query >= info[2]).astype(jnp.int32) + (query >= info[1]).astype(jnp.int32)
    allowed = jnp.logical_and(key_doc == query_doc, key <= query)
    mask[chunk] = jnp.where(allowed, 0.0, MASK_FLOOR).astype(F32)


def attend_kernel(info, kv, q, out, lse, keys, mask, best, total, acc):
    head = pl.program_id(0)
    span = q.shape[-1]
    mine = info[0]
    chunks = mine + 1

    @pl.when(head == 0)
    def _():
        def fill(chunk, carry):
            slot = jnp.bitwise_xor(chunk, mine)
            keys[chunk] = kv[slot, :HD, :].astype(F32).T.astype(BF16)
            fill_mask(info, mask, chunk, span)
            return carry

        lax.fori_loop(0, chunks, fill, 0)

    best[...] = jnp.full(best.shape, MASK_FLOOR, F32)
    total[...] = jnp.zeros(total.shape, F32)
    acc[...] = jnp.zeros(acc.shape, F32)
    queries = q[0]

    def step(index, carry):
        chunk = mine - index
        slot = jnp.bitwise_xor(chunk, mine)
        scores = jnp.dot(keys[chunk], queries, preferred_element_type=F32) + mask[chunk]
        old = best[...]
        new = jnp.maximum(old, jnp.max(scores, axis=0, keepdims=True))
        present = jnp.exp(scores - new)
        shrink = jnp.exp(old - new)
        best[...] = new
        total[...] = total[...] * shrink + jnp.sum(present, axis=0, keepdims=True)
        acc[...] = acc[...] * shrink + jnp.dot(
            kv[slot, HD:, :], present.astype(BF16), preferred_element_type=F32
        )
        return carry

    lax.fori_loop(0, chunks, step, 0)
    out[0] = acc[...] / total[...]
    lse[0] = best[...] + jnp.log(total[...])


def attend_back_kernel(
    info, kv, q, dout, lse, delta, before, dq, dkv, keys, values, mask, dk, dv, acc
):
    head = pl.program_id(0)
    span = q.shape[-1]
    mine = info[0]
    chunks = mine + 1
    n_ctx = kv.shape[0]

    @pl.when(head == 0)
    def _():
        dk[...] = jnp.zeros(dk.shape, F32)
        dv[...] = jnp.zeros(dv.shape, F32)

        def fill(chunk, carry):
            slot = jnp.bitwise_xor(chunk, mine)
            keys[chunk] = kv[slot, :HD, :].astype(F32).T.astype(BF16)
            values[chunk] = kv[slot, HD:, :].astype(F32).T.astype(BF16)
            fill_mask(info, mask, chunk, span)
            return carry

        lax.fori_loop(0, chunks, fill, 0)

    acc[...] = jnp.zeros(acc.shape, F32)
    queries = q[0]
    douts = dout[0]
    query_rows = queries.astype(F32).T.astype(BF16)
    dout_rows = douts.astype(F32).T.astype(BF16)

    def step(chunk, carry):
        slot = jnp.bitwise_xor(chunk, mine)
        value_sum, key_sum = dv[chunk], dk[chunk]
        for lanes in halves_of(span):
            scores = (
                jnp.dot(keys[chunk], queries[:, lanes], preferred_element_type=F32)
                + mask[chunk, :, lanes]
            )
            shares = jnp.exp(scores - lse[0, :, lanes])
            share_grad = jnp.dot(values[chunk], douts[:, lanes], preferred_element_type=F32)
            score_grad = (shares * (share_grad - delta[0, :, lanes])).astype(BF16)
            value_sum += jnp.dot(
                shares.astype(BF16), dout_rows[lanes, :], preferred_element_type=F32
            )
            key_sum += jnp.dot(score_grad, query_rows[lanes, :], preferred_element_type=F32)
            acc[:, lanes] += jnp.dot(kv[slot, :HD, :], score_grad, preferred_element_type=F32)
        dv[chunk], dk[chunk] = value_sum, key_sum
        return carry

    lax.fori_loop(0, chunks, step, 0)
    dq[0] = acc[...] * HD ** (-0.5)

    @pl.when(head == pl.num_programs(0) - 1)
    def _():
        for chunk in range(n_ctx):
            sums = jnp.concatenate([dk[chunk].T, dv[chunk].T], axis=0)
            if before is not None:
                sums += before[chunk].astype(F32)
            dkv[chunk] = sums.astype(BF16)


def attend(info, kv, q):
    heads, _, span = q.shape
    n_ctx = kv.shape[0]
    per_head = lambda rows: pl.BlockSpec((1, rows, span), lambda head: (head, 0, 0))
    return pl.pallas_call(
        attend_kernel,
        grid=(heads,),
        in_specs=[
            pl.BlockSpec(memory_space=pltpu.SMEM),
            pl.BlockSpec(kv.shape, lambda head: (0, 0, 0)),
            per_head(HD),
        ],
        out_specs=[per_head(HD), per_head(1)],
        out_shape=[
            jax.ShapeDtypeStruct((heads, HD, span), F32),
            jax.ShapeDtypeStruct((heads, 1, span), F32),
        ],
        scratch_shapes=[
            pltpu.VMEM((n_ctx, span, HD), BF16),
            pltpu.VMEM((n_ctx, span, span), F32),
            pltpu.VMEM((1, span), F32),
            pltpu.VMEM((1, span), F32),
            pltpu.VMEM((HD, span), F32),
        ],
        compiler_params=pltpu.CompilerParams(vmem_limit_bytes=40 * 1024 * 1024),
        cost_estimate=pl.CostEstimate(
            flops=4 * heads * span * span * n_ctx * HD * 4,
            bytes_accessed=4 * heads * span * HD * 2,
            transcendentals=heads * span * span * n_ctx,
        ),
        name="attend",
    )(info, kv, q)


def attend_back(info, kv, q, dout, lse, delta, before):
    heads, _, span = q.shape
    n_ctx = kv.shape[0]
    per_head = lambda rows: pl.BlockSpec((1, rows, span), lambda head: (head, 0, 0))
    whole = pl.BlockSpec(kv.shape, lambda head: (0, 0, 0))
    if before is None:
        body = lambda *refs: attend_back_kernel(*refs[:6], None, *refs[6:])
    else:
        body = attend_back_kernel
    return pl.pallas_call(
        body,
        grid=(heads,),
        in_specs=[
            pl.BlockSpec(memory_space=pltpu.SMEM),
            whole,
            per_head(HD),
            per_head(HD),
            per_head(1),
            per_head(1),
        ]
        + [whole] * (before is not None),
        out_specs=[per_head(HD), whole],
        out_shape=[
            jax.ShapeDtypeStruct((heads, HD, span), F32),
            jax.ShapeDtypeStruct(kv.shape, BF16),
        ],
        scratch_shapes=[
            pltpu.VMEM((n_ctx, span, HD), BF16),
            pltpu.VMEM((n_ctx, span, HD), BF16),
            pltpu.VMEM((n_ctx, span, span), F32),
            pltpu.VMEM((n_ctx, span, HD), F32),
            pltpu.VMEM((n_ctx, span, HD), F32),
            pltpu.VMEM((HD, span), F32),
        ],
        compiler_params=pltpu.CompilerParams(vmem_limit_bytes=40 * 1024 * 1024),
        cost_estimate=pl.CostEstimate(
            flops=10 * heads * span * span * n_ctx * HD * 4,
            bytes_accessed=8 * heads * span * HD * 2,
            transcendentals=heads * span * span * n_ctx,
        ),
        name="attend_back",
    )(*[info, kv, q, dout, lse, delta] + [before] * (before is not None))


def forward_backward_kernel(
    x0, x1, dy0, dy1, gate, up, down, act_out, gate_back_out, up_back_out, x_out, dy_out, back_out
):
    first = pl.program_id(0) == 0
    x = jnp.where(first, x0[...], x1[...])
    dy = jnp.where(first, dy0[...], dy1[...])
    x_out[...] = x
    dy_out[...] = dy
    gate_pre = jnp.dot(x, gate[...], preferred_element_type=F32)
    up_pre = jnp.dot(x, up[...], preferred_element_type=F32)
    grad_act = mm(dy, down[...], ((1,), (1,)))
    sigmoid_gate = jax.nn.sigmoid(gate_pre)
    swish = gate_pre * sigmoid_gate
    slope = sigmoid_gate * (1.0 + gate_pre * (1.0 - sigmoid_gate))
    act_out[...] = (swish * up_pre).astype(BF16)
    gate_back = (grad_act * up_pre * slope).astype(BF16)
    up_back = (grad_act * swish).astype(BF16)
    gate_back_out[...] = gate_back
    up_back_out[...] = up_back
    back_out[...] = (
        mm(gate_back, gate[...], ((1,), (1,))) + mm(up_back, up[...], ((1,), (1,)))
    ).astype(BF16)


def feed_forward(x, dy, gate, up, down, blocks, earlier):
    span, width = x[0].shape
    units = gate.shape[1]
    first = 0 if earlier is None else 2
    whole = lambda shape: pl.BlockSpec(shape, lambda block: (0, 0))
    line = lambda columns, offset: pl.BlockSpec(
        (span, columns), lambda block: (block + offset, 0)
    )
    columns = [units, units, units, width, width]
    shapes = [jax.ShapeDtypeStruct((blocks * span, count), BF16) for count in columns]
    in_specs = [whole((span, width))] * 4 + [whole((width, units))] * 2 + [whole((units, width))]
    operands = [*x, *dy, gate, up, down]
    aliases = {}
    body = forward_backward_kernel
    if earlier is not None:
        in_specs += [pl.BlockSpec(memory_space=pl.ANY)] * 5
        operands += list(earlier)
        aliases = {7 + index: index for index in range(5)}
        body = lambda *refs: forward_backward_kernel(*refs[:7], *refs[12:])
    results = pl.pallas_call(
        body,
        grid=(2,),
        in_specs=in_specs,
        out_specs=[line(count, first) for count in columns] + [line(width, 0)],
        out_shape=shapes + [jax.ShapeDtypeStruct((2 * span, width), BF16)],
        input_output_aliases=aliases,
        compiler_params=pltpu.CompilerParams(vmem_limit_bytes=58 * 1024 * 1024),
        cost_estimate=pl.CostEstimate(
            flops=20 * span * width * units,
            bytes_accessed=6 * width * units + 2 * span * 10 * width,
            transcendentals=2 * span * units,
        ),
        name="feed_forward",
    )(*operands)
    return results[:5], results[5]


BLOCK = 128


def block_pairs(count):
    return [(low, high) for low in range(count) for high in range(low, count)]


def gram_kernel(rows, out):
    count = rows.shape[1] // BLOCK
    place = 0
    for low in range(count):
        line = lax.dot_general(
            rows[:, low * BLOCK : (low + 1) * BLOCK],
            rows[:, low * BLOCK :],
            (((0,), (0,)), ((), ())),
            preferred_element_type=F32,
        ).astype(BF16)
        for high in range(low, count):
            out[place] = line[:, (high - low) * BLOCK : (high - low + 1) * BLOCK]
            place += 1
    for extra in range(place, out.shape[0]):
        out[extra] = jnp.zeros((BLOCK, BLOCK), BF16)


def gram_blocks(rows, places):
    return pl.pallas_call(
        gram_kernel,
        out_shape=jax.ShapeDtypeStruct((places, BLOCK, BLOCK), BF16),
        compiler_params=pltpu.CompilerParams(vmem_limit_bytes=32 * 1024 * 1024),
        name="gram",
    )(rows)


def newton_schulz(gram, low, poly, mixed, rows):
    size = gram.shape[0]
    part = size // 2 if size % 16 == 0 and size > BLOCK else size
    parts = [pl.ds(begin, part) for begin in range(0, size, part)]
    row_id = lax.broadcasted_iota(jnp.int32, (size, size), 0)
    column_id = lax.broadcasted_iota(jnp.int32, (size, size), 1)
    square = jnp.where(row_id == column_id, gram[...], 0.0)
    square = jnp.sum(jnp.sum(square, axis=0, keepdims=True), axis=1, keepdims=True)
    scale = 1.0 / (jnp.sqrt(square) + 1e-07)
    for place in parts:
        scaled = gram[place, :] * (scale * scale)
        gram[place, :] = scaled
        low[place, :] = scaled.astype(BF16)
    work = (rows * scale).astype(BF16)
    for step in range(NS_STEPS):
        for place in parts:
            second = jnp.dot(low[place, :], low[...], preferred_element_type=F32)
            poly[place, :] = (NS_SQUARE * gram[place, :] + NS_CUBIC * second).astype(BF16)
        moved = jnp.dot(work, poly[...], preferred_element_type=F32)
        work = (NS_LINEAR * work.astype(F32) + moved).astype(BF16)
        if step + 1 < NS_STEPS:
            for place in parts:
                first = jnp.dot(poly[place, :], low[...], preferred_element_type=F32)
                mixed[place, :] = first.astype(BF16)
                gram[place, :] = (
                    NS_LINEAR * NS_LINEAR * gram[place, :] + (2.0 * NS_LINEAR) * first
                )
            for place in parts:
                second = jnp.dot(poly[place, :], mixed[...], preferred_element_type=F32)
                renewed = gram[place, :] + second
                gram[place, :] = renewed
                low[place, :] = renewed.astype(BF16)
    return work


def wide_kernel(blocks, rows, out, gram, low, poly, mixed):
    for place, (first, second) in enumerate(block_pairs(gram.shape[0] // BLOCK)):
        tile = blocks[place].astype(F32)
        gram[first * BLOCK : (first + 1) * BLOCK, second * BLOCK : (second + 1) * BLOCK] = tile
        if first != second:
            gram[second * BLOCK : (second + 1) * BLOCK, first * BLOCK : (first + 1) * BLOCK] = tile.T
    out[...] = newton_schulz(gram, low, poly, mixed, rows[...].astype(F32))


def square_scratch(size):
    return [
        pltpu.VMEM((size, size), F32),
        pltpu.VMEM((size, size), BF16),
        pltpu.VMEM((size, size), BF16),
        pltpu.VMEM((size, size), BF16),
    ]


def orthogonal_wide(blocks, rows):
    return pl.pallas_call(
        wide_kernel,
        out_shape=jax.ShapeDtypeStruct(rows.shape, BF16),
        scratch_shapes=square_scratch(rows.shape[1]),
        compiler_params=pltpu.CompilerParams(vmem_limit_bytes=40 * 1024 * 1024),
        cost_estimate=pl.CostEstimate(
            flops=14 * rows.shape[1] ** 3, bytes_accessed=4 * rows.size, transcendentals=0
        ),
        name="newton_wide",
    )(blocks, rows)


def whole_kernel(widths, whole, rows, out, *scratch):
    begin = 0
    for index, width in enumerate(widths):
        gram, low, poly, mixed = scratch[4 * index : 4 * index + 4]
        for first in range(0, width, BLOCK):
            gram[first : first + BLOCK, :] = lax.dot_general(
                whole[:, begin + first : begin + first + BLOCK],
                whole[:, begin : begin + width],
                (((0,), (0,)), ((), ())),
                preferred_element_type=F32,
            )
        out[:, begin : begin + width] = newton_schulz(
            gram, low, poly, mixed, rows[:, begin : begin + width]
        )
        begin += width


def orthogonal_whole(whole, rows, widths):
    scratch = []
    for width in widths:
        scratch += square_scratch(width)
    return pl.pallas_call(
        lambda *refs: whole_kernel(widths, *refs),
        out_shape=jax.ShapeDtypeStruct(rows.shape, BF16),
        scratch_shapes=scratch,
        compiler_params=pltpu.CompilerParams(vmem_limit_bytes=48 * 1024 * 1024),
        cost_estimate=pl.CostEstimate(
            flops=16 * sum(width**3 for width in widths),
            bytes_accessed=2 * whole.size,
            transcendentals=0,
        ),
        name="newton_whole",
    )(whole, rows)


def from_flat(flat, base, target, height, breadth):
    lines = breadth // LANES
    for begin in range(0, height, 8):
        count = min(8, height - begin)
        for index in range(lines):
            start = base + begin * lines + index
            if lines == 1:
                tile = flat[start : start + count, :]
            else:
                tile = flat[pl.ds(start, count, stride=lines), :]
            target[begin : begin + count, index * LANES : (index + 1) * LANES] = tile


def to_flat(flat, base, value, height, breadth):
    lines = breadth // LANES
    for begin in range(0, height, 8):
        count = min(8, height - begin)
        for index in range(lines):
            start = base + begin * lines + index
            tile = value(slice(begin, begin + count), slice(index * LANES, (index + 1) * LANES))
            if lines == 1:
                flat[start : start + count, :] = tile
            else:
                flat[pl.ds(start, count, stride=lines), :] = tile


def section_bases(devices):
    bases = []
    base = 0
    for height, breadth in matrix_shapes():
        bases.append(base)
        base += height // devices * breadth // LANES
    return bases


def pack_kernel(devices, group, flat, extra, qkv_out, out_out, wide_out, down_out, qkv, out, wide, down):
    rows = D // devices
    frows = FF // devices
    bases = section_bases(devices)
    qkv[...] = jnp.zeros(qkv.shape, F32)
    out[...] = jnp.zeros(out.shape, F32)
    from_flat(flat, bases[0], qkv.at[:, :QD], rows, QD)
    from_flat(flat, bases[1], qkv.at[:, QD : QD + KVD], rows, KVD)
    from_flat(flat, bases[2], qkv.at[:, QD + KVD :], rows, KVD)
    if extra is not None:
        qkv[rows : rows + 1, :LANES] = extra[...]
    from_flat(flat, bases[3], out, rows, D)
    from_flat(flat, bases[6], down, FF // devices, D)
    qkv_out[...] = qkv[...].astype(qkv_out.dtype)
    out_out[...] = out[...].astype(out_out.dtype)
    down_out[...] = down[...].astype(down_out.dtype)
    for which in range(2):
        from_flat(flat, bases[4 + which], wide, rows, FF)
        targets = devices // group
        for target in range(targets):
            piece = jnp.concatenate(
                [
                    wide[:, (turn * targets + target) * frows : (turn * targets + target + 1) * frows]
                    for turn in range(group)
                ],
                axis=1,
            )
            if group == 1:
                wide_out[target, :, which * frows : (which + 1) * frows] = piece.astype(wide_out.dtype)
            else:
                wide_out[target, which] = piece.astype(wide_out.dtype)


def pack(flat, extra, devices, group, dtype):
    rows = D // devices
    frows = FF // devices
    padded = (rows // 16 + 1) * 16
    targets = devices // group
    wide = (targets, rows, 2 * frows) if group == 1 else (targets, 2, rows, group * frows)
    shapes = [(padded, QD + 2 * KVD), (padded, D), wide, (frows, D)]
    types = [dtype, dtype, BF16, dtype]
    if extra is None:
        body = lambda flat_ref, *refs: pack_kernel(devices, group, flat_ref, None, *refs)
        operands = [flat]
    else:
        body = lambda *refs: pack_kernel(devices, group, *refs)
        operands = [flat, extra]
    return pl.pallas_call(
        body,
        out_shape=[jax.ShapeDtypeStruct(shape, kind) for shape, kind in zip(shapes, types)],
        scratch_shapes=[
            pltpu.VMEM((padded, QD + 2 * KVD), F32),
            pltpu.VMEM((padded, D), F32),
            pltpu.VMEM((rows, FF), F32),
            pltpu.VMEM((frows, D), F32),
        ],
        compiler_params=pltpu.CompilerParams(vmem_limit_bytes=32 * 1024 * 1024),
        cost_estimate=pl.CostEstimate(flops=0, bytes_accessed=6 * flat.size, transcendentals=0),
        name="pack",
    )(*operands)


def update_kernel(devices, decay, factors, flat, qkv, out, wide, down, result, moved, rows_wide):
    rows = D // devices
    frows = FF // devices
    bases = section_bases(devices)
    whole = qkv[...].astype(F32)
    out_whole = out[...].astype(F32)
    down_whole = down[...].astype(F32)
    parts = [
        lambda r, c: whole[r, c],
        lambda r, c: whole[r, slice(QD + c.start, QD + c.stop)],
        lambda r, c: whole[r, slice(QD + KVD + c.start, QD + KVD + c.stop)],
        lambda r, c: out_whole[r, c],
    ]
    shapes = matrix_shapes()
    for index, part in enumerate(parts):
        to_flat(
            moved, bases[index], lambda r, c: part(r, c) * factors[index], rows, shapes[index][1]
        )
    to_flat(moved, bases[6], lambda r, c: down_whole[r, c] * factors[6], frows, D)
    for which in range(2):
        for source in range(devices):
            rows_wide[:, source * frows : (source + 1) * frows] = wide[
                source, :, which * frows : (which + 1) * frows
            ].astype(F32)
        to_flat(
            moved, bases[4 + which], lambda r, c: rows_wide[r, c] * factors[4 + which], rows, FF
        )
    result[...] = decay * flat[...] + moved[...]


def update(flat, qkv, out, wide, down, devices, decay, factors):
    return pl.pallas_call(
        lambda *refs: update_kernel(devices, decay, factors, *refs),
        out_shape=jax.ShapeDtypeStruct(flat.shape, F32),
        scratch_shapes=[
            pltpu.VMEM(flat.shape, F32),
            pltpu.VMEM((D // devices, FF), F32),
        ],
        compiler_params=pltpu.CompilerParams(vmem_limit_bytes=32 * 1024 * 1024),
        cost_estimate=pl.CostEstimate(flops=0, bytes_accessed=10 * flat.size, transcendentals=0),
        name="update",
    )(flat, qkv, out, wide, down)


def combine_kernel(old_pair, gate, up, old_down, down, old_out, out, mats, lines):
    devices, rows, _ = old_pair.shape
    frows = gate.shape[0]
    padded = out.shape[0]
    lines[...] = jnp.zeros(lines.shape, F32)
    for source in range(devices):
        lines[source * rows : (source + 1) * rows, : 2 * frows] = old_pair[source].astype(F32)
    old = lines[...].T
    mats[0] = (MOMENTUM_DECAY * old[:frows] + gate[...].astype(F32)).astype(BF16)
    mats[1] = (MOMENTUM_DECAY * old[frows : 2 * frows] + up[...].astype(F32)).astype(BF16)
    mats[2] = (MOMENTUM_DECAY * old_down[...] + down[...].astype(F32)).astype(BF16)
    last = MOMENTUM_DECAY * old_out[...] + out[...].astype(F32)
    mats[3] = jnp.concatenate(
        [last, jnp.zeros((frows - padded, last.shape[1]), F32)], axis=0
    ).astype(BF16)


def combine(old_pair, gate, up, old_down, down, old_out, out):
    frows, width = gate.shape
    return pl.pallas_call(
        combine_kernel,
        out_shape=jax.ShapeDtypeStruct((4, frows, width), BF16),
        scratch_shapes=[pltpu.VMEM((width, -(-2 * frows // LANES) * LANES), F32)],
        compiler_params=pltpu.CompilerParams(vmem_limit_bytes=32 * 1024 * 1024),
        name="combine",
    )(old_pair, gate, up, old_down, down, old_out, out)


def turn_kernel(gate, up, out, columns):
    devices, rows, _ = out.shape
    frows = gate.shape[0]
    columns[...] = jnp.zeros(columns.shape, F32)
    columns[:frows] = gate[...].astype(F32)
    columns[frows : 2 * frows] = up[...].astype(F32)
    lines = columns[...].T
    for target in range(devices):
        out[target] = lines[target * rows : (target + 1) * rows, : 2 * frows].astype(BF16)


def turn(gate, up, devices):
    frows, width = gate.shape
    return pl.pallas_call(
        turn_kernel,
        out_shape=jax.ShapeDtypeStruct((devices, width // devices, 2 * frows), BF16),
        scratch_shapes=[pltpu.VMEM((-(-2 * frows // LANES) * LANES, width), F32)],
        compiler_params=pltpu.CompilerParams(vmem_limit_bytes=32 * 1024 * 1024),
        name="turn",
    )(gate, up)


def on_device(
    block_input,
    cotangent,
    lengths,
    doc_starts,
    master,
    momentum,
    vectors,
    vector_first,
    vector_second,
):
    n_dp = lax.axis_size("dp")
    n_ctx = lax.axis_size("ctx")
    devices = n_dp * n_ctx
    rows = D // devices
    frows = FF // devices
    fblock = FF // n_ctx
    slots, span, width = block_input.shape
    tokens = slots * span
    group = HEADS // KVH
    qkv = QD + 2 * KVD
    my_ctx = lax.axis_index("ctx")
    me = lax.axis_index("dp") * n_ctx + my_ctx
    core_bit, x_bit = 1, 2
    ctx_bits = [core_bit, x_bit]
    dp_bits = [n_ctx << index for index in range(n_dp.bit_length() - 1)]
    all_bits = ctx_bits + dp_bits
    many = tuple([2] * len(all_bits))
    padded = (rows // 16 + 1) * 16

    master_flat = master.reshape(-1, LANES)
    momentum_flat = momentum.reshape(-1, LANES)
    small = jnp.pad(vectors, ((0, 0), (0, LANES - vectors.shape[1])))
    qkv_local, out_local, gate_up, down_local = pack(master_flat, small, devices, n_dp, BF16)

    attn_full = gather_bits(
        jnp.concatenate([qkv_local, out_local], axis=1), dp_bits[::-1], me, devices
    )
    qkv_full = gather_bits(attn_full[..., :qkv], ctx_bits[::-1], me, devices, dp_bits)
    qkv_full = qkv_full.reshape(devices, padded, qkv)
    gain_first, gain_second, bias_query, bias_key, bias_value = [
        piece.astype(F32) for piece in split_small(qkv_full[:, rows], devices)
    ]
    w_qkv = qkv_full[:, :rows].reshape(D, qkv)

    came = [choose(gate_up, my_ctx, 0)] + [
        swap(choose(gate_up, my_ctx ^ mask, 0), mask, devices) for mask in range(1, n_ctx)
    ]
    came, _ = lax.optimization_barrier((came, attn_full))
    ordered = []
    for source in range(n_ctx):
        piece = came[0]
        for mask in range(1, n_ctx):
            piece = jnp.where(my_ctx ^ mask == source, came[mask], piece)
        ordered.append(piece)
    gate_up = jnp.concatenate(ordered, axis=1)
    w_gate, w_up = [lax.all_gather(gate_up[index], "dp", axis=0, tiled=True) for index in range(2)]

    def to_rows(gate, up):
        return lax.all_to_all(
            turn(gate, up, devices), BOTH, split_axis=0, concat_axis=0, tiled=True
        )

    length, second = lengths[0], doc_starts[0]
    places = my_ctx * span + jnp.arange(span, dtype=jnp.int32)
    doc_begin = jnp.where(places >= length, length, jnp.where(places >= second, second, 0))
    position = (places - doc_begin).astype(F32)
    live = (places < length)[:, None]
    info = jnp.stack([my_ctx, length, second]).astype(jnp.int32)
    inverse = ROPE_BASE ** (-2.0 * jnp.arange(HD // 2, dtype=F32) / HD)
    angles = inverse[:, None] * position[None, :]
    cosine, sine_part = jnp.cos(angles), jnp.sin(angles)
    cosine = jnp.concatenate([cosine, cosine], axis=0)[None]
    sine_part = jnp.concatenate([sine_part, sine_part], axis=0)[None]

    def from_ctx(value, other_x=None):
        other_core = swap(value, core_bit, devices)
        if other_x is None:
            other_x = swap(value, x_bit, devices)
        return value, other_core, other_x

    cot_here = jnp.where(live, cotangent.reshape(tokens, width), jnp.zeros((), BF16))

    def pair_of_heads(kv, index):
        begin = index * HD
        return jnp.concatenate(
            [kv[:, begin : begin + HD], kv[:, KVD + begin : KVD + begin + HD]], axis=1
        )

    inputs = block_input.astype(F32).reshape(tokens, width)
    scale_one = lax.rsqrt(jnp.mean(inputs * inputs, axis=-1, keepdims=True) + NORM_EPS)
    normed_one = (inputs * scale_one * gain_first).astype(BF16)
    bias = jnp.concatenate([bias_query, bias_key, bias_value])
    pre = mm(w_qkv, normed_one, ((0,), (1,))) + bias[:, None]
    turned = rotate(
        pre[: QD + KVD].reshape(HEADS + KVH, HD, tokens), cosine, sine_part
    )
    queries = (turned[:HEADS].astype(BF16).astype(F32) * HD ** (-0.5)).astype(BF16)
    kv_here = jnp.concatenate(
        [turned[HEADS:].astype(BF16).reshape(KVD, tokens), pre[QD + KVD :].astype(BF16)], axis=0
    )
    kv = from_ctx(kv_here)
    kv = jnp.stack(kv + (swap(kv[2], core_bit, devices),))
    down_bits = dp_bits[::-1]
    down_part, _ = lax.optimization_barrier((down_local, kv_here))
    down_part = gather_bits(down_part, down_bits[:1], me, devices)
    back_one = jnp.pad(
        normed_one.T.reshape(devices, rows, tokens), ((0, 0), (0, padded - rows), (0, 0))
    ).reshape(devices * padded, tokens)
    back_one, kv = lax.optimization_barrier((back_one, kv))
    out_full, _ = lax.optimization_barrier((attn_full[..., qkv:], kv))
    halves = []
    for index in range(KVH):
        if index == 1:
            out_full, down_part, cot_here, _ = lax.optimization_barrier(
                (out_full, down_part, cot_here, halves)
            )
            cot_far = swap(cot_here, x_bit, devices)
            down_part = gather_bits(down_part, down_bits[1:2], me, devices, down_bits[:1])
        out_full = gather_bits(
            out_full, ctx_bits[::-1][index : index + 1], me, devices, dp_bits + ctx_bits[::-1][:index]
        )
        kv_one = pair_of_heads(kv, index)
        halves.append(attend(info, kv_one, queries[index * group : (index + 1) * group]))
    down_part, _ = lax.optimization_barrier((down_part, halves))
    halves, cot_far = lax.optimization_barrier((halves, cot_far))
    attended = jnp.concatenate([half[0] for half in halves], axis=0)
    log_total = jnp.concatenate([half[1] for half in halves], axis=0)
    out_pieces = out_full.reshape(devices * padded, D)
    w_down = gather_bits(down_part, down_bits[2:], me, devices, down_bits[:2])
    w_down = w_down.reshape(fblock, D)

    mixed_pieces = jnp.pad(
        attended.reshape(devices, rows, tokens).astype(BF16), ((0, 0), (0, padded - rows), (0, 0))
    ).reshape(devices * padded, tokens)
    hidden = inputs + mm(mixed_pieces, out_pieces, ((0,), (0,)))
    scale_two = lax.rsqrt(jnp.mean(hidden * hidden, axis=-1, keepdims=True) + NORM_EPS)
    normed_two = (hidden * scale_two * gain_second).astype(BF16)

    normed = from_ctx(normed_two)
    out_pieces, _ = lax.optimization_barrier((out_pieces, normed_two))
    w_out = out_pieces.reshape(devices, padded, D)[:, :rows].reshape(QD, D)
    cot = from_ctx(cot_here, cot_far)
    kept, near_part = feed_forward(normed[:2], cot[:2], w_gate, w_up, w_down, n_ctx, None)
    (far_x, far_dy), kept = lax.optimization_barrier(((normed[2], cot[2]), kept))
    kept, far_part = feed_forward(
        (far_x, swap(far_x, core_bit, devices)),
        (far_dy, swap(far_dy, core_bit, devices)),
        w_gate,
        w_up,
        w_down,
        n_ctx,
        kept,
    )
    acts, gate_backs, up_backs, normed_all, cot_all = kept
    back_parts = (near_part, far_part)

    def to_ctx(halves):
        crossed = swap(halves[1][span:], core_bit, devices)
        far = (halves[1][:span].astype(F32) + crossed.astype(F32)).astype(BF16)
        near = swap(halves[0][span:], core_bit, devices)
        near = halves[0][:span].astype(F32) + near.astype(F32)
        return near + swap(far, x_bit, devices).astype(F32), far

    normed_two_grad, ready = to_ctx(back_parts)
    (acts, gate_backs, up_backs), ready = lax.optimization_barrier(
        ((acts, gate_backs, up_backs), ready)
    )

    dp_shape = tuple([2] * len(dp_bits)) + (frows, D)
    dp_order = dp_bits[1:] + dp_bits[:1]
    down_value = mm(acts, cot_all, ((0,), (0,))).astype(BF16)
    gate_value = mm(gate_backs, normed_all, ((0,), (0,))).astype(BF16)
    up_value = mm(up_backs, normed_all, ((0,), (0,))).astype(BF16)
    down_parts, gate_parts, up_parts = [
        scatter_start(value.reshape(dp_shape), dp_bits, bit, me, devices)
        for value, bit in (
            (down_value, dp_order[0]),
            (gate_value, dp_bits[0]),
            (up_value, dp_bits[0]),
        )
    ]
    momentum_flat, acts, _ = lax.optimization_barrier((momentum_flat, acts, (down_value, gate_value, up_value)))
    old_qkv, old_out, old_pair, old_down = pack(momentum_flat, None, devices, 1, F32)
    old_pair = lax.all_to_all(old_pair, BOTH, split_axis=0, concat_axis=0, tiled=True)

    out_grad = cot_here.astype(F32)
    hidden_norm_grad, grad_gain_second = norm_backward(
        hidden, scale_two, gain_second, normed_two_grad
    )
    hidden_grad = out_grad + hidden_norm_grad
    hidden_low = hidden_grad.astype(BF16)
    heads_grad = mm(w_out, hidden_low, ((1,), (1,))).astype(BF16).reshape(HEADS, HD, tokens)
    delta = jnp.sum(heads_grad.astype(F32) * attended, axis=1, keepdims=True)
    grad_output = mm(mixed_pieces, hidden_low)
    query_grads, kv_parts = [], []
    sent, kept = scatter_split(
        grad_output.astype(BF16).reshape(many + (padded, D)), all_bits, all_bits[0], me
    )
    wide_parts = [gate_parts, up_parts, down_parts, (kept, swap(sent, all_bits[0], devices))]
    wide_orders = [list(dp_bits), list(dp_bits), list(dp_order), list(all_bits)]
    steps = [[2, 3], [0, 1, 3], [2, 0, 3], [1, 3]]
    shares = [4, 3]
    ready = [sent]
    for index in range(KVH):
        kv_one = pair_of_heads(kv, index)
        kv_grad = None
        begin = index * group
        for count in shares:
            chosen = slice(begin, begin + count)
            begin += count
            query_part, ready = lax.optimization_barrier((queries[chosen], ready))
            query_grad, kv_grad = attend_back(
                info, kv_one, query_part, heads_grad[chosen], log_total[chosen], delta[chosen], kv_grad
            )
            query_grads.append(query_grad)
            ready = []
            for which in steps.pop(0):
                order = wide_orders[which]
                parts, _ = lax.optimization_barrier((wide_parts[which], query_grad))
                order.pop(0)
                sent, kept = scatter_split(scatter_end(parts), order, order[0], me)
                ready.append(sent)
                wide_parts[which] = (kept, swap(sent, order[0], devices))
        kv_parts.append(
            scatter_sum(kv_grad.reshape(2, 2, 2 * HD, span), ctx_bits, me, devices)
        )
    kv_grads = [part.astype(F32).reshape(2, HD, span) for part in kv_parts]
    acts, _ = lax.optimization_barrier((acts, query_grads[2]))
    out_part = mm(acts, w_down).astype(BF16)
    out_sum, _ = to_ctx([out_part[: 2 * span], out_part[2 * span :]])
    layer_out = jnp.where(live, hidden + out_sum, 0.0)
    qk_grad = jnp.concatenate(query_grads + [grad[:1] for grad in kv_grads], axis=0)
    qk_back = rotate_back(qk_grad, cosine, sine_part).reshape(QD + KVD, tokens)
    qkv_back = jnp.concatenate(
        [qk_back] + [grad[1] for grad in kv_grads], axis=0
    ).astype(BF16)
    grad_qkv = mm(back_one, qkv_back, ((1,), (1,)))
    grad_bias = jnp.sum(qkv_back.astype(F32), axis=1)
    normed_one_grad = mm(qkv_back, w_qkv, ((0,), (1,)))
    input_norm_grad, grad_gain_first = norm_backward(inputs, scale_one, gain_first, normed_one_grad)
    input_grad = (hidden_grad + input_norm_grad).astype(BF16).reshape(slots, span, width)

    vector_part = join_small(
        [
            grad_gain_first,
            grad_gain_second,
            grad_bias[:QD],
            grad_bias[QD : QD + KVD],
            grad_bias[QD + KVD :],
        ],
        devices,
    )
    vector_grad = jnp.sum(
        lax.all_to_all(vector_part, BOTH, split_axis=0, concat_axis=0, tiled=True),
        axis=0,
        keepdims=True,
    )
    sent, kept = scatter_split(
        grad_qkv.astype(BF16).reshape(many + (padded, qkv)), all_bits, all_bits[0], me
    )
    wide_parts, sent = lax.optimization_barrier((wide_parts, sent))
    qkv_parts = (kept, swap(sent, all_bits[0], devices))
    gate_sum, up_sum, down_sum, out_sum_rows = [
        scatter_sum(scatter_end(parts), order[1:], me, devices)
        for parts, order in zip(wide_parts, wide_orders)
    ]
    qkv_sum_rows = scatter_sum(scatter_end(qkv_parts), all_bits[1:], me, devices)
    moved_qkv = MOMENTUM_DECAY * old_qkv + qkv_sum_rows.astype(F32)
    mats = combine(old_pair, gate_sum, up_sum, old_down, down_sum, old_out, out_sum_rows)
    owned = to_owner(mats.reshape(2, 2, frows, D), core_bit, x_bit, me, devices)
    owned = owned.reshape(n_ctx * frows, D)
    count = len(block_pairs(D // BLOCK))
    places = (count + n_dp - 1) // n_dp * n_dp
    dp_many = tuple([2] * len(dp_bits))
    gram = gram_blocks(owned, places).reshape(dp_many + (places // n_dp, BLOCK, BLOCK))
    (gate_sum, up_sum), owned = lax.optimization_barrier(((gate_sum, up_sum), owned))
    new_momentum = update(
        momentum_flat,
        qkv_sum_rows,
        out_sum_rows,
        to_rows(gate_sum, up_sum),
        down_sum,
        devices,
        MOMENTUM_DECAY,
        [1.0] * 7,
    ).reshape(momentum.shape)
    gram = scatter_sum(gram, dp_bits, me, devices)
    gram = gather_bits(gram, dp_bits[::-1], me, devices).reshape(places, BLOCK, BLOCK)
    moved_low = moved_qkv.astype(BF16)
    new_momentum, moved_low, gram = lax.optimization_barrier((new_momentum, moved_low, gram))
    ortho = orthogonal_wide(gram, owned).reshape(2, 2, frows, D)
    ortho = from_owner(ortho, core_bit, x_bit, me, devices).reshape(n_ctx, frows, D)
    ortho_pair = to_rows(ortho[0], ortho[1])

    qkv_all = lax.all_gather(moved_low, BOTH, axis=0, tiled=True)
    ortho_qkv = orthogonal_whole(qkv_all, moved_qkv, (QD, KVD, KVD))
    factors = [
        -MUON_RATE * math.sqrt(max(1.0, breadth / height)) for height, breadth in matrix_shapes()
    ]
    new_master = update(
        master_flat,
        ortho_qkv,
        ortho[3, :padded],
        ortho_pair,
        ortho[2],
        devices,
        1.0 - MUON_RATE * MUON_DECAY,
        factors,
    ).reshape(master.shape)
    first_new = BETA_FIRST * vector_first + (1.0 - BETA_FIRST) * vector_grad
    second_new = BETA_SECOND * vector_second + (1.0 - BETA_SECOND) * vector_grad * vector_grad
    adjusted = (
        first_new
        / (1.0 - BETA_FIRST**STEP)
        / (jnp.sqrt(second_new / (1.0 - BETA_SECOND**STEP)) + ADAM_EPS)
    )
    new_vectors = vectors - ADAM_RATE * adjusted
    return (
        layer_out.astype(BF16).reshape(slots, span, width),
        input_grad,
        new_master,
        new_momentum,
        new_master.astype(BF16),
        new_vectors,
        first_new,
        second_new,
    )


def solution(mesh):
    return jax.shard_map(
        on_device,
        mesh=mesh,
        in_specs=(
            P("dp", "ctx", None),
            P("dp", "ctx", None),
            P("dp"),
            P("dp"),
            P(BOTH, None),
            P(BOTH, None),
            P(BOTH, None),
            P(BOTH, None),
            P(BOTH, None),
        ),
        out_specs=(
            P("dp", "ctx", None),
            P("dp", "ctx", None),
            P(BOTH, None),
            P(BOTH, None),
            P(BOTH, None),
            P(BOTH, None),
            P(BOTH, None),
            P(BOTH, None),
        ),
        check_vma=False,
    )
```

```python
import math

import jax
import jax.numpy as jnp
from jax import lax
from jax.experimental import pallas as pl
from jax.experimental.pallas import tpu as pltpu
from jax.sharding import PartitionSpec as P

D = 896
HEADS = 14
KVH = 2
HD = 64
FF = 4864
SLOT = 2048
NS_STEPS = 3
STEP = 10
QD = 896
KVD = 128

NORM_EPS = 1e-06
ROPE_BASE = 1000000.0
NS_LINEAR = 3.4445
NS_SQUARE = -4.775
NS_CUBIC = 2.0315
MOMENTUM_DECAY = 0.5
MUON_RATE = 0.6
MUON_DECAY = 0.1
ADAM_RATE = 0.2
BETA_FIRST = 0.9
BETA_SECOND = 0.95
ADAM_EPS = 1e-08
MASK_FLOOR = -1e30

F32 = jnp.float32
BF16 = jnp.bfloat16
BOTH = ("dp", "ctx")
LANES = 128


def matrix_shapes():
    return [(D, QD), (D, KVD), (D, KVD), (QD, D), (D, FF), (D, FF), (FF, D)]


def vector_sizes():
    return [D, D, QD, KVD, KVD]


def mm(left, right, contract=((1,), (0,))):
    return lax.dot_general(left, right, (contract, ((), ())), preferred_element_type=F32)


def split_small(flat, devices):
    result = []
    offset = 0
    for extent_all in vector_sizes():
        extent = extent_all // devices
        result.append(flat[:, offset : offset + extent].reshape(extent_all))
        offset += extent
    return result


def join_small(pieces, devices):
    return jnp.concatenate([piece.reshape(devices, -1) for piece in pieces], axis=1)


def swap(value, mask, devices):
    return lax.ppermute(value, BOTH, [(index, index ^ mask) for index in range(devices)])


def gather_bits(value, bits, me, devices, before=()):
    held = value
    done = list(before)
    for bit in bits:
        place = sum(1 for other in done if other > bit)
        got = swap(held, bit, devices)
        mine = (me & bit) != 0
        held = jnp.where(
            mine, jnp.stack([got, held], axis=place), jnp.stack([held, got], axis=place)
        )
        done.append(bit)
    return held


def scatter_split(held, left, bit, me):
    axis = sorted(left, reverse=True).index(bit)
    mine = jnp.where((me & bit) != 0, 1, 0)
    return choose(held, 1 - mine, axis).astype(BF16), choose(held, mine, axis)


def scatter_start(held, left, bit, me, devices):
    sent, kept = scatter_split(held, left, bit, me)
    return kept, swap(sent, bit, devices)


def scatter_end(parts):
    return (parts[0].astype(F32) + parts[1].astype(F32)).astype(BF16)


def scatter_sum(value, bits, me, devices):
    left = list(bits)
    held = value
    for bit in bits:
        held = scatter_end(scatter_start(held, left, bit, me, devices))
        left.remove(bit)
    return held


def choose(value, mine, axis):
    return lax.dynamic_index_in_dim(value, mine, axis, keepdims=False)


def to_owner(value, core_bit, x_bit, me, devices):
    core = jnp.where((me & core_bit) != 0, 1, 0)
    across = jnp.where((me & x_bit) != 0, 1, 0)
    got = swap(choose(value, 1 - core, 1), core_bit, devices)
    value = jnp.stack([choose(value, core, 1), got], axis=1)
    got = swap(choose(value, 1 - across, 0), x_bit, devices)
    return jnp.stack([choose(value, across, 0), got])


def from_owner(value, core_bit, x_bit, me, devices):
    got = swap(value[1], x_bit, devices)
    value = jnp.where(
        (me & x_bit) != 0, jnp.stack([got, value[0]]), jnp.stack([value[0], got])
    )
    got = swap(value[:, 1], core_bit, devices)
    return jnp.where(
        (me & core_bit) != 0,
        jnp.stack([got, value[:, 0]], axis=1),
        jnp.stack([value[:, 0], got], axis=1),
    )


def rotate(values, cosine, sine_part):
    midpoint = HD // 2
    turned = jnp.concatenate([-values[:, midpoint:], values[:, :midpoint]], axis=1)
    return values * cosine + turned * sine_part


def rotate_back(gradient, cosine, sine_part):
    midpoint = HD // 2
    scaled = gradient * sine_part
    turned = jnp.concatenate([scaled[:, midpoint:], -scaled[:, :midpoint]], axis=1)
    return gradient * cosine + turned


def norm_backward(source, scale_row, gain, incoming):
    gain_grad = jnp.sum(incoming * source * scale_row, axis=0)
    weighted = incoming * gain
    result = scale_row * weighted - source * scale_row**3 * jnp.mean(
        weighted * source, axis=-1, keepdims=True
    )
    return (result, gain_grad)


def halves_of(span):
    return [slice(0, span // 2), slice(span // 2, span)]


def fill_mask(info, mask, chunk, span):
    key = chunk * span + lax.broadcasted_iota(jnp.int32, (span, span), 0)
    query = info[0] * span + lax.broadcasted_iota(jnp.int32, (span, span), 1)
    key_doc = (key >= info[2]).astype(jnp.int32) + (key >= info[1]).astype(jnp.int32)
    query_doc = (query >= info[2]).astype(jnp.int32) + (query >= info[1]).astype(jnp.int32)
    allowed = jnp.logical_and(key_doc == query_doc, key <= query)
    mask[chunk] = jnp.where(allowed, 0.0, MASK_FLOOR).astype(F32)


def attend_kernel(info, kv, q, out, lse, keys, mask, best, total, acc):
    head = pl.program_id(0)
    span = q.shape[-1]
    mine = info[0]
    chunks = mine + 1

    @pl.when(head == 0)
    def _():
        def fill(chunk, carry):
            slot = jnp.bitwise_xor(chunk, mine)
            keys[chunk] = kv[slot, :HD, :].astype(F32).T.astype(BF16)
            fill_mask(info, mask, chunk, span)
            return carry

        lax.fori_loop(0, chunks, fill, 0)

    best[...] = jnp.full(best.shape, MASK_FLOOR, F32)
    total[...] = jnp.zeros(total.shape, F32)
    acc[...] = jnp.zeros(acc.shape, F32)
    queries = q[0]

    def step(index, carry):
        chunk = mine - index
        slot = jnp.bitwise_xor(chunk, mine)
        scores = jnp.dot(keys[chunk], queries, preferred_element_type=F32) + mask[chunk]
        old = best[...]
        new = jnp.maximum(old, jnp.max(scores, axis=0, keepdims=True))
        present = jnp.exp(scores - new)
        shrink = jnp.exp(old - new)
        best[...] = new
        total[...] = total[...] * shrink + jnp.sum(present, axis=0, keepdims=True)
        acc[...] = acc[...] * shrink + jnp.dot(
            kv[slot, HD:, :], present.astype(BF16), preferred_element_type=F32
        )
        return carry

    lax.fori_loop(0, chunks, step, 0)
    out[0] = acc[...] / total[...]
    lse[0] = best[...] + jnp.log(total[...])


def attend_back_kernel(
    info, kv, q, dout, lse, delta, before, dq, dkv, keys, values, mask, dk, dv, acc
):
    head = pl.program_id(0)
    span = q.shape[-1]
    mine = info[0]
    chunks = mine + 1
    n_ctx = kv.shape[0]

    @pl.when(head == 0)
    def _():
        dk[...] = jnp.zeros(dk.shape, F32)
        dv[...] = jnp.zeros(dv.shape, F32)

        def fill(chunk, carry):
            slot = jnp.bitwise_xor(chunk, mine)
            keys[chunk] = kv[slot, :HD, :].astype(F32).T.astype(BF16)
            values[chunk] = kv[slot, HD:, :].astype(F32).T.astype(BF16)
            fill_mask(info, mask, chunk, span)
            return carry

        lax.fori_loop(0, chunks, fill, 0)

    acc[...] = jnp.zeros(acc.shape, F32)
    queries = q[0]
    douts = dout[0]
    query_rows = queries.astype(F32).T.astype(BF16)
    dout_rows = douts.astype(F32).T.astype(BF16)

    def step(chunk, carry):
        slot = jnp.bitwise_xor(chunk, mine)
        value_sum, key_sum = dv[chunk], dk[chunk]
        for lanes in halves_of(span):
            scores = (
                jnp.dot(keys[chunk], queries[:, lanes], preferred_element_type=F32)
                + mask[chunk, :, lanes]
            )
            shares = jnp.exp(scores - lse[0, :, lanes])
            share_grad = jnp.dot(values[chunk], douts[:, lanes], preferred_element_type=F32)
            score_grad = (shares * (share_grad - delta[0, :, lanes])).astype(BF16)
            value_sum += jnp.dot(
                shares.astype(BF16), dout_rows[lanes, :], preferred_element_type=F32
            )
            key_sum += jnp.dot(score_grad, query_rows[lanes, :], preferred_element_type=F32)
            acc[:, lanes] += jnp.dot(kv[slot, :HD, :], score_grad, preferred_element_type=F32)
        dv[chunk], dk[chunk] = value_sum, key_sum
        return carry

    lax.fori_loop(0, chunks, step, 0)
    dq[0] = acc[...] * HD ** (-0.5)

    @pl.when(head == pl.num_programs(0) - 1)
    def _():
        for chunk in range(n_ctx):
            sums = jnp.concatenate([dk[chunk].T, dv[chunk].T], axis=0)
            if before is not None:
                sums += before[chunk].astype(F32)
            dkv[chunk] = sums.astype(BF16)


def attend(info, kv, q):
    heads, _, span = q.shape
    n_ctx = kv.shape[0]
    per_head = lambda rows: pl.BlockSpec((1, rows, span), lambda head: (head, 0, 0))
    return pl.pallas_call(
        attend_kernel,
        grid=(heads,),
        in_specs=[
            pl.BlockSpec(memory_space=pltpu.SMEM),
            pl.BlockSpec(kv.shape, lambda head: (0, 0, 0)),
            per_head(HD),
        ],
        out_specs=[per_head(HD), per_head(1)],
        out_shape=[
            jax.ShapeDtypeStruct((heads, HD, span), F32),
            jax.ShapeDtypeStruct((heads, 1, span), F32),
        ],
        scratch_shapes=[
            pltpu.VMEM((n_ctx, span, HD), BF16),
            pltpu.VMEM((n_ctx, span, span), F32),
            pltpu.VMEM((1, span), F32),
            pltpu.VMEM((1, span), F32),
            pltpu.VMEM((HD, span), F32),
        ],
        compiler_params=pltpu.CompilerParams(vmem_limit_bytes=40 * 1024 * 1024),
        cost_estimate=pl.CostEstimate(
            flops=4 * heads * span * span * n_ctx * HD * 4,
            bytes_accessed=4 * heads * span * HD * 2,
            transcendentals=heads * span * span * n_ctx,
        ),
        name="attend",
    )(info, kv, q)


def attend_back(info, kv, q, dout, lse, delta, before):
    heads, _, span = q.shape
    n_ctx = kv.shape[0]
    per_head = lambda rows: pl.BlockSpec((1, rows, span), lambda head: (head, 0, 0))
    whole = pl.BlockSpec(kv.shape, lambda head: (0, 0, 0))
    if before is None:
        body = lambda *refs: attend_back_kernel(*refs[:6], None, *refs[6:])
    else:
        body = attend_back_kernel
    return pl.pallas_call(
        body,
        grid=(heads,),
        in_specs=[
            pl.BlockSpec(memory_space=pltpu.SMEM),
            whole,
            per_head(HD),
            per_head(HD),
            per_head(1),
            per_head(1),
        ]
        + [whole] * (before is not None),
        out_specs=[per_head(HD), whole],
        out_shape=[
            jax.ShapeDtypeStruct((heads, HD, span), F32),
            jax.ShapeDtypeStruct(kv.shape, BF16),
        ],
        scratch_shapes=[
            pltpu.VMEM((n_ctx, span, HD), BF16),
            pltpu.VMEM((n_ctx, span, HD), BF16),
            pltpu.VMEM((n_ctx, span, span), F32),
            pltpu.VMEM((n_ctx, span, HD), F32),
            pltpu.VMEM((n_ctx, span, HD), F32),
            pltpu.VMEM((HD, span), F32),
        ],
        compiler_params=pltpu.CompilerParams(vmem_limit_bytes=40 * 1024 * 1024),
        cost_estimate=pl.CostEstimate(
            flops=10 * heads * span * span * n_ctx * HD * 4,
            bytes_accessed=8 * heads * span * HD * 2,
            transcendentals=heads * span * span * n_ctx,
        ),
        name="attend_back",
    )(*[info, kv, q, dout, lse, delta] + [before] * (before is not None))


def forward_backward_kernel(
    x0, x1, dy0, dy1, gate, up, down, act_out, gate_back_out, up_back_out, x_out, dy_out, back_out
):
    first = pl.program_id(0) == 0
    x = jnp.where(first, x0[...], x1[...])
    dy = jnp.where(first, dy0[...], dy1[...])
    x_out[...] = x
    dy_out[...] = dy
    gate_pre = jnp.dot(x, gate[...], preferred_element_type=F32)
    up_pre = jnp.dot(x, up[...], preferred_element_type=F32)
    grad_act = mm(dy, down[...], ((1,), (1,)))
    sigmoid_gate = jax.nn.sigmoid(gate_pre)
    swish = gate_pre * sigmoid_gate
    slope = sigmoid_gate * (1.0 + gate_pre * (1.0 - sigmoid_gate))
    act_out[...] = (swish * up_pre).astype(BF16)
    gate_back = (grad_act * up_pre * slope).astype(BF16)
    up_back = (grad_act * swish).astype(BF16)
    gate_back_out[...] = gate_back
    up_back_out[...] = up_back
    back_out[...] = (
        mm(gate_back, gate[...], ((1,), (1,))) + mm(up_back, up[...], ((1,), (1,)))
    ).astype(BF16)


def feed_forward(x, dy, gate, up, down, blocks, earlier):
    span, width = x[0].shape
    units = gate.shape[1]
    first = 0 if earlier is None else 2
    whole = lambda shape: pl.BlockSpec(shape, lambda block: (0, 0))
    line = lambda columns, offset: pl.BlockSpec(
        (span, columns), lambda block: (block + offset, 0)
    )
    columns = [units, units, units, width, width]
    shapes = [jax.ShapeDtypeStruct((blocks * span, count), BF16) for count in columns]
    in_specs = [whole((span, width))] * 4 + [whole((width, units))] * 2 + [whole((units, width))]
    operands = [*x, *dy, gate, up, down]
    aliases = {}
    body = forward_backward_kernel
    if earlier is not None:
        in_specs += [pl.BlockSpec(memory_space=pl.ANY)] * 5
        operands += list(earlier)
        aliases = {7 + index: index for index in range(5)}
        body = lambda *refs: forward_backward_kernel(*refs[:7], *refs[12:])
    results = pl.pallas_call(
        body,
        grid=(2,),
        in_specs=in_specs,
        out_specs=[line(count, first) for count in columns] + [line(width, 0)],
        out_shape=shapes + [jax.ShapeDtypeStruct((2 * span, width), BF16)],
        input_output_aliases=aliases,
        compiler_params=pltpu.CompilerParams(vmem_limit_bytes=58 * 1024 * 1024),
        cost_estimate=pl.CostEstimate(
            flops=20 * span * width * units,
            bytes_accessed=6 * width * units + 2 * span * 10 * width,
            transcendentals=2 * span * units,
        ),
        name="feed_forward",
    )(*operands)
    return results[:5], results[5]


BLOCK = 128


def block_pairs(count):
    return [(low, high) for low in range(count) for high in range(low, count)]


def gram_kernel(rows, out):
    count = rows.shape[1] // BLOCK
    place = 0
    for low in range(count):
        line = lax.dot_general(
            rows[:, low * BLOCK : (low + 1) * BLOCK],
            rows[:, low * BLOCK :],
            (((0,), (0,)), ((), ())),
            preferred_element_type=F32,
        ).astype(BF16)
        for high in range(low, count):
            out[place] = line[:, (high - low) * BLOCK : (high - low + 1) * BLOCK]
            place += 1
    for extra in range(place, out.shape[0]):
        out[extra] = jnp.zeros((BLOCK, BLOCK), BF16)


def gram_blocks(rows, places):
    return pl.pallas_call(
        gram_kernel,
        out_shape=jax.ShapeDtypeStruct((places, BLOCK, BLOCK), BF16),
        compiler_params=pltpu.CompilerParams(vmem_limit_bytes=32 * 1024 * 1024),
        name="gram",
    )(rows)


def newton_schulz(gram, low, poly, mixed, rows):
    size = gram.shape[0]
    part = size // 2 if size % 16 == 0 and size > BLOCK else size
    parts = [pl.ds(begin, part) for begin in range(0, size, part)]
    row_id = lax.broadcasted_iota(jnp.int32, (size, size), 0)
    column_id = lax.broadcasted_iota(jnp.int32, (size, size), 1)
    square = jnp.where(row_id == column_id, gram[...], 0.0)
    square = jnp.sum(jnp.sum(square, axis=0, keepdims=True), axis=1, keepdims=True)
    scale = 1.0 / (jnp.sqrt(square) + 1e-07)
    for place in parts:
        scaled = gram[place, :] * (scale * scale)
        gram[place, :] = scaled
        low[place, :] = scaled.astype(BF16)
    work = (rows * scale).astype(BF16)
    for step in range(NS_STEPS):
        for place in parts:
            second = jnp.dot(low[place, :], low[...], preferred_element_type=F32)
            poly[place, :] = (NS_SQUARE * gram[place, :] + NS_CUBIC * second).astype(BF16)
        moved = jnp.dot(work, poly[...], preferred_element_type=F32)
        work = (NS_LINEAR * work.astype(F32) + moved).astype(BF16)
        if step + 1 < NS_STEPS:
            for place in parts:
                first = jnp.dot(poly[place, :], low[...], preferred_element_type=F32)
                mixed[place, :] = first.astype(BF16)
                gram[place, :] = (
                    NS_LINEAR * NS_LINEAR * gram[place, :] + (2.0 * NS_LINEAR) * first
                )
            for place in parts:
                second = jnp.dot(poly[place, :], mixed[...], preferred_element_type=F32)
                renewed = gram[place, :] + second
                gram[place, :] = renewed
                low[place, :] = renewed.astype(BF16)
    return work


def wide_kernel(blocks, rows, out, gram, low, poly, mixed):
    for place, (first, second) in enumerate(block_pairs(gram.shape[0] // BLOCK)):
        tile = blocks[place].astype(F32)
        gram[first * BLOCK : (first + 1) * BLOCK, second * BLOCK : (second + 1) * BLOCK] = tile
        if first != second:
            gram[second * BLOCK : (second + 1) * BLOCK, first * BLOCK : (first + 1) * BLOCK] = tile.T
    out[...] = newton_schulz(gram, low, poly, mixed, rows[...].astype(F32))


def square_scratch(size):
    return [
        pltpu.VMEM((size, size), F32),
        pltpu.VMEM((size, size), BF16),
        pltpu.VMEM((size, size), BF16),
        pltpu.VMEM((size, size), BF16),
    ]


def orthogonal_wide(blocks, rows):
    return pl.pallas_call(
        wide_kernel,
        out_shape=jax.ShapeDtypeStruct(rows.shape, BF16),
        scratch_shapes=square_scratch(rows.shape[1]),
        compiler_params=pltpu.CompilerParams(vmem_limit_bytes=40 * 1024 * 1024),
        cost_estimate=pl.CostEstimate(
            flops=14 * rows.shape[1] ** 3, bytes_accessed=4 * rows.size, transcendentals=0
        ),
        name="newton_wide",
    )(blocks, rows)


def whole_kernel(widths, whole, rows, out, *scratch):
    begin = 0
    for index, width in enumerate(widths):
        gram, low, poly, mixed = scratch[4 * index : 4 * index + 4]
        for first in range(0, width, BLOCK):
            gram[first : first + BLOCK, :] = lax.dot_general(
                whole[:, begin + first : begin + first + BLOCK],
                whole[:, begin : begin + width],
                (((0,), (0,)), ((), ())),
                preferred_element_type=F32,
            )
        out[:, begin : begin + width] = newton_schulz(
            gram, low, poly, mixed, rows[:, begin : begin + width]
        )
        begin += width


def orthogonal_whole(whole, rows, widths):
    scratch = []
    for width in widths:
        scratch += square_scratch(width)
    return pl.pallas_call(
        lambda *refs: whole_kernel(widths, *refs),
        out_shape=jax.ShapeDtypeStruct(rows.shape, BF16),
        scratch_shapes=scratch,
        compiler_params=pltpu.CompilerParams(vmem_limit_bytes=48 * 1024 * 1024),
        cost_estimate=pl.CostEstimate(
            flops=16 * sum(width**3 for width in widths),
            bytes_accessed=2 * whole.size,
            transcendentals=0,
        ),
        name="newton_whole",
    )(whole, rows)


def from_flat(flat, base, target, height, breadth):
    lines = breadth // LANES
    for begin in range(0, height, 8):
        count = min(8, height - begin)
        for index in range(lines):
            start = base + begin * lines + index
            if lines == 1:
                tile = flat[start : start + count, :]
            else:
                tile = flat[pl.ds(start, count, stride=lines), :]
            target[begin : begin + count, index * LANES : (index + 1) * LANES] = tile


def to_flat(flat, base, value, height, breadth):
    lines = breadth // LANES
    for begin in range(0, height, 8):
        count = min(8, height - begin)
        for index in range(lines):
            start = base + begin * lines + index
            tile = value(slice(begin, begin + count), slice(index * LANES, (index + 1) * LANES))
            if lines == 1:
                flat[start : start + count, :] = tile
            else:
                flat[pl.ds(start, count, stride=lines), :] = tile


def section_bases(devices):
    bases = []
    base = 0
    for height, breadth in matrix_shapes():
        bases.append(base)
        base += height // devices * breadth // LANES
    return bases


def pack_kernel(devices, group, flat, extra, qkv_out, out_out, wide_out, down_out, qkv, out, wide, down):
    rows = D // devices
    frows = FF // devices
    bases = section_bases(devices)
    qkv[...] = jnp.zeros(qkv.shape, F32)
    out[...] = jnp.zeros(out.shape, F32)
    from_flat(flat, bases[0], qkv.at[:, :QD], rows, QD)
    from_flat(flat, bases[1], qkv.at[:, QD : QD + KVD], rows, KVD)
    from_flat(flat, bases[2], qkv.at[:, QD + KVD :], rows, KVD)
    if extra is not None:
        qkv[rows : rows + 1, :LANES] = extra[...]
    from_flat(flat, bases[3], out, rows, D)
    from_flat(flat, bases[6], down, FF // devices, D)
    qkv_out[...] = qkv[...].astype(qkv_out.dtype)
    out_out[...] = out[...].astype(out_out.dtype)
    down_out[...] = down[...].astype(down_out.dtype)
    for which in range(2):
        from_flat(flat, bases[4 + which], wide, rows, FF)
        targets = devices // group
        for target in range(targets):
            piece = jnp.concatenate(
                [
                    wide[:, (turn * targets + target) * frows : (turn * targets + target + 1) * frows]
                    for turn in range(group)
                ],
                axis=1,
            )
            if group == 1:
                wide_out[target, :, which * frows : (which + 1) * frows] = piece.astype(wide_out.dtype)
            else:
                wide_out[target, which] = piece.astype(wide_out.dtype)


def pack(flat, extra, devices, group, dtype):
    rows = D // devices
    frows = FF // devices
    padded = (rows // 16 + 1) * 16
    targets = devices // group
    wide = (targets, rows, 2 * frows) if group == 1 else (targets, 2, rows, group * frows)
    shapes = [(padded, QD + 2 * KVD), (padded, D), wide, (frows, D)]
    types = [dtype, dtype, BF16, dtype]
    if extra is None:
        body = lambda flat_ref, *refs: pack_kernel(devices, group, flat_ref, None, *refs)
        operands = [flat]
    else:
        body = lambda *refs: pack_kernel(devices, group, *refs)
        operands = [flat, extra]
    return pl.pallas_call(
        body,
        out_shape=[jax.ShapeDtypeStruct(shape, kind) for shape, kind in zip(shapes, types)],
        scratch_shapes=[
            pltpu.VMEM((padded, QD + 2 * KVD), F32),
            pltpu.VMEM((padded, D), F32),
            pltpu.VMEM((rows, FF), F32),
            pltpu.VMEM((frows, D), F32),
        ],
        compiler_params=pltpu.CompilerParams(vmem_limit_bytes=32 * 1024 * 1024),
        cost_estimate=pl.CostEstimate(flops=0, bytes_accessed=6 * flat.size, transcendentals=0),
        name="pack",
    )(*operands)


def update_kernel(devices, decay, factors, flat, qkv, out, wide, down, result, moved, rows_wide):
    rows = D // devices
    frows = FF // devices
    bases = section_bases(devices)
    whole = qkv[...].astype(F32)
    out_whole = out[...].astype(F32)
    down_whole = down[...].astype(F32)
    parts = [
        lambda r, c: whole[r, c],
        lambda r, c: whole[r, slice(QD + c.start, QD + c.stop)],
        lambda r, c: whole[r, slice(QD + KVD + c.start, QD + KVD + c.stop)],
        lambda r, c: out_whole[r, c],
    ]
    shapes = matrix_shapes()
    for index, part in enumerate(parts):
        to_flat(
            moved, bases[index], lambda r, c: part(r, c) * factors[index], rows, shapes[index][1]
        )
    to_flat(moved, bases[6], lambda r, c: down_whole[r, c] * factors[6], frows, D)
    for which in range(2):
        for source in range(devices):
            rows_wide[:, source * frows : (source + 1) * frows] = wide[
                source, :, which * frows : (which + 1) * frows
            ].astype(F32)
        to_flat(
            moved, bases[4 + which], lambda r, c: rows_wide[r, c] * factors[4 + which], rows, FF
        )
    result[...] = decay * flat[...] + moved[...]


def update(flat, qkv, out, wide, down, devices, decay, factors):
    return pl.pallas_call(
        lambda *refs: update_kernel(devices, decay, factors, *refs),
        out_shape=jax.ShapeDtypeStruct(flat.shape, F32),
        scratch_shapes=[
            pltpu.VMEM(flat.shape, F32),
            pltpu.VMEM((D // devices, FF), F32),
        ],
        compiler_params=pltpu.CompilerParams(vmem_limit_bytes=32 * 1024 * 1024),
        cost_estimate=pl.CostEstimate(flops=0, bytes_accessed=10 * flat.size, transcendentals=0),
        name="update",
    )(flat, qkv, out, wide, down)


def combine_kernel(old_pair, gate, up, old_down, down, old_out, out, mats, lines):
    devices, rows, _ = old_pair.shape
    frows = gate.shape[0]
    padded = out.shape[0]
    lines[...] = jnp.zeros(lines.shape, F32)
    for source in range(devices):
        lines[source * rows : (source + 1) * rows, : 2 * frows] = old_pair[source].astype(F32)
    old = lines[...].T
    mats[0] = (MOMENTUM_DECAY * old[:frows] + gate[...].astype(F32)).astype(BF16)
    mats[1] = (MOMENTUM_DECAY * old[frows : 2 * frows] + up[...].astype(F32)).astype(BF16)
    mats[2] = (MOMENTUM_DECAY * old_down[...] + down[...].astype(F32)).astype(BF16)
    last = MOMENTUM_DECAY * old_out[...] + out[...].astype(F32)
    mats[3] = jnp.concatenate(
        [last, jnp.zeros((frows - padded, last.shape[1]), F32)], axis=0
    ).astype(BF16)


def combine(old_pair, gate, up, old_down, down, old_out, out):
    frows, width = gate.shape
    return pl.pallas_call(
        combine_kernel,
        out_shape=jax.ShapeDtypeStruct((4, frows, width), BF16),
        scratch_shapes=[pltpu.VMEM((width, -(-2 * frows // LANES) * LANES), F32)],
        compiler_params=pltpu.CompilerParams(vmem_limit_bytes=32 * 1024 * 1024),
        name="combine",
    )(old_pair, gate, up, old_down, down, old_out, out)


def turn_kernel(gate, up, out, columns):
    devices, rows, _ = out.shape
    frows = gate.shape[0]
    columns[...] = jnp.zeros(columns.shape, F32)
    columns[:frows] = gate[...].astype(F32)
    columns[frows : 2 * frows] = up[...].astype(F32)
    lines = columns[...].T
    for target in range(devices):
        out[target] = lines[target * rows : (target + 1) * rows, : 2 * frows].astype(BF16)


def turn(gate, up, devices):
    frows, width = gate.shape
    return pl.pallas_call(
        turn_kernel,
        out_shape=jax.ShapeDtypeStruct((devices, width // devices, 2 * frows), BF16),
        scratch_shapes=[pltpu.VMEM((-(-2 * frows // LANES) * LANES, width), F32)],
        compiler_params=pltpu.CompilerParams(vmem_limit_bytes=32 * 1024 * 1024),
        name="turn",
    )(gate, up)


def on_device(
    block_input,
    cotangent,
    lengths,
    doc_starts,
    master,
    momentum,
    vectors,
    vector_first,
    vector_second,
):
    n_dp = lax.axis_size("dp")
    n_ctx = lax.axis_size("ctx")
    devices = n_dp * n_ctx
    rows = D // devices
    frows = FF // devices
    fblock = FF // n_ctx
    slots, span, width = block_input.shape
    tokens = slots * span
    group = HEADS // KVH
    qkv = QD + 2 * KVD
    my_ctx = lax.axis_index("ctx")
    me = lax.axis_index("dp") * n_ctx + my_ctx
    core_bit, x_bit = 1, 2
    ctx_bits = [core_bit, x_bit]
    dp_bits = [n_ctx << index for index in range(n_dp.bit_length() - 1)]
    all_bits = ctx_bits + dp_bits
    many = tuple([2] * len(all_bits))
    padded = (rows // 16 + 1) * 16

    master_flat = master.reshape(-1, LANES)
    momentum_flat = momentum.reshape(-1, LANES)
    small = jnp.pad(vectors, ((0, 0), (0, LANES - vectors.shape[1])))
    qkv_local, out_local, gate_up, down_local = pack(master_flat, small, devices, n_dp, BF16)

    attn_full = gather_bits(
        jnp.concatenate([qkv_local, out_local], axis=1), dp_bits[::-1], me, devices
    )
    down_bits = dp_bits[::-1]
    down_part, _ = lax.optimization_barrier((down_local, attn_full))
    down_part = gather_bits(down_part, down_bits[:1], me, devices)
    qkv_full = gather_bits(attn_full[..., :qkv], [x_bit], me, devices, dp_bits)
    qkv_full, down_part = lax.optimization_barrier((qkv_full, down_part))
    qkv_full = gather_bits(qkv_full, [core_bit], me, devices, dp_bits + [x_bit])
    down_part = gather_bits(down_part, down_bits[1:2], me, devices, down_bits[:1])
    qkv_full = qkv_full.reshape(devices, padded, qkv)
    gain_first, gain_second, bias_query, bias_key, bias_value = [
        piece.astype(F32) for piece in split_small(qkv_full[:, rows], devices)
    ]
    w_qkv = qkv_full[:, :rows].reshape(D, qkv)

    came = [choose(gate_up, my_ctx, 0)] + [
        swap(choose(gate_up, my_ctx ^ mask, 0), mask, devices) for mask in range(1, n_ctx)
    ]
    came, _ = lax.optimization_barrier((came, attn_full))
    ordered = []
    for source in range(n_ctx):
        piece = came[0]
        for mask in range(1, n_ctx):
            piece = jnp.where(my_ctx ^ mask == source, came[mask], piece)
        ordered.append(piece)
    gate_up = jnp.concatenate(ordered, axis=1)
    w_gate, w_up = [lax.all_gather(gate_up[index], "dp", axis=0, tiled=True) for index in range(2)]

    def to_rows(gate, up):
        return lax.all_to_all(
            turn(gate, up, devices), BOTH, split_axis=0, concat_axis=0, tiled=True
        )

    length, second = lengths[0], doc_starts[0]
    places = my_ctx * span + jnp.arange(span, dtype=jnp.int32)
    doc_begin = jnp.where(places >= length, length, jnp.where(places >= second, second, 0))
    position = (places - doc_begin).astype(F32)
    live = (places < length)[:, None]
    info = jnp.stack([my_ctx, length, second]).astype(jnp.int32)
    inverse = ROPE_BASE ** (-2.0 * jnp.arange(HD // 2, dtype=F32) / HD)
    angles = inverse[:, None] * position[None, :]
    cosine, sine_part = jnp.cos(angles), jnp.sin(angles)
    cosine = jnp.concatenate([cosine, cosine], axis=0)[None]
    sine_part = jnp.concatenate([sine_part, sine_part], axis=0)[None]

    def from_ctx(value, other_x=None):
        other_core = swap(value, core_bit, devices)
        if other_x is None:
            other_x = swap(value, x_bit, devices)
        return value, other_core, other_x

    cot_here = jnp.where(live, cotangent.reshape(tokens, width), jnp.zeros((), BF16))

    def pair_of_heads(kv, index):
        begin = index * HD
        return jnp.concatenate(
            [kv[:, begin : begin + HD], kv[:, KVD + begin : KVD + begin + HD]], axis=1
        )

    inputs = block_input.astype(F32).reshape(tokens, width)
    scale_one = lax.rsqrt(jnp.mean(inputs * inputs, axis=-1, keepdims=True) + NORM_EPS)
    normed_one = (inputs * scale_one * gain_first).astype(BF16)
    bias = jnp.concatenate([bias_query, bias_key, bias_value])
    pre = mm(w_qkv, normed_one, ((0,), (1,))) + bias[:, None]
    turned = rotate(
        pre[: QD + KVD].reshape(HEADS + KVH, HD, tokens), cosine, sine_part
    )
    queries = (turned[:HEADS].astype(BF16).astype(F32) * HD ** (-0.5)).astype(BF16)
    kv_here = jnp.concatenate(
        [turned[HEADS:].astype(BF16).reshape(KVD, tokens), pre[QD + KVD :].astype(BF16)], axis=0
    )
    kv = from_ctx(kv_here)
    kv = jnp.stack(kv + (swap(kv[2], core_bit, devices),))
    kv, down_part = lax.optimization_barrier((kv, down_part))
    down_part = gather_bits(down_part, down_bits[2:], me, devices, down_bits[:2])
    back_one = jnp.pad(
        normed_one.T.reshape(devices, rows, tokens), ((0, 0), (0, padded - rows), (0, 0))
    ).reshape(devices * padded, tokens)
    back_one, kv = lax.optimization_barrier((back_one, kv))
    out_full, _ = lax.optimization_barrier((attn_full[..., qkv:], kv))
    halves = []
    for index in range(KVH):
        if index == 1:
            out_full, cot_here, _ = lax.optimization_barrier((out_full, cot_here, halves))
            cot_far = swap(cot_here, x_bit, devices)
        out_full = gather_bits(
            out_full, ctx_bits[::-1][index : index + 1], me, devices, dp_bits + ctx_bits[::-1][:index]
        )
        kv_one = pair_of_heads(kv, index)
        halves.append(attend(info, kv_one, queries[index * group : (index + 1) * group]))
    halves, cot_far, down_part = lax.optimization_barrier((halves, cot_far, down_part))
    attended = jnp.concatenate([half[0] for half in halves], axis=0)
    log_total = jnp.concatenate([half[1] for half in halves], axis=0)
    out_pieces = out_full.reshape(devices * padded, D)
    w_down = down_part.reshape(fblock, D)

    mixed_pieces = jnp.pad(
        attended.reshape(devices, rows, tokens).astype(BF16), ((0, 0), (0, padded - rows), (0, 0))
    ).reshape(devices * padded, tokens)
    hidden = inputs + mm(mixed_pieces, out_pieces, ((0,), (0,)))
    scale_two = lax.rsqrt(jnp.mean(hidden * hidden, axis=-1, keepdims=True) + NORM_EPS)
    normed_two = (hidden * scale_two * gain_second).astype(BF16)

    normed = from_ctx(normed_two)
    out_pieces, _ = lax.optimization_barrier((out_pieces, normed_two))
    w_out = out_pieces.reshape(devices, padded, D)[:, :rows].reshape(QD, D)
    cot = from_ctx(cot_here, cot_far)
    kept, near_part = feed_forward(normed[:2], cot[:2], w_gate, w_up, w_down, n_ctx, None)
    (far_x, far_dy), kept = lax.optimization_barrier(((normed[2], cot[2]), kept))
    kept, far_part = feed_forward(
        (far_x, swap(far_x, core_bit, devices)),
        (far_dy, swap(far_dy, core_bit, devices)),
        w_gate,
        w_up,
        w_down,
        n_ctx,
        kept,
    )
    acts, gate_backs, up_backs, normed_all, cot_all = kept
    back_parts = (near_part, far_part)

    def to_ctx(halves):
        crossed = swap(halves[1][span:], core_bit, devices)
        far = (halves[1][:span].astype(F32) + crossed.astype(F32)).astype(BF16)
        near = swap(halves[0][span:], core_bit, devices)
        near = halves[0][:span].astype(F32) + near.astype(F32)
        return near + swap(far, x_bit, devices).astype(F32), far

    normed_two_grad, ready = to_ctx(back_parts)
    (acts, gate_backs, up_backs), ready = lax.optimization_barrier(
        ((acts, gate_backs, up_backs), ready)
    )

    dp_shape = tuple([2] * len(dp_bits)) + (frows, D)
    dp_order = dp_bits[1:] + dp_bits[:1]
    down_value = mm(acts, cot_all, ((0,), (0,))).astype(BF16)
    gate_value = mm(gate_backs, normed_all, ((0,), (0,))).astype(BF16)
    up_value = mm(up_backs, normed_all, ((0,), (0,))).astype(BF16)
    down_parts, gate_parts, up_parts = [
        scatter_start(value.reshape(dp_shape), dp_bits, bit, me, devices)
        for value, bit in (
            (down_value, dp_order[0]),
            (gate_value, dp_bits[0]),
            (up_value, dp_bits[0]),
        )
    ]
    momentum_flat, acts, _ = lax.optimization_barrier((momentum_flat, acts, (down_value, gate_value, up_value)))
    old_qkv, old_out, old_pair, old_down = pack(momentum_flat, None, devices, 1, F32)
    old_pair = lax.all_to_all(old_pair, BOTH, split_axis=0, concat_axis=0, tiled=True)

    out_grad = cot_here.astype(F32)
    hidden_norm_grad, grad_gain_second = norm_backward(
        hidden, scale_two, gain_second, normed_two_grad
    )
    hidden_grad = out_grad + hidden_norm_grad
    hidden_low = hidden_grad.astype(BF16)
    heads_grad = mm(w_out, hidden_low, ((1,), (1,))).astype(BF16).reshape(HEADS, HD, tokens)
    delta = jnp.sum(heads_grad.astype(F32) * attended, axis=1, keepdims=True)
    grad_output = mm(mixed_pieces, hidden_low)
    query_grads, kv_parts = [], []
    sent, kept = scatter_split(
        grad_output.astype(BF16).reshape(many + (padded, D)), all_bits, all_bits[0], me
    )
    wide_parts = [gate_parts, up_parts, down_parts, (kept, swap(sent, all_bits[0], devices))]
    wide_orders = [list(dp_bits), list(dp_bits), list(dp_order), list(all_bits)]
    steps = [[2, 3], [0, 1, 3], [2, 0, 3], [1, 3]]
    shares = [4, 3]
    ready = [sent]
    for index in range(KVH):
        kv_one = pair_of_heads(kv, index)
        kv_grad = None
        begin = index * group
        for count in shares:
            chosen = slice(begin, begin + count)
            begin += count
            query_part, ready = lax.optimization_barrier((queries[chosen], ready))
            query_grad, kv_grad = attend_back(
                info, kv_one, query_part, heads_grad[chosen], log_total[chosen], delta[chosen], kv_grad
            )
            query_grads.append(query_grad)
            ready = []
            for which in steps.pop(0):
                order = wide_orders[which]
                parts, _ = lax.optimization_barrier((wide_parts[which], query_grad))
                order.pop(0)
                sent, kept = scatter_split(scatter_end(parts), order, order[0], me)
                ready.append(sent)
                wide_parts[which] = (kept, swap(sent, order[0], devices))
        kv_parts.append(
            scatter_sum(kv_grad.reshape(2, 2, 2 * HD, span), ctx_bits, me, devices)
        )
    kv_grads = [part.astype(F32).reshape(2, HD, span) for part in kv_parts]
    qk_grad = jnp.concatenate(query_grads + [grad[:1] for grad in kv_grads], axis=0)
    qk_back = rotate_back(qk_grad, cosine, sine_part).reshape(QD + KVD, tokens)
    qkv_back = jnp.concatenate(
        [qk_back] + [grad[1] for grad in kv_grads], axis=0
    ).astype(BF16)
    grad_qkv = mm(back_one, qkv_back, ((1,), (1,)))
    grad_bias = jnp.sum(qkv_back.astype(F32), axis=1)
    normed_one_grad = mm(qkv_back, w_qkv, ((0,), (1,)))
    input_norm_grad, grad_gain_first = norm_backward(inputs, scale_one, gain_first, normed_one_grad)
    input_grad = (hidden_grad + input_norm_grad).astype(BF16).reshape(slots, span, width)

    vector_part = join_small(
        [
            grad_gain_first,
            grad_gain_second,
            grad_bias[:QD],
            grad_bias[QD : QD + KVD],
            grad_bias[QD + KVD :],
        ],
        devices,
    )
    vector_grad = jnp.sum(
        lax.all_to_all(vector_part, BOTH, split_axis=0, concat_axis=0, tiled=True),
        axis=0,
        keepdims=True,
    )
    sent, kept = scatter_split(
        grad_qkv.astype(BF16).reshape(many + (padded, qkv)), all_bits, all_bits[0], me
    )
    wide_parts, sent = lax.optimization_barrier((wide_parts, sent))
    qkv_parts = (kept, swap(sent, all_bits[0], devices))
    acts, _ = lax.optimization_barrier((acts, sent))
    out_part = mm(acts, w_down).astype(BF16)
    out_sum, _ = to_ctx([out_part[: 2 * span], out_part[2 * span :]])
    layer_out = jnp.where(live, hidden + out_sum, 0.0)
    gate_sum, up_sum, down_sum, out_sum_rows = [
        scatter_sum(scatter_end(parts), order[1:], me, devices)
        for parts, order in zip(wide_parts, wide_orders)
    ]
    qkv_sum_rows = scatter_sum(scatter_end(qkv_parts), all_bits[1:], me, devices)
    moved_qkv = MOMENTUM_DECAY * old_qkv + qkv_sum_rows.astype(F32)
    mats = combine(old_pair, gate_sum, up_sum, old_down, down_sum, old_out, out_sum_rows)
    owned = to_owner(mats.reshape(2, 2, frows, D), core_bit, x_bit, me, devices)
    owned = owned.reshape(n_ctx * frows, D)
    count = len(block_pairs(D // BLOCK))
    places = (count + n_dp - 1) // n_dp * n_dp
    dp_many = tuple([2] * len(dp_bits))
    gram = gram_blocks(owned, places).reshape(dp_many + (places // n_dp, BLOCK, BLOCK))
    gram = scatter_sum(gram, dp_bits, me, devices)
    gram = gather_bits(gram, dp_bits[::-1], me, devices).reshape(places, BLOCK, BLOCK)
    moved_low = moved_qkv.astype(BF16)
    layer_out, moved_low, gram = lax.optimization_barrier((layer_out, moved_low, gram))
    (gate_sum, up_sum), _ = lax.optimization_barrier(((gate_sum, up_sum), gram))
    new_momentum = update(
        momentum_flat,
        qkv_sum_rows,
        out_sum_rows,
        to_rows(gate_sum, up_sum),
        down_sum,
        devices,
        MOMENTUM_DECAY,
        [1.0] * 7,
    ).reshape(momentum.shape)
    ortho = orthogonal_wide(gram, owned).reshape(2, 2, frows, D)
    ortho = from_owner(ortho, core_bit, x_bit, me, devices).reshape(n_ctx, frows, D)
    ortho_pair = to_rows(ortho[0], ortho[1])

    qkv_all = lax.all_gather(moved_low, BOTH, axis=0, tiled=True)
    ortho_qkv = orthogonal_whole(qkv_all, moved_qkv, (QD, KVD, KVD))
    factors = [
        -MUON_RATE * math.sqrt(max(1.0, breadth / height)) for height, breadth in matrix_shapes()
    ]
    new_master = update(
        master_flat,
        ortho_qkv,
        ortho[3, :padded],
        ortho_pair,
        ortho[2],
        devices,
        1.0 - MUON_RATE * MUON_DECAY,
        factors,
    ).reshape(master.shape)
    first_new = BETA_FIRST * vector_first + (1.0 - BETA_FIRST) * vector_grad
    second_new = BETA_SECOND * vector_second + (1.0 - BETA_SECOND) * vector_grad * vector_grad
    adjusted = (
        first_new
        / (1.0 - BETA_FIRST**STEP)
        / (jnp.sqrt(second_new / (1.0 - BETA_SECOND**STEP)) + ADAM_EPS)
    )
    new_vectors = vectors - ADAM_RATE * adjusted
    return (
        layer_out.astype(BF16).reshape(slots, span, width),
        input_grad,
        new_master,
        new_momentum,
        new_master.astype(BF16),
        new_vectors,
        first_new,
        second_new,
    )


def solution(mesh):
    return jax.shard_map(
        on_device,
        mesh=mesh,
        in_specs=(
            P("dp", "ctx", None),
            P("dp", "ctx", None),
            P("dp"),
            P("dp"),
            P(BOTH, None),
            P(BOTH, None),
            P(BOTH, None),
            P(BOTH, None),
            P(BOTH, None),
        ),
        out_specs=(
            P("dp", "ctx", None),
            P("dp", "ctx", None),
            P(BOTH, None),
            P(BOTH, None),
            P(BOTH, None),
            P(BOTH, None),
            P(BOTH, None),
            P(BOTH, None),
        ),
        check_vma=False,
    )
```

```python
import math

import jax
import jax.numpy as jnp
from jax import lax
from jax.experimental import pallas as pl
from jax.experimental.pallas import tpu as pltpu
from jax.sharding import PartitionSpec as P

D = 896
HEADS = 14
KVH = 2
HD = 64
FF = 4864
SLOT = 2048
NS_STEPS = 3
STEP = 10
QD = 896
KVD = 128

NORM_EPS = 1e-06
ROPE_BASE = 1000000.0
NS_LINEAR = 3.4445
NS_SQUARE = -4.775
NS_CUBIC = 2.0315
MOMENTUM_DECAY = 0.5
MUON_RATE = 0.6
MUON_DECAY = 0.1
ADAM_RATE = 0.2
BETA_FIRST = 0.9
BETA_SECOND = 0.95
ADAM_EPS = 1e-08
MASK_FLOOR = -1e30

F32 = jnp.float32
BF16 = jnp.bfloat16
BOTH = ("dp", "ctx")
LANES = 128


def matrix_shapes():
    return [(D, QD), (D, KVD), (D, KVD), (QD, D), (D, FF), (D, FF), (FF, D)]


def vector_sizes():
    return [D, D, QD, KVD, KVD]


def mm(left, right, contract=((1,), (0,))):
    return lax.dot_general(left, right, (contract, ((), ())), preferred_element_type=F32)


def split_small(flat, devices):
    result = []
    offset = 0
    for extent_all in vector_sizes():
        extent = extent_all // devices
        result.append(flat[:, offset : offset + extent].reshape(extent_all))
        offset += extent
    return result


def join_small(pieces, devices):
    return jnp.concatenate([piece.reshape(devices, -1) for piece in pieces], axis=1)


def swap(value, mask, devices):
    return lax.ppermute(value, BOTH, [(index, index ^ mask) for index in range(devices)])


def gather_bits(value, bits, me, devices, before=()):
    held = value
    done = list(before)
    for bit in bits:
        place = sum(1 for other in done if other > bit)
        got = swap(held, bit, devices)
        mine = (me & bit) != 0
        held = jnp.where(
            mine, jnp.stack([got, held], axis=place), jnp.stack([held, got], axis=place)
        )
        done.append(bit)
    return held


def scatter_split(held, left, bit, me, lead=0):
    axis = sorted(left, reverse=True).index(bit) + lead
    mine = jnp.where((me & bit) != 0, 1, 0)
    return choose(held, 1 - mine, axis).astype(BF16), choose(held, mine, axis)


def scatter_start(held, left, bit, me, devices):
    sent, kept = scatter_split(held, left, bit, me)
    return kept, swap(sent, bit, devices)


def scatter_end(parts):
    return (parts[0].astype(F32) + parts[1].astype(F32)).astype(BF16)


def scatter_rest(held, bits, me, devices, lead):
    left = list(bits)
    for bit in bits:
        sent, kept = scatter_split(held, left, bit, me, lead)
        held = scatter_end((kept, swap(sent, bit, devices)))
        left.remove(bit)
    return held


def scatter_sum(value, bits, me, devices):
    left = list(bits)
    held = value
    for bit in bits:
        held = scatter_end(scatter_start(held, left, bit, me, devices))
        left.remove(bit)
    return held


def choose(value, mine, axis):
    return lax.dynamic_index_in_dim(value, mine, axis, keepdims=False)


def to_owner(value, core_bit, x_bit, me, devices):
    core = jnp.where((me & core_bit) != 0, 1, 0)
    across = jnp.where((me & x_bit) != 0, 1, 0)
    got = swap(choose(value, 1 - core, 1), core_bit, devices)
    value = jnp.stack([choose(value, core, 1), got], axis=1)
    got = swap(choose(value, 1 - across, 0), x_bit, devices)
    return jnp.stack([choose(value, across, 0), got])


def from_owner(value, core_bit, x_bit, me, devices):
    got = swap(value[1], x_bit, devices)
    value = jnp.where(
        (me & x_bit) != 0, jnp.stack([got, value[0]]), jnp.stack([value[0], got])
    )
    got = swap(value[:, 1], core_bit, devices)
    return jnp.where(
        (me & core_bit) != 0,
        jnp.stack([got, value[:, 0]], axis=1),
        jnp.stack([value[:, 0], got], axis=1),
    )


def rotate(values, cosine, sine_part):
    midpoint = HD // 2
    turned = jnp.concatenate([-values[:, midpoint:], values[:, :midpoint]], axis=1)
    return values * cosine + turned * sine_part


def rotate_back(gradient, cosine, sine_part):
    midpoint = HD // 2
    scaled = gradient * sine_part
    turned = jnp.concatenate([scaled[:, midpoint:], -scaled[:, :midpoint]], axis=1)
    return gradient * cosine + turned


def norm_backward(source, scale_row, gain, incoming):
    gain_grad = jnp.sum(incoming * source * scale_row, axis=0)
    weighted = incoming * gain
    result = scale_row * weighted - source * scale_row**3 * jnp.mean(
        weighted * source, axis=-1, keepdims=True
    )
    return (result, gain_grad)


def halves_of(span):
    return [slice(0, span // 2), slice(span // 2, span)]


def fill_mask(info, mask, chunk, span):
    key = chunk * span + lax.broadcasted_iota(jnp.int32, (span, span), 0)
    query = info[0] * span + lax.broadcasted_iota(jnp.int32, (span, span), 1)
    key_doc = (key >= info[2]).astype(jnp.int32) + (key >= info[1]).astype(jnp.int32)
    query_doc = (query >= info[2]).astype(jnp.int32) + (query >= info[1]).astype(jnp.int32)
    allowed = jnp.logical_and(key_doc == query_doc, key <= query)
    mask[chunk] = jnp.where(allowed, 0.0, MASK_FLOOR).astype(F32)


def attend_kernel(info, kv, q, out, lse, keys, mask, best, total, acc):
    head = pl.program_id(0)
    span = q.shape[-1]
    mine = info[0]
    chunks = mine + 1

    @pl.when(head == 0)
    def _():
        def fill(chunk, carry):
            slot = jnp.bitwise_xor(chunk, mine)
            keys[chunk] = kv[slot, :HD, :].astype(F32).T.astype(BF16)
            fill_mask(info, mask, chunk, span)
            return carry

        lax.fori_loop(0, chunks, fill, 0)

    best[...] = jnp.full(best.shape, MASK_FLOOR, F32)
    total[...] = jnp.zeros(total.shape, F32)
    acc[...] = jnp.zeros(acc.shape, F32)
    queries = q[0]

    def step(index, carry):
        chunk = mine - index
        slot = jnp.bitwise_xor(chunk, mine)
        scores = jnp.dot(keys[chunk], queries, preferred_element_type=F32) + mask[chunk]
        old = best[...]
        new = jnp.maximum(old, jnp.max(scores, axis=0, keepdims=True))
        present = jnp.exp(scores - new)
        shrink = jnp.exp(old - new)
        best[...] = new
        total[...] = total[...] * shrink + jnp.sum(present, axis=0, keepdims=True)
        acc[...] = acc[...] * shrink + jnp.dot(
            kv[slot, HD:, :], present.astype(BF16), preferred_element_type=F32
        )
        return carry

    lax.fori_loop(0, chunks, step, 0)
    out[0] = acc[...] / total[...]
    lse[0] = best[...] + jnp.log(total[...])


def attend_back_kernel(
    info, kv, q, dout, lse, delta, before, dq, dkv, keys, values, mask, dk, dv, acc
):
    head = pl.program_id(0)
    span = q.shape[-1]
    mine = info[0]
    chunks = mine + 1
    n_ctx = kv.shape[0]

    @pl.when(head == 0)
    def _():
        dk[...] = jnp.zeros(dk.shape, F32)
        dv[...] = jnp.zeros(dv.shape, F32)

        def fill(chunk, carry):
            slot = jnp.bitwise_xor(chunk, mine)
            keys[chunk] = kv[slot, :HD, :].astype(F32).T.astype(BF16)
            values[chunk] = kv[slot, HD:, :].astype(F32).T.astype(BF16)
            fill_mask(info, mask, chunk, span)
            return carry

        lax.fori_loop(0, chunks, fill, 0)

    acc[...] = jnp.zeros(acc.shape, F32)
    queries = q[0]
    douts = dout[0]
    query_rows = queries.astype(F32).T.astype(BF16)
    dout_rows = douts.astype(F32).T.astype(BF16)

    def step(chunk, carry):
        slot = jnp.bitwise_xor(chunk, mine)
        value_sum, key_sum = dv[chunk], dk[chunk]
        for lanes in halves_of(span):
            scores = (
                jnp.dot(keys[chunk], queries[:, lanes], preferred_element_type=F32)
                + mask[chunk, :, lanes]
            )
            shares = jnp.exp(scores - lse[0, :, lanes])
            share_grad = jnp.dot(values[chunk], douts[:, lanes], preferred_element_type=F32)
            score_grad = (shares * (share_grad - delta[0, :, lanes])).astype(BF16)
            value_sum += jnp.dot(
                shares.astype(BF16), dout_rows[lanes, :], preferred_element_type=F32
            )
            key_sum += jnp.dot(score_grad, query_rows[lanes, :], preferred_element_type=F32)
            acc[:, lanes] += jnp.dot(kv[slot, :HD, :], score_grad, preferred_element_type=F32)
        dv[chunk], dk[chunk] = value_sum, key_sum
        return carry

    lax.fori_loop(0, chunks, step, 0)
    dq[0] = acc[...] * HD ** (-0.5)

    @pl.when(head == pl.num_programs(0) - 1)
    def _():
        for chunk in range(n_ctx):
            sums = jnp.concatenate([dk[chunk].T, dv[chunk].T], axis=0)
            if before is not None:
                sums += before[chunk].astype(F32)
            dkv[chunk] = sums.astype(BF16)


def attend(info, kv, q):
    heads, _, span = q.shape
    n_ctx = kv.shape[0]
    per_head = lambda rows: pl.BlockSpec((1, rows, span), lambda head: (head, 0, 0))
    return pl.pallas_call(
        attend_kernel,
        grid=(heads,),
        in_specs=[
            pl.BlockSpec(memory_space=pltpu.SMEM),
            pl.BlockSpec(kv.shape, lambda head: (0, 0, 0)),
            per_head(HD),
        ],
        out_specs=[per_head(HD), per_head(1)],
        out_shape=[
            jax.ShapeDtypeStruct((heads, HD, span), F32),
            jax.ShapeDtypeStruct((heads, 1, span), F32),
        ],
        scratch_shapes=[
            pltpu.VMEM((n_ctx, span, HD), BF16),
            pltpu.VMEM((n_ctx, span, span), F32),
            pltpu.VMEM((1, span), F32),
            pltpu.VMEM((1, span), F32),
            pltpu.VMEM((HD, span), F32),
        ],
        compiler_params=pltpu.CompilerParams(vmem_limit_bytes=40 * 1024 * 1024),
        cost_estimate=pl.CostEstimate(
            flops=4 * heads * span * span * n_ctx * HD * 4,
            bytes_accessed=4 * heads * span * HD * 2,
            transcendentals=heads * span * span * n_ctx,
        ),
        name="attend",
    )(info, kv, q)


def attend_back(info, kv, q, dout, lse, delta, before):
    heads, _, span = q.shape
    n_ctx = kv.shape[0]
    per_head = lambda rows: pl.BlockSpec((1, rows, span), lambda head: (head, 0, 0))
    whole = pl.BlockSpec(kv.shape, lambda head: (0, 0, 0))
    if before is None:
        body = lambda *refs: attend_back_kernel(*refs[:6], None, *refs[6:])
    else:
        body = attend_back_kernel
    return pl.pallas_call(
        body,
        grid=(heads,),
        in_specs=[
            pl.BlockSpec(memory_space=pltpu.SMEM),
            whole,
            per_head(HD),
            per_head(HD),
            per_head(1),
            per_head(1),
        ]
        + [whole] * (before is not None),
        out_specs=[per_head(HD), whole],
        out_shape=[
            jax.ShapeDtypeStruct((heads, HD, span), F32),
            jax.ShapeDtypeStruct(kv.shape, BF16),
        ],
        scratch_shapes=[
            pltpu.VMEM((n_ctx, span, HD), BF16),
            pltpu.VMEM((n_ctx, span, HD), BF16),
            pltpu.VMEM((n_ctx, span, span), F32),
            pltpu.VMEM((n_ctx, span, HD), F32),
            pltpu.VMEM((n_ctx, span, HD), F32),
            pltpu.VMEM((HD, span), F32),
        ],
        compiler_params=pltpu.CompilerParams(vmem_limit_bytes=40 * 1024 * 1024),
        cost_estimate=pl.CostEstimate(
            flops=10 * heads * span * span * n_ctx * HD * 4,
            bytes_accessed=8 * heads * span * HD * 2,
            transcendentals=heads * span * span * n_ctx,
        ),
        name="attend_back",
    )(*[info, kv, q, dout, lse, delta] + [before] * (before is not None))


def forward_backward_kernel(
    x0, x1, dy0, dy1, wide, down, act_out, both_out, x_out, dy_out, back0, back1
):
    first = pl.program_id(0) == 0
    units = down.shape[0]
    x = jnp.where(first, x0[...], x1[...])
    dy = jnp.where(first, dy0[...], dy1[...])
    x_out[...] = x
    dy_out[...] = dy
    both = jnp.dot(x, wide[...], preferred_element_type=F32)
    gate_pre = both[:, :units]
    up_pre = both[:, units:]
    grad_act = mm(dy, down[...], ((1,), (1,)))
    sigmoid_gate = jax.nn.sigmoid(gate_pre)
    swish = gate_pre * sigmoid_gate
    slope = sigmoid_gate * (1.0 + gate_pre * (1.0 - sigmoid_gate))
    act_out[...] = (swish * up_pre).astype(BF16)
    both_back = jnp.concatenate([grad_act * up_pre * slope, grad_act * swish], axis=1).astype(BF16)
    both_out[...] = both_back
    back = mm(both_back, wide[...], ((1,), (1,))).astype(BF16)

    @pl.when(first)
    def _():
        back0[...] = back

    @pl.when(jnp.logical_not(first))
    def _():
        back1[...] = back


def feed_forward(x, dy, wide, down, blocks, earlier):
    span, width = x[0].shape
    units = down.shape[0]
    first = 0 if earlier is None else 2
    whole = lambda shape: pl.BlockSpec(
        shape, lambda block: (0, 0), pipeline_mode=pl.Buffered(1)
    )
    line = lambda columns: pl.BlockSpec((span, columns), lambda block: (block + first, 0))
    columns = [units, 2 * units, width, width]
    shapes = [jax.ShapeDtypeStruct((blocks * span, count), BF16) for count in columns]
    in_specs = [whole((span, width))] * 4 + [whole((width, 2 * units)), whole((units, width))]
    operands = [*x, *dy, wide, down]
    aliases = {}
    body = forward_backward_kernel
    if earlier is not None:
        in_specs += [pl.BlockSpec(memory_space=pl.ANY)] * 4
        operands += list(earlier)
        aliases = {6 + index: index for index in range(4)}
        body = lambda *refs: forward_backward_kernel(*refs[:6], *refs[10:])
    back = pl.BlockSpec((span, width), lambda block: (0, 0))
    results = pl.pallas_call(
        body,
        grid=(2,),
        in_specs=in_specs,
        out_specs=[line(count) for count in columns] + [back, back],
        out_shape=shapes + [jax.ShapeDtypeStruct((span, width), BF16)] * 2,
        input_output_aliases=aliases,
        compiler_params=pltpu.CompilerParams(vmem_limit_bytes=60 * 1024 * 1024),
        cost_estimate=pl.CostEstimate(
            flops=20 * span * width * units,
            bytes_accessed=6 * width * units + 2 * span * 10 * width,
            transcendentals=2 * span * units,
        ),
        name="feed_forward",
    )(*operands)
    return results[:4], results[4:]


BLOCK = 128


def block_pairs(count):
    return [(low, high) for low in range(count) for high in range(low, count)]


def gram_kernel(rows, out):
    count = rows.shape[1] // BLOCK
    place = 0
    for low in range(count):
        line = lax.dot_general(
            rows[:, low * BLOCK : (low + 1) * BLOCK],
            rows[:, low * BLOCK :],
            (((0,), (0,)), ((), ())),
            preferred_element_type=F32,
        ).astype(BF16)
        for high in range(low, count):
            out[place] = line[:, (high - low) * BLOCK : (high - low + 1) * BLOCK]
            place += 1
    for extra in range(place, out.shape[0]):
        out[extra] = jnp.zeros((BLOCK, BLOCK), BF16)


def gram_blocks(rows, places):
    return pl.pallas_call(
        gram_kernel,
        out_shape=jax.ShapeDtypeStruct((places, BLOCK, BLOCK), BF16),
        compiler_params=pltpu.CompilerParams(vmem_limit_bytes=32 * 1024 * 1024),
        name="gram",
    )(rows)


def newton_schulz(gram, low, poly, mixed, rows):
    size = gram.shape[0]
    part = size // 2 if size % 16 == 0 and size > BLOCK else size
    parts = [pl.ds(begin, part) for begin in range(0, size, part)]
    row_id = lax.broadcasted_iota(jnp.int32, (size, size), 0)
    column_id = lax.broadcasted_iota(jnp.int32, (size, size), 1)
    square = jnp.where(row_id == column_id, gram[...], 0.0)
    square = jnp.sum(jnp.sum(square, axis=0, keepdims=True), axis=1, keepdims=True)
    scale = 1.0 / (jnp.sqrt(square) + 1e-07)
    for place in parts:
        scaled = gram[place, :] * (scale * scale)
        gram[place, :] = scaled
        low[place, :] = scaled.astype(BF16)
    work = (rows * scale).astype(BF16)
    for step in range(NS_STEPS):
        for place in parts:
            second = jnp.dot(low[place, :], low[...], preferred_element_type=F32)
            poly[place, :] = (NS_SQUARE * gram[place, :] + NS_CUBIC * second).astype(BF16)
        moved = jnp.dot(work, poly[...], preferred_element_type=F32)
        work = (NS_LINEAR * work.astype(F32) + moved).astype(BF16)
        if step + 1 < NS_STEPS:
            for place in parts:
                first = jnp.dot(poly[place, :], low[...], preferred_element_type=F32)
                mixed[place, :] = first.astype(BF16)
                gram[place, :] = (
                    NS_LINEAR * NS_LINEAR * gram[place, :] + (2.0 * NS_LINEAR) * first
                )
            for place in parts:
                second = jnp.dot(poly[place, :], mixed[...], preferred_element_type=F32)
                renewed = gram[place, :] + second
                gram[place, :] = renewed
                low[place, :] = renewed.astype(BF16)
    return work


def wide_kernel(blocks, rows, out, gram, low, poly, mixed):
    for place, (first, second) in enumerate(block_pairs(gram.shape[0] // BLOCK)):
        tile = blocks[place].astype(F32)
        gram[first * BLOCK : (first + 1) * BLOCK, second * BLOCK : (second + 1) * BLOCK] = tile
        if first != second:
            gram[second * BLOCK : (second + 1) * BLOCK, first * BLOCK : (first + 1) * BLOCK] = tile.T
    out[...] = newton_schulz(gram, low, poly, mixed, rows[...].astype(F32))


def square_scratch(size):
    return [
        pltpu.VMEM((size, size), F32),
        pltpu.VMEM((size, size), BF16),
        pltpu.VMEM((size, size), BF16),
        pltpu.VMEM((size, size), BF16),
    ]


def orthogonal_wide(blocks, rows):
    return pl.pallas_call(
        wide_kernel,
        out_shape=jax.ShapeDtypeStruct(rows.shape, BF16),
        scratch_shapes=square_scratch(rows.shape[1]),
        compiler_params=pltpu.CompilerParams(vmem_limit_bytes=40 * 1024 * 1024),
        cost_estimate=pl.CostEstimate(
            flops=14 * rows.shape[1] ** 3, bytes_accessed=4 * rows.size, transcendentals=0
        ),
        name="newton_wide",
    )(blocks, rows)


def whole_kernel(widths, whole, rows, out, *scratch):
    begin = 0
    for index, width in enumerate(widths):
        gram, low, poly, mixed = scratch[4 * index : 4 * index + 4]
        for first in range(0, width, BLOCK):
            gram[first : first + BLOCK, :] = lax.dot_general(
                whole[:, begin + first : begin + first + BLOCK],
                whole[:, begin : begin + width],
                (((0,), (0,)), ((), ())),
                preferred_element_type=F32,
            )
        out[:, begin : begin + width] = newton_schulz(
            gram, low, poly, mixed, rows[:, begin : begin + width]
        )
        begin += width


def orthogonal_whole(whole, rows, widths):
    scratch = []
    for width in widths:
        scratch += square_scratch(width)
    return pl.pallas_call(
        lambda *refs: whole_kernel(widths, *refs),
        out_shape=jax.ShapeDtypeStruct(rows.shape, BF16),
        scratch_shapes=scratch,
        compiler_params=pltpu.CompilerParams(vmem_limit_bytes=48 * 1024 * 1024),
        cost_estimate=pl.CostEstimate(
            flops=16 * sum(width**3 for width in widths),
            bytes_accessed=2 * whole.size,
            transcendentals=0,
        ),
        name="newton_whole",
    )(whole, rows)


def from_flat(flat, base, target, height, breadth):
    lines = breadth // LANES
    for begin in range(0, height, 8):
        count = min(8, height - begin)
        for index in range(lines):
            start = base + begin * lines + index
            if lines == 1:
                tile = flat[start : start + count, :]
            else:
                tile = flat[pl.ds(start, count, stride=lines), :]
            target[begin : begin + count, index * LANES : (index + 1) * LANES] = tile


def to_flat(flat, base, value, height, breadth):
    lines = breadth // LANES
    for begin in range(0, height, 8):
        count = min(8, height - begin)
        for index in range(lines):
            start = base + begin * lines + index
            tile = value(slice(begin, begin + count), slice(index * LANES, (index + 1) * LANES))
            if lines == 1:
                flat[start : start + count, :] = tile
            else:
                flat[pl.ds(start, count, stride=lines), :] = tile


def section_bases(devices):
    bases = []
    base = 0
    for height, breadth in matrix_shapes():
        bases.append(base)
        base += height // devices * breadth // LANES
    return bases


def pack_kernel(devices, group, flat, extra, qkv_out, out_out, wide_out, down_out, qkv, out, wide, down):
    rows = D // devices
    frows = FF // devices
    bases = section_bases(devices)
    qkv[...] = jnp.zeros(qkv.shape, F32)
    out[...] = jnp.zeros(out.shape, F32)
    from_flat(flat, bases[0], qkv.at[:, :QD], rows, QD)
    from_flat(flat, bases[1], qkv.at[:, QD : QD + KVD], rows, KVD)
    from_flat(flat, bases[2], qkv.at[:, QD + KVD :], rows, KVD)
    if extra is not None:
        qkv[rows : rows + 1, :LANES] = extra[...]
    from_flat(flat, bases[3], out, rows, D)
    from_flat(flat, bases[6], down, FF // devices, D)
    qkv_out[...] = qkv[...].astype(qkv_out.dtype)
    out_out[...] = out[...].astype(out_out.dtype)
    down_out[...] = down[...].astype(down_out.dtype)
    for which in range(2):
        from_flat(flat, bases[4 + which], wide, rows, FF)
        targets = devices // group
        for target in range(targets):
            piece = jnp.concatenate(
                [
                    wide[:, (turn * targets + target) * frows : (turn * targets + target + 1) * frows]
                    for turn in range(group)
                ],
                axis=1,
            )
            width = group * frows
            wide_out[target, :, which * width : (which + 1) * width] = piece.astype(wide_out.dtype)


def pack(flat, extra, devices, group, dtype):
    rows = D // devices
    frows = FF // devices
    padded = (rows // 16 + 1) * 16
    targets = devices // group
    wide = (targets, rows, 2 * group * frows)
    shapes = [(padded, QD + 2 * KVD), (padded, D), wide, (frows, D)]
    types = [dtype, dtype, BF16, dtype]
    if extra is None:
        body = lambda flat_ref, *refs: pack_kernel(devices, group, flat_ref, None, *refs)
        operands = [flat]
    else:
        body = lambda *refs: pack_kernel(devices, group, *refs)
        operands = [flat, extra]
    return pl.pallas_call(
        body,
        out_shape=[jax.ShapeDtypeStruct(shape, kind) for shape, kind in zip(shapes, types)],
        scratch_shapes=[
            pltpu.VMEM((padded, QD + 2 * KVD), F32),
            pltpu.VMEM((padded, D), F32),
            pltpu.VMEM((rows, FF), F32),
            pltpu.VMEM((frows, D), F32),
        ],
        compiler_params=pltpu.CompilerParams(vmem_limit_bytes=32 * 1024 * 1024),
        cost_estimate=pl.CostEstimate(flops=0, bytes_accessed=6 * flat.size, transcendentals=0),
        name="pack",
    )(*operands)


def update_kernel(devices, decay, factors, flat, qkv, out, wide, down, result, moved, rows_wide):
    rows = D // devices
    frows = FF // devices
    bases = section_bases(devices)
    whole = qkv[...].astype(F32)
    out_whole = out[...].astype(F32)
    down_whole = down[...].astype(F32)
    parts = [
        lambda r, c: whole[r, c],
        lambda r, c: whole[r, slice(QD + c.start, QD + c.stop)],
        lambda r, c: whole[r, slice(QD + KVD + c.start, QD + KVD + c.stop)],
        lambda r, c: out_whole[r, c],
    ]
    shapes = matrix_shapes()
    for index, part in enumerate(parts):
        to_flat(
            moved, bases[index], lambda r, c: part(r, c) * factors[index], rows, shapes[index][1]
        )
    to_flat(moved, bases[6], lambda r, c: down_whole[r, c] * factors[6], frows, D)
    for which in range(2):
        for source in range(devices):
            rows_wide[:, source * frows : (source + 1) * frows] = wide[
                source, :, which * frows : (which + 1) * frows
            ].astype(F32)
        to_flat(
            moved, bases[4 + which], lambda r, c: rows_wide[r, c] * factors[4 + which], rows, FF
        )
    result[...] = decay * flat[...] + moved[...]


def update(flat, qkv, out, wide, down, devices, decay, factors):
    return pl.pallas_call(
        lambda *refs: update_kernel(devices, decay, factors, *refs),
        out_shape=jax.ShapeDtypeStruct(flat.shape, F32),
        scratch_shapes=[
            pltpu.VMEM(flat.shape, F32),
            pltpu.VMEM((D // devices, FF), F32),
        ],
        compiler_params=pltpu.CompilerParams(vmem_limit_bytes=32 * 1024 * 1024),
        cost_estimate=pl.CostEstimate(flops=0, bytes_accessed=10 * flat.size, transcendentals=0),
        name="update",
    )(flat, qkv, out, wide, down)


def combine_kernel(old_pair, gate, up, old_down, down, old_out, out, mats, lines):
    devices, rows, _ = old_pair.shape
    frows = gate.shape[0]
    padded = out.shape[0]
    lines[...] = jnp.zeros(lines.shape, F32)
    for source in range(devices):
        lines[source * rows : (source + 1) * rows, : 2 * frows] = old_pair[source].astype(F32)
    old = lines[...].T
    mats[0] = (MOMENTUM_DECAY * old[:frows] + gate[...].astype(F32)).astype(BF16)
    mats[1] = (MOMENTUM_DECAY * old[frows : 2 * frows] + up[...].astype(F32)).astype(BF16)
    mats[2] = (MOMENTUM_DECAY * old_down[...] + down[...].astype(F32)).astype(BF16)
    last = MOMENTUM_DECAY * old_out[...] + out[...].astype(F32)
    mats[3] = jnp.concatenate(
        [last, jnp.zeros((frows - padded, last.shape[1]), F32)], axis=0
    ).astype(BF16)


def combine(old_pair, gate, up, old_down, down, old_out, out):
    frows, width = gate.shape
    return pl.pallas_call(
        combine_kernel,
        out_shape=jax.ShapeDtypeStruct((4, frows, width), BF16),
        scratch_shapes=[pltpu.VMEM((width, -(-2 * frows // LANES) * LANES), F32)],
        compiler_params=pltpu.CompilerParams(vmem_limit_bytes=32 * 1024 * 1024),
        name="combine",
    )(old_pair, gate, up, old_down, down, old_out, out)


def turn_kernel(gate, up, out, columns):
    devices, rows, _ = out.shape
    frows = gate.shape[0]
    columns[...] = jnp.zeros(columns.shape, F32)
    columns[:frows] = gate[...].astype(F32)
    columns[frows : 2 * frows] = up[...].astype(F32)
    lines = columns[...].T
    for target in range(devices):
        out[target] = lines[target * rows : (target + 1) * rows, : 2 * frows].astype(BF16)


def turn(gate, up, devices):
    frows, width = gate.shape
    return pl.pallas_call(
        turn_kernel,
        out_shape=jax.ShapeDtypeStruct((devices, width // devices, 2 * frows), BF16),
        scratch_shapes=[pltpu.VMEM((-(-2 * frows // LANES) * LANES, width), F32)],
        compiler_params=pltpu.CompilerParams(vmem_limit_bytes=32 * 1024 * 1024),
        name="turn",
    )(gate, up)


def on_device(
    block_input,
    cotangent,
    lengths,
    doc_starts,
    master,
    momentum,
    vectors,
    vector_first,
    vector_second,
):
    n_dp = lax.axis_size("dp")
    n_ctx = lax.axis_size("ctx")
    devices = n_dp * n_ctx
    rows = D // devices
    frows = FF // devices
    fblock = FF // n_ctx
    slots, span, width = block_input.shape
    tokens = slots * span
    group = HEADS // KVH
    qkv = QD + 2 * KVD
    my_ctx = lax.axis_index("ctx")
    me = lax.axis_index("dp") * n_ctx + my_ctx
    core_bit, x_bit = 1, 2
    ctx_bits = [core_bit, x_bit]
    dp_bits = [n_ctx << index for index in range(n_dp.bit_length() - 1)]
    all_bits = ctx_bits + dp_bits
    many = tuple([2] * len(all_bits))
    padded = (rows // 16 + 1) * 16

    master_flat = master.reshape(-1, LANES)
    momentum_flat = momentum.reshape(-1, LANES)
    small = jnp.pad(vectors, ((0, 0), (0, LANES - vectors.shape[1])))
    qkv_local, out_local, gate_up, down_local = pack(master_flat, small, devices, n_dp, BF16)

    attn_full = gather_bits(
        jnp.concatenate([qkv_local, out_local], axis=1), dp_bits[::-1], me, devices
    )
    down_bits = dp_bits[::-1]
    down_part, _ = lax.optimization_barrier((down_local, attn_full))
    high, low = down_bits[:2]
    down_came = [swap(down_part, mask, devices) for mask in (low, high, high + low)]
    qkv_full = gather_bits(attn_full[..., :qkv], ctx_bits[::-1], me, devices, dp_bits)
    qkv_full = qkv_full.reshape(devices, padded, qkv)
    gain_first, gain_second, bias_query, bias_key, bias_value = [
        piece.astype(F32) for piece in split_small(qkv_full[:, rows], devices)
    ]
    w_qkv = qkv_full[:, :rows].reshape(D, qkv)

    came = [choose(gate_up, my_ctx, 0)] + [
        swap(choose(gate_up, my_ctx ^ mask, 0), mask, devices) for mask in range(1, n_ctx)
    ]
    came, _ = lax.optimization_barrier((came, attn_full))
    ordered = []
    for source in range(n_ctx):
        piece = came[0]
        for mask in range(1, n_ctx):
            piece = jnp.where(my_ctx ^ mask == source, came[mask], piece)
        ordered.append(piece)
    w_wide = lax.all_gather(jnp.concatenate(ordered, axis=0), "dp", axis=0, tiled=True)

    def to_rows(gate, up):
        return lax.all_to_all(
            turn(gate, up, devices), BOTH, split_axis=0, concat_axis=0, tiled=True
        )

    length, second = lengths[0], doc_starts[0]
    places = my_ctx * span + jnp.arange(span, dtype=jnp.int32)
    doc_begin = jnp.where(places >= length, length, jnp.where(places >= second, second, 0))
    position = (places - doc_begin).astype(F32)
    live = (places < length)[:, None]
    info = jnp.stack([my_ctx, length, second]).astype(jnp.int32)
    inverse = ROPE_BASE ** (-2.0 * jnp.arange(HD // 2, dtype=F32) / HD)
    angles = inverse[:, None] * position[None, :]
    cosine, sine_part = jnp.cos(angles), jnp.sin(angles)
    cosine = jnp.concatenate([cosine, cosine], axis=0)[None]
    sine_part = jnp.concatenate([sine_part, sine_part], axis=0)[None]

    def from_ctx(value, other_x=None):
        other_core = swap(value, core_bit, devices)
        if other_x is None:
            other_x = swap(value, x_bit, devices)
        return value, other_core, other_x

    cot_here = jnp.where(live, cotangent.reshape(tokens, width), jnp.zeros((), BF16))

    def pair_of_heads(kv, index):
        begin = index * HD
        return jnp.concatenate(
            [kv[:, begin : begin + HD], kv[:, KVD + begin : KVD + begin + HD]], axis=1
        )

    inputs = block_input.astype(F32).reshape(tokens, width)
    scale_one = lax.rsqrt(jnp.mean(inputs * inputs, axis=-1, keepdims=True) + NORM_EPS)
    normed_one = (inputs * scale_one * gain_first).astype(BF16)
    bias = jnp.concatenate([bias_query, bias_key, bias_value])
    pre = mm(w_qkv, normed_one, ((0,), (1,))) + bias[:, None]
    turned = rotate(
        pre[: QD + KVD].reshape(HEADS + KVH, HD, tokens), cosine, sine_part
    )
    queries = (turned[:HEADS].astype(BF16).astype(F32) * HD ** (-0.5)).astype(BF16)
    kv_here = jnp.concatenate(
        [turned[HEADS:].astype(BF16).reshape(KVD, tokens), pre[QD + KVD :].astype(BF16)], axis=0
    )
    kv = from_ctx(kv_here)
    kv = jnp.stack(kv + (swap(kv[2], core_bit, devices),))
    back_one = jnp.pad(
        normed_one.T.reshape(devices, rows, tokens), ((0, 0), (0, padded - rows), (0, 0))
    ).reshape(devices * padded, tokens)
    back_one, kv = lax.optimization_barrier((back_one, kv))
    out_full, _ = lax.optimization_barrier((attn_full[..., qkv:], kv))
    halves = []
    for index in range(KVH):
        if index == 1:
            out_full, cot_here, down_came, _ = lax.optimization_barrier(
                (out_full, cot_here, down_came, halves)
            )
            down_came = [down_part] + down_came
            at_z = jnp.where((me & high) != 0, 2, 0) + jnp.where((me & low) != 0, 1, 0)
            ordered = []
            for source in range(4):
                piece = down_came[0]
                for mask in range(1, 4):
                    piece = jnp.where(at_z ^ mask == source, down_came[mask], piece)
                ordered.append(piece)
            down_part = jnp.stack(ordered).reshape(2, 2, frows, D)
            down_part = gather_bits(down_part, down_bits[2:], me, devices, down_bits[:2])
            cot_far = swap(cot_here, x_bit, devices)
        out_full = gather_bits(
            out_full, ctx_bits[::-1][index : index + 1], me, devices, dp_bits + ctx_bits[::-1][:index]
        )
        kv_one = pair_of_heads(kv, index)
        halves.append(attend(info, kv_one, queries[index * group : (index + 1) * group]))
    halves, cot_far, down_part = lax.optimization_barrier((halves, cot_far, down_part))
    attended = jnp.concatenate([half[0] for half in halves], axis=0)
    log_total = jnp.concatenate([half[1] for half in halves], axis=0)
    out_pieces = out_full.reshape(devices * padded, D)
    w_down = down_part.reshape(fblock, D)

    mixed_pieces = jnp.pad(
        attended.reshape(devices, rows, tokens).astype(BF16), ((0, 0), (0, padded - rows), (0, 0))
    ).reshape(devices * padded, tokens)
    hidden = inputs + mm(mixed_pieces, out_pieces, ((0,), (0,)))
    scale_two = lax.rsqrt(jnp.mean(hidden * hidden, axis=-1, keepdims=True) + NORM_EPS)
    normed_two = (hidden * scale_two * gain_second).astype(BF16)

    normed = from_ctx(normed_two)
    out_pieces, _ = lax.optimization_barrier((out_pieces, normed_two))
    w_out = out_pieces.reshape(devices, padded, D)[:, :rows].reshape(QD, D)
    cot = from_ctx(cot_here, cot_far)
    kept, near_parts = feed_forward(normed[:2], cot[:2], w_wide, w_down, n_ctx, None)
    (far_x, far_dy), kept = lax.optimization_barrier(((normed[2], cot[2]), kept))
    kept, far_parts = feed_forward(
        (far_x, swap(far_x, core_bit, devices)),
        (far_dy, swap(far_dy, core_bit, devices)),
        w_wide,
        w_down,
        n_ctx,
        kept,
    )
    acts, both_backs, normed_all, cot_all = kept

    def to_ctx(near, far):
        crossed = swap(far[1], core_bit, devices)
        far = (far[0].astype(F32) + crossed.astype(F32)).astype(BF16)
        crossed = swap(near[1], core_bit, devices)
        near = near[0].astype(F32) + crossed.astype(F32)
        return near + swap(far, x_bit, devices).astype(F32), far

    normed_two_grad, ready = to_ctx(near_parts, far_parts)
    (acts, both_backs), ready = lax.optimization_barrier(((acts, both_backs), ready))

    dp_shape = tuple([2] * len(dp_bits)) + (frows, D)
    dp_order = dp_bits[1:] + dp_bits[:1]
    down_value = mm(acts, cot_all, ((0,), (0,))).astype(BF16)
    both_value = mm(both_backs, normed_all, ((0,), (0,))).astype(BF16)
    sent, kept = scatter_split(down_value.reshape(dp_shape), dp_bits, dp_order[0], me)
    down_parts = (kept, swap(sent, dp_order[0], devices))
    sent, kept = scatter_split(both_value.reshape((2,) + dp_shape), dp_bits, dp_bits[0], me, 1)
    both_parts = (kept, swap(sent, dp_bits[0], devices))
    momentum_flat, acts, _ = lax.optimization_barrier((momentum_flat, acts, (down_value, both_value)))
    old_qkv, old_out, old_pair, old_down = pack(momentum_flat, None, devices, 1, F32)
    old_pair = lax.all_to_all(old_pair, BOTH, split_axis=0, concat_axis=0, tiled=True)

    out_grad = cot_here.astype(F32)
    hidden_norm_grad, grad_gain_second = norm_backward(
        hidden, scale_two, gain_second, normed_two_grad
    )
    hidden_grad = out_grad + hidden_norm_grad
    hidden_low = hidden_grad.astype(BF16)
    heads_grad = mm(w_out, hidden_low, ((1,), (1,))).astype(BF16).reshape(HEADS, HD, tokens)
    delta = jnp.sum(heads_grad.astype(F32) * attended, axis=1, keepdims=True)
    grad_output = mm(mixed_pieces, hidden_low)
    query_grads, kv_parts = [], []
    sent, kept = scatter_split(
        grad_output.astype(BF16).reshape(many + (padded, D)), all_bits, all_bits[0], me
    )
    wide_parts = [both_parts, down_parts, (kept, swap(sent, all_bits[0], devices))]
    wide_orders = [list(dp_bits), list(dp_order), list(all_bits)]
    leads = [1, 0, 0]
    steps = [[1, 2], [0, 2], [1, 2], [0, 2]]
    shares = [4, 3]
    ready = [sent]
    for index in range(KVH):
        kv_one = pair_of_heads(kv, index)
        kv_grad = None
        begin = index * group
        for count in shares:
            chosen = slice(begin, begin + count)
            begin += count
            query_part, ready = lax.optimization_barrier((queries[chosen], ready))
            query_grad, kv_grad = attend_back(
                info, kv_one, query_part, heads_grad[chosen], log_total[chosen], delta[chosen], kv_grad
            )
            query_grads.append(query_grad)
            ready = []
            for which in steps.pop(0):
                order = wide_orders[which]
                parts, _ = lax.optimization_barrier((wide_parts[which], query_grad))
                order.pop(0)
                sent, kept = scatter_split(scatter_end(parts), order, order[0], me, leads[which])
                ready.append(sent)
                wide_parts[which] = (kept, swap(sent, order[0], devices))
        kv_parts.append(
            scatter_sum(kv_grad.reshape(2, 2, 2 * HD, span), ctx_bits, me, devices)
        )
    kv_grads = [part.astype(F32).reshape(2, HD, span) for part in kv_parts]
    qk_grad = jnp.concatenate(query_grads + [grad[:1] for grad in kv_grads], axis=0)
    qk_back = rotate_back(qk_grad, cosine, sine_part).reshape(QD + KVD, tokens)
    qkv_back = jnp.concatenate(
        [qk_back] + [grad[1] for grad in kv_grads], axis=0
    ).astype(BF16)
    grad_qkv = mm(back_one, qkv_back, ((1,), (1,)))
    grad_bias = jnp.sum(qkv_back.astype(F32), axis=1)
    normed_one_grad = mm(qkv_back, w_qkv, ((0,), (1,)))
    input_norm_grad, grad_gain_first = norm_backward(inputs, scale_one, gain_first, normed_one_grad)
    input_grad = (hidden_grad + input_norm_grad).astype(BF16).reshape(slots, span, width)

    vector_part = join_small(
        [
            grad_gain_first,
            grad_gain_second,
            grad_bias[:QD],
            grad_bias[QD : QD + KVD],
            grad_bias[QD + KVD :],
        ],
        devices,
    )
    vector_rows = lax.all_to_all(vector_part, BOTH, split_axis=0, concat_axis=0, tiled=True)
    here_core = jnp.where((me & core_bit) != 0, 1, 0)
    here_x = jnp.where((me & x_bit) != 0, 1, 0)
    left = list(all_bits)
    qkv_order = [core_bit, dp_bits[0], x_bit] + dp_bits[1:]
    sent, kept = scatter_split(
        grad_qkv.astype(BF16).reshape(many + (padded, qkv)), left, core_bit, me
    )
    wide_parts, sent = lax.optimization_barrier((wide_parts, sent))
    qkv_parts = (kept, swap(sent, core_bit, devices))
    left.remove(core_bit)
    both_sum, down_sum, out_sum_rows = [
        scatter_rest(scatter_end(parts), order[1:], me, devices, lead)
        for parts, order, lead in zip(wide_parts, wide_orders, leads)
    ]
    mats = combine(old_pair, both_sum[0], both_sum[1], old_down, down_sum, old_out, out_sum_rows)
    mats = mats.reshape(2, 2, frows, D)
    row_parts = (choose(mats, here_core, 1), swap(choose(mats, 1 - here_core, 1), core_bit, devices))
    count = len(block_pairs(D // BLOCK))
    places = (count + n_dp - 1) // n_dp * n_dp
    dp_many = tuple([2] * len(dp_bits))
    gram_left = list(dp_bits)
    for step, bit in enumerate(qkv_order[1:]):
        qkv_parts, row_parts = lax.optimization_barrier((qkv_parts, row_parts))
        sent, kept = scatter_split(scatter_end(qkv_parts), left, bit, me)
        left.remove(bit)
        qkv_parts = (kept, swap(sent, bit, devices))
        if step == 0:
            mats = jnp.stack(row_parts, axis=1)
            row_parts = (choose(mats, here_x, 0), swap(choose(mats, 1 - here_x, 0), x_bit, devices))
            continue
        if step == 1:
            owned = jnp.stack(row_parts).reshape(n_ctx * frows, D)
            gram = gram_blocks(owned, places).reshape(dp_many + (places // n_dp, BLOCK, BLOCK))
        else:
            gram = scatter_end(row_parts)
        sent, kept = scatter_split(gram, gram_left, gram_left[0], me)
        row_parts = (kept, swap(sent, gram_left.pop(0), devices))
    qkv_parts, row_parts = lax.optimization_barrier((qkv_parts, row_parts))
    qkv_sum_rows = scatter_end(qkv_parts)
    moved_qkv = MOMENTUM_DECAY * old_qkv + qkv_sum_rows.astype(F32)
    moved_low = moved_qkv.astype(BF16)
    qkv_all = lax.all_gather(moved_low, BOTH, axis=0, tiled=True)
    gram = gather_bits(scatter_end(row_parts), dp_bits[::-1], me, devices)
    gram = gram.reshape(places, BLOCK, BLOCK)

    acts, _ = lax.optimization_barrier((acts, moved_low))
    out_part = mm(acts, w_down).astype(BF16).reshape(n_ctx, span, D)
    out_sum, _ = to_ctx((out_part[0], out_part[1]), (out_part[2], out_part[3]))
    layer_out = jnp.where(live, hidden + out_sum, 0.0)

    both_sum, moved_low, gram = lax.optimization_barrier((both_sum, moved_low, gram))
    pair_rows = to_rows(both_sum[0], both_sum[1])
    ortho = orthogonal_wide(gram, owned).reshape(2, 2, frows, D)
    ortho, pair_rows = lax.optimization_barrier((ortho, pair_rows))
    ortho = from_owner(ortho, core_bit, x_bit, me, devices).reshape(n_ctx, frows, D)
    ortho_pair = to_rows(ortho[0], ortho[1])
    layer_out, qkv_all = lax.optimization_barrier((layer_out, qkv_all))
    ortho_qkv = orthogonal_whole(qkv_all, moved_qkv, (QD, KVD, KVD))
    new_momentum = update(
        momentum_flat,
        qkv_sum_rows,
        out_sum_rows,
        pair_rows,
        down_sum,
        devices,
        MOMENTUM_DECAY,
        [1.0] * 7,
    ).reshape(momentum.shape)

    factors = [
        -MUON_RATE * math.sqrt(max(1.0, breadth / height)) for height, breadth in matrix_shapes()
    ]
    new_master = update(
        master_flat,
        ortho_qkv,
        ortho[3, :padded],
        ortho_pair,
        ortho[2],
        devices,
        1.0 - MUON_RATE * MUON_DECAY,
        factors,
    ).reshape(master.shape)
    vector_rows, _ = lax.optimization_barrier((vector_rows, ortho_qkv))
    vector_grad = jnp.sum(vector_rows, axis=0, keepdims=True)
    first_new = BETA_FIRST * vector_first + (1.0 - BETA_FIRST) * vector_grad
    second_new = BETA_SECOND * vector_second + (1.0 - BETA_SECOND) * vector_grad * vector_grad
    adjusted = (
        first_new
        / (1.0 - BETA_FIRST**STEP)
        / (jnp.sqrt(second_new / (1.0 - BETA_SECOND**STEP)) + ADAM_EPS)
    )
    new_vectors = vectors - ADAM_RATE * adjusted
    return (
        layer_out.astype(BF16).reshape(slots, span, width),
        input_grad,
        new_master,
        new_momentum,
        new_master.astype(BF16),
        new_vectors,
        first_new,
        second_new,
    )


def solution(mesh):
    return jax.shard_map(
        on_device,
        mesh=mesh,
        in_specs=(
            P("dp", "ctx", None),
            P("dp", "ctx", None),
            P("dp"),
            P("dp"),
            P(BOTH, None),
            P(BOTH, None),
            P(BOTH, None),
            P(BOTH, None),
            P(BOTH, None),
        ),
        out_specs=(
            P("dp", "ctx", None),
            P("dp", "ctx", None),
            P(BOTH, None),
            P(BOTH, None),
            P(BOTH, None),
            P(BOTH, None),
            P(BOTH, None),
            P(BOTH, None),
        ),
        check_vma=False,
    )
```

```python
import math

import jax
import jax.numpy as jnp
from jax import lax
from jax.experimental import pallas as pl
from jax.experimental.pallas import tpu as pltpu
from jax.sharding import PartitionSpec as P

D = 896
HEADS = 14
KVH = 2
HD = 64
FF = 4864
SLOT = 2048
NS_STEPS = 3
STEP = 10
QD = 896
KVD = 128

NORM_EPS = 1e-06
ROPE_BASE = 1000000.0
NS_LINEAR = 3.4445
NS_SQUARE = -4.775
NS_CUBIC = 2.0315
MOMENTUM_DECAY = 0.5
MUON_RATE = 0.6
MUON_DECAY = 0.1
ADAM_RATE = 0.2
BETA_FIRST = 0.9
BETA_SECOND = 0.95
ADAM_EPS = 1e-08
MASK_FLOOR = -1e30

F32 = jnp.float32
BF16 = jnp.bfloat16
BOTH = ("dp", "ctx")
LANES = 128


def matrix_shapes():
    return [(D, QD), (D, KVD), (D, KVD), (QD, D), (D, FF), (D, FF), (FF, D)]


def vector_sizes():
    return [D, D, QD, KVD, KVD]


def mm(left, right, contract=((1,), (0,))):
    return lax.dot_general(left, right, (contract, ((), ())), preferred_element_type=F32)


def split_small(flat, devices):
    result = []
    offset = 0
    for extent_all in vector_sizes():
        extent = extent_all // devices
        result.append(flat[:, offset : offset + extent].reshape(extent_all))
        offset += extent
    return result


def join_small(pieces, devices):
    return jnp.concatenate([piece.reshape(devices, -1) for piece in pieces], axis=1)


def swap(value, mask, devices):
    return lax.ppermute(value, BOTH, [(index, index ^ mask) for index in range(devices)])


def gather_bits(value, bits, me, devices, before=()):
    held = value
    done = list(before)
    for bit in bits:
        place = sum(1 for other in done if other > bit)
        got = swap(held, bit, devices)
        mine = (me & bit) != 0
        held = jnp.where(
            mine, jnp.stack([got, held], axis=place), jnp.stack([held, got], axis=place)
        )
        done.append(bit)
    return held


def scatter_split(held, left, bit, me, lead=0):
    axis = sorted(left, reverse=True).index(bit) + lead
    mine = jnp.where((me & bit) != 0, 1, 0)
    return choose(held, 1 - mine, axis).astype(BF16), choose(held, mine, axis)


def scatter_start(held, left, bit, me, devices):
    sent, kept = scatter_split(held, left, bit, me)
    return kept, swap(sent, bit, devices)


def scatter_end(parts):
    return (parts[0].astype(F32) + parts[1].astype(F32)).astype(BF16)


def scatter_sum(value, bits, me, devices):
    left = list(bits)
    held = value
    for bit in bits:
        held = scatter_end(scatter_start(held, left, bit, me, devices))
        left.remove(bit)
    return held


def choose(value, mine, axis):
    return lax.dynamic_index_in_dim(value, mine, axis, keepdims=False)


def to_owner(value, core_bit, x_bit, me, devices):
    core = jnp.where((me & core_bit) != 0, 1, 0)
    across = jnp.where((me & x_bit) != 0, 1, 0)
    got = swap(choose(value, 1 - core, 1), core_bit, devices)
    value = jnp.stack([choose(value, core, 1), got], axis=1)
    got = swap(choose(value, 1 - across, 0), x_bit, devices)
    return jnp.stack([choose(value, across, 0), got])


def from_owner(value, core_bit, x_bit, me, devices):
    got = swap(value[1], x_bit, devices)
    value = jnp.where(
        (me & x_bit) != 0, jnp.stack([got, value[0]]), jnp.stack([value[0], got])
    )
    got = swap(value[:, 1], core_bit, devices)
    return jnp.where(
        (me & core_bit) != 0,
        jnp.stack([got, value[:, 0]], axis=1),
        jnp.stack([value[:, 0], got], axis=1),
    )


def rotate(values, cosine, sine_part):
    midpoint = HD // 2
    turned = jnp.concatenate([-values[:, midpoint:], values[:, :midpoint]], axis=1)
    return values * cosine + turned * sine_part


def rotate_back(gradient, cosine, sine_part):
    midpoint = HD // 2
    scaled = gradient * sine_part
    turned = jnp.concatenate([scaled[:, midpoint:], -scaled[:, :midpoint]], axis=1)
    return gradient * cosine + turned


def norm_backward(source, scale_row, gain, incoming):
    gain_grad = jnp.sum(incoming * source * scale_row, axis=0)
    weighted = incoming * gain
    result = scale_row * weighted - source * scale_row**3 * jnp.mean(
        weighted * source, axis=-1, keepdims=True
    )
    return (result, gain_grad)


def halves_of(span):
    return [slice(0, span // 2), slice(span // 2, span)]


def fill_mask(info, mask, chunk, span):
    key = chunk * span + lax.broadcasted_iota(jnp.int32, (span, span), 0)
    query = info[0] * span + lax.broadcasted_iota(jnp.int32, (span, span), 1)
    key_doc = (key >= info[2]).astype(jnp.int32) + (key >= info[1]).astype(jnp.int32)
    query_doc = (query >= info[2]).astype(jnp.int32) + (query >= info[1]).astype(jnp.int32)
    allowed = jnp.logical_and(key_doc == query_doc, key <= query)
    mask[chunk] = jnp.where(allowed, 0.0, MASK_FLOOR).astype(F32)


def attend_kernel(info, kv, q, out, lse, keys, mask, best, total, acc):
    head = pl.program_id(0)
    span = q.shape[-1]
    mine = info[0]
    chunks = mine + 1

    @pl.when(head == 0)
    def _():
        def fill(chunk, carry):
            slot = jnp.bitwise_xor(chunk, mine)
            keys[chunk] = kv[slot, :HD, :].astype(F32).T.astype(BF16)
            fill_mask(info, mask, chunk, span)
            return carry

        lax.fori_loop(0, chunks, fill, 0)

    best[...] = jnp.full(best.shape, MASK_FLOOR, F32)
    total[...] = jnp.zeros(total.shape, F32)
    acc[...] = jnp.zeros(acc.shape, F32)
    queries = q[0]

    def step(index, carry):
        chunk = mine - index
        slot = jnp.bitwise_xor(chunk, mine)
        scores = jnp.dot(keys[chunk], queries, preferred_element_type=F32) + mask[chunk]
        old = best[...]
        new = jnp.maximum(old, jnp.max(scores, axis=0, keepdims=True))
        present = jnp.exp(scores - new)
        shrink = jnp.exp(old - new)
        best[...] = new
        total[...] = total[...] * shrink + jnp.sum(present, axis=0, keepdims=True)
        acc[...] = acc[...] * shrink + jnp.dot(
            kv[slot, HD:, :], present.astype(BF16), preferred_element_type=F32
        )
        return carry

    lax.fori_loop(0, chunks, step, 0)
    out[0] = acc[...] / total[...]
    lse[0] = best[...] + jnp.log(total[...])


def attend_back_kernel(
    info, kv, q, dout, lse, delta, before, dq, dkv, keys, values, mask, dk, dv, acc
):
    head = pl.program_id(0)
    span = q.shape[-1]
    mine = info[0]
    chunks = mine + 1
    n_ctx = kv.shape[0]

    @pl.when(head == 0)
    def _():
        dk[...] = jnp.zeros(dk.shape, F32)
        dv[...] = jnp.zeros(dv.shape, F32)

        def fill(chunk, carry):
            slot = jnp.bitwise_xor(chunk, mine)
            keys[chunk] = kv[slot, :HD, :].astype(F32).T.astype(BF16)
            values[chunk] = kv[slot, HD:, :].astype(F32).T.astype(BF16)
            fill_mask(info, mask, chunk, span)
            return carry

        lax.fori_loop(0, chunks, fill, 0)

    acc[...] = jnp.zeros(acc.shape, F32)
    queries = q[0]
    douts = dout[0]
    query_rows = queries.astype(F32).T.astype(BF16)
    dout_rows = douts.astype(F32).T.astype(BF16)

    def step(chunk, carry):
        slot = jnp.bitwise_xor(chunk, mine)
        value_sum, key_sum = dv[chunk], dk[chunk]
        for lanes in halves_of(span):
            scores = (
                jnp.dot(keys[chunk], queries[:, lanes], preferred_element_type=F32)
                + mask[chunk, :, lanes]
            )
            shares = jnp.exp(scores - lse[0, :, lanes])
            share_grad = jnp.dot(values[chunk], douts[:, lanes], preferred_element_type=F32)
            score_grad = (shares * (share_grad - delta[0, :, lanes])).astype(BF16)
            value_sum += jnp.dot(
                shares.astype(BF16), dout_rows[lanes, :], preferred_element_type=F32
            )
            key_sum += jnp.dot(score_grad, query_rows[lanes, :], preferred_element_type=F32)
            acc[:, lanes] += jnp.dot(kv[slot, :HD, :], score_grad, preferred_element_type=F32)
        dv[chunk], dk[chunk] = value_sum, key_sum
        return carry

    lax.fori_loop(0, chunks, step, 0)
    dq[0] = acc[...] * HD ** (-0.5)

    @pl.when(head == pl.num_programs(0) - 1)
    def _():
        for chunk in range(n_ctx):
            sums = jnp.concatenate([dk[chunk].T, dv[chunk].T], axis=0)
            if before is not None:
                sums += before[chunk].astype(F32)
            dkv[chunk] = sums.astype(BF16)


def attend(info, kv, q):
    heads, _, span = q.shape
    n_ctx = kv.shape[0]
    per_head = lambda rows: pl.BlockSpec((1, rows, span), lambda head: (head, 0, 0))
    return pl.pallas_call(
        attend_kernel,
        grid=(heads,),
        in_specs=[
            pl.BlockSpec(memory_space=pltpu.SMEM),
            pl.BlockSpec(kv.shape, lambda head: (0, 0, 0)),
            per_head(HD),
        ],
        out_specs=[per_head(HD), per_head(1)],
        out_shape=[
            jax.ShapeDtypeStruct((heads, HD, span), F32),
            jax.ShapeDtypeStruct((heads, 1, span), F32),
        ],
        scratch_shapes=[
            pltpu.VMEM((n_ctx, span, HD), BF16),
            pltpu.VMEM((n_ctx, span, span), F32),
            pltpu.VMEM((1, span), F32),
            pltpu.VMEM((1, span), F32),
            pltpu.VMEM((HD, span), F32),
        ],
        compiler_params=pltpu.CompilerParams(vmem_limit_bytes=40 * 1024 * 1024),
        cost_estimate=pl.CostEstimate(
            flops=4 * heads * span * span * n_ctx * HD * 4,
            bytes_accessed=4 * heads * span * HD * 2,
            transcendentals=heads * span * span * n_ctx,
        ),
        name="attend",
    )(info, kv, q)


def attend_back(info, kv, q, dout, lse, delta, before):
    heads, _, span = q.shape
    n_ctx = kv.shape[0]
    per_head = lambda rows: pl.BlockSpec((1, rows, span), lambda head: (head, 0, 0))
    whole = pl.BlockSpec(kv.shape, lambda head: (0, 0, 0))
    if before is None:
        body = lambda *refs: attend_back_kernel(*refs[:6], None, *refs[6:])
    else:
        body = attend_back_kernel
    return pl.pallas_call(
        body,
        grid=(heads,),
        in_specs=[
            pl.BlockSpec(memory_space=pltpu.SMEM),
            whole,
            per_head(HD),
            per_head(HD),
            per_head(1),
            per_head(1),
        ]
        + [whole] * (before is not None),
        out_specs=[per_head(HD), whole],
        out_shape=[
            jax.ShapeDtypeStruct((heads, HD, span), F32),
            jax.ShapeDtypeStruct(kv.shape, BF16),
        ],
        scratch_shapes=[
            pltpu.VMEM((n_ctx, span, HD), BF16),
            pltpu.VMEM((n_ctx, span, HD), BF16),
            pltpu.VMEM((n_ctx, span, span), F32),
            pltpu.VMEM((n_ctx, span, HD), F32),
            pltpu.VMEM((n_ctx, span, HD), F32),
            pltpu.VMEM((HD, span), F32),
        ],
        compiler_params=pltpu.CompilerParams(vmem_limit_bytes=40 * 1024 * 1024),
        cost_estimate=pl.CostEstimate(
            flops=10 * heads * span * span * n_ctx * HD * 4,
            bytes_accessed=8 * heads * span * HD * 2,
            transcendentals=heads * span * span * n_ctx,
        ),
        name="attend_back",
    )(*[info, kv, q, dout, lse, delta] + [before] * (before is not None))


def forward_backward_kernel(
    x0, x1, dy0, dy1, wide, down, act_out, both_out, x_out, dy_out, back0, back1
):
    first = pl.program_id(0) == 0
    units = down.shape[0]
    x = jnp.where(first, x0[...], x1[...])
    dy = jnp.where(first, dy0[...], dy1[...])
    x_out[...] = x
    dy_out[...] = dy
    both = jnp.dot(x, wide[...], preferred_element_type=F32)
    gate_pre = both[:, :units]
    up_pre = both[:, units:]
    grad_act = mm(dy, down[...], ((1,), (1,)))
    sigmoid_gate = jax.nn.sigmoid(gate_pre)
    swish = gate_pre * sigmoid_gate
    slope = sigmoid_gate * (1.0 + gate_pre * (1.0 - sigmoid_gate))
    act_out[...] = (swish * up_pre).astype(BF16)
    both_back = jnp.concatenate([grad_act * up_pre * slope, grad_act * swish], axis=1).astype(BF16)
    both_out[...] = both_back
    back = mm(both_back, wide[...], ((1,), (1,))).astype(BF16)

    @pl.when(first)
    def _():
        back0[...] = back

    @pl.when(jnp.logical_not(first))
    def _():
        back1[...] = back


def feed_forward(x, dy, wide, down, blocks, earlier):
    span, width = x[0].shape
    units = down.shape[0]
    first = 0 if earlier is None else 2
    whole = lambda shape: pl.BlockSpec(
        shape, lambda block: (0, 0), pipeline_mode=pl.Buffered(1)
    )
    line = lambda columns: pl.BlockSpec((span, columns), lambda block: (block + first, 0))
    columns = [units, 2 * units, width, width]
    shapes = [jax.ShapeDtypeStruct((blocks * span, count), BF16) for count in columns]
    in_specs = [whole((span, width))] * 4 + [whole((width, 2 * units)), whole((units, width))]
    operands = [*x, *dy, wide, down]
    aliases = {}
    body = forward_backward_kernel
    if earlier is not None:
        in_specs += [pl.BlockSpec(memory_space=pl.ANY)] * 4
        operands += list(earlier)
        aliases = {6 + index: index for index in range(4)}
        body = lambda *refs: forward_backward_kernel(*refs[:6], *refs[10:])
    back = pl.BlockSpec((span, width), lambda block: (0, 0))
    results = pl.pallas_call(
        body,
        grid=(2,),
        in_specs=in_specs,
        out_specs=[line(count) for count in columns] + [back, back],
        out_shape=shapes + [jax.ShapeDtypeStruct((span, width), BF16)] * 2,
        input_output_aliases=aliases,
        compiler_params=pltpu.CompilerParams(vmem_limit_bytes=60 * 1024 * 1024),
        cost_estimate=pl.CostEstimate(
            flops=20 * span * width * units,
            bytes_accessed=6 * width * units + 2 * span * 10 * width,
            transcendentals=2 * span * units,
        ),
        name="feed_forward",
    )(*operands)
    return results[:4], results[4:]


BLOCK = 128


def block_pairs(count):
    return [(low, high) for low in range(count) for high in range(low, count)]


def gram_kernel(rows, out):
    count = rows.shape[1] // BLOCK
    place = 0
    for low in range(count):
        line = lax.dot_general(
            rows[:, low * BLOCK : (low + 1) * BLOCK],
            rows[:, low * BLOCK :],
            (((0,), (0,)), ((), ())),
            preferred_element_type=F32,
        ).astype(BF16)
        for high in range(low, count):
            out[place] = line[:, (high - low) * BLOCK : (high - low + 1) * BLOCK]
            place += 1
    for extra in range(place, out.shape[0]):
        out[extra] = jnp.zeros((BLOCK, BLOCK), BF16)


def gram_blocks(rows, places):
    return pl.pallas_call(
        gram_kernel,
        out_shape=jax.ShapeDtypeStruct((places, BLOCK, BLOCK), BF16),
        compiler_params=pltpu.CompilerParams(vmem_limit_bytes=32 * 1024 * 1024),
        name="gram",
    )(rows)


def newton_schulz(gram, low, poly, mixed, rows):
    size = gram.shape[0]
    part = size // 2 if size % 16 == 0 and size > BLOCK else size
    parts = [pl.ds(begin, part) for begin in range(0, size, part)]
    row_id = lax.broadcasted_iota(jnp.int32, (size, size), 0)
    column_id = lax.broadcasted_iota(jnp.int32, (size, size), 1)
    square = jnp.where(row_id == column_id, gram[...], 0.0)
    square = jnp.sum(jnp.sum(square, axis=0, keepdims=True), axis=1, keepdims=True)
    scale = 1.0 / (jnp.sqrt(square) + 1e-07)
    for place in parts:
        scaled = gram[place, :] * (scale * scale)
        gram[place, :] = scaled
        low[place, :] = scaled.astype(BF16)
    work = (rows * scale).astype(BF16)
    for step in range(NS_STEPS):
        for place in parts:
            second = jnp.dot(low[place, :], low[...], preferred_element_type=F32)
            poly[place, :] = (NS_SQUARE * gram[place, :] + NS_CUBIC * second).astype(BF16)
        moved = jnp.dot(work, poly[...], preferred_element_type=F32)
        work = (NS_LINEAR * work.astype(F32) + moved).astype(BF16)
        if step + 1 < NS_STEPS:
            for place in parts:
                first = jnp.dot(poly[place, :], low[...], preferred_element_type=F32)
                mixed[place, :] = first.astype(BF16)
                gram[place, :] = (
                    NS_LINEAR * NS_LINEAR * gram[place, :] + (2.0 * NS_LINEAR) * first
                )
            for place in parts:
                second = jnp.dot(poly[place, :], mixed[...], preferred_element_type=F32)
                renewed = gram[place, :] + second
                gram[place, :] = renewed
                low[place, :] = renewed.astype(BF16)
    return work


def wide_kernel(blocks, rows, out, gram, low, poly, mixed):
    for place, (first, second) in enumerate(block_pairs(gram.shape[0] // BLOCK)):
        tile = blocks[place].astype(F32)
        gram[first * BLOCK : (first + 1) * BLOCK, second * BLOCK : (second + 1) * BLOCK] = tile
        if first != second:
            gram[second * BLOCK : (second + 1) * BLOCK, first * BLOCK : (first + 1) * BLOCK] = tile.T
    out[...] = newton_schulz(gram, low, poly, mixed, rows[...].astype(F32))


def square_scratch(size):
    return [
        pltpu.VMEM((size, size), F32),
        pltpu.VMEM((size, size), BF16),
        pltpu.VMEM((size, size), BF16),
        pltpu.VMEM((size, size), BF16),
    ]


def orthogonal_wide(blocks, rows):
    return pl.pallas_call(
        wide_kernel,
        out_shape=jax.ShapeDtypeStruct(rows.shape, BF16),
        scratch_shapes=square_scratch(rows.shape[1]),
        compiler_params=pltpu.CompilerParams(vmem_limit_bytes=40 * 1024 * 1024),
        cost_estimate=pl.CostEstimate(
            flops=14 * rows.shape[1] ** 3, bytes_accessed=4 * rows.size, transcendentals=0
        ),
        name="newton_wide",
    )(blocks, rows)


def whole_kernel(widths, whole, rows, out, *scratch):
    begin = 0
    for index, width in enumerate(widths):
        gram, low, poly, mixed = scratch[4 * index : 4 * index + 4]
        for first in range(0, width, BLOCK):
            gram[first : first + BLOCK, :] = lax.dot_general(
                whole[:, begin + first : begin + first + BLOCK],
                whole[:, begin : begin + width],
                (((0,), (0,)), ((), ())),
                preferred_element_type=F32,
            )
        out[:, begin : begin + width] = newton_schulz(
            gram, low, poly, mixed, rows[:, begin : begin + width]
        )
        begin += width


def orthogonal_whole(whole, rows, widths):
    scratch = []
    for width in widths:
        scratch += square_scratch(width)
    return pl.pallas_call(
        lambda *refs: whole_kernel(widths, *refs),
        out_shape=jax.ShapeDtypeStruct(rows.shape, BF16),
        scratch_shapes=scratch,
        compiler_params=pltpu.CompilerParams(vmem_limit_bytes=48 * 1024 * 1024),
        cost_estimate=pl.CostEstimate(
            flops=16 * sum(width**3 for width in widths),
            bytes_accessed=2 * whole.size,
            transcendentals=0,
        ),
        name="newton_whole",
    )(whole, rows)


def from_flat(flat, base, target, height, breadth):
    lines = breadth // LANES
    for begin in range(0, height, 8):
        count = min(8, height - begin)
        for index in range(lines):
            start = base + begin * lines + index
            if lines == 1:
                tile = flat[start : start + count, :]
            else:
                tile = flat[pl.ds(start, count, stride=lines), :]
            target[begin : begin + count, index * LANES : (index + 1) * LANES] = tile


def to_flat(flat, base, value, height, breadth):
    lines = breadth // LANES
    for begin in range(0, height, 8):
        count = min(8, height - begin)
        for index in range(lines):
            start = base + begin * lines + index
            tile = value(slice(begin, begin + count), slice(index * LANES, (index + 1) * LANES))
            if lines == 1:
                flat[start : start + count, :] = tile
            else:
                flat[pl.ds(start, count, stride=lines), :] = tile


def section_bases(devices):
    bases = []
    base = 0
    for height, breadth in matrix_shapes():
        bases.append(base)
        base += height // devices * breadth // LANES
    return bases


def pack_kernel(devices, group, flat, extra, qkv_out, out_out, wide_out, down_out, qkv, out, wide, down):
    rows = D // devices
    frows = FF // devices
    bases = section_bases(devices)
    qkv[...] = jnp.zeros(qkv.shape, F32)
    out[...] = jnp.zeros(out.shape, F32)
    from_flat(flat, bases[0], qkv.at[:, :QD], rows, QD)
    from_flat(flat, bases[1], qkv.at[:, QD : QD + KVD], rows, KVD)
    from_flat(flat, bases[2], qkv.at[:, QD + KVD :], rows, KVD)
    if extra is not None:
        qkv[rows : rows + 1, :LANES] = extra[...]
    from_flat(flat, bases[3], out, rows, D)
    from_flat(flat, bases[6], down, FF // devices, D)
    qkv_out[...] = qkv[...].astype(qkv_out.dtype)
    out_out[...] = out[...].astype(out_out.dtype)
    down_out[...] = down[...].astype(down_out.dtype)
    for which in range(2):
        from_flat(flat, bases[4 + which], wide, rows, FF)
        targets = devices // group
        for target in range(targets):
            piece = jnp.concatenate(
                [
                    wide[:, (turn * targets + target) * frows : (turn * targets + target + 1) * frows]
                    for turn in range(group)
                ],
                axis=1,
            )
            width = group * frows
            wide_out[target, :, which * width : (which + 1) * width] = piece.astype(wide_out.dtype)


def pack(flat, extra, devices, group, dtype):
    rows = D // devices
    frows = FF // devices
    padded = (rows // 16 + 1) * 16
    targets = devices // group
    wide = (targets, rows, 2 * group * frows)
    shapes = [(padded, QD + 2 * KVD), (padded, D), wide, (frows, D)]
    types = [dtype, dtype, BF16, dtype]
    if extra is None:
        body = lambda flat_ref, *refs: pack_kernel(devices, group, flat_ref, None, *refs)
        operands = [flat]
    else:
        body = lambda *refs: pack_kernel(devices, group, *refs)
        operands = [flat, extra]
    return pl.pallas_call(
        body,
        out_shape=[jax.ShapeDtypeStruct(shape, kind) for shape, kind in zip(shapes, types)],
        scratch_shapes=[
            pltpu.VMEM((padded, QD + 2 * KVD), F32),
            pltpu.VMEM((padded, D), F32),
            pltpu.VMEM((rows, FF), F32),
            pltpu.VMEM((frows, D), F32),
        ],
        compiler_params=pltpu.CompilerParams(vmem_limit_bytes=32 * 1024 * 1024),
        cost_estimate=pl.CostEstimate(flops=0, bytes_accessed=6 * flat.size, transcendentals=0),
        name="pack",
    )(*operands)


def update_kernel(devices, decay, factors, flat, qkv, out, wide, down, result, moved, rows_wide):
    rows = D // devices
    frows = FF // devices
    bases = section_bases(devices)
    whole = qkv[...].astype(F32)
    out_whole = out[...].astype(F32)
    down_whole = down[...].astype(F32)
    parts = [
        lambda r, c: whole[r, c],
        lambda r, c: whole[r, slice(QD + c.start, QD + c.stop)],
        lambda r, c: whole[r, slice(QD + KVD + c.start, QD + KVD + c.stop)],
        lambda r, c: out_whole[r, c],
    ]
    shapes = matrix_shapes()
    for index, part in enumerate(parts):
        to_flat(
            moved, bases[index], lambda r, c: part(r, c) * factors[index], rows, shapes[index][1]
        )
    to_flat(moved, bases[6], lambda r, c: down_whole[r, c] * factors[6], frows, D)
    for which in range(2):
        for source in range(devices):
            rows_wide[:, source * frows : (source + 1) * frows] = wide[
                source, :, which * frows : (which + 1) * frows
            ].astype(F32)
        to_flat(
            moved, bases[4 + which], lambda r, c: rows_wide[r, c] * factors[4 + which], rows, FF
        )
    result[...] = decay * flat[...] + moved[...]


def update(flat, qkv, out, wide, down, devices, decay, factors):
    return pl.pallas_call(
        lambda *refs: update_kernel(devices, decay, factors, *refs),
        out_shape=jax.ShapeDtypeStruct(flat.shape, F32),
        scratch_shapes=[
            pltpu.VMEM(flat.shape, F32),
            pltpu.VMEM((D // devices, FF), F32),
        ],
        compiler_params=pltpu.CompilerParams(vmem_limit_bytes=32 * 1024 * 1024),
        cost_estimate=pl.CostEstimate(flops=0, bytes_accessed=10 * flat.size, transcendentals=0),
        name="update",
    )(flat, qkv, out, wide, down)


def combine_kernel(old_pair, gate, up, old_down, down, old_out, out, mats, lines):
    devices, rows, _ = old_pair.shape
    frows = gate.shape[0]
    padded = out.shape[0]
    lines[...] = jnp.zeros(lines.shape, F32)
    for source in range(devices):
        lines[source * rows : (source + 1) * rows, : 2 * frows] = old_pair[source].astype(F32)
    old = lines[...].T
    mats[0] = (MOMENTUM_DECAY * old[:frows] + gate[...].astype(F32)).astype(BF16)
    mats[1] = (MOMENTUM_DECAY * old[frows : 2 * frows] + up[...].astype(F32)).astype(BF16)
    mats[2] = (MOMENTUM_DECAY * old_down[...] + down[...].astype(F32)).astype(BF16)
    last = MOMENTUM_DECAY * old_out[...] + out[...].astype(F32)
    mats[3] = jnp.concatenate(
        [last, jnp.zeros((frows - padded, last.shape[1]), F32)], axis=0
    ).astype(BF16)


def combine(old_pair, gate, up, old_down, down, old_out, out):
    frows, width = gate.shape
    return pl.pallas_call(
        combine_kernel,
        out_shape=jax.ShapeDtypeStruct((4, frows, width), BF16),
        scratch_shapes=[pltpu.VMEM((width, -(-2 * frows // LANES) * LANES), F32)],
        compiler_params=pltpu.CompilerParams(vmem_limit_bytes=32 * 1024 * 1024),
        name="combine",
    )(old_pair, gate, up, old_down, down, old_out, out)


def turn_kernel(gate, up, out, columns):
    devices, rows, _ = out.shape
    frows = gate.shape[0]
    columns[...] = jnp.zeros(columns.shape, F32)
    columns[:frows] = gate[...].astype(F32)
    columns[frows : 2 * frows] = up[...].astype(F32)
    lines = columns[...].T
    for target in range(devices):
        out[target] = lines[target * rows : (target + 1) * rows, : 2 * frows].astype(BF16)


def turn(gate, up, devices):
    frows, width = gate.shape
    return pl.pallas_call(
        turn_kernel,
        out_shape=jax.ShapeDtypeStruct((devices, width // devices, 2 * frows), BF16),
        scratch_shapes=[pltpu.VMEM((-(-2 * frows // LANES) * LANES, width), F32)],
        compiler_params=pltpu.CompilerParams(vmem_limit_bytes=32 * 1024 * 1024),
        name="turn",
    )(gate, up)


def on_device(
    block_input,
    cotangent,
    lengths,
    doc_starts,
    master,
    momentum,
    vectors,
    vector_first,
    vector_second,
):
    n_dp = lax.axis_size("dp")
    n_ctx = lax.axis_size("ctx")
    devices = n_dp * n_ctx
    rows = D // devices
    frows = FF // devices
    fblock = FF // n_ctx
    slots, span, width = block_input.shape
    tokens = slots * span
    group = HEADS // KVH
    qkv = QD + 2 * KVD
    my_ctx = lax.axis_index("ctx")
    me = lax.axis_index("dp") * n_ctx + my_ctx
    core_bit, x_bit = 1, 2
    ctx_bits = [core_bit, x_bit]
    dp_bits = [n_ctx << index for index in range(n_dp.bit_length() - 1)]
    all_bits = ctx_bits + dp_bits
    many = tuple([2] * len(all_bits))
    padded = (rows // 16 + 1) * 16

    master_flat = master.reshape(-1, LANES)
    momentum_flat = momentum.reshape(-1, LANES)
    small = jnp.pad(vectors, ((0, 0), (0, LANES - vectors.shape[1])))
    qkv_local, out_local, gate_up, down_local = pack(master_flat, small, devices, n_dp, BF16)

    attn_full = gather_bits(
        jnp.concatenate([qkv_local, out_local], axis=1), dp_bits[::-1], me, devices
    )
    down_bits = dp_bits[::-1]
    down_part, _ = lax.optimization_barrier((down_local, attn_full))
    high, low = down_bits[:2]
    down_came = [swap(down_part, mask, devices) for mask in (low, high, high + low)]
    qkv_full = gather_bits(attn_full[..., :qkv], ctx_bits[::-1], me, devices, dp_bits)
    qkv_full = qkv_full.reshape(devices, padded, qkv)
    gain_first, gain_second, bias_query, bias_key, bias_value = [
        piece.astype(F32) for piece in split_small(qkv_full[:, rows], devices)
    ]
    w_qkv = qkv_full[:, :rows].reshape(D, qkv)

    came = [choose(gate_up, my_ctx, 0)] + [
        swap(choose(gate_up, my_ctx ^ mask, 0), mask, devices) for mask in range(1, n_ctx)
    ]
    came, _ = lax.optimization_barrier((came, attn_full))
    ordered = []
    for source in range(n_ctx):
        piece = came[0]
        for mask in range(1, n_ctx):
            piece = jnp.where(my_ctx ^ mask == source, came[mask], piece)
        ordered.append(piece)
    w_wide = lax.all_gather(jnp.concatenate(ordered, axis=0), "dp", axis=0, tiled=True)

    def to_rows(gate, up):
        return lax.all_to_all(
            turn(gate, up, devices), BOTH, split_axis=0, concat_axis=0, tiled=True
        )

    length, second = lengths[0], doc_starts[0]
    places = my_ctx * span + jnp.arange(span, dtype=jnp.int32)
    doc_begin = jnp.where(places >= length, length, jnp.where(places >= second, second, 0))
    position = (places - doc_begin).astype(F32)
    live = (places < length)[:, None]
    info = jnp.stack([my_ctx, length, second]).astype(jnp.int32)
    inverse = ROPE_BASE ** (-2.0 * jnp.arange(HD // 2, dtype=F32) / HD)
    angles = inverse[:, None] * position[None, :]
    cosine, sine_part = jnp.cos(angles), jnp.sin(angles)
    cosine = jnp.concatenate([cosine, cosine], axis=0)[None]
    sine_part = jnp.concatenate([sine_part, sine_part], axis=0)[None]

    def from_ctx(value, other_x=None):
        other_core = swap(value, core_bit, devices)
        if other_x is None:
            other_x = swap(value, x_bit, devices)
        return value, other_core, other_x

    cot_here = jnp.where(live, cotangent.reshape(tokens, width), jnp.zeros((), BF16))

    def pair_of_heads(kv, index):
        begin = index * HD
        return jnp.concatenate(
            [kv[:, begin : begin + HD], kv[:, KVD + begin : KVD + begin + HD]], axis=1
        )

    inputs = block_input.astype(F32).reshape(tokens, width)
    scale_one = lax.rsqrt(jnp.mean(inputs * inputs, axis=-1, keepdims=True) + NORM_EPS)
    normed_one = (inputs * scale_one * gain_first).astype(BF16)
    bias = jnp.concatenate([bias_query, bias_key, bias_value])
    pre = mm(w_qkv, normed_one, ((0,), (1,))) + bias[:, None]
    turned = rotate(
        pre[: QD + KVD].reshape(HEADS + KVH, HD, tokens), cosine, sine_part
    )
    queries = (turned[:HEADS].astype(BF16).astype(F32) * HD ** (-0.5)).astype(BF16)
    kv_here = jnp.concatenate(
        [turned[HEADS:].astype(BF16).reshape(KVD, tokens), pre[QD + KVD :].astype(BF16)], axis=0
    )
    kv = from_ctx(kv_here)
    kv = jnp.stack(kv + (swap(kv[2], core_bit, devices),))
    back_one = jnp.pad(
        normed_one.T.reshape(devices, rows, tokens), ((0, 0), (0, padded - rows), (0, 0))
    ).reshape(devices * padded, tokens)
    back_one, kv = lax.optimization_barrier((back_one, kv))
    out_full, _ = lax.optimization_barrier((attn_full[..., qkv:], kv))
    halves = []
    for index in range(KVH):
        if index == 1:
            out_full, cot_here, down_came, _ = lax.optimization_barrier(
                (out_full, cot_here, down_came, halves)
            )
            down_came = [down_part] + down_came
            at_z = jnp.where((me & high) != 0, 2, 0) + jnp.where((me & low) != 0, 1, 0)
            ordered = []
            for source in range(4):
                piece = down_came[0]
                for mask in range(1, 4):
                    piece = jnp.where(at_z ^ mask == source, down_came[mask], piece)
                ordered.append(piece)
            down_part = jnp.stack(ordered).reshape(2, 2, frows, D)
            down_part = gather_bits(down_part, down_bits[2:], me, devices, down_bits[:2])
            cot_far = swap(cot_here, x_bit, devices)
        out_full = gather_bits(
            out_full, ctx_bits[::-1][index : index + 1], me, devices, dp_bits + ctx_bits[::-1][:index]
        )
        kv_one = pair_of_heads(kv, index)
        halves.append(attend(info, kv_one, queries[index * group : (index + 1) * group]))
    halves, cot_far = lax.optimization_barrier((halves, cot_far))
    attended = jnp.concatenate([half[0] for half in halves], axis=0)
    log_total = jnp.concatenate([half[1] for half in halves], axis=0)
    out_pieces = out_full.reshape(devices * padded, D)

    mixed_pieces = jnp.pad(
        attended.reshape(devices, rows, tokens).astype(BF16), ((0, 0), (0, padded - rows), (0, 0))
    ).reshape(devices * padded, tokens)
    hidden = inputs + mm(mixed_pieces, out_pieces, ((0,), (0,)))
    scale_two = lax.rsqrt(jnp.mean(hidden * hidden, axis=-1, keepdims=True) + NORM_EPS)
    normed_two = (hidden * scale_two * gain_second).astype(BF16)

    normed_two, down_part = lax.optimization_barrier((normed_two, down_part))
    w_down = down_part.reshape(fblock, D)
    normed = from_ctx(normed_two)
    out_pieces, _ = lax.optimization_barrier((out_pieces, normed_two))
    w_out = out_pieces.reshape(devices, padded, D)[:, :rows].reshape(QD, D)
    cot = from_ctx(cot_here, cot_far)
    kept, near_parts = feed_forward(normed[:2], cot[:2], w_wide, w_down, n_ctx, None)
    (far_x, far_dy), momentum_flat, kept = lax.optimization_barrier(
        ((normed[2], cot[2]), momentum_flat, kept)
    )
    old_qkv, old_out, old_pair, old_down = pack(momentum_flat, None, devices, 1, F32)
    old_pair = lax.all_to_all(old_pair, BOTH, split_axis=0, concat_axis=0, tiled=True)
    kept, far_parts = feed_forward(
        (far_x, swap(far_x, core_bit, devices)),
        (far_dy, swap(far_dy, core_bit, devices)),
        w_wide,
        w_down,
        n_ctx,
        kept,
    )
    acts, both_backs, normed_all, cot_all = kept

    def to_ctx(near, far):
        crossed = swap(far[1], core_bit, devices)
        far = (far[0].astype(F32) + crossed.astype(F32)).astype(BF16)
        crossed = swap(near[1], core_bit, devices)
        near = near[0].astype(F32) + crossed.astype(F32)
        return near + swap(far, x_bit, devices).astype(F32), far

    normed_two_grad, ready = to_ctx(near_parts, far_parts)
    (acts, both_backs), old_pair, ready = lax.optimization_barrier(
        ((acts, both_backs), old_pair, ready)
    )

    dp_shape = tuple([2] * len(dp_bits)) + (frows, D)
    dp_order = dp_bits[1:] + dp_bits[:1]
    down_value = mm(acts, cot_all, ((0,), (0,))).astype(BF16)
    both_value = mm(both_backs, normed_all, ((0,), (0,))).astype(BF16)
    values = [both_value[:fblock], both_value[fblock:], down_value]
    orders = [dp_bits, dp_order, dp_bits]
    started = []
    for index in (2, 1, 0):
        sent, kept = scatter_split(values[index].reshape(dp_shape), dp_bits, orders[index][0], me)
        started.insert(0, (kept, swap(sent, orders[index][0], devices)))

    out_grad = cot_here.astype(F32)
    hidden_norm_grad, grad_gain_second = norm_backward(
        hidden, scale_two, gain_second, normed_two_grad
    )
    hidden_grad = out_grad + hidden_norm_grad
    hidden_low = hidden_grad.astype(BF16)
    heads_grad = mm(w_out, hidden_low, ((1,), (1,))).astype(BF16).reshape(HEADS, HD, tokens)
    delta = jnp.sum(heads_grad.astype(F32) * attended, axis=1, keepdims=True)
    grad_output = mm(mixed_pieces, hidden_low)
    query_grads, kv_parts = [], []
    sent, kept = scatter_split(
        grad_output.astype(BF16).reshape(many + (padded, D)), all_bits, all_bits[0], me
    )
    wide_parts = started + [(kept, swap(sent, all_bits[0], devices))]
    wide_orders = [list(order) for order in orders] + [list(all_bits)]
    steps = [[2, 1, 3], [0, 3], [2, 1, 3], [0, 3]]
    shares = [4, 3]
    ready = [sent]
    for index in range(KVH):
        kv_one = pair_of_heads(kv, index)
        kv_grad = None
        begin = index * group
        for count in shares:
            chosen = slice(begin, begin + count)
            begin += count
            query_part, ready = lax.optimization_barrier((queries[chosen], ready))
            query_grad, kv_grad = attend_back(
                info, kv_one, query_part, heads_grad[chosen], log_total[chosen], delta[chosen], kv_grad
            )
            query_grads.append(query_grad)
            ready = []
            if len(steps) == 3:
                acts, _ = lax.optimization_barrier((acts, query_grad))
                out_part = mm(acts, w_down).astype(BF16).reshape(n_ctx, span, D)
                out_sum, _ = to_ctx((out_part[0], out_part[1]), (out_part[2], out_part[3]))
                layer_out = jnp.where(live, hidden + out_sum, 0.0).astype(BF16)
            if len(steps) == 2:
                ready.append(layer_out)
            for which in steps.pop(0):
                order = wide_orders[which]
                parts, _ = lax.optimization_barrier((wide_parts[which], query_grad))
                order.pop(0)
                sent, kept = scatter_split(scatter_end(parts), order, order[0], me)
                ready.append(sent)
                wide_parts[which] = (kept, swap(sent, order[0], devices))
        kv_parts.append(
            scatter_sum(kv_grad.reshape(2, 2, 2 * HD, span), ctx_bits, me, devices)
        )
    kv_grads = [part.astype(F32).reshape(2, HD, span) for part in kv_parts]
    qk_grad = jnp.concatenate(query_grads + [grad[:1] for grad in kv_grads], axis=0)
    qk_back = rotate_back(qk_grad, cosine, sine_part).reshape(QD + KVD, tokens)
    qkv_back = jnp.concatenate(
        [qk_back] + [grad[1] for grad in kv_grads], axis=0
    ).astype(BF16)
    grad_qkv = mm(back_one, qkv_back, ((1,), (1,)))
    grad_bias = jnp.sum(qkv_back.astype(F32), axis=1)
    normed_one_grad = mm(qkv_back, w_qkv, ((0,), (1,)))
    input_norm_grad, grad_gain_first = norm_backward(inputs, scale_one, gain_first, normed_one_grad)
    input_grad = (hidden_grad + input_norm_grad).astype(BF16).reshape(slots, span, width)

    vector_part = join_small(
        [
            grad_gain_first,
            grad_gain_second,
            grad_bias[:QD],
            grad_bias[QD : QD + KVD],
            grad_bias[QD + KVD :],
        ],
        devices,
    )
    vector_rows = lax.all_to_all(vector_part, BOTH, split_axis=0, concat_axis=0, tiled=True)
    here_core = jnp.where((me & core_bit) != 0, 1, 0)
    here_x = jnp.where((me & x_bit) != 0, 1, 0)
    left = list(all_bits)
    qkv_order = [core_bit, dp_bits[0], x_bit] + dp_bits[1:]
    sent, kept = scatter_split(
        grad_qkv.astype(BF16).reshape(many + (padded, qkv)), left, core_bit, me
    )
    wide_parts, sent = lax.optimization_barrier((wide_parts, sent))
    qkv_parts = (kept, swap(sent, core_bit, devices))
    left.remove(core_bit)
    gate_sum, up_sum, down_sum, out_sum_rows = [
        scatter_sum(scatter_end(parts), order[1:], me, devices)
        for parts, order in zip(wide_parts, wide_orders)
    ]
    mats = combine(old_pair, gate_sum, up_sum, old_down, down_sum, old_out, out_sum_rows)
    mats = mats.reshape(2, 2, frows, D)
    row_parts = (choose(mats, here_core, 1), swap(choose(mats, 1 - here_core, 1), core_bit, devices))
    count = len(block_pairs(D // BLOCK))
    places = (count + n_dp - 1) // n_dp * n_dp
    dp_many = tuple([2] * len(dp_bits))
    gram_left = list(dp_bits)
    for step, bit in enumerate(qkv_order[1:]):
        qkv_parts, row_parts = lax.optimization_barrier((qkv_parts, row_parts))
        sent, kept = scatter_split(scatter_end(qkv_parts), left, bit, me)
        left.remove(bit)
        qkv_parts = (kept, swap(sent, bit, devices))
        if step == 0:
            mats = jnp.stack(row_parts, axis=1)
            row_parts = (choose(mats, here_x, 0), swap(choose(mats, 1 - here_x, 0), x_bit, devices))
            continue
        if step == 1:
            owned = jnp.stack(row_parts).reshape(n_ctx * frows, D)
            gram = gram_blocks(owned, places).reshape(dp_many + (places // n_dp, BLOCK, BLOCK))
        else:
            gram = scatter_end(row_parts)
        sent, kept = scatter_split(gram, gram_left, gram_left[0], me)
        row_parts = (kept, swap(sent, gram_left.pop(0), devices))
    qkv_parts, row_parts = lax.optimization_barrier((qkv_parts, row_parts))
    qkv_sum_rows = scatter_end(qkv_parts)
    moved_qkv = MOMENTUM_DECAY * old_qkv + qkv_sum_rows.astype(F32)
    moved_low = moved_qkv.astype(BF16)
    qkv_all = lax.all_gather(moved_low, BOTH, axis=0, tiled=True)
    gram = gather_bits(scatter_end(row_parts), dp_bits[::-1], me, devices)
    gram = gram.reshape(places, BLOCK, BLOCK)

    (gate_sum, up_sum), moved_low, vector_rows, gram = lax.optimization_barrier(
        ((gate_sum, up_sum), moved_low, vector_rows, gram)
    )
    pair_rows = to_rows(gate_sum, up_sum)
    ortho = orthogonal_wide(gram, owned).reshape(2, 2, frows, D)
    ortho, pair_rows = lax.optimization_barrier((ortho, pair_rows))
    ortho = from_owner(ortho, core_bit, x_bit, me, devices).reshape(n_ctx, frows, D)
    turned = turn(ortho[0], ortho[1], devices)
    momentum_flat, turned = lax.optimization_barrier((momentum_flat, turned))
    ortho_pair = lax.all_to_all(turned, BOTH, split_axis=0, concat_axis=0, tiled=True)
    ortho_qkv = orthogonal_whole(qkv_all, moved_qkv, (QD, KVD, KVD))
    new_momentum = update(
        momentum_flat,
        qkv_sum_rows,
        out_sum_rows,
        pair_rows,
        down_sum,
        devices,
        MOMENTUM_DECAY,
        [1.0] * 7,
    ).reshape(momentum.shape)

    factors = [
        -MUON_RATE * math.sqrt(max(1.0, breadth / height)) for height, breadth in matrix_shapes()
    ]
    new_master = update(
        master_flat,
        ortho_qkv,
        ortho[3, :padded],
        ortho_pair,
        ortho[2],
        devices,
        1.0 - MUON_RATE * MUON_DECAY,
        factors,
    ).reshape(master.shape)
    vector_grad = jnp.sum(vector_rows, axis=0, keepdims=True)
    first_new = BETA_FIRST * vector_first + (1.0 - BETA_FIRST) * vector_grad
    second_new = BETA_SECOND * vector_second + (1.0 - BETA_SECOND) * vector_grad * vector_grad
    adjusted = (
        first_new
        / (1.0 - BETA_FIRST**STEP)
        / (jnp.sqrt(second_new / (1.0 - BETA_SECOND**STEP)) + ADAM_EPS)
    )
    new_vectors = vectors - ADAM_RATE * adjusted
    return (
        layer_out.reshape(slots, span, width),
        input_grad,
        new_master,
        new_momentum,
        new_master.astype(BF16),
        new_vectors,
        first_new,
        second_new,
    )


def solution(mesh):
    return jax.shard_map(
        on_device,
        mesh=mesh,
        in_specs=(
            P("dp", "ctx", None),
            P("dp", "ctx", None),
            P("dp"),
            P("dp"),
            P(BOTH, None),
            P(BOTH, None),
            P(BOTH, None),
            P(BOTH, None),
            P(BOTH, None),
        ),
        out_specs=(
            P("dp", "ctx", None),
            P("dp", "ctx", None),
            P(BOTH, None),
            P(BOTH, None),
            P(BOTH, None),
            P(BOTH, None),
            P(BOTH, None),
            P(BOTH, None),
        ),
        check_vma=False,
    )
```

```python
import math

import jax
import jax.numpy as jnp
from jax import lax
from jax.experimental import pallas as pl
from jax.experimental.pallas import tpu as pltpu
from jax.sharding import PartitionSpec as P

D = 896
HEADS = 14
KVH = 2
HD = 64
FF = 4864
SLOT = 2048
NS_STEPS = 3
STEP = 10
QD = 896
KVD = 128

NORM_EPS = 1e-06
ROPE_BASE = 1000000.0
NS_LINEAR = 3.4445
NS_SQUARE = -4.775
NS_CUBIC = 2.0315
MOMENTUM_DECAY = 0.5
MUON_RATE = 0.6
MUON_DECAY = 0.1
ADAM_RATE = 0.2
BETA_FIRST = 0.9
BETA_SECOND = 0.95
ADAM_EPS = 1e-08
MASK_FLOOR = -1e30

F32 = jnp.float32
BF16 = jnp.bfloat16
BOTH = ("dp", "ctx")
LANES = 128


def matrix_shapes():
    return [(D, QD), (D, KVD), (D, KVD), (QD, D), (D, FF), (D, FF), (FF, D)]


def vector_sizes():
    return [D, D, QD, KVD, KVD]


def mm(left, right, contract=((1,), (0,))):
    return lax.dot_general(left, right, (contract, ((), ())), preferred_element_type=F32)


def split_small(flat, devices):
    result = []
    offset = 0
    for extent_all in vector_sizes():
        extent = extent_all // devices
        result.append(flat[:, offset : offset + extent].reshape(extent_all))
        offset += extent
    return result


def join_small(pieces, devices):
    return jnp.concatenate([piece.reshape(devices, -1) for piece in pieces], axis=1)


def swap(value, mask, devices):
    return lax.ppermute(value, BOTH, [(index, index ^ mask) for index in range(devices)])


def gather_bits(value, bits, me, devices, before=()):
    held = value
    done = list(before)
    for bit in bits:
        place = sum(1 for other in done if other > bit)
        got = swap(held, bit, devices)
        mine = (me & bit) != 0
        held = jnp.where(
            mine, jnp.stack([got, held], axis=place), jnp.stack([held, got], axis=place)
        )
        done.append(bit)
    return held


def scatter_split(held, left, bit, me, lead=0):
    axis = sorted(left, reverse=True).index(bit) + lead
    mine = jnp.where((me & bit) != 0, 1, 0)
    return choose(held, 1 - mine, axis).astype(BF16), choose(held, mine, axis)


def scatter_start(held, left, bit, me, devices):
    sent, kept = scatter_split(held, left, bit, me)
    return kept, swap(sent, bit, devices)


def scatter_end(parts):
    return (parts[0].astype(F32) + parts[1].astype(F32)).astype(BF16)


def scatter_sum(value, bits, me, devices):
    left = list(bits)
    held = value
    for bit in bits:
        held = scatter_end(scatter_start(held, left, bit, me, devices))
        left.remove(bit)
    return held


def choose(value, mine, axis):
    return lax.dynamic_index_in_dim(value, mine, axis, keepdims=False)


def rotate(values, cosine, sine_part):
    midpoint = HD // 2
    turned = jnp.concatenate([-values[:, midpoint:], values[:, :midpoint]], axis=1)
    return values * cosine + turned * sine_part


def rotate_back(gradient, cosine, sine_part):
    midpoint = HD // 2
    scaled = gradient * sine_part
    turned = jnp.concatenate([scaled[:, midpoint:], -scaled[:, :midpoint]], axis=1)
    return gradient * cosine + turned


def norm_backward(source, scale_row, gain, incoming):
    gain_grad = jnp.sum(incoming * source * scale_row, axis=0)
    weighted = incoming * gain
    result = scale_row * weighted - source * scale_row**3 * jnp.mean(
        weighted * source, axis=-1, keepdims=True
    )
    return (result, gain_grad)


def halves_of(span):
    return [slice(0, span // 2), slice(span // 2, span)]


def fill_mask(info, mask, chunk, span):
    key = chunk * span + lax.broadcasted_iota(jnp.int32, (span, span), 0)
    query = info[0] * span + lax.broadcasted_iota(jnp.int32, (span, span), 1)
    key_doc = (key >= info[2]).astype(jnp.int32) + (key >= info[1]).astype(jnp.int32)
    query_doc = (query >= info[2]).astype(jnp.int32) + (query >= info[1]).astype(jnp.int32)
    allowed = jnp.logical_and(key_doc == query_doc, key <= query)
    mask[chunk] = jnp.where(allowed, 0.0, MASK_FLOOR).astype(F32)


def attend_kernel(info, kv, q, out, lse, keys, mask, best, total, acc):
    head = pl.program_id(0)
    span = q.shape[-1]
    mine = info[0]
    chunks = mine + 1

    @pl.when(head == 0)
    def _():
        def fill(chunk, carry):
            slot = jnp.bitwise_xor(chunk, mine)
            keys[chunk] = kv[slot, :HD, :].astype(F32).T.astype(BF16)
            fill_mask(info, mask, chunk, span)
            return carry

        lax.fori_loop(0, chunks, fill, 0)

    best[...] = jnp.full(best.shape, MASK_FLOOR, F32)
    total[...] = jnp.zeros(total.shape, F32)
    acc[...] = jnp.zeros(acc.shape, F32)
    queries = q[0]

    def step(index, carry):
        chunk = mine - index
        slot = jnp.bitwise_xor(chunk, mine)
        scores = jnp.dot(keys[chunk], queries, preferred_element_type=F32) + mask[chunk]
        old = best[...]
        new = jnp.maximum(old, jnp.max(scores, axis=0, keepdims=True))
        present = jnp.exp(scores - new)
        shrink = jnp.exp(old - new)
        best[...] = new
        total[...] = total[...] * shrink + jnp.sum(present, axis=0, keepdims=True)
        acc[...] = acc[...] * shrink + jnp.dot(
            kv[slot, HD:, :], present.astype(BF16), preferred_element_type=F32
        )
        return carry

    lax.fori_loop(0, chunks, step, 0)
    out[0] = acc[...] / total[...]
    lse[0] = best[...] + jnp.log(total[...])


def attend_back_kernel(
    info, kv, q, dout, lse, delta, before, dq, dkv, keys, values, mask, dk, dv, acc
):
    head = pl.program_id(0)
    span = q.shape[-1]
    mine = info[0]
    chunks = mine + 1
    n_ctx = kv.shape[0]

    @pl.when(head == 0)
    def _():
        dk[...] = jnp.zeros(dk.shape, F32)
        dv[...] = jnp.zeros(dv.shape, F32)

        def fill(chunk, carry):
            slot = jnp.bitwise_xor(chunk, mine)
            keys[chunk] = kv[slot, :HD, :].astype(F32).T.astype(BF16)
            values[chunk] = kv[slot, HD:, :].astype(F32).T.astype(BF16)
            fill_mask(info, mask, chunk, span)
            return carry

        lax.fori_loop(0, chunks, fill, 0)

    acc[...] = jnp.zeros(acc.shape, F32)
    queries = q[0]
    douts = dout[0]
    query_rows = queries.astype(F32).T.astype(BF16)
    dout_rows = douts.astype(F32).T.astype(BF16)

    def step(chunk, carry):
        slot = jnp.bitwise_xor(chunk, mine)
        value_sum, key_sum = dv[chunk], dk[chunk]
        for lanes in halves_of(span):
            scores = (
                jnp.dot(keys[chunk], queries[:, lanes], preferred_element_type=F32)
                + mask[chunk, :, lanes]
            )
            shares = jnp.exp(scores - lse[0, :, lanes])
            share_grad = jnp.dot(values[chunk], douts[:, lanes], preferred_element_type=F32)
            score_grad = (shares * (share_grad - delta[0, :, lanes])).astype(BF16)
            value_sum += jnp.dot(
                shares.astype(BF16), dout_rows[lanes, :], preferred_element_type=F32
            )
            key_sum += jnp.dot(score_grad, query_rows[lanes, :], preferred_element_type=F32)
            acc[:, lanes] += jnp.dot(kv[slot, :HD, :], score_grad, preferred_element_type=F32)
        dv[chunk], dk[chunk] = value_sum, key_sum
        return carry

    lax.fori_loop(0, chunks, step, 0)
    dq[0] = acc[...] * HD ** (-0.5)

    @pl.when(head == pl.num_programs(0) - 1)
    def _():
        for chunk in range(n_ctx):
            sums = jnp.concatenate([dk[chunk].T, dv[chunk].T], axis=0)
            if before is not None:
                sums += before[chunk].astype(F32)
            dkv[chunk] = sums.astype(BF16)


def attend(info, kv, q):
    heads, _, span = q.shape
    n_ctx = kv.shape[0]
    per_head = lambda rows: pl.BlockSpec((1, rows, span), lambda head: (head, 0, 0))
    return pl.pallas_call(
        attend_kernel,
        grid=(heads,),
        in_specs=[
            pl.BlockSpec(memory_space=pltpu.SMEM),
            pl.BlockSpec(kv.shape, lambda head: (0, 0, 0)),
            per_head(HD),
        ],
        out_specs=[per_head(HD), per_head(1)],
        out_shape=[
            jax.ShapeDtypeStruct((heads, HD, span), F32),
            jax.ShapeDtypeStruct((heads, 1, span), F32),
        ],
        scratch_shapes=[
            pltpu.VMEM((n_ctx, span, HD), BF16),
            pltpu.VMEM((n_ctx, span, span), F32),
            pltpu.VMEM((1, span), F32),
            pltpu.VMEM((1, span), F32),
            pltpu.VMEM((HD, span), F32),
        ],
        compiler_params=pltpu.CompilerParams(vmem_limit_bytes=40 * 1024 * 1024),
        cost_estimate=pl.CostEstimate(
            flops=4 * heads * span * span * n_ctx * HD * 4,
            bytes_accessed=4 * heads * span * HD * 2,
            transcendentals=heads * span * span * n_ctx,
        ),
        name="attend",
    )(info, kv, q)


def attend_back(info, kv, q, dout, lse, delta, before):
    heads, _, span = q.shape
    n_ctx = kv.shape[0]
    per_head = lambda rows: pl.BlockSpec((1, rows, span), lambda head: (head, 0, 0))
    whole = pl.BlockSpec(kv.shape, lambda head: (0, 0, 0))
    if before is None:
        body = lambda *refs: attend_back_kernel(*refs[:6], None, *refs[6:])
    else:
        body = attend_back_kernel
    return pl.pallas_call(
        body,
        grid=(heads,),
        in_specs=[
            pl.BlockSpec(memory_space=pltpu.SMEM),
            whole,
            per_head(HD),
            per_head(HD),
            per_head(1),
            per_head(1),
        ]
        + [whole] * (before is not None),
        out_specs=[per_head(HD), whole],
        out_shape=[
            jax.ShapeDtypeStruct((heads, HD, span), F32),
            jax.ShapeDtypeStruct(kv.shape, BF16),
        ],
        scratch_shapes=[
            pltpu.VMEM((n_ctx, span, HD), BF16),
            pltpu.VMEM((n_ctx, span, HD), BF16),
            pltpu.VMEM((n_ctx, span, span), F32),
            pltpu.VMEM((n_ctx, span, HD), F32),
            pltpu.VMEM((n_ctx, span, HD), F32),
            pltpu.VMEM((HD, span), F32),
        ],
        compiler_params=pltpu.CompilerParams(vmem_limit_bytes=40 * 1024 * 1024),
        cost_estimate=pl.CostEstimate(
            flops=10 * heads * span * span * n_ctx * HD * 4,
            bytes_accessed=8 * heads * span * HD * 2,
            transcendentals=heads * span * span * n_ctx,
        ),
        name="attend_back",
    )(*[info, kv, q, dout, lse, delta] + [before] * (before is not None))


def forward_backward_kernel(
    x0, x1, dy0, dy1, wide, down, act_out, both_out, x_out, dy_out, back0, back1
):
    first = pl.program_id(0) == 0
    units = down.shape[0]
    x = jnp.where(first, x0[...], x1[...])
    dy = jnp.where(first, dy0[...], dy1[...])
    x_out[...] = x
    dy_out[...] = dy
    both = jnp.dot(x, wide[...], preferred_element_type=F32)
    gate_pre = both[:, :units]
    up_pre = both[:, units:]
    grad_act = mm(dy, down[...], ((1,), (1,)))
    sigmoid_gate = jax.nn.sigmoid(gate_pre)
    swish = gate_pre * sigmoid_gate
    slope = sigmoid_gate * (1.0 + gate_pre * (1.0 - sigmoid_gate))
    act_out[...] = (swish * up_pre).astype(BF16)
    both_back = jnp.concatenate([grad_act * up_pre * slope, grad_act * swish], axis=1).astype(BF16)
    both_out[...] = both_back
    back = mm(both_back, wide[...], ((1,), (1,))).astype(BF16)

    @pl.when(first)
    def _():
        back0[...] = back

    @pl.when(jnp.logical_not(first))
    def _():
        back1[...] = back


def feed_forward(x, dy, wide, down, blocks, earlier):
    span, width = x[0].shape
    units = down.shape[0]
    first = 0 if earlier is None else 2
    whole = lambda shape: pl.BlockSpec(
        shape, lambda block: (0, 0), pipeline_mode=pl.Buffered(1)
    )
    line = lambda columns: pl.BlockSpec((span, columns), lambda block: (block + first, 0))
    columns = [units, 2 * units, width, width]
    shapes = [jax.ShapeDtypeStruct((blocks * span, count), BF16) for count in columns]
    in_specs = [whole((span, width))] * 4 + [whole((width, 2 * units)), whole((units, width))]
    operands = [*x, *dy, wide, down]
    aliases = {}
    body = forward_backward_kernel
    if earlier is not None:
        in_specs += [pl.BlockSpec(memory_space=pl.ANY)] * 4
        operands += list(earlier)
        aliases = {6 + index: index for index in range(4)}
        body = lambda *refs: forward_backward_kernel(*refs[:6], *refs[10:])
    back = pl.BlockSpec((span, width), lambda block: (0, 0))
    results = pl.pallas_call(
        body,
        grid=(2,),
        in_specs=in_specs,
        out_specs=[line(count) for count in columns] + [back, back],
        out_shape=shapes + [jax.ShapeDtypeStruct((span, width), BF16)] * 2,
        input_output_aliases=aliases,
        compiler_params=pltpu.CompilerParams(vmem_limit_bytes=60 * 1024 * 1024),
        cost_estimate=pl.CostEstimate(
            flops=20 * span * width * units,
            bytes_accessed=6 * width * units + 2 * span * 10 * width,
            transcendentals=2 * span * units,
        ),
        name="feed_forward",
    )(*operands)
    return results[:4], results[4:]


BLOCK = 128


def block_pairs(count):
    return [(low, high) for low in range(count) for high in range(low, count)]


def gram_kernel(rows, out):
    count = rows.shape[1] // BLOCK
    place = 0
    for low in range(count):
        line = lax.dot_general(
            rows[:, low * BLOCK : (low + 1) * BLOCK],
            rows[:, low * BLOCK :],
            (((0,), (0,)), ((), ())),
            preferred_element_type=F32,
        ).astype(BF16)
        for high in range(low, count):
            out[place] = line[:, (high - low) * BLOCK : (high - low + 1) * BLOCK]
            place += 1
    for extra in range(place, out.shape[0]):
        out[extra] = jnp.zeros((BLOCK, BLOCK), BF16)


def gram_blocks(rows, places):
    return pl.pallas_call(
        gram_kernel,
        out_shape=jax.ShapeDtypeStruct((places, BLOCK, BLOCK), BF16),
        compiler_params=pltpu.CompilerParams(vmem_limit_bytes=32 * 1024 * 1024),
        name="gram",
    )(rows)


def newton_schulz(gram, low, poly, mixed, rows):
    size = gram.shape[0]
    part = size // 2 if size % 16 == 0 and size > BLOCK else size
    parts = [pl.ds(begin, part) for begin in range(0, size, part)]
    row_id = lax.broadcasted_iota(jnp.int32, (size, size), 0)
    column_id = lax.broadcasted_iota(jnp.int32, (size, size), 1)
    square = jnp.where(row_id == column_id, gram[...], 0.0)
    square = jnp.sum(jnp.sum(square, axis=0, keepdims=True), axis=1, keepdims=True)
    scale = 1.0 / (jnp.sqrt(square) + 1e-07)
    for place in parts:
        scaled = gram[place, :] * (scale * scale)
        gram[place, :] = scaled
        low[place, :] = scaled.astype(BF16)
    work = (rows * scale).astype(BF16)
    for step in range(NS_STEPS):
        for place in parts:
            second = jnp.dot(low[place, :], low[...], preferred_element_type=F32)
            poly[place, :] = (NS_SQUARE * gram[place, :] + NS_CUBIC * second).astype(BF16)
        moved = jnp.dot(work, poly[...], preferred_element_type=F32)
        work = (NS_LINEAR * work.astype(F32) + moved).astype(BF16)
        if step + 1 < NS_STEPS:
            for place in parts:
                first = jnp.dot(poly[place, :], low[...], preferred_element_type=F32)
                mixed[place, :] = first.astype(BF16)
                gram[place, :] = (
                    NS_LINEAR * NS_LINEAR * gram[place, :] + (2.0 * NS_LINEAR) * first
                )
            for place in parts:
                second = jnp.dot(poly[place, :], mixed[...], preferred_element_type=F32)
                renewed = gram[place, :] + second
                gram[place, :] = renewed
                low[place, :] = renewed.astype(BF16)
    return work


def wide_kernel(blocks, rows, out, gram, low, poly, mixed):
    for place, (first, second) in enumerate(block_pairs(gram.shape[0] // BLOCK)):
        tile = blocks[place].astype(F32)
        gram[first * BLOCK : (first + 1) * BLOCK, second * BLOCK : (second + 1) * BLOCK] = tile
        if first != second:
            gram[second * BLOCK : (second + 1) * BLOCK, first * BLOCK : (first + 1) * BLOCK] = tile.T
    out[...] = newton_schulz(gram, low, poly, mixed, rows[...].astype(F32))


def square_scratch(size):
    return [
        pltpu.VMEM((size, size), F32),
        pltpu.VMEM((size, size), BF16),
        pltpu.VMEM((size, size), BF16),
        pltpu.VMEM((size, size), BF16),
    ]


def orthogonal_wide(blocks, rows):
    return pl.pallas_call(
        wide_kernel,
        out_shape=jax.ShapeDtypeStruct(rows.shape, BF16),
        scratch_shapes=square_scratch(rows.shape[1]),
        compiler_params=pltpu.CompilerParams(vmem_limit_bytes=40 * 1024 * 1024),
        cost_estimate=pl.CostEstimate(
            flops=14 * rows.shape[1] ** 3, bytes_accessed=4 * rows.size, transcendentals=0
        ),
        name="newton_wide",
    )(blocks, rows)


def whole_kernel(widths, whole, rows, out, *scratch):
    begin = 0
    for index, width in enumerate(widths):
        gram, low, poly, mixed = scratch[4 * index : 4 * index + 4]
        for first in range(0, width, BLOCK):
            gram[first : first + BLOCK, :] = lax.dot_general(
                whole[:, begin + first : begin + first + BLOCK],
                whole[:, begin : begin + width],
                (((0,), (0,)), ((), ())),
                preferred_element_type=F32,
            )
        out[:, begin : begin + width] = newton_schulz(
            gram, low, poly, mixed, rows[:, begin : begin + width]
        )
        begin += width


def orthogonal_whole(whole, rows, widths):
    scratch = []
    for width in widths:
        scratch += square_scratch(width)
    return pl.pallas_call(
        lambda *refs: whole_kernel(widths, *refs),
        out_shape=jax.ShapeDtypeStruct(rows.shape, BF16),
        scratch_shapes=scratch,
        compiler_params=pltpu.CompilerParams(vmem_limit_bytes=48 * 1024 * 1024),
        cost_estimate=pl.CostEstimate(
            flops=16 * sum(width**3 for width in widths),
            bytes_accessed=2 * whole.size,
            transcendentals=0,
        ),
        name="newton_whole",
    )(whole, rows)


def from_flat(flat, base, target, height, breadth):
    lines = breadth // LANES
    for begin in range(0, height, 8):
        count = min(8, height - begin)
        for index in range(lines):
            start = base + begin * lines + index
            if lines == 1:
                tile = flat[start : start + count, :]
            else:
                tile = flat[pl.ds(start, count, stride=lines), :]
            target[begin : begin + count, index * LANES : (index + 1) * LANES] = tile


def to_flat(flat, base, value, height, breadth):
    lines = breadth // LANES
    for begin in range(0, height, 8):
        count = min(8, height - begin)
        for index in range(lines):
            start = base + begin * lines + index
            tile = value(slice(begin, begin + count), slice(index * LANES, (index + 1) * LANES))
            if lines == 1:
                flat[start : start + count, :] = tile
            else:
                flat[pl.ds(start, count, stride=lines), :] = tile


def section_bases(devices):
    bases = []
    base = 0
    for height, breadth in matrix_shapes():
        bases.append(base)
        base += height // devices * breadth // LANES
    return bases


def pack_kernel(devices, group, flat, extra, qkv_out, out_out, wide_out, down_out, qkv, out, wide, down):
    rows = D // devices
    frows = FF // devices
    bases = section_bases(devices)
    qkv[...] = jnp.zeros(qkv.shape, F32)
    out[...] = jnp.zeros(out.shape, F32)
    from_flat(flat, bases[0], qkv.at[:, :QD], rows, QD)
    from_flat(flat, bases[1], qkv.at[:, QD : QD + KVD], rows, KVD)
    from_flat(flat, bases[2], qkv.at[:, QD + KVD :], rows, KVD)
    if extra is not None:
        qkv[rows : rows + 1, :LANES] = extra[...]
    from_flat(flat, bases[3], out, rows, D)
    from_flat(flat, bases[6], down, FF // devices, D)
    qkv_out[...] = qkv[...].astype(qkv_out.dtype)
    out_out[...] = out[...].astype(out_out.dtype)
    down_out[...] = down[...].astype(down_out.dtype)
    for which in range(2):
        from_flat(flat, bases[4 + which], wide, rows, FF)
        targets = devices // group
        for target in range(targets):
            piece = jnp.concatenate(
                [
                    wide[:, (turn * targets + target) * frows : (turn * targets + target + 1) * frows]
                    for turn in range(group)
                ],
                axis=1,
            )
            width = group * frows
            wide_out[target, :, which * width : (which + 1) * width] = piece.astype(wide_out.dtype)


def pack(flat, extra, devices, group, dtype):
    rows = D // devices
    frows = FF // devices
    padded = (rows // 16 + 1) * 16
    targets = devices // group
    wide = (targets, rows, 2 * group * frows)
    shapes = [(padded, QD + 2 * KVD), (padded, D), wide, (frows, D)]
    types = [dtype, dtype, BF16, dtype]
    if extra is None:
        body = lambda flat_ref, *refs: pack_kernel(devices, group, flat_ref, None, *refs)
        operands = [flat]
    else:
        body = lambda *refs: pack_kernel(devices, group, *refs)
        operands = [flat, extra]
    return pl.pallas_call(
        body,
        out_shape=[jax.ShapeDtypeStruct(shape, kind) for shape, kind in zip(shapes, types)],
        scratch_shapes=[
            pltpu.VMEM((padded, QD + 2 * KVD), F32),
            pltpu.VMEM((padded, D), F32),
            pltpu.VMEM((rows, FF), F32),
            pltpu.VMEM((frows, D), F32),
        ],
        compiler_params=pltpu.CompilerParams(vmem_limit_bytes=32 * 1024 * 1024),
        cost_estimate=pl.CostEstimate(flops=0, bytes_accessed=6 * flat.size, transcendentals=0),
        name="pack",
    )(*operands)


def update_kernel(devices, decay, factors, flat, qkv, out, wide, down, result, moved, rows_wide):
    rows = D // devices
    frows = FF // devices
    bases = section_bases(devices)
    whole = qkv[...].astype(F32)
    out_whole = out[...].astype(F32)
    down_whole = down[...].astype(F32)
    parts = [
        lambda r, c: whole[r, c],
        lambda r, c: whole[r, slice(QD + c.start, QD + c.stop)],
        lambda r, c: whole[r, slice(QD + KVD + c.start, QD + KVD + c.stop)],
        lambda r, c: out_whole[r, c],
    ]
    shapes = matrix_shapes()
    for index, part in enumerate(parts):
        to_flat(
            moved, bases[index], lambda r, c: part(r, c) * factors[index], rows, shapes[index][1]
        )
    to_flat(moved, bases[6], lambda r, c: down_whole[r, c] * factors[6], frows, D)
    for which in range(2):
        for source in range(devices):
            rows_wide[:, source * frows : (source + 1) * frows] = wide[
                source, :, which * frows : (which + 1) * frows
            ].astype(F32)
        to_flat(
            moved, bases[4 + which], lambda r, c: rows_wide[r, c] * factors[4 + which], rows, FF
        )
    result[...] = decay * flat[...] + moved[...]


def update(flat, qkv, out, wide, down, devices, decay, factors):
    return pl.pallas_call(
        lambda *refs: update_kernel(devices, decay, factors, *refs),
        out_shape=jax.ShapeDtypeStruct(flat.shape, F32),
        scratch_shapes=[
            pltpu.VMEM(flat.shape, F32),
            pltpu.VMEM((D // devices, FF), F32),
        ],
        compiler_params=pltpu.CompilerParams(vmem_limit_bytes=32 * 1024 * 1024),
        cost_estimate=pl.CostEstimate(flops=0, bytes_accessed=10 * flat.size, transcendentals=0),
        name="update",
    )(flat, qkv, out, wide, down)


def combine_kernel(old_pair, gate, up, old_down, down, old_out, out, mats, lines):
    devices, rows, _ = old_pair.shape
    frows = gate.shape[0]
    padded = out.shape[0]
    lines[...] = jnp.zeros(lines.shape, F32)
    for source in range(devices):
        lines[source * rows : (source + 1) * rows, : 2 * frows] = old_pair[source].astype(F32)
    old = lines[...].T
    mats[0] = (MOMENTUM_DECAY * old[:frows] + gate[...].astype(F32)).astype(BF16)
    mats[1] = (MOMENTUM_DECAY * old[frows : 2 * frows] + up[...].astype(F32)).astype(BF16)
    mats[2] = (MOMENTUM_DECAY * old_down[...] + down[...].astype(F32)).astype(BF16)
    last = MOMENTUM_DECAY * old_out[...] + out[...].astype(F32)
    mats[3] = jnp.concatenate(
        [last, jnp.zeros((frows - padded, last.shape[1]), F32)], axis=0
    ).astype(BF16)


def combine(old_pair, gate, up, old_down, down, old_out, out):
    frows, width = gate.shape
    return pl.pallas_call(
        combine_kernel,
        out_shape=jax.ShapeDtypeStruct((4, frows, width), BF16),
        scratch_shapes=[pltpu.VMEM((width, -(-2 * frows // LANES) * LANES), F32)],
        compiler_params=pltpu.CompilerParams(vmem_limit_bytes=32 * 1024 * 1024),
        name="combine",
    )(old_pair, gate, up, old_down, down, old_out, out)


def turn_kernel(gate, up, out, columns):
    devices, rows, _ = out.shape
    frows = gate.shape[0]
    columns[...] = jnp.zeros(columns.shape, F32)
    columns[:frows] = gate[...].astype(F32)
    columns[frows : 2 * frows] = up[...].astype(F32)
    lines = columns[...].T
    for target in range(devices):
        out[target] = lines[target * rows : (target + 1) * rows, : 2 * frows].astype(BF16)


def turn(gate, up, devices):
    frows, width = gate.shape
    return pl.pallas_call(
        turn_kernel,
        out_shape=jax.ShapeDtypeStruct((devices, width // devices, 2 * frows), BF16),
        scratch_shapes=[pltpu.VMEM((-(-2 * frows // LANES) * LANES, width), F32)],
        compiler_params=pltpu.CompilerParams(vmem_limit_bytes=32 * 1024 * 1024),
        name="turn",
    )(gate, up)


def on_device(
    block_input,
    cotangent,
    lengths,
    doc_starts,
    master,
    momentum,
    vectors,
    vector_first,
    vector_second,
):
    n_dp = lax.axis_size("dp")
    n_ctx = lax.axis_size("ctx")
    devices = n_dp * n_ctx
    rows = D // devices
    frows = FF // devices
    fblock = FF // n_ctx
    slots, span, width = block_input.shape
    tokens = slots * span
    group = HEADS // KVH
    qkv = QD + 2 * KVD
    my_ctx = lax.axis_index("ctx")
    me = lax.axis_index("dp") * n_ctx + my_ctx
    core_bit, x_bit = 1, 2
    ctx_bits = [core_bit, x_bit]
    dp_bits = [n_ctx << index for index in range(n_dp.bit_length() - 1)]
    all_bits = ctx_bits + dp_bits
    many = tuple([2] * len(all_bits))
    padded = (rows // 16 + 1) * 16

    master_flat = master.reshape(-1, LANES)
    momentum_flat = momentum.reshape(-1, LANES)
    small = jnp.pad(vectors, ((0, 0), (0, LANES - vectors.shape[1])))
    qkv_local, out_local, gate_up, down_local = pack(master_flat, small, devices, n_dp, BF16)

    attn_full = gather_bits(
        jnp.concatenate([qkv_local, out_local], axis=1), dp_bits[::-1], me, devices
    )
    down_bits = dp_bits[::-1]
    down_part, attn_full = lax.optimization_barrier((down_local, attn_full))
    high, low = down_bits[:2]
    down_came = [swap(down_part, mask, devices) for mask in (low, high, high + low)]
    qkv_full = gather_bits(attn_full[..., :qkv], ctx_bits[::-1], me, devices, dp_bits)
    qkv_full = qkv_full.reshape(devices, padded, qkv)
    gain_first, gain_second, bias_query, bias_key, bias_value = [
        piece.astype(F32) for piece in split_small(qkv_full[:, rows], devices)
    ]
    w_qkv = qkv_full[:, :rows].reshape(D, qkv)

    came = [choose(gate_up, my_ctx, 0)] + [
        swap(choose(gate_up, my_ctx ^ mask, 0), mask, devices) for mask in range(1, n_ctx)
    ]
    came, attn_full = lax.optimization_barrier((came, attn_full))
    ordered = []
    for source in range(n_ctx):
        piece = came[0]
        for mask in range(1, n_ctx):
            piece = jnp.where(my_ctx ^ mask == source, came[mask], piece)
        ordered.append(piece)
    w_wide = lax.all_gather(jnp.concatenate(ordered, axis=0), "dp", axis=0, tiled=True)

    def to_rows(gate, up):
        return lax.all_to_all(
            turn(gate, up, devices), BOTH, split_axis=0, concat_axis=0, tiled=True
        )

    length, second = lengths[0], doc_starts[0]
    places = my_ctx * span + jnp.arange(span, dtype=jnp.int32)
    doc_begin = jnp.where(places >= length, length, jnp.where(places >= second, second, 0))
    position = (places - doc_begin).astype(F32)
    live = (places < length)[:, None]
    info = jnp.stack([my_ctx, length, second]).astype(jnp.int32)
    inverse = ROPE_BASE ** (-2.0 * jnp.arange(HD // 2, dtype=F32) / HD)
    angles = inverse[:, None] * position[None, :]
    cosine, sine_part = jnp.cos(angles), jnp.sin(angles)
    cosine = jnp.concatenate([cosine, cosine], axis=0)[None]
    sine_part = jnp.concatenate([sine_part, sine_part], axis=0)[None]

    def from_ctx(value, other_x=None):
        other_core = swap(value, core_bit, devices)
        if other_x is None:
            other_x = swap(value, x_bit, devices)
        return value, other_core, other_x

    cot_here = jnp.where(live, cotangent.reshape(tokens, width), jnp.zeros((), BF16))

    def pair_of_heads(kv, index):
        begin = index * HD
        return jnp.concatenate(
            [kv[:, begin : begin + HD], kv[:, KVD + begin : KVD + begin + HD]], axis=1
        )

    inputs = block_input.astype(F32).reshape(tokens, width)
    scale_one = lax.rsqrt(jnp.mean(inputs * inputs, axis=-1, keepdims=True) + NORM_EPS)
    normed_one = (inputs * scale_one * gain_first).astype(BF16)
    bias = jnp.concatenate([bias_query, bias_key, bias_value])
    pre = mm(w_qkv, normed_one, ((0,), (1,))) + bias[:, None]
    turned = rotate(
        pre[: QD + KVD].reshape(HEADS + KVH, HD, tokens), cosine, sine_part
    )
    queries = (turned[:HEADS].astype(BF16).astype(F32) * HD ** (-0.5)).astype(BF16)
    kv_here = jnp.concatenate(
        [turned[HEADS:].astype(BF16).reshape(KVD, tokens), pre[QD + KVD :].astype(BF16)], axis=0
    )
    kv = from_ctx(kv_here)
    kv = jnp.stack(kv + (swap(kv[2], core_bit, devices),))
    back_one = jnp.pad(
        normed_one.T.reshape(devices, rows, tokens), ((0, 0), (0, padded - rows), (0, 0))
    ).reshape(devices * padded, tokens)
    back_one, kv = lax.optimization_barrier((back_one, kv))
    down_came = [down_part] + down_came
    at_z = jnp.where((me & high) != 0, 2, 0) + jnp.where((me & low) != 0, 1, 0)
    ordered = []
    for source in range(4):
        piece = down_came[0]
        for mask in range(1, 4):
            piece = jnp.where(at_z ^ mask == source, down_came[mask], piece)
        ordered.append(piece)
    down_part = jnp.stack(ordered).reshape(2, 2, frows, D)
    kv, down_part = lax.optimization_barrier((kv, down_part))
    down_came = swap(down_part, down_bits[2], devices)
    out_full, kv = lax.optimization_barrier((attn_full[..., qkv:], kv))
    halves = []
    for index in range(KVH):
        if index == 1:
            out_full, cot_here, halves = lax.optimization_barrier((out_full, cot_here, halves))
            cot_far = swap(cot_here, x_bit, devices)
        out_full = gather_bits(
            out_full, ctx_bits[::-1][index : index + 1], me, devices, dp_bits + ctx_bits[::-1][:index]
        )
        kv_one = pair_of_heads(kv, index)
        halves.append(attend(info, kv_one, queries[index * group : (index + 1) * group]))
    halves, cot_far, down_came = lax.optimization_barrier((halves, cot_far, down_came))
    down_part = jnp.where(
        (me & down_bits[2]) != 0,
        jnp.stack([down_came, down_part], axis=2),
        jnp.stack([down_part, down_came], axis=2),
    )
    down_part = gather_bits(down_part, down_bits[3:], me, devices, down_bits[:3])
    attended = jnp.concatenate([half[0] for half in halves], axis=0)
    log_total = jnp.concatenate([half[1] for half in halves], axis=0)
    out_pieces = out_full.reshape(devices * padded, D)

    mixed_pieces = jnp.pad(
        attended.reshape(devices, rows, tokens).astype(BF16), ((0, 0), (0, padded - rows), (0, 0))
    ).reshape(devices * padded, tokens)
    hidden = inputs + mm(mixed_pieces, out_pieces, ((0,), (0,)))
    scale_two = lax.rsqrt(jnp.mean(hidden * hidden, axis=-1, keepdims=True) + NORM_EPS)
    normed_two = (hidden * scale_two * gain_second).astype(BF16)

    normed_two, down_part = lax.optimization_barrier((normed_two, down_part))
    w_down = down_part.reshape(fblock, D)
    normed = from_ctx(normed_two)
    out_pieces, own = lax.optimization_barrier((out_pieces, normed[0]))
    normed = (own,) + normed[1:]
    w_out = out_pieces.reshape(devices, padded, D)[:, :rows].reshape(QD, D)
    cot = from_ctx(cot_here, cot_far)
    kept, near_parts = feed_forward(normed[:2], cot[:2], w_wide, w_down, n_ctx, None)
    (far_x, far_dy), momentum_flat, kept = lax.optimization_barrier(
        ((normed[2], cot[2]), momentum_flat, kept)
    )
    old_qkv, old_out, old_pair, old_down = pack(momentum_flat, None, devices, 1, F32)
    old_pair, far_x = lax.optimization_barrier((old_pair, far_x))
    old_pair = lax.all_to_all(old_pair, BOTH, split_axis=0, concat_axis=0, tiled=True)
    kept, far_parts = feed_forward(
        (far_x, swap(far_x, core_bit, devices)),
        (far_dy, swap(far_dy, core_bit, devices)),
        w_wide,
        w_down,
        n_ctx,
        kept,
    )
    kept, far_parts, old_pair = lax.optimization_barrier((kept, far_parts, old_pair))
    acts, both_backs, normed_all, cot_all = kept

    def to_ctx(near, far):
        crossed = swap(far[1], core_bit, devices)
        far = (far[0].astype(F32) + crossed.astype(F32)).astype(BF16)
        crossed = swap(near[1], core_bit, devices)
        near = near[0].astype(F32) + crossed.astype(F32)
        return near + swap(far, x_bit, devices).astype(F32), far

    normed_two_grad, ready = to_ctx(near_parts, far_parts)
    (acts, both_backs), ready = lax.optimization_barrier(((acts, both_backs), ready))

    dp_shape = tuple([2] * len(dp_bits)) + (frows, D)
    dp_order = dp_bits[1:] + dp_bits[:1]
    down_value = mm(acts, cot_all, ((0,), (0,))).astype(BF16)
    both_value = mm(both_backs, normed_all, ((0,), (0,))).astype(BF16)
    values = [both_value[:fblock], both_value[fblock:], down_value]
    orders = [dp_bits, dp_order, dp_bits]
    started = []
    for index in (2, 1, 0):
        sent, kept = scatter_split(values[index].reshape(dp_shape), dp_bits, orders[index][0], me)
        started.insert(0, (kept, swap(sent, orders[index][0], devices)))

    out_grad = cot_here.astype(F32)
    hidden_norm_grad, grad_gain_second = norm_backward(
        hidden, scale_two, gain_second, normed_two_grad
    )
    hidden_grad = out_grad + hidden_norm_grad
    hidden_low = hidden_grad.astype(BF16)
    heads_grad = mm(w_out, hidden_low, ((1,), (1,))).astype(BF16).reshape(HEADS, HD, tokens)
    delta = jnp.sum(heads_grad.astype(F32) * attended, axis=1, keepdims=True)
    grad_output = mm(mixed_pieces, hidden_low)
    query_grads, kv_parts = [], []
    sent, kept = scatter_split(
        grad_output.astype(BF16).reshape(many + (padded, D)), all_bits, all_bits[0], me
    )
    wide_parts = started + [(kept, swap(sent, all_bits[0], devices))]
    wide_orders = [list(order) for order in orders] + [list(all_bits)]
    steps = [[2, 1, 3], [0, 3], [2, 1, 3], [0, 3]]
    shares = [4, 3]
    ready = [sent]
    for index in range(KVH):
        kv_one = pair_of_heads(kv, index)
        kv_grad = None
        begin = index * group
        for count in shares:
            chosen = slice(begin, begin + count)
            begin += count
            query_part, ready = lax.optimization_barrier((queries[chosen], ready))
            query_grad, kv_grad = attend_back(
                info, kv_one, query_part, heads_grad[chosen], log_total[chosen], delta[chosen], kv_grad
            )
            query_grads.append(query_grad)
            ready = []
            if len(steps) == 3:
                acts, query_grads[-1] = lax.optimization_barrier((acts, query_grad))
                out_part = mm(acts, w_down).astype(BF16).reshape(n_ctx, span, D)
                out_sum, _ = to_ctx((out_part[0], out_part[1]), (out_part[2], out_part[3]))
                layer_out = jnp.where(live, hidden + out_sum, 0.0).astype(BF16)
            for which in steps.pop(0):
                order = wide_orders[which]
                parts, query_grads[-1] = lax.optimization_barrier(
                    (wide_parts[which], query_grads[-1])
                )
                order.pop(0)
                sent, kept = scatter_split(scatter_end(parts), order, order[0], me)
                ready.append(sent)
                wide_parts[which] = (kept, swap(sent, order[0], devices))
        kv_parts.append(
            scatter_sum(kv_grad.reshape(2, 2, 2 * HD, span), ctx_bits, me, devices)
        )
    kv_grads = [part.astype(F32).reshape(2, HD, span) for part in kv_parts]
    qk_grad = jnp.concatenate(query_grads + [grad[:1] for grad in kv_grads], axis=0)
    qk_back = rotate_back(qk_grad, cosine, sine_part).reshape(QD + KVD, tokens)
    qkv_back = jnp.concatenate(
        [qk_back] + [grad[1] for grad in kv_grads], axis=0
    ).astype(BF16)
    grad_qkv = mm(back_one, qkv_back, ((1,), (1,)))
    here_core = jnp.where((me & core_bit) != 0, 1, 0)
    here_x = jnp.where((me & x_bit) != 0, 1, 0)
    left = list(all_bits)
    qkv_order = [core_bit, dp_bits[0], x_bit] + dp_bits[1:]
    sent, kept = scatter_split(
        grad_qkv.astype(BF16).reshape(many + (padded, qkv)), left, core_bit, me
    )
    wide_parts, layer_out, sent = lax.optimization_barrier((wide_parts, layer_out, sent))
    qkv_parts = (kept, swap(sent, core_bit, devices))
    left.remove(core_bit)
    gate_sum, up_sum, down_sum, out_sum_rows = [
        scatter_sum(scatter_end(parts), order[1:], me, devices)
        for parts, order in zip(wide_parts, wide_orders)
    ]
    mats = combine(old_pair, gate_sum, up_sum, old_down, down_sum, old_out, out_sum_rows)
    mats = mats.reshape(2, 2, frows, D)
    row_parts = (choose(mats, here_core, 1), swap(choose(mats, 1 - here_core, 1), core_bit, devices))
    count = len(block_pairs(D // BLOCK))
    places = (count + n_dp - 1) // n_dp * n_dp
    dp_many = tuple([2] * len(dp_bits))
    gram_left = list(dp_bits)
    for step, bit in enumerate(qkv_order[1:]):
        qkv_parts, row_parts = lax.optimization_barrier((qkv_parts, row_parts))
        sent, kept = scatter_split(scatter_end(qkv_parts), left, bit, me)
        left.remove(bit)
        qkv_parts = (kept, swap(sent, bit, devices))
        if step == 0:
            mats = jnp.stack(row_parts, axis=1)
            row_parts = (choose(mats, here_x, 0), swap(choose(mats, 1 - here_x, 0), x_bit, devices))
            continue
        if step == 1:
            owned = jnp.stack(row_parts).reshape(n_ctx * frows, D)
            gram = gram_blocks(owned, places).reshape(dp_many + (places // n_dp, BLOCK, BLOCK))
        else:
            gram = scatter_end(row_parts)
        sent, kept = scatter_split(gram, gram_left, gram_left[0], me)
        row_parts = (kept, swap(sent, gram_left.pop(0), devices))
    qkv_parts, row_parts = lax.optimization_barrier((qkv_parts, row_parts))
    qkv_sum_rows = scatter_end(qkv_parts)
    moved_qkv = MOMENTUM_DECAY * old_qkv + qkv_sum_rows.astype(F32)
    moved_low = moved_qkv.astype(BF16)
    qkv_all = lax.all_gather(moved_low, BOTH, axis=0, tiled=True)
    gram = gather_bits(scatter_end(row_parts), dp_bits[::-1], me, devices)
    gram = gram.reshape(places, BLOCK, BLOCK)

    (gate_sum, up_sum), moved_low, gram = lax.optimization_barrier(
        ((gate_sum, up_sum), moved_low, gram)
    )
    pair_rows = to_rows(gate_sum, up_sum)
    ortho = orthogonal_wide(gram, owned).reshape(2, 2, frows, D)
    got = swap(ortho[1], x_bit, devices)
    qkv_back, ortho = lax.optimization_barrier((qkv_back, ortho))
    grad_bias = jnp.sum(qkv_back.astype(F32), axis=1)
    normed_one_grad = mm(qkv_back, w_qkv, ((0,), (1,)))
    input_norm_grad, grad_gain_first = norm_backward(inputs, scale_one, gain_first, normed_one_grad)
    input_grad = (hidden_grad + input_norm_grad).astype(BF16).reshape(slots, span, width)

    vector_part = join_small(
        [
            grad_gain_first,
            grad_gain_second,
            grad_bias[:QD],
            grad_bias[QD : QD + KVD],
            grad_bias[QD + KVD :],
        ],
        devices,
    )
    vector_rows = lax.all_to_all(vector_part, BOTH, split_axis=0, concat_axis=0, tiled=True)
    own, pair_rows, vector_part = lax.optimization_barrier((ortho[0], pair_rows, vector_part))
    ortho = jnp.where((me & x_bit) != 0, jnp.stack([got, own]), jnp.stack([own, got]))
    got = swap(ortho[:, 1], core_bit, devices)
    ortho = jnp.where(
        (me & core_bit) != 0,
        jnp.stack([got, ortho[:, 0]], axis=1),
        jnp.stack([ortho[:, 0], got], axis=1),
    ).reshape(n_ctx, frows, D)
    turned = turn(ortho[0], ortho[1], devices)
    momentum_flat, turned = lax.optimization_barrier((momentum_flat, turned))
    ortho_pair = lax.all_to_all(turned, BOTH, split_axis=0, concat_axis=0, tiled=True)
    ortho_qkv = orthogonal_whole(qkv_all, moved_qkv, (QD, KVD, KVD))
    vector_rows, ortho_qkv = lax.optimization_barrier((vector_rows, ortho_qkv))
    new_momentum = update(
        momentum_flat,
        qkv_sum_rows,
        out_sum_rows,
        pair_rows,
        down_sum,
        devices,
        MOMENTUM_DECAY,
        [1.0] * 7,
    ).reshape(momentum.shape)

    factors = [
        -MUON_RATE * math.sqrt(max(1.0, breadth / height)) for height, breadth in matrix_shapes()
    ]
    new_master = update(
        master_flat,
        ortho_qkv,
        ortho[3, :padded],
        ortho_pair,
        ortho[2],
        devices,
        1.0 - MUON_RATE * MUON_DECAY,
        factors,
    ).reshape(master.shape)
    vector_grad = jnp.sum(vector_rows, axis=0, keepdims=True)
    first_new = BETA_FIRST * vector_first + (1.0 - BETA_FIRST) * vector_grad
    second_new = BETA_SECOND * vector_second + (1.0 - BETA_SECOND) * vector_grad * vector_grad
    adjusted = (
        first_new
        / (1.0 - BETA_FIRST**STEP)
        / (jnp.sqrt(second_new / (1.0 - BETA_SECOND**STEP)) + ADAM_EPS)
    )
    new_vectors = vectors - ADAM_RATE * adjusted
    return (
        layer_out.reshape(slots, span, width),
        input_grad,
        new_master,
        new_momentum,
        new_master.astype(BF16),
        new_vectors,
        first_new,
        second_new,
    )


def solution(mesh):
    return jax.shard_map(
        on_device,
        mesh=mesh,
        in_specs=(
            P("dp", "ctx", None),
            P("dp", "ctx", None),
            P("dp"),
            P("dp"),
            P(BOTH, None),
            P(BOTH, None),
            P(BOTH, None),
            P(BOTH, None),
            P(BOTH, None),
        ),
        out_specs=(
            P("dp", "ctx", None),
            P("dp", "ctx", None),
            P(BOTH, None),
            P(BOTH, None),
            P(BOTH, None),
            P(BOTH, None),
            P(BOTH, None),
            P(BOTH, None),
        ),
        check_vma=False,
    )
```

```python
import math

import jax
import jax.numpy as jnp
from jax import lax
from jax.experimental import pallas as pl
from jax.experimental.pallas import tpu as pltpu
from jax.sharding import PartitionSpec as P

D = 896
HEADS = 14
KVH = 2
HD = 64
FF = 4864
SLOT = 2048
NS_STEPS = 3
STEP = 10
QD = 896
KVD = 128

NORM_EPS = 1e-06
ROPE_BASE = 1000000.0
NS_LINEAR = 3.4445
NS_SQUARE = -4.775
NS_CUBIC = 2.0315
MOMENTUM_DECAY = 0.5
MUON_RATE = 0.6
MUON_DECAY = 0.1
ADAM_RATE = 0.2
BETA_FIRST = 0.9
BETA_SECOND = 0.95
ADAM_EPS = 1e-08
MASK_FLOOR = -1e30

F32 = jnp.float32
BF16 = jnp.bfloat16
BOTH = ("dp", "ctx")
LANES = 128


def matrix_shapes():
    return [(D, QD), (D, KVD), (D, KVD), (QD, D), (D, FF), (D, FF), (FF, D)]


def vector_sizes():
    return [D, D, QD, KVD, KVD]


def mm(left, right, contract=((1,), (0,))):
    return lax.dot_general(left, right, (contract, ((), ())), preferred_element_type=F32)


def split_small(flat, devices):
    result = []
    offset = 0
    for extent_all in vector_sizes():
        extent = extent_all // devices
        result.append(flat[:, offset : offset + extent].reshape(extent_all))
        offset += extent
    return result


def join_small(pieces, devices):
    return jnp.concatenate([piece.reshape(devices, -1) for piece in pieces], axis=1)


def swap(value, mask, devices):
    return lax.ppermute(value, BOTH, [(index, index ^ mask) for index in range(devices)])


def gather_bits(value, bits, me, devices, before=()):
    held = value
    done = list(before)
    for bit in bits:
        place = sum(1 for other in done if other > bit)
        got = swap(held, bit, devices)
        mine = (me & bit) != 0
        held = jnp.where(
            mine, jnp.stack([got, held], axis=place), jnp.stack([held, got], axis=place)
        )
        done.append(bit)
    return held


def scatter_split(held, left, bit, me, lead=0):
    axis = sorted(left, reverse=True).index(bit) + lead
    mine = jnp.where((me & bit) != 0, 1, 0)
    return choose(held, 1 - mine, axis).astype(BF16), choose(held, mine, axis)


def scatter_start(held, left, bit, me, devices):
    sent, kept = scatter_split(held, left, bit, me)
    return kept, swap(sent, bit, devices)


def scatter_end(parts):
    return (parts[0].astype(F32) + parts[1].astype(F32)).astype(BF16)


def scatter_sum(value, bits, me, devices):
    left = list(bits)
    held = value
    for bit in bits:
        held = scatter_end(scatter_start(held, left, bit, me, devices))
        left.remove(bit)
    return held


def choose(value, mine, axis):
    return lax.dynamic_index_in_dim(value, mine, axis, keepdims=False)


def rotate(values, cosine, sine_part):
    midpoint = HD // 2
    turned = jnp.concatenate([-values[:, midpoint:], values[:, :midpoint]], axis=1)
    return values * cosine + turned * sine_part


def rotate_back(gradient, cosine, sine_part):
    midpoint = HD // 2
    scaled = gradient * sine_part
    turned = jnp.concatenate([scaled[:, midpoint:], -scaled[:, :midpoint]], axis=1)
    return gradient * cosine + turned


def norm_backward(source, scale_row, gain, incoming):
    gain_grad = jnp.sum(incoming * source * scale_row, axis=0)
    weighted = incoming * gain
    result = scale_row * weighted - source * scale_row**3 * jnp.mean(
        weighted * source, axis=-1, keepdims=True
    )
    return (result, gain_grad)


def halves_of(span):
    return [slice(0, span // 2), slice(span // 2, span)]


def fill_mask(info, mask, chunk, span):
    key = chunk * span + lax.broadcasted_iota(jnp.int32, (span, span), 0)
    query = info[0] * span + lax.broadcasted_iota(jnp.int32, (span, span), 1)
    key_doc = (key >= info[2]).astype(jnp.int32) + (key >= info[1]).astype(jnp.int32)
    query_doc = (query >= info[2]).astype(jnp.int32) + (query >= info[1]).astype(jnp.int32)
    allowed = jnp.logical_and(key_doc == query_doc, key <= query)
    mask[chunk] = jnp.where(allowed, 0.0, MASK_FLOOR).astype(F32)


def attend_kernel(info, kv, q, out, lse, keys, mask, best, total, acc):
    head = pl.program_id(0)
    span = q.shape[-1]
    mine = info[0]
    chunks = mine + 1

    @pl.when(head == 0)
    def _():
        def fill(chunk, carry):
            slot = jnp.bitwise_xor(chunk, mine)
            keys[chunk] = kv[slot, :HD, :].astype(F32).T.astype(BF16)
            fill_mask(info, mask, chunk, span)
            return carry

        lax.fori_loop(0, chunks, fill, 0)

    best[...] = jnp.full(best.shape, MASK_FLOOR, F32)
    total[...] = jnp.zeros(total.shape, F32)
    acc[...] = jnp.zeros(acc.shape, F32)
    queries = q[0]

    def step(index, carry):
        chunk = mine - index
        slot = jnp.bitwise_xor(chunk, mine)
        scores = jnp.dot(keys[chunk], queries, preferred_element_type=F32) + mask[chunk]
        old = best[...]
        new = jnp.maximum(old, jnp.max(scores, axis=0, keepdims=True))
        present = jnp.exp(scores - new)
        shrink = jnp.exp(old - new)
        best[...] = new
        total[...] = total[...] * shrink + jnp.sum(present, axis=0, keepdims=True)
        acc[...] = acc[...] * shrink + jnp.dot(
            kv[slot, HD:, :], present.astype(BF16), preferred_element_type=F32
        )
        return carry

    lax.fori_loop(0, chunks, step, 0)
    out[0] = acc[...] / total[...]
    lse[0] = best[...] + jnp.log(total[...])


def attend_back_kernel(
    info, kv, q, dout, lse, delta, before, dq, dkv, keys, values, mask, dk, dv, acc
):
    head = pl.program_id(0)
    span = q.shape[-1]
    mine = info[0]
    chunks = mine + 1
    n_ctx = kv.shape[0]

    @pl.when(head == 0)
    def _():
        dk[...] = jnp.zeros(dk.shape, F32)
        dv[...] = jnp.zeros(dv.shape, F32)

        def fill(chunk, carry):
            slot = jnp.bitwise_xor(chunk, mine)
            keys[chunk] = kv[slot, :HD, :].astype(F32).T.astype(BF16)
            values[chunk] = kv[slot, HD:, :].astype(F32).T.astype(BF16)
            fill_mask(info, mask, chunk, span)
            return carry

        lax.fori_loop(0, chunks, fill, 0)

    acc[...] = jnp.zeros(acc.shape, F32)
    queries = q[0]
    douts = dout[0]
    query_rows = queries.astype(F32).T.astype(BF16)
    dout_rows = douts.astype(F32).T.astype(BF16)

    def step(chunk, carry):
        slot = jnp.bitwise_xor(chunk, mine)
        value_sum, key_sum = dv[chunk], dk[chunk]
        for lanes in halves_of(span):
            scores = (
                jnp.dot(keys[chunk], queries[:, lanes], preferred_element_type=F32)
                + mask[chunk, :, lanes]
            )
            shares = jnp.exp(scores - lse[0, :, lanes])
            share_grad = jnp.dot(values[chunk], douts[:, lanes], preferred_element_type=F32)
            score_grad = (shares * (share_grad - delta[0, :, lanes])).astype(BF16)
            value_sum += jnp.dot(
                shares.astype(BF16), dout_rows[lanes, :], preferred_element_type=F32
            )
            key_sum += jnp.dot(score_grad, query_rows[lanes, :], preferred_element_type=F32)
            acc[:, lanes] += jnp.dot(kv[slot, :HD, :], score_grad, preferred_element_type=F32)
        dv[chunk], dk[chunk] = value_sum, key_sum
        return carry

    lax.fori_loop(0, chunks, step, 0)
    dq[0] = acc[...] * HD ** (-0.5)

    @pl.when(head == pl.num_programs(0) - 1)
    def _():
        for chunk in range(n_ctx):
            sums = jnp.concatenate([dk[chunk].T, dv[chunk].T], axis=0)
            if before is not None:
                sums += before[chunk].astype(F32)
            dkv[chunk] = sums.astype(BF16)


def attend(info, kv, q):
    heads, _, span = q.shape
    n_ctx = kv.shape[0]
    per_head = lambda rows: pl.BlockSpec((1, rows, span), lambda head: (head, 0, 0))
    return pl.pallas_call(
        attend_kernel,
        grid=(heads,),
        in_specs=[
            pl.BlockSpec(memory_space=pltpu.SMEM),
            pl.BlockSpec(kv.shape, lambda head: (0, 0, 0)),
            per_head(HD),
        ],
        out_specs=[per_head(HD), per_head(1)],
        out_shape=[
            jax.ShapeDtypeStruct((heads, HD, span), F32),
            jax.ShapeDtypeStruct((heads, 1, span), F32),
        ],
        scratch_shapes=[
            pltpu.VMEM((n_ctx, span, HD), BF16),
            pltpu.VMEM((n_ctx, span, span), F32),
            pltpu.VMEM((1, span), F32),
            pltpu.VMEM((1, span), F32),
            pltpu.VMEM((HD, span), F32),
        ],
        compiler_params=pltpu.CompilerParams(vmem_limit_bytes=40 * 1024 * 1024),
        cost_estimate=pl.CostEstimate(
            flops=4 * heads * span * span * n_ctx * HD * 4,
            bytes_accessed=4 * heads * span * HD * 2,
            transcendentals=heads * span * span * n_ctx,
        ),
        name="attend",
    )(info, kv, q)


def attend_back(info, kv, q, dout, lse, delta, before):
    heads, _, span = q.shape
    n_ctx = kv.shape[0]
    per_head = lambda rows: pl.BlockSpec((1, rows, span), lambda head: (head, 0, 0))
    whole = pl.BlockSpec(kv.shape, lambda head: (0, 0, 0))
    if before is None:
        body = lambda *refs: attend_back_kernel(*refs[:6], None, *refs[6:])
    else:
        body = attend_back_kernel
    return pl.pallas_call(
        body,
        grid=(heads,),
        in_specs=[
            pl.BlockSpec(memory_space=pltpu.SMEM),
            whole,
            per_head(HD),
            per_head(HD),
            per_head(1),
            per_head(1),
        ]
        + [whole] * (before is not None),
        out_specs=[per_head(HD), whole],
        out_shape=[
            jax.ShapeDtypeStruct((heads, HD, span), F32),
            jax.ShapeDtypeStruct(kv.shape, BF16),
        ],
        scratch_shapes=[
            pltpu.VMEM((n_ctx, span, HD), BF16),
            pltpu.VMEM((n_ctx, span, HD), BF16),
            pltpu.VMEM((n_ctx, span, span), F32),
            pltpu.VMEM((n_ctx, span, HD), F32),
            pltpu.VMEM((n_ctx, span, HD), F32),
            pltpu.VMEM((HD, span), F32),
        ],
        compiler_params=pltpu.CompilerParams(vmem_limit_bytes=40 * 1024 * 1024),
        cost_estimate=pl.CostEstimate(
            flops=10 * heads * span * span * n_ctx * HD * 4,
            bytes_accessed=8 * heads * span * HD * 2,
            transcendentals=heads * span * span * n_ctx,
        ),
        name="attend_back",
    )(*[info, kv, q, dout, lse, delta] + [before] * (before is not None))


def forward_backward_kernel(
    x0, x1, dy0, dy1, wide, down, act_out, both_out, x_out, dy_out, back0, back1
):
    first = pl.program_id(0) == 0
    units = down.shape[0]
    x = jnp.where(first, x0[...], x1[...])
    dy = jnp.where(first, dy0[...], dy1[...])
    x_out[...] = x
    dy_out[...] = dy
    both = jnp.dot(x, wide[...], preferred_element_type=F32)
    gate_pre = both[:, :units]
    up_pre = both[:, units:]
    grad_act = mm(dy, down[...], ((1,), (1,)))
    sigmoid_gate = jax.nn.sigmoid(gate_pre)
    swish = gate_pre * sigmoid_gate
    slope = sigmoid_gate * (1.0 + gate_pre * (1.0 - sigmoid_gate))
    act_out[...] = (swish * up_pre).astype(BF16)
    both_back = jnp.concatenate([grad_act * up_pre * slope, grad_act * swish], axis=1).astype(BF16)
    both_out[...] = both_back
    back = mm(both_back, wide[...], ((1,), (1,))).astype(BF16)

    @pl.when(first)
    def _():
        back0[...] = back

    @pl.when(jnp.logical_not(first))
    def _():
        back1[...] = back


def feed_forward(x, dy, wide, down, blocks, earlier):
    span, width = x[0].shape
    units = down.shape[0]
    first = 0 if earlier is None else 2
    whole = lambda shape: pl.BlockSpec(
        shape, lambda block: (0, 0), pipeline_mode=pl.Buffered(1)
    )
    line = lambda columns: pl.BlockSpec((span, columns), lambda block: (block + first, 0))
    columns = [units, 2 * units, width, width]
    shapes = [jax.ShapeDtypeStruct((blocks * span, count), BF16) for count in columns]
    in_specs = [whole((span, width))] * 4 + [whole((width, 2 * units)), whole((units, width))]
    operands = [*x, *dy, wide, down]
    aliases = {}
    body = forward_backward_kernel
    if earlier is not None:
        in_specs += [pl.BlockSpec(memory_space=pl.ANY)] * 4
        operands += list(earlier)
        aliases = {6 + index: index for index in range(4)}
        body = lambda *refs: forward_backward_kernel(*refs[:6], *refs[10:])
    back = pl.BlockSpec((span, width), lambda block: (0, 0))
    results = pl.pallas_call(
        body,
        grid=(2,),
        in_specs=in_specs,
        out_specs=[line(count) for count in columns] + [back, back],
        out_shape=shapes + [jax.ShapeDtypeStruct((span, width), BF16)] * 2,
        input_output_aliases=aliases,
        compiler_params=pltpu.CompilerParams(vmem_limit_bytes=60 * 1024 * 1024),
        cost_estimate=pl.CostEstimate(
            flops=20 * span * width * units,
            bytes_accessed=6 * width * units + 2 * span * 10 * width,
            transcendentals=2 * span * units,
        ),
        name="feed_forward",
    )(*operands)
    return results[:4], results[4:]


BLOCK = 128


def block_pairs(count):
    return [(low, high) for low in range(count) for high in range(low, count)]


def gram_kernel(rows, out):
    count = rows.shape[1] // BLOCK
    place = 0
    for low in range(count):
        line = lax.dot_general(
            rows[:, low * BLOCK : (low + 1) * BLOCK],
            rows[:, low * BLOCK :],
            (((0,), (0,)), ((), ())),
            preferred_element_type=F32,
        ).astype(BF16)
        for high in range(low, count):
            out[place] = line[:, (high - low) * BLOCK : (high - low + 1) * BLOCK]
            place += 1
    for extra in range(place, out.shape[0]):
        out[extra] = jnp.zeros((BLOCK, BLOCK), BF16)


def gram_blocks(rows, places):
    return pl.pallas_call(
        gram_kernel,
        out_shape=jax.ShapeDtypeStruct((places, BLOCK, BLOCK), BF16),
        compiler_params=pltpu.CompilerParams(vmem_limit_bytes=32 * 1024 * 1024),
        name="gram",
    )(rows)


def newton_schulz(gram, low, poly, mixed, rows):
    size = gram.shape[0]
    part = size // 2 if size % 16 == 0 and size > BLOCK else size
    parts = [pl.ds(begin, part) for begin in range(0, size, part)]
    row_id = lax.broadcasted_iota(jnp.int32, (size, size), 0)
    column_id = lax.broadcasted_iota(jnp.int32, (size, size), 1)
    square = jnp.where(row_id == column_id, gram[...], 0.0)
    square = jnp.sum(jnp.sum(square, axis=0, keepdims=True), axis=1, keepdims=True)
    scale = 1.0 / (jnp.sqrt(square) + 1e-07)
    for place in parts:
        scaled = gram[place, :] * (scale * scale)
        gram[place, :] = scaled
        low[place, :] = scaled.astype(BF16)
    work = (rows * scale).astype(BF16)
    for step in range(NS_STEPS):
        for place in parts:
            second = jnp.dot(low[place, :], low[...], preferred_element_type=F32)
            poly[place, :] = (NS_SQUARE * gram[place, :] + NS_CUBIC * second).astype(BF16)
        moved = jnp.dot(work, poly[...], preferred_element_type=F32)
        work = (NS_LINEAR * work.astype(F32) + moved).astype(BF16)
        if step + 1 < NS_STEPS:
            for place in parts:
                first = jnp.dot(poly[place, :], low[...], preferred_element_type=F32)
                mixed[place, :] = first.astype(BF16)
                gram[place, :] = (
                    NS_LINEAR * NS_LINEAR * gram[place, :] + (2.0 * NS_LINEAR) * first
                )
            for place in parts:
                second = jnp.dot(poly[place, :], mixed[...], preferred_element_type=F32)
                renewed = gram[place, :] + second
                gram[place, :] = renewed
                low[place, :] = renewed.astype(BF16)
    return work


def wide_kernel(blocks, rows, out, gram, low, poly, mixed):
    for place, (first, second) in enumerate(block_pairs(gram.shape[0] // BLOCK)):
        tile = blocks[place].astype(F32)
        gram[first * BLOCK : (first + 1) * BLOCK, second * BLOCK : (second + 1) * BLOCK] = tile
        if first != second:
            gram[second * BLOCK : (second + 1) * BLOCK, first * BLOCK : (first + 1) * BLOCK] = tile.T
    out[...] = newton_schulz(gram, low, poly, mixed, rows[...].astype(F32))


def square_scratch(size):
    return [
        pltpu.VMEM((size, size), F32),
        pltpu.VMEM((size, size), BF16),
        pltpu.VMEM((size, size), BF16),
        pltpu.VMEM((size, size), BF16),
    ]


def orthogonal_wide(blocks, rows):
    return pl.pallas_call(
        wide_kernel,
        out_shape=jax.ShapeDtypeStruct(rows.shape, BF16),
        scratch_shapes=square_scratch(rows.shape[1]),
        compiler_params=pltpu.CompilerParams(vmem_limit_bytes=40 * 1024 * 1024),
        cost_estimate=pl.CostEstimate(
            flops=14 * rows.shape[1] ** 3, bytes_accessed=4 * rows.size, transcendentals=0
        ),
        name="newton_wide",
    )(blocks, rows)


def whole_kernel(widths, whole, rows, out, *scratch):
    begin = 0
    for index, width in enumerate(widths):
        gram, low, poly, mixed = scratch[4 * index : 4 * index + 4]
        for first in range(0, width, BLOCK):
            gram[first : first + BLOCK, :] = lax.dot_general(
                whole[:, begin + first : begin + first + BLOCK],
                whole[:, begin : begin + width],
                (((0,), (0,)), ((), ())),
                preferred_element_type=F32,
            )
        out[:, begin : begin + width] = newton_schulz(
            gram, low, poly, mixed, rows[:, begin : begin + width]
        )
        begin += width


def orthogonal_whole(whole, rows, widths):
    scratch = []
    for width in widths:
        scratch += square_scratch(width)
    return pl.pallas_call(
        lambda *refs: whole_kernel(widths, *refs),
        out_shape=jax.ShapeDtypeStruct(rows.shape, BF16),
        scratch_shapes=scratch,
        compiler_params=pltpu.CompilerParams(vmem_limit_bytes=48 * 1024 * 1024),
        cost_estimate=pl.CostEstimate(
            flops=16 * sum(width**3 for width in widths),
            bytes_accessed=2 * whole.size,
            transcendentals=0,
        ),
        name="newton_whole",
    )(whole, rows)


def from_flat(flat, base, target, height, breadth):
    lines = breadth // LANES
    for begin in range(0, height, 8):
        count = min(8, height - begin)
        for index in range(lines):
            start = base + begin * lines + index
            if lines == 1:
                tile = flat[start : start + count, :]
            else:
                tile = flat[pl.ds(start, count, stride=lines), :]
            target[begin : begin + count, index * LANES : (index + 1) * LANES] = tile


def to_flat(flat, base, value, height, breadth):
    lines = breadth // LANES
    for begin in range(0, height, 8):
        count = min(8, height - begin)
        for index in range(lines):
            start = base + begin * lines + index
            tile = value(slice(begin, begin + count), slice(index * LANES, (index + 1) * LANES))
            if lines == 1:
                flat[start : start + count, :] = tile
            else:
                flat[pl.ds(start, count, stride=lines), :] = tile


def section_bases(devices):
    bases = []
    base = 0
    for height, breadth in matrix_shapes():
        bases.append(base)
        base += height // devices * breadth // LANES
    return bases


def pack_kernel(devices, group, flat, extra, qkv_out, out_out, wide_out, down_out, qkv, out, wide, down):
    rows = D // devices
    frows = FF // devices
    bases = section_bases(devices)
    qkv[...] = jnp.zeros(qkv.shape, F32)
    out[...] = jnp.zeros(out.shape, F32)
    from_flat(flat, bases[0], qkv.at[:, :QD], rows, QD)
    from_flat(flat, bases[1], qkv.at[:, QD : QD + KVD], rows, KVD)
    from_flat(flat, bases[2], qkv.at[:, QD + KVD :], rows, KVD)
    if extra is not None:
        qkv[rows : rows + 1, :LANES] = extra[...]
    from_flat(flat, bases[3], out, rows, D)
    from_flat(flat, bases[6], down, FF // devices, D)
    qkv_out[...] = qkv[...].astype(qkv_out.dtype)
    out_out[...] = out[...].astype(out_out.dtype)
    down_out[...] = down[...].astype(down_out.dtype)
    for which in range(2):
        from_flat(flat, bases[4 + which], wide, rows, FF)
        targets = devices // group
        for target in range(targets):
            piece = jnp.concatenate(
                [
                    wide[:, (turn * targets + target) * frows : (turn * targets + target + 1) * frows]
                    for turn in range(group)
                ],
                axis=1,
            )
            width = group * frows
            wide_out[target, :, which * width : (which + 1) * width] = piece.astype(wide_out.dtype)


def pack(flat, extra, devices, group, dtype):
    rows = D // devices
    frows = FF // devices
    padded = (rows // 16 + 1) * 16
    targets = devices // group
    wide = (targets, rows, 2 * group * frows)
    shapes = [(padded, QD + 2 * KVD), (padded, D), wide, (frows, D)]
    types = [dtype, dtype, BF16, dtype]
    if extra is None:
        body = lambda flat_ref, *refs: pack_kernel(devices, group, flat_ref, None, *refs)
        operands = [flat]
    else:
        body = lambda *refs: pack_kernel(devices, group, *refs)
        operands = [flat, extra]
    return pl.pallas_call(
        body,
        out_shape=[jax.ShapeDtypeStruct(shape, kind) for shape, kind in zip(shapes, types)],
        scratch_shapes=[
            pltpu.VMEM((padded, QD + 2 * KVD), F32),
            pltpu.VMEM((padded, D), F32),
            pltpu.VMEM((rows, FF), F32),
            pltpu.VMEM((frows, D), F32),
        ],
        compiler_params=pltpu.CompilerParams(vmem_limit_bytes=32 * 1024 * 1024),
        cost_estimate=pl.CostEstimate(flops=0, bytes_accessed=6 * flat.size, transcendentals=0),
        name="pack",
    )(*operands)


def update_kernel(devices, decay, factors, flat, qkv, out, wide, down, result, moved, rows_wide):
    rows = D // devices
    frows = FF // devices
    bases = section_bases(devices)
    whole = qkv[...].astype(F32)
    out_whole = out[...].astype(F32)
    down_whole = down[...].astype(F32)
    parts = [
        lambda r, c: whole[r, c],
        lambda r, c: whole[r, slice(QD + c.start, QD + c.stop)],
        lambda r, c: whole[r, slice(QD + KVD + c.start, QD + KVD + c.stop)],
        lambda r, c: out_whole[r, c],
    ]
    shapes = matrix_shapes()
    for index, part in enumerate(parts):
        to_flat(
            moved, bases[index], lambda r, c: part(r, c) * factors[index], rows, shapes[index][1]
        )
    to_flat(moved, bases[6], lambda r, c: down_whole[r, c] * factors[6], frows, D)
    for which in range(2):
        for source in range(devices):
            rows_wide[:, source * frows : (source + 1) * frows] = wide[
                source, :, which * frows : (which + 1) * frows
            ].astype(F32)
        to_flat(
            moved, bases[4 + which], lambda r, c: rows_wide[r, c] * factors[4 + which], rows, FF
        )
    result[...] = decay * flat[...] + moved[...]


def update(flat, qkv, out, wide, down, devices, decay, factors):
    return pl.pallas_call(
        lambda *refs: update_kernel(devices, decay, factors, *refs),
        out_shape=jax.ShapeDtypeStruct(flat.shape, F32),
        scratch_shapes=[
            pltpu.VMEM(flat.shape, F32),
            pltpu.VMEM((D // devices, FF), F32),
        ],
        compiler_params=pltpu.CompilerParams(vmem_limit_bytes=32 * 1024 * 1024),
        cost_estimate=pl.CostEstimate(flops=0, bytes_accessed=10 * flat.size, transcendentals=0),
        name="update",
    )(flat, qkv, out, wide, down)


def combine_kernel(old_pair, gate, up, old_down, down, old_out, out, mats, lines):
    devices, rows, _ = old_pair.shape
    frows = gate.shape[0]
    padded = out.shape[0]
    lines[...] = jnp.zeros(lines.shape, F32)
    for source in range(devices):
        lines[source * rows : (source + 1) * rows, : 2 * frows] = old_pair[source].astype(F32)
    old = lines[...].T
    mats[0] = (MOMENTUM_DECAY * old[:frows] + gate[...].astype(F32)).astype(BF16)
    mats[1] = (MOMENTUM_DECAY * old[frows : 2 * frows] + up[...].astype(F32)).astype(BF16)
    mats[2] = (MOMENTUM_DECAY * old_down[...] + down[...].astype(F32)).astype(BF16)
    last = MOMENTUM_DECAY * old_out[...] + out[...].astype(F32)
    mats[3] = jnp.concatenate(
        [last, jnp.zeros((frows - padded, last.shape[1]), F32)], axis=0
    ).astype(BF16)


def combine(old_pair, gate, up, old_down, down, old_out, out):
    frows, width = gate.shape
    return pl.pallas_call(
        combine_kernel,
        out_shape=jax.ShapeDtypeStruct((4, frows, width), BF16),
        scratch_shapes=[pltpu.VMEM((width, -(-2 * frows // LANES) * LANES), F32)],
        compiler_params=pltpu.CompilerParams(vmem_limit_bytes=32 * 1024 * 1024),
        name="combine",
    )(old_pair, gate, up, old_down, down, old_out, out)


def turn_kernel(gate, up, out, columns):
    devices, rows, _ = out.shape
    frows = gate.shape[0]
    columns[...] = jnp.zeros(columns.shape, F32)
    columns[:frows] = gate[...].astype(F32)
    columns[frows : 2 * frows] = up[...].astype(F32)
    lines = columns[...].T
    for target in range(devices):
        out[target] = lines[target * rows : (target + 1) * rows, : 2 * frows].astype(BF16)


def turn(gate, up, devices):
    frows, width = gate.shape
    return pl.pallas_call(
        turn_kernel,
        out_shape=jax.ShapeDtypeStruct((devices, width // devices, 2 * frows), BF16),
        scratch_shapes=[pltpu.VMEM((-(-2 * frows // LANES) * LANES, width), F32)],
        compiler_params=pltpu.CompilerParams(vmem_limit_bytes=32 * 1024 * 1024),
        name="turn",
    )(gate, up)


def on_device(
    block_input,
    cotangent,
    lengths,
    doc_starts,
    master,
    momentum,
    vectors,
    vector_first,
    vector_second,
):
    n_dp = lax.axis_size("dp")
    n_ctx = lax.axis_size("ctx")
    devices = n_dp * n_ctx
    rows = D // devices
    frows = FF // devices
    fblock = FF // n_ctx
    slots, span, width = block_input.shape
    tokens = slots * span
    group = HEADS // KVH
    qkv = QD + 2 * KVD
    my_ctx = lax.axis_index("ctx")
    me = lax.axis_index("dp") * n_ctx + my_ctx
    core_bit, x_bit = 1, 2
    ctx_bits = [core_bit, x_bit]
    dp_bits = [n_ctx << index for index in range(n_dp.bit_length() - 1)]
    all_bits = ctx_bits + dp_bits
    many = tuple([2] * len(all_bits))
    padded = (rows // 16 + 1) * 16

    master_flat = master.reshape(-1, LANES)
    momentum_flat = momentum.reshape(-1, LANES)
    small = jnp.pad(vectors, ((0, 0), (0, LANES - vectors.shape[1])))
    qkv_local, out_local, gate_up, down_local = pack(master_flat, small, devices, n_dp, BF16)

    attn_full = gather_bits(
        jnp.concatenate([qkv_local, out_local], axis=1), dp_bits[::-1], me, devices
    )
    down_bits = dp_bits[::-1]
    down_part, attn_full = lax.optimization_barrier((down_local, attn_full))
    high, low = down_bits[:2]
    down_came = [swap(down_part, mask, devices) for mask in (low, high, high + low)]
    qkv_full = gather_bits(attn_full[..., :qkv], ctx_bits[::-1], me, devices, dp_bits)
    qkv_full = qkv_full.reshape(devices, padded, qkv)
    gain_first, gain_second, bias_query, bias_key, bias_value = [
        piece.astype(F32) for piece in split_small(qkv_full[:, rows], devices)
    ]
    w_qkv = qkv_full[:, :rows].reshape(D, qkv)

    came = [choose(gate_up, my_ctx, 0)] + [
        swap(choose(gate_up, my_ctx ^ mask, 0), mask, devices) for mask in range(1, n_ctx)
    ]
    came, attn_full = lax.optimization_barrier((came, attn_full))
    ordered = []
    for source in range(n_ctx):
        piece = came[0]
        for mask in range(1, n_ctx):
            piece = jnp.where(my_ctx ^ mask == source, came[mask], piece)
        ordered.append(piece)
    w_wide = lax.all_gather(jnp.concatenate(ordered, axis=0), "dp", axis=0, tiled=True)

    def to_rows(gate, up):
        return lax.all_to_all(
            turn(gate, up, devices), BOTH, split_axis=0, concat_axis=0, tiled=True
        )

    length, second = lengths[0], doc_starts[0]
    places = my_ctx * span + jnp.arange(span, dtype=jnp.int32)
    doc_begin = jnp.where(places >= length, length, jnp.where(places >= second, second, 0))
    position = (places - doc_begin).astype(F32)
    live = (places < length)[:, None]
    info = jnp.stack([my_ctx, length, second]).astype(jnp.int32)
    inverse = ROPE_BASE ** (-2.0 * jnp.arange(HD // 2, dtype=F32) / HD)
    angles = inverse[:, None] * position[None, :]
    cosine, sine_part = jnp.cos(angles), jnp.sin(angles)
    cosine = jnp.concatenate([cosine, cosine], axis=0)[None]
    sine_part = jnp.concatenate([sine_part, sine_part], axis=0)[None]

    def from_ctx(value, other_x=None):
        other_core = swap(value, core_bit, devices)
        if other_x is None:
            other_x = swap(value, x_bit, devices)
        return value, other_core, other_x

    cot_here = jnp.where(live, cotangent.reshape(tokens, width), jnp.zeros((), BF16))

    def pair_of_heads(kv, index):
        begin = index * HD
        return jnp.concatenate(
            [kv[:, begin : begin + HD], kv[:, KVD + begin : KVD + begin + HD]], axis=1
        )

    inputs = block_input.astype(F32).reshape(tokens, width)
    scale_one = lax.rsqrt(jnp.mean(inputs * inputs, axis=-1, keepdims=True) + NORM_EPS)
    normed_one = (inputs * scale_one * gain_first).astype(BF16)
    bias = jnp.concatenate([bias_query, bias_key, bias_value])
    pre = mm(w_qkv, normed_one, ((0,), (1,))) + bias[:, None]
    turned = rotate(
        pre[: QD + KVD].reshape(HEADS + KVH, HD, tokens), cosine, sine_part
    )
    queries = (turned[:HEADS].astype(BF16).astype(F32) * HD ** (-0.5)).astype(BF16)
    kv_here = jnp.concatenate(
        [turned[HEADS:].astype(BF16).reshape(KVD, tokens), pre[QD + KVD :].astype(BF16)], axis=0
    )
    kv = from_ctx(kv_here)
    kv = jnp.stack(kv + (swap(kv[2], core_bit, devices),))
    back_one = jnp.pad(
        normed_one.T.reshape(devices, rows, tokens), ((0, 0), (0, padded - rows), (0, 0))
    ).reshape(devices * padded, tokens)
    back_one, kv = lax.optimization_barrier((back_one, kv))
    down_came = [down_part] + down_came
    at_z = jnp.where((me & high) != 0, 2, 0) + jnp.where((me & low) != 0, 1, 0)
    ordered = []
    for source in range(4):
        piece = down_came[0]
        for mask in range(1, 4):
            piece = jnp.where(at_z ^ mask == source, down_came[mask], piece)
        ordered.append(piece)
    down_part = jnp.stack(ordered).reshape(2, 2, frows, D)
    kv, down_part = lax.optimization_barrier((kv, down_part))
    down_came = swap(down_part, down_bits[2], devices)
    out_full, kv = lax.optimization_barrier((attn_full[..., qkv:], kv))
    halves = []
    for index in range(KVH):
        if index == 1:
            out_full, cot_here, halves = lax.optimization_barrier((out_full, cot_here, halves))
            cot_far = swap(cot_here, x_bit, devices)
        out_full = gather_bits(
            out_full, ctx_bits[::-1][index : index + 1], me, devices, dp_bits + ctx_bits[::-1][:index]
        )
        kv_one = pair_of_heads(kv, index)
        halves.append(attend(info, kv_one, queries[index * group : (index + 1) * group]))
    halves, cot_far, down_came = lax.optimization_barrier((halves, cot_far, down_came))
    down_part = jnp.where(
        (me & down_bits[2]) != 0,
        jnp.stack([down_came, down_part], axis=2),
        jnp.stack([down_part, down_came], axis=2),
    )
    down_part = gather_bits(down_part, down_bits[3:], me, devices, down_bits[:3])
    attended = jnp.concatenate([half[0] for half in halves], axis=0)
    log_total = jnp.concatenate([half[1] for half in halves], axis=0)
    out_pieces = out_full.reshape(devices * padded, D)

    mixed_pieces = jnp.pad(
        attended.reshape(devices, rows, tokens).astype(BF16), ((0, 0), (0, padded - rows), (0, 0))
    ).reshape(devices * padded, tokens)
    hidden = inputs + mm(mixed_pieces, out_pieces, ((0,), (0,)))
    scale_two = lax.rsqrt(jnp.mean(hidden * hidden, axis=-1, keepdims=True) + NORM_EPS)
    normed_two = (hidden * scale_two * gain_second).astype(BF16)

    normed_two, down_part = lax.optimization_barrier((normed_two, down_part))
    w_down = down_part.reshape(fblock, D)
    normed = from_ctx(normed_two)
    out_pieces, own = lax.optimization_barrier((out_pieces, normed[0]))
    normed = (own,) + normed[1:]
    w_out = out_pieces.reshape(devices, padded, D)[:, :rows].reshape(QD, D)
    cot = from_ctx(cot_here, cot_far)
    kept, near_parts = feed_forward(normed[:2], cot[:2], w_wide, w_down, n_ctx, None)
    (far_x, far_dy), momentum_flat, kept = lax.optimization_barrier(
        ((normed[2], cot[2]), momentum_flat, kept)
    )
    old_qkv, old_out, old_pair, old_down = pack(momentum_flat, None, devices, 1, F32)
    old_pair, far_x = lax.optimization_barrier((old_pair, far_x))
    old_pair = lax.all_to_all(old_pair, BOTH, split_axis=0, concat_axis=0, tiled=True)
    kept, far_parts = feed_forward(
        (far_x, swap(far_x, core_bit, devices)),
        (far_dy, swap(far_dy, core_bit, devices)),
        w_wide,
        w_down,
        n_ctx,
        kept,
    )
    kept, far_parts, old_pair = lax.optimization_barrier((kept, far_parts, old_pair))
    acts, both_backs, normed_all, cot_all = kept

    def to_ctx(near, far):
        crossed = swap(far[1], core_bit, devices)
        far = (far[0].astype(F32) + crossed.astype(F32)).astype(BF16)
        crossed = swap(near[1], core_bit, devices)
        near = near[0].astype(F32) + crossed.astype(F32)
        return near + swap(far, x_bit, devices).astype(F32), far

    normed_two_grad, ready = to_ctx(near_parts, far_parts)
    (acts, both_backs), ready = lax.optimization_barrier(((acts, both_backs), ready))

    dp_shape = tuple([2] * len(dp_bits)) + (frows, D)
    dp_order = dp_bits[1:] + dp_bits[:1]
    down_value = mm(acts, cot_all, ((0,), (0,))).astype(BF16)
    both_value = mm(both_backs, normed_all, ((0,), (0,))).astype(BF16)
    values = [both_value[:fblock], both_value[fblock:], down_value]
    orders = [dp_bits, dp_order, dp_bits]
    started = []
    for index in (2, 1, 0):
        sent, kept = scatter_split(values[index].reshape(dp_shape), dp_bits, orders[index][0], me)
        started.insert(0, (kept, swap(sent, orders[index][0], devices)))

    out_grad = cot_here.astype(F32)
    hidden_norm_grad, grad_gain_second = norm_backward(
        hidden, scale_two, gain_second, normed_two_grad
    )
    hidden_grad = out_grad + hidden_norm_grad
    hidden_low = hidden_grad.astype(BF16)
    heads_grad = mm(w_out, hidden_low, ((1,), (1,))).astype(BF16).reshape(HEADS, HD, tokens)
    delta = jnp.sum(heads_grad.astype(F32) * attended, axis=1, keepdims=True)
    grad_output = mm(mixed_pieces, hidden_low)
    query_grads, kv_parts = [], []
    sent, kept = scatter_split(
        grad_output.astype(BF16).reshape(many + (padded, D)), all_bits, all_bits[0], me
    )
    wide_parts = started + [(kept, swap(sent, all_bits[0], devices))]
    wide_orders = [list(order) for order in orders] + [list(all_bits)]
    steps = [[1, 0, 3], [2, 3], [1, 0, 3], [2, 3]]
    shares = [4, 3]
    ready = [sent]
    for index in range(KVH):
        kv_one = pair_of_heads(kv, index)
        kv_grad = None
        begin = index * group
        for count in shares:
            chosen = slice(begin, begin + count)
            begin += count
            query_part, ready = lax.optimization_barrier((queries[chosen], ready))
            query_grad, kv_grad = attend_back(
                info, kv_one, query_part, heads_grad[chosen], log_total[chosen], delta[chosen], kv_grad
            )
            query_grads.append(query_grad)
            ready = []
            if len(steps) == 3:
                acts, query_grads[-1] = lax.optimization_barrier((acts, query_grad))
                out_part = mm(acts, w_down).astype(BF16).reshape(n_ctx, span, D)
                out_sum, out_far = to_ctx((out_part[0], out_part[1]), (out_part[2], out_part[3]))
                layer_out = jnp.where(live, hidden + out_sum, 0.0).astype(BF16)
                ready.append(out_far)
            if len(steps) == 2:
                ready.append(layer_out)
            for which in steps.pop(0):
                order = wide_orders[which]
                parts, query_grads[-1] = lax.optimization_barrier(
                    (wide_parts[which], query_grads[-1])
                )
                order.pop(0)
                sent, kept = scatter_split(scatter_end(parts), order, order[0], me)
                ready.append(sent)
                wide_parts[which] = (kept, swap(sent, order[0], devices))
        kv_parts.append(
            scatter_sum(kv_grad.reshape(2, 2, 2 * HD, span), ctx_bits, me, devices)
        )
    kv_grads = [part.astype(F32).reshape(2, HD, span) for part in kv_parts]
    qk_grad = jnp.concatenate(query_grads + [grad[:1] for grad in kv_grads], axis=0)
    qk_back = rotate_back(qk_grad, cosine, sine_part).reshape(QD + KVD, tokens)
    qkv_back = jnp.concatenate(
        [qk_back] + [grad[1] for grad in kv_grads], axis=0
    ).astype(BF16)
    grad_qkv = mm(back_one, qkv_back, ((1,), (1,)))
    here_core = jnp.where((me & core_bit) != 0, 1, 0)
    here_x = jnp.where((me & x_bit) != 0, 1, 0)
    left = list(all_bits)
    qkv_order = [core_bit, dp_bits[0], x_bit] + dp_bits[1:]
    sent, kept = scatter_split(
        grad_qkv.astype(BF16).reshape(many + (padded, qkv)), left, core_bit, me
    )
    wide_parts, layer_out, sent = lax.optimization_barrier((wide_parts, layer_out, sent))
    qkv_parts = (kept, swap(sent, core_bit, devices))
    left.remove(core_bit)
    gate_sum, up_sum, down_sum, out_sum_rows = [
        scatter_sum(scatter_end(parts), order[1:], me, devices)
        for parts, order in zip(wide_parts, wide_orders)
    ]
    mats = combine(old_pair, gate_sum, up_sum, old_down, down_sum, old_out, out_sum_rows)
    mats = mats.reshape(2, 2, frows, D)
    row_parts = (choose(mats, here_core, 1), swap(choose(mats, 1 - here_core, 1), core_bit, devices))
    count = len(block_pairs(D // BLOCK))
    places = (count + n_dp - 1) // n_dp * n_dp
    dp_many = tuple([2] * len(dp_bits))
    gram_left = list(dp_bits)
    for step, bit in enumerate(qkv_order[1:]):
        qkv_parts, row_parts = lax.optimization_barrier((qkv_parts, row_parts))
        sent, kept = scatter_split(scatter_end(qkv_parts), left, bit, me)
        left.remove(bit)
        qkv_parts = (kept, swap(sent, bit, devices))
        if step == 0:
            mats = jnp.stack(row_parts, axis=1)
            row_parts = (choose(mats, here_x, 0), swap(choose(mats, 1 - here_x, 0), x_bit, devices))
            continue
        if step == 1:
            owned = jnp.stack(row_parts).reshape(n_ctx * frows, D)
            gram = gram_blocks(owned, places).reshape(dp_many + (places // n_dp, BLOCK, BLOCK))
        else:
            gram = scatter_end(row_parts)
        sent, kept = scatter_split(gram, gram_left, gram_left[0], me)
        row_parts = (kept, swap(sent, gram_left.pop(0), devices))
    qkv_parts, row_parts = lax.optimization_barrier((qkv_parts, row_parts))
    qkv_sum_rows = scatter_end(qkv_parts)
    moved_qkv = MOMENTUM_DECAY * old_qkv + qkv_sum_rows.astype(F32)
    moved_low = moved_qkv.astype(BF16)
    qkv_all = lax.all_gather(moved_low, BOTH, axis=0, tiled=True)
    gram = gather_bits(scatter_end(row_parts), dp_bits[::-1], me, devices)
    gram = gram.reshape(places, BLOCK, BLOCK)

    (gate_sum, up_sum), moved_low, gram = lax.optimization_barrier(
        ((gate_sum, up_sum), moved_low, gram)
    )
    pair_rows = to_rows(gate_sum, up_sum)
    ortho = orthogonal_wide(gram, owned).reshape(2, 2, frows, D)
    ortho, pair_rows = lax.optimization_barrier((ortho, pair_rows))
    got = swap(ortho[1], x_bit, devices)
    qkv_back, own = lax.optimization_barrier((qkv_back, ortho[0]))
    grad_bias = jnp.sum(qkv_back.astype(F32), axis=1)
    normed_one_grad = mm(qkv_back, w_qkv, ((0,), (1,)))
    input_norm_grad, grad_gain_first = norm_backward(inputs, scale_one, gain_first, normed_one_grad)
    input_grad = (hidden_grad + input_norm_grad).astype(BF16).reshape(slots, span, width)

    vector_part = join_small(
        [
            grad_gain_first,
            grad_gain_second,
            grad_bias[:QD],
            grad_bias[QD : QD + KVD],
            grad_bias[QD + KVD :],
        ],
        devices,
    )
    vector_rows = lax.all_to_all(vector_part, BOTH, split_axis=0, concat_axis=0, tiled=True)
    own, vector_part = lax.optimization_barrier((own, vector_part))
    ortho = jnp.where((me & x_bit) != 0, jnp.stack([got, own]), jnp.stack([own, got]))
    got = swap(ortho[:, 1], core_bit, devices)
    ortho = jnp.where(
        (me & core_bit) != 0,
        jnp.stack([got, ortho[:, 0]], axis=1),
        jnp.stack([ortho[:, 0], got], axis=1),
    ).reshape(n_ctx, frows, D)
    turned = turn(ortho[0], ortho[1], devices)
    momentum_flat, turned = lax.optimization_barrier((momentum_flat, turned))
    ortho_pair = lax.all_to_all(turned, BOTH, split_axis=0, concat_axis=0, tiled=True)
    ortho_qkv = orthogonal_whole(qkv_all, moved_qkv, (QD, KVD, KVD))
    vector_rows, ortho_qkv = lax.optimization_barrier((vector_rows, ortho_qkv))
    new_momentum = update(
        momentum_flat,
        qkv_sum_rows,
        out_sum_rows,
        pair_rows,
        down_sum,
        devices,
        MOMENTUM_DECAY,
        [1.0] * 7,
    ).reshape(momentum.shape)

    factors = [
        -MUON_RATE * math.sqrt(max(1.0, breadth / height)) for height, breadth in matrix_shapes()
    ]
    new_master = update(
        master_flat,
        ortho_qkv,
        ortho[3, :padded],
        ortho_pair,
        ortho[2],
        devices,
        1.0 - MUON_RATE * MUON_DECAY,
        factors,
    ).reshape(master.shape)
    vector_grad = jnp.sum(vector_rows, axis=0, keepdims=True)
    first_new = BETA_FIRST * vector_first + (1.0 - BETA_FIRST) * vector_grad
    second_new = BETA_SECOND * vector_second + (1.0 - BETA_SECOND) * vector_grad * vector_grad
    adjusted = (
        first_new
        / (1.0 - BETA_FIRST**STEP)
        / (jnp.sqrt(second_new / (1.0 - BETA_SECOND**STEP)) + ADAM_EPS)
    )
    new_vectors = vectors - ADAM_RATE * adjusted
    return (
        layer_out.reshape(slots, span, width),
        input_grad,
        new_master,
        new_momentum,
        new_master.astype(BF16),
        new_vectors,
        first_new,
        second_new,
    )


def solution(mesh):
    return jax.shard_map(
        on_device,
        mesh=mesh,
        in_specs=(
            P("dp", "ctx", None),
            P("dp", "ctx", None),
            P("dp"),
            P("dp"),
            P(BOTH, None),
            P(BOTH, None),
            P(BOTH, None),
            P(BOTH, None),
            P(BOTH, None),
        ),
        out_specs=(
            P("dp", "ctx", None),
            P("dp", "ctx", None),
            P(BOTH, None),
            P(BOTH, None),
            P(BOTH, None),
            P(BOTH, None),
            P(BOTH, None),
            P(BOTH, None),
        ),
        check_vma=False,
    )
```

```python
import math

import jax
import jax.numpy as jnp
from jax import lax
from jax.experimental import pallas as pl
from jax.experimental.pallas import tpu as pltpu
from jax.sharding import PartitionSpec as P

D = 896
HEADS = 14
KVH = 2
HD = 64
FF = 4864
SLOT = 2048
NS_STEPS = 3
STEP = 10
QD = 896
KVD = 128

NORM_EPS = 1e-06
ROPE_BASE = 1000000.0
NS_LINEAR = 3.4445
NS_SQUARE = -4.775
NS_CUBIC = 2.0315
MOMENTUM_DECAY = 0.5
MUON_RATE = 0.6
MUON_DECAY = 0.1
ADAM_RATE = 0.2
BETA_FIRST = 0.9
BETA_SECOND = 0.95
ADAM_EPS = 1e-08
MASK_FLOOR = -1e30

F32 = jnp.float32
BF16 = jnp.bfloat16
BOTH = ("dp", "ctx")
LANES = 128


def matrix_shapes():
    return [(D, QD), (D, KVD), (D, KVD), (QD, D), (D, FF), (D, FF), (FF, D)]


def vector_sizes():
    return [D, D, QD, KVD, KVD]


def mm(left, right, contract=((1,), (0,))):
    return lax.dot_general(left, right, (contract, ((), ())), preferred_element_type=F32)


def split_small(flat, devices):
    result = []
    offset = 0
    for extent_all in vector_sizes():
        extent = extent_all // devices
        result.append(flat[:, offset : offset + extent].reshape(extent_all))
        offset += extent
    return result


def join_small(pieces, devices):
    return jnp.concatenate([piece.reshape(devices, -1) for piece in pieces], axis=1)


def swap(value, mask, devices):
    return lax.ppermute(value, BOTH, [(index, index ^ mask) for index in range(devices)])


def gather_bits(value, bits, me, devices, before=()):
    held = value
    done = list(before)
    for bit in bits:
        place = sum(1 for other in done if other > bit)
        got = swap(held, bit, devices)
        mine = (me & bit) != 0
        held = jnp.where(
            mine, jnp.stack([got, held], axis=place), jnp.stack([held, got], axis=place)
        )
        done.append(bit)
    return held


def scatter_split(held, left, bit, me, lead=0):
    axis = sorted(left, reverse=True).index(bit) + lead
    mine = jnp.where((me & bit) != 0, 1, 0)
    return choose(held, 1 - mine, axis).astype(BF16), choose(held, mine, axis)


def scatter_start(held, left, bit, me, devices):
    sent, kept = scatter_split(held, left, bit, me)
    return kept, swap(sent, bit, devices)


def scatter_end(parts):
    return (parts[0].astype(F32) + parts[1].astype(F32)).astype(BF16)


def scatter_sum(value, bits, me, devices):
    left = list(bits)
    held = value
    for bit in bits:
        held = scatter_end(scatter_start(held, left, bit, me, devices))
        left.remove(bit)
    return held


def choose(value, mine, axis):
    return lax.dynamic_index_in_dim(value, mine, axis, keepdims=False)


def rotate(values, cosine, sine_part):
    midpoint = HD // 2
    turned = jnp.concatenate([-values[:, midpoint:], values[:, :midpoint]], axis=1)
    return values * cosine + turned * sine_part


def rotate_back(gradient, cosine, sine_part):
    midpoint = HD // 2
    scaled = gradient * sine_part
    turned = jnp.concatenate([scaled[:, midpoint:], -scaled[:, :midpoint]], axis=1)
    return gradient * cosine + turned


def norm_backward(source, scale_row, gain, incoming):
    gain_grad = jnp.sum(incoming * source * scale_row, axis=0)
    weighted = incoming * gain
    result = scale_row * weighted - source * scale_row**3 * jnp.mean(
        weighted * source, axis=-1, keepdims=True
    )
    return (result, gain_grad)


def halves_of(span):
    return [slice(0, span // 2), slice(span // 2, span)]


def fill_mask(info, mask, chunk, span):
    key = chunk * span + lax.broadcasted_iota(jnp.int32, (span, span), 0)
    query = info[0] * span + lax.broadcasted_iota(jnp.int32, (span, span), 1)
    key_doc = (key >= info[2]).astype(jnp.int32) + (key >= info[1]).astype(jnp.int32)
    query_doc = (query >= info[2]).astype(jnp.int32) + (query >= info[1]).astype(jnp.int32)
    allowed = jnp.logical_and(key_doc == query_doc, key <= query)
    mask[chunk] = jnp.where(allowed, 0.0, MASK_FLOOR).astype(F32)


def attend_kernel(info, kv, q, out, lse, keys, mask, best, total, acc):
    head = pl.program_id(0)
    span = q.shape[-1]
    mine = info[0]
    chunks = mine + 1

    @pl.when(head == 0)
    def _():
        def fill(chunk, carry):
            slot = jnp.bitwise_xor(chunk, mine)
            keys[chunk] = kv[slot, :HD, :].astype(F32).T.astype(BF16)
            fill_mask(info, mask, chunk, span)
            return carry

        lax.fori_loop(0, chunks, fill, 0)

    best[...] = jnp.full(best.shape, MASK_FLOOR, F32)
    total[...] = jnp.zeros(total.shape, F32)
    acc[...] = jnp.zeros(acc.shape, F32)
    queries = q[0]

    def step(index, carry):
        chunk = mine - index
        slot = jnp.bitwise_xor(chunk, mine)
        scores = jnp.dot(keys[chunk], queries, preferred_element_type=F32) + mask[chunk]
        old = best[...]
        new = jnp.maximum(old, jnp.max(scores, axis=0, keepdims=True))
        present = jnp.exp(scores - new)
        shrink = jnp.exp(old - new)
        best[...] = new
        total[...] = total[...] * shrink + jnp.sum(present, axis=0, keepdims=True)
        acc[...] = acc[...] * shrink + jnp.dot(
            kv[slot, HD:, :], present.astype(BF16), preferred_element_type=F32
        )
        return carry

    lax.fori_loop(0, chunks, step, 0)
    out[0] = acc[...] / total[...]
    lse[0] = best[...] + jnp.log(total[...])


def attend_back_kernel(
    info, kv, q, dout, lse, delta, before, dq, dkv, keys, values, mask, dk, dv, acc
):
    head = pl.program_id(0)
    span = q.shape[-1]
    mine = info[0]
    chunks = mine + 1
    n_ctx = kv.shape[0]

    @pl.when(head == 0)
    def _():
        dk[...] = jnp.zeros(dk.shape, F32)
        dv[...] = jnp.zeros(dv.shape, F32)

        def fill(chunk, carry):
            slot = jnp.bitwise_xor(chunk, mine)
            keys[chunk] = kv[slot, :HD, :].astype(F32).T.astype(BF16)
            values[chunk] = kv[slot, HD:, :].astype(F32).T.astype(BF16)
            fill_mask(info, mask, chunk, span)
            return carry

        lax.fori_loop(0, chunks, fill, 0)

    acc[...] = jnp.zeros(acc.shape, F32)
    queries = q[0]
    douts = dout[0]
    query_rows = queries.astype(F32).T.astype(BF16)
    dout_rows = douts.astype(F32).T.astype(BF16)

    def step(chunk, carry):
        slot = jnp.bitwise_xor(chunk, mine)
        value_sum, key_sum = dv[chunk], dk[chunk]
        for lanes in halves_of(span):
            scores = (
                jnp.dot(keys[chunk], queries[:, lanes], preferred_element_type=F32)
                + mask[chunk, :, lanes]
            )
            shares = jnp.exp(scores - lse[0, :, lanes])
            share_grad = jnp.dot(values[chunk], douts[:, lanes], preferred_element_type=F32)
            score_grad = (shares * (share_grad - delta[0, :, lanes])).astype(BF16)
            value_sum += jnp.dot(
                shares.astype(BF16), dout_rows[lanes, :], preferred_element_type=F32
            )
            key_sum += jnp.dot(score_grad, query_rows[lanes, :], preferred_element_type=F32)
            acc[:, lanes] += jnp.dot(kv[slot, :HD, :], score_grad, preferred_element_type=F32)
        dv[chunk], dk[chunk] = value_sum, key_sum
        return carry

    lax.fori_loop(0, chunks, step, 0)
    dq[0] = acc[...] * HD ** (-0.5)

    @pl.when(head == pl.num_programs(0) - 1)
    def _():
        for chunk in range(n_ctx):
            sums = jnp.concatenate([dk[chunk].T, dv[chunk].T], axis=0)
            if before is not None:
                sums += before[chunk].astype(F32)
            dkv[chunk] = sums.astype(BF16)


def attend(info, kv, q):
    heads, _, span = q.shape
    n_ctx = kv.shape[0]
    per_head = lambda rows: pl.BlockSpec((1, rows, span), lambda head: (head, 0, 0))
    return pl.pallas_call(
        attend_kernel,
        grid=(heads,),
        in_specs=[
            pl.BlockSpec(memory_space=pltpu.SMEM),
            pl.BlockSpec(kv.shape, lambda head: (0, 0, 0)),
            per_head(HD),
        ],
        out_specs=[per_head(HD), per_head(1)],
        out_shape=[
            jax.ShapeDtypeStruct((heads, HD, span), F32),
            jax.ShapeDtypeStruct((heads, 1, span), F32),
        ],
        scratch_shapes=[
            pltpu.VMEM((n_ctx, span, HD), BF16),
            pltpu.VMEM((n_ctx, span, span), F32),
            pltpu.VMEM((1, span), F32),
            pltpu.VMEM((1, span), F32),
            pltpu.VMEM((HD, span), F32),
        ],
        compiler_params=pltpu.CompilerParams(vmem_limit_bytes=40 * 1024 * 1024),
        cost_estimate=pl.CostEstimate(
            flops=4 * heads * span * span * n_ctx * HD * 4,
            bytes_accessed=4 * heads * span * HD * 2,
            transcendentals=heads * span * span * n_ctx,
        ),
        name="attend",
    )(info, kv, q)


def attend_back(info, kv, q, dout, lse, delta, before):
    heads, _, span = q.shape
    n_ctx = kv.shape[0]
    per_head = lambda rows: pl.BlockSpec((1, rows, span), lambda head: (head, 0, 0))
    whole = pl.BlockSpec(kv.shape, lambda head: (0, 0, 0))
    if before is None:
        body = lambda *refs: attend_back_kernel(*refs[:6], None, *refs[6:])
    else:
        body = attend_back_kernel
    return pl.pallas_call(
        body,
        grid=(heads,),
        in_specs=[
            pl.BlockSpec(memory_space=pltpu.SMEM),
            whole,
            per_head(HD),
            per_head(HD),
            per_head(1),
            per_head(1),
        ]
        + [whole] * (before is not None),
        out_specs=[per_head(HD), whole],
        out_shape=[
            jax.ShapeDtypeStruct((heads, HD, span), F32),
            jax.ShapeDtypeStruct(kv.shape, BF16),
        ],
        scratch_shapes=[
            pltpu.VMEM((n_ctx, span, HD), BF16),
            pltpu.VMEM((n_ctx, span, HD), BF16),
            pltpu.VMEM((n_ctx, span, span), F32),
            pltpu.VMEM((n_ctx, span, HD), F32),
            pltpu.VMEM((n_ctx, span, HD), F32),
            pltpu.VMEM((HD, span), F32),
        ],
        compiler_params=pltpu.CompilerParams(vmem_limit_bytes=40 * 1024 * 1024),
        cost_estimate=pl.CostEstimate(
            flops=10 * heads * span * span * n_ctx * HD * 4,
            bytes_accessed=8 * heads * span * HD * 2,
            transcendentals=heads * span * span * n_ctx,
        ),
        name="attend_back",
    )(*[info, kv, q, dout, lse, delta] + [before] * (before is not None))


def forward_backward_kernel(
    x0, x1, dy0, dy1, wide, down, act_out, both_out, x_out, dy_out, back0, back1
):
    first = pl.program_id(0) == 0
    units = down.shape[0]
    x = jnp.where(first, x0[...], x1[...])
    dy = jnp.where(first, dy0[...], dy1[...])
    x_out[...] = x
    dy_out[...] = dy
    both = jnp.dot(x, wide[...], preferred_element_type=F32)
    gate_pre = both[:, :units]
    up_pre = both[:, units:]
    grad_act = mm(dy, down[...], ((1,), (1,)))
    sigmoid_gate = jax.nn.sigmoid(gate_pre)
    swish = gate_pre * sigmoid_gate
    slope = sigmoid_gate * (1.0 + gate_pre * (1.0 - sigmoid_gate))
    act_out[...] = (swish * up_pre).astype(BF16)
    both_back = jnp.concatenate([grad_act * up_pre * slope, grad_act * swish], axis=1).astype(BF16)
    both_out[...] = both_back
    back = mm(both_back, wide[...], ((1,), (1,))).astype(BF16)

    @pl.when(first)
    def _():
        back0[...] = back

    @pl.when(jnp.logical_not(first))
    def _():
        back1[...] = back


def feed_forward(x, dy, wide, down, blocks, earlier):
    span, width = x[0].shape
    units = down.shape[0]
    first = 0 if earlier is None else 2
    whole = lambda shape: pl.BlockSpec(
        shape, lambda block: (0, 0), pipeline_mode=pl.Buffered(1)
    )
    line = lambda columns: pl.BlockSpec((span, columns), lambda block: (block + first, 0))
    columns = [units, 2 * units, width, width]
    shapes = [jax.ShapeDtypeStruct((blocks * span, count), BF16) for count in columns]
    in_specs = [whole((span, width))] * 4 + [whole((width, 2 * units)), whole((units, width))]
    operands = [*x, *dy, wide, down]
    aliases = {}
    body = forward_backward_kernel
    if earlier is not None:
        in_specs += [pl.BlockSpec(memory_space=pl.ANY)] * 4
        operands += list(earlier)
        aliases = {6 + index: index for index in range(4)}
        body = lambda *refs: forward_backward_kernel(*refs[:6], *refs[10:])
    back = pl.BlockSpec((span, width), lambda block: (0, 0))
    results = pl.pallas_call(
        body,
        grid=(2,),
        in_specs=in_specs,
        out_specs=[line(count) for count in columns] + [back, back],
        out_shape=shapes + [jax.ShapeDtypeStruct((span, width), BF16)] * 2,
        input_output_aliases=aliases,
        compiler_params=pltpu.CompilerParams(vmem_limit_bytes=60 * 1024 * 1024),
        cost_estimate=pl.CostEstimate(
            flops=20 * span * width * units,
            bytes_accessed=6 * width * units + 2 * span * 10 * width,
            transcendentals=2 * span * units,
        ),
        name="feed_forward",
    )(*operands)
    return results[:4], results[4:]


BLOCK = 128


def block_pairs(count):
    return [(low, high) for low in range(count) for high in range(low, count)]


def gram_kernel(rows, out):
    count = rows.shape[1] // BLOCK
    place = 0
    for low in range(count):
        line = lax.dot_general(
            rows[:, low * BLOCK : (low + 1) * BLOCK],
            rows[:, low * BLOCK :],
            (((0,), (0,)), ((), ())),
            preferred_element_type=F32,
        ).astype(BF16)
        for high in range(low, count):
            out[place] = line[:, (high - low) * BLOCK : (high - low + 1) * BLOCK]
            place += 1
    for extra in range(place, out.shape[0]):
        out[extra] = jnp.zeros((BLOCK, BLOCK), BF16)


def gram_blocks(rows, places):
    return pl.pallas_call(
        gram_kernel,
        out_shape=jax.ShapeDtypeStruct((places, BLOCK, BLOCK), BF16),
        compiler_params=pltpu.CompilerParams(vmem_limit_bytes=32 * 1024 * 1024),
        name="gram",
    )(rows)


def newton_schulz(gram, low, poly, mixed, rows):
    size = gram.shape[0]
    part = size // 2 if size % 16 == 0 and size > BLOCK else size
    parts = [pl.ds(begin, part) for begin in range(0, size, part)]
    row_id = lax.broadcasted_iota(jnp.int32, (size, size), 0)
    column_id = lax.broadcasted_iota(jnp.int32, (size, size), 1)
    square = jnp.where(row_id == column_id, gram[...], 0.0)
    square = jnp.sum(jnp.sum(square, axis=0, keepdims=True), axis=1, keepdims=True)
    scale = 1.0 / (jnp.sqrt(square) + 1e-07)
    for place in parts:
        scaled = gram[place, :] * (scale * scale)
        gram[place, :] = scaled
        low[place, :] = scaled.astype(BF16)
    work = (rows * scale).astype(BF16)
    for step in range(NS_STEPS):
        for place in parts:
            second = jnp.dot(low[place, :], low[...], preferred_element_type=F32)
            poly[place, :] = (NS_SQUARE * gram[place, :] + NS_CUBIC * second).astype(BF16)
        moved = jnp.dot(work, poly[...], preferred_element_type=F32)
        work = (NS_LINEAR * work.astype(F32) + moved).astype(BF16)
        if step + 1 < NS_STEPS:
            for place in parts:
                first = jnp.dot(poly[place, :], low[...], preferred_element_type=F32)
                mixed[place, :] = first.astype(BF16)
                gram[place, :] = (
                    NS_LINEAR * NS_LINEAR * gram[place, :] + (2.0 * NS_LINEAR) * first
                )
            for place in parts:
                second = jnp.dot(poly[place, :], mixed[...], preferred_element_type=F32)
                renewed = gram[place, :] + second
                gram[place, :] = renewed
                low[place, :] = renewed.astype(BF16)
    return work


def wide_kernel(blocks, rows, out, gram, low, poly, mixed):
    for place, (first, second) in enumerate(block_pairs(gram.shape[0] // BLOCK)):
        tile = blocks[place].astype(F32)
        gram[first * BLOCK : (first + 1) * BLOCK, second * BLOCK : (second + 1) * BLOCK] = tile
        if first != second:
            gram[second * BLOCK : (second + 1) * BLOCK, first * BLOCK : (first + 1) * BLOCK] = tile.T
    out[...] = newton_schulz(gram, low, poly, mixed, rows[...].astype(F32))


def square_scratch(size):
    return [
        pltpu.VMEM((size, size), F32),
        pltpu.VMEM((size, size), BF16),
        pltpu.VMEM((size, size), BF16),
        pltpu.VMEM((size, size), BF16),
    ]


def orthogonal_wide(blocks, rows):
    return pl.pallas_call(
        wide_kernel,
        out_shape=jax.ShapeDtypeStruct(rows.shape, BF16),
        scratch_shapes=square_scratch(rows.shape[1]),
        compiler_params=pltpu.CompilerParams(vmem_limit_bytes=40 * 1024 * 1024),
        cost_estimate=pl.CostEstimate(
            flops=14 * rows.shape[1] ** 3, bytes_accessed=4 * rows.size, transcendentals=0
        ),
        name="newton_wide",
    )(blocks, rows)


def whole_kernel(widths, whole, rows, out, *scratch):
    begin = 0
    for index, width in enumerate(widths):
        gram, low, poly, mixed = scratch[4 * index : 4 * index + 4]
        for first in range(0, width, BLOCK):
            gram[first : first + BLOCK, :] = lax.dot_general(
                whole[:, begin + first : begin + first + BLOCK],
                whole[:, begin : begin + width],
                (((0,), (0,)), ((), ())),
                preferred_element_type=F32,
            )
        out[:, begin : begin + width] = newton_schulz(
            gram, low, poly, mixed, rows[:, begin : begin + width]
        )
        begin += width


def orthogonal_whole(whole, rows, widths):
    scratch = []
    for width in widths:
        scratch += square_scratch(width)
    return pl.pallas_call(
        lambda *refs: whole_kernel(widths, *refs),
        out_shape=jax.ShapeDtypeStruct(rows.shape, BF16),
        scratch_shapes=scratch,
        compiler_params=pltpu.CompilerParams(vmem_limit_bytes=48 * 1024 * 1024),
        cost_estimate=pl.CostEstimate(
            flops=16 * sum(width**3 for width in widths),
            bytes_accessed=2 * whole.size,
            transcendentals=0,
        ),
        name="newton_whole",
    )(whole, rows)


def from_flat(flat, base, target, height, breadth):
    lines = breadth // LANES
    for begin in range(0, height, 8):
        count = min(8, height - begin)
        for index in range(lines):
            start = base + begin * lines + index
            if lines == 1:
                tile = flat[start : start + count, :]
            else:
                tile = flat[pl.ds(start, count, stride=lines), :]
            target[begin : begin + count, index * LANES : (index + 1) * LANES] = tile


def to_flat(flat, base, value, height, breadth):
    lines = breadth // LANES
    for begin in range(0, height, 8):
        count = min(8, height - begin)
        for index in range(lines):
            start = base + begin * lines + index
            tile = value(slice(begin, begin + count), slice(index * LANES, (index + 1) * LANES))
            if lines == 1:
                flat[start : start + count, :] = tile
            else:
                flat[pl.ds(start, count, stride=lines), :] = tile


def section_bases(devices):
    bases = []
    base = 0
    for height, breadth in matrix_shapes():
        bases.append(base)
        base += height // devices * breadth // LANES
    return bases


def pack_kernel(devices, group, flat, extra, qkv_out, out_out, wide_out, down_out, qkv, out, wide, down):
    rows = D // devices
    frows = FF // devices
    bases = section_bases(devices)
    qkv[...] = jnp.zeros(qkv.shape, F32)
    out[...] = jnp.zeros(out.shape, F32)
    from_flat(flat, bases[0], qkv.at[:, :QD], rows, QD)
    from_flat(flat, bases[1], qkv.at[:, QD : QD + KVD], rows, KVD)
    from_flat(flat, bases[2], qkv.at[:, QD + KVD :], rows, KVD)
    if extra is not None:
        qkv[rows : rows + 1, :LANES] = extra[...]
    from_flat(flat, bases[3], out, rows, D)
    from_flat(flat, bases[6], down, FF // devices, D)
    qkv_out[...] = qkv[...].astype(qkv_out.dtype)
    out_out[...] = out[...].astype(out_out.dtype)
    down_out[...] = down[...].astype(down_out.dtype)
    for which in range(2):
        from_flat(flat, bases[4 + which], wide, rows, FF)
        targets = devices // group
        for target in range(targets):
            piece = jnp.concatenate(
                [
                    wide[:, (turn * targets + target) * frows : (turn * targets + target + 1) * frows]
                    for turn in range(group)
                ],
                axis=1,
            )
            width = group * frows
            wide_out[target, :, which * width : (which + 1) * width] = piece.astype(wide_out.dtype)


def pack(flat, extra, devices, group, dtype):
    rows = D // devices
    frows = FF // devices
    padded = (rows // 16 + 1) * 16
    targets = devices // group
    wide = (targets, rows, 2 * group * frows)
    shapes = [(padded, QD + 2 * KVD), (padded, D), wide, (frows, D)]
    types = [dtype, dtype, BF16, dtype]
    if extra is None:
        body = lambda flat_ref, *refs: pack_kernel(devices, group, flat_ref, None, *refs)
        operands = [flat]
    else:
        body = lambda *refs: pack_kernel(devices, group, *refs)
        operands = [flat, extra]
    return pl.pallas_call(
        body,
        out_shape=[jax.ShapeDtypeStruct(shape, kind) for shape, kind in zip(shapes, types)],
        scratch_shapes=[
            pltpu.VMEM((padded, QD + 2 * KVD), F32),
            pltpu.VMEM((padded, D), F32),
            pltpu.VMEM((rows, FF), F32),
            pltpu.VMEM((frows, D), F32),
        ],
        compiler_params=pltpu.CompilerParams(vmem_limit_bytes=32 * 1024 * 1024),
        cost_estimate=pl.CostEstimate(flops=0, bytes_accessed=6 * flat.size, transcendentals=0),
        name="pack",
    )(*operands)


def update_kernel(devices, decay, factors, flat, qkv, out, wide, down, result, moved, rows_wide):
    rows = D // devices
    frows = FF // devices
    bases = section_bases(devices)
    whole = qkv[...].astype(F32)
    out_whole = out[...].astype(F32)
    down_whole = down[...].astype(F32)
    parts = [
        lambda r, c: whole[r, c],
        lambda r, c: whole[r, slice(QD + c.start, QD + c.stop)],
        lambda r, c: whole[r, slice(QD + KVD + c.start, QD + KVD + c.stop)],
        lambda r, c: out_whole[r, c],
    ]
    shapes = matrix_shapes()
    for index, part in enumerate(parts):
        to_flat(
            moved, bases[index], lambda r, c: part(r, c) * factors[index], rows, shapes[index][1]
        )
    to_flat(moved, bases[6], lambda r, c: down_whole[r, c] * factors[6], frows, D)
    for which in range(2):
        for source in range(devices):
            rows_wide[:, source * frows : (source + 1) * frows] = wide[
                source, :, which * frows : (which + 1) * frows
            ].astype(F32)
        to_flat(
            moved, bases[4 + which], lambda r, c: rows_wide[r, c] * factors[4 + which], rows, FF
        )
    result[...] = decay * flat[...] + moved[...]


def update(flat, qkv, out, wide, down, devices, decay, factors):
    return pl.pallas_call(
        lambda *refs: update_kernel(devices, decay, factors, *refs),
        out_shape=jax.ShapeDtypeStruct(flat.shape, F32),
        scratch_shapes=[
            pltpu.VMEM(flat.shape, F32),
            pltpu.VMEM((D // devices, FF), F32),
        ],
        compiler_params=pltpu.CompilerParams(vmem_limit_bytes=32 * 1024 * 1024),
        cost_estimate=pl.CostEstimate(flops=0, bytes_accessed=10 * flat.size, transcendentals=0),
        name="update",
    )(flat, qkv, out, wide, down)


def combine_kernel(old_pair, gate, up, old_down, down, old_out, out, mats, lines):
    devices, rows, _ = old_pair.shape
    frows = gate.shape[0]
    padded = out.shape[0]
    lines[...] = jnp.zeros(lines.shape, F32)
    for source in range(devices):
        lines[source * rows : (source + 1) * rows, : 2 * frows] = old_pair[source].astype(F32)
    old = lines[...].T
    mats[0] = (MOMENTUM_DECAY * old[:frows] + gate[...].astype(F32)).astype(BF16)
    mats[1] = (MOMENTUM_DECAY * old[frows : 2 * frows] + up[...].astype(F32)).astype(BF16)
    mats[2] = (MOMENTUM_DECAY * old_down[...] + down[...].astype(F32)).astype(BF16)
    last = MOMENTUM_DECAY * old_out[...] + out[...].astype(F32)
    mats[3] = jnp.concatenate(
        [last, jnp.zeros((frows - padded, last.shape[1]), F32)], axis=0
    ).astype(BF16)


def combine(old_pair, gate, up, old_down, down, old_out, out):
    frows, width = gate.shape
    return pl.pallas_call(
        combine_kernel,
        out_shape=jax.ShapeDtypeStruct((4, frows, width), BF16),
        scratch_shapes=[pltpu.VMEM((width, -(-2 * frows // LANES) * LANES), F32)],
        compiler_params=pltpu.CompilerParams(vmem_limit_bytes=32 * 1024 * 1024),
        name="combine",
    )(old_pair, gate, up, old_down, down, old_out, out)


def turn_kernel(gate, up, out, columns):
    devices, rows, _ = out.shape
    frows = gate.shape[0]
    columns[...] = jnp.zeros(columns.shape, F32)
    columns[:frows] = gate[...].astype(F32)
    columns[frows : 2 * frows] = up[...].astype(F32)
    lines = columns[...].T
    for target in range(devices):
        out[target] = lines[target * rows : (target + 1) * rows, : 2 * frows].astype(BF16)


def turn(gate, up, devices):
    frows, width = gate.shape
    return pl.pallas_call(
        turn_kernel,
        out_shape=jax.ShapeDtypeStruct((devices, width // devices, 2 * frows), BF16),
        scratch_shapes=[pltpu.VMEM((-(-2 * frows // LANES) * LANES, width), F32)],
        compiler_params=pltpu.CompilerParams(vmem_limit_bytes=32 * 1024 * 1024),
        name="turn",
    )(gate, up)


def on_device(
    block_input,
    cotangent,
    lengths,
    doc_starts,
    master,
    momentum,
    vectors,
    vector_first,
    vector_second,
):
    n_dp = lax.axis_size("dp")
    n_ctx = lax.axis_size("ctx")
    devices = n_dp * n_ctx
    rows = D // devices
    frows = FF // devices
    fblock = FF // n_ctx
    slots, span, width = block_input.shape
    tokens = slots * span
    group = HEADS // KVH
    qkv = QD + 2 * KVD
    my_ctx = lax.axis_index("ctx")
    me = lax.axis_index("dp") * n_ctx + my_ctx
    core_bit, x_bit = 1, 2
    ctx_bits = [core_bit, x_bit]
    dp_bits = [n_ctx << index for index in range(n_dp.bit_length() - 1)]
    all_bits = ctx_bits + dp_bits
    many = tuple([2] * len(all_bits))
    padded = (rows // 16 + 1) * 16

    master_flat = master.reshape(-1, LANES)
    momentum_flat = momentum.reshape(-1, LANES)
    small = jnp.pad(vectors, ((0, 0), (0, LANES - vectors.shape[1])))
    qkv_local, out_local, gate_up, down_local = pack(master_flat, small, devices, n_dp, BF16)

    attn_full = gather_bits(
        jnp.concatenate([qkv_local, out_local], axis=1), dp_bits[::-1], me, devices
    )
    down_bits = dp_bits[::-1]
    down_part, attn_full = lax.optimization_barrier((down_local, attn_full))
    high, low = down_bits[:2]
    down_came = [swap(down_part, mask, devices) for mask in (low, high, high + low)]
    qkv_full = gather_bits(attn_full[..., :qkv], ctx_bits[::-1], me, devices, dp_bits)
    qkv_full = qkv_full.reshape(devices, padded, qkv)
    gain_first, gain_second, bias_query, bias_key, bias_value = [
        piece.astype(F32) for piece in split_small(qkv_full[:, rows], devices)
    ]
    w_qkv = qkv_full[:, :rows].reshape(D, qkv)

    came = [choose(gate_up, my_ctx, 0)] + [
        swap(choose(gate_up, my_ctx ^ mask, 0), mask, devices) for mask in range(1, n_ctx)
    ]
    came, attn_full = lax.optimization_barrier((came, attn_full))
    ordered = []
    for source in range(n_ctx):
        piece = came[0]
        for mask in range(1, n_ctx):
            piece = jnp.where(my_ctx ^ mask == source, came[mask], piece)
        ordered.append(piece)
    w_wide = lax.all_gather(jnp.concatenate(ordered, axis=0), "dp", axis=0, tiled=True)

    def to_rows(gate, up):
        return lax.all_to_all(
            turn(gate, up, devices), BOTH, split_axis=0, concat_axis=0, tiled=True
        )

    length, second = lengths[0], doc_starts[0]
    places = my_ctx * span + jnp.arange(span, dtype=jnp.int32)
    doc_begin = jnp.where(places >= length, length, jnp.where(places >= second, second, 0))
    position = (places - doc_begin).astype(F32)
    live = (places < length)[:, None]
    info = jnp.stack([my_ctx, length, second]).astype(jnp.int32)
    inverse = ROPE_BASE ** (-2.0 * jnp.arange(HD // 2, dtype=F32) / HD)
    angles = inverse[:, None] * position[None, :]
    cosine, sine_part = jnp.cos(angles), jnp.sin(angles)
    cosine = jnp.concatenate([cosine, cosine], axis=0)[None]
    sine_part = jnp.concatenate([sine_part, sine_part], axis=0)[None]

    def from_ctx(value, other_x=None):
        other_core = swap(value, core_bit, devices)
        if other_x is None:
            other_x = swap(value, x_bit, devices)
        return value, other_core, other_x

    cot_here = jnp.where(live, cotangent.reshape(tokens, width), jnp.zeros((), BF16))

    def pair_of_heads(kv, index):
        begin = index * HD
        return jnp.concatenate(
            [kv[:, begin : begin + HD], kv[:, KVD + begin : KVD + begin + HD]], axis=1
        )

    inputs = block_input.astype(F32).reshape(tokens, width)
    scale_one = lax.rsqrt(jnp.mean(inputs * inputs, axis=-1, keepdims=True) + NORM_EPS)
    normed_one = (inputs * scale_one * gain_first).astype(BF16)
    bias = jnp.concatenate([bias_query, bias_key, bias_value])
    pre = mm(w_qkv, normed_one, ((0,), (1,))) + bias[:, None]
    turned = rotate(
        pre[: QD + KVD].reshape(HEADS + KVH, HD, tokens), cosine, sine_part
    )
    queries = (turned[:HEADS].astype(BF16).astype(F32) * HD ** (-0.5)).astype(BF16)
    kv_here = jnp.concatenate(
        [turned[HEADS:].astype(BF16).reshape(KVD, tokens), pre[QD + KVD :].astype(BF16)], axis=0
    )
    kv = from_ctx(kv_here)
    kv = jnp.stack(kv + (swap(kv[2], core_bit, devices),))
    back_one = jnp.pad(
        normed_one.T.reshape(devices, rows, tokens), ((0, 0), (0, padded - rows), (0, 0))
    ).reshape(devices * padded, tokens)
    back_one, kv = lax.optimization_barrier((back_one, kv))
    down_came = [down_part] + down_came
    at_z = jnp.where((me & high) != 0, 2, 0) + jnp.where((me & low) != 0, 1, 0)
    ordered = []
    for source in range(4):
        piece = down_came[0]
        for mask in range(1, 4):
            piece = jnp.where(at_z ^ mask == source, down_came[mask], piece)
        ordered.append(piece)
    down_part = jnp.stack(ordered).reshape(2, 2, frows, D)
    kv, down_part = lax.optimization_barrier((kv, down_part))
    down_came = swap(down_part, down_bits[2], devices)
    out_full, kv = lax.optimization_barrier((attn_full[..., qkv:], kv))
    halves = []
    for index in range(KVH):
        if index == 1:
            out_full, cot_here, halves = lax.optimization_barrier((out_full, cot_here, halves))
            cot_far = swap(cot_here, x_bit, devices)
        out_full = gather_bits(
            out_full, ctx_bits[::-1][index : index + 1], me, devices, dp_bits + ctx_bits[::-1][:index]
        )
        kv_one = pair_of_heads(kv, index)
        halves.append(attend(info, kv_one, queries[index * group : (index + 1) * group]))
    halves, cot_far, down_came = lax.optimization_barrier((halves, cot_far, down_came))
    down_part = jnp.where(
        (me & down_bits[2]) != 0,
        jnp.stack([down_came, down_part], axis=2),
        jnp.stack([down_part, down_came], axis=2),
    )
    down_part = gather_bits(down_part, down_bits[3:], me, devices, down_bits[:3])
    attended = jnp.concatenate([half[0] for half in halves], axis=0)
    log_total = jnp.concatenate([half[1] for half in halves], axis=0)
    out_pieces = out_full.reshape(devices * padded, D)

    mixed_pieces = jnp.pad(
        attended.reshape(devices, rows, tokens).astype(BF16), ((0, 0), (0, padded - rows), (0, 0))
    ).reshape(devices * padded, tokens)
    hidden = inputs + mm(mixed_pieces, out_pieces, ((0,), (0,)))
    scale_two = lax.rsqrt(jnp.mean(hidden * hidden, axis=-1, keepdims=True) + NORM_EPS)
    normed_two = (hidden * scale_two * gain_second).astype(BF16)

    normed_two, down_part = lax.optimization_barrier((normed_two, down_part))
    w_down = down_part.reshape(fblock, D)
    normed = from_ctx(normed_two)
    out_pieces, own = lax.optimization_barrier((out_pieces, normed[0]))
    normed = (own,) + normed[1:]
    w_out = out_pieces.reshape(devices, padded, D)[:, :rows].reshape(QD, D)
    cot = from_ctx(cot_here, cot_far)
    kept, near_parts = feed_forward(normed[:2], cot[:2], w_wide, w_down, n_ctx, None)
    (far_x, far_dy), momentum_flat, kept = lax.optimization_barrier(
        ((normed[2], cot[2]), momentum_flat, kept)
    )
    old_qkv, old_out, old_pair, old_down = pack(momentum_flat, None, devices, 1, F32)
    old_pair, far_x = lax.optimization_barrier((old_pair, far_x))
    old_pair = lax.all_to_all(old_pair, BOTH, split_axis=0, concat_axis=0, tiled=True)
    kept, far_parts = feed_forward(
        (far_x, swap(far_x, core_bit, devices)),
        (far_dy, swap(far_dy, core_bit, devices)),
        w_wide,
        w_down,
        n_ctx,
        kept,
    )
    kept, far_parts, old_pair = lax.optimization_barrier((kept, far_parts, old_pair))
    acts, both_backs, normed_all, cot_all = kept

    def to_ctx(near, far):
        crossed = swap(far[1], core_bit, devices)
        far = (far[0].astype(F32) + crossed.astype(F32)).astype(BF16)
        crossed = swap(near[1], core_bit, devices)
        near = near[0].astype(F32) + crossed.astype(F32)
        return near + swap(far, x_bit, devices).astype(F32), far

    normed_two_grad, ready = to_ctx(near_parts, far_parts)
    (acts, both_backs), ready = lax.optimization_barrier(((acts, both_backs), ready))

    dp_shape = tuple([2] * len(dp_bits)) + (frows, D)
    dp_order = dp_bits[1:] + dp_bits[:1]
    down_value = mm(acts, cot_all, ((0,), (0,))).astype(BF16)
    both_value = mm(both_backs, normed_all, ((0,), (0,))).astype(BF16)
    values = [both_value[:fblock], both_value[fblock:], down_value]
    orders = [dp_bits, dp_order, dp_bits]
    started = []
    for index in (2, 1, 0):
        sent, kept = scatter_split(values[index].reshape(dp_shape), dp_bits, orders[index][0], me)
        started.insert(0, (kept, swap(sent, orders[index][0], devices)))

    out_grad = cot_here.astype(F32)
    hidden_norm_grad, grad_gain_second = norm_backward(
        hidden, scale_two, gain_second, normed_two_grad
    )
    hidden_grad = out_grad + hidden_norm_grad
    hidden_low = hidden_grad.astype(BF16)
    heads_grad = mm(w_out, hidden_low, ((1,), (1,))).astype(BF16).reshape(HEADS, HD, tokens)
    delta = jnp.sum(heads_grad.astype(F32) * attended, axis=1, keepdims=True)
    grad_output = mm(mixed_pieces, hidden_low)
    query_grads, kv_parts = [], []
    sent, kept = scatter_split(
        grad_output.astype(BF16).reshape(many + (padded, D)), all_bits, all_bits[0], me
    )
    wide_parts = started + [(kept, swap(sent, all_bits[0], devices))]
    wide_orders = [list(order) for order in orders] + [list(all_bits)]
    steps = [[1, 0, 3], [2, 3], [1, 0, 3], [2, 3]]
    shares = [4, 3]
    ready = [sent]
    for index in range(KVH):
        kv_one = pair_of_heads(kv, index)
        kv_grad = None
        begin = index * group
        for count in shares:
            chosen = slice(begin, begin + count)
            begin += count
            query_part, ready = lax.optimization_barrier((queries[chosen], ready))
            query_grad, kv_grad = attend_back(
                info, kv_one, query_part, heads_grad[chosen], log_total[chosen], delta[chosen], kv_grad
            )
            query_grads.append(query_grad)
            ready = []
            if len(steps) == 3:
                acts, query_grads[-1] = lax.optimization_barrier((acts, query_grad))
                out_part = mm(acts, w_down).astype(BF16).reshape(n_ctx, span, D)
                out_near = (out_part[0], swap(out_part[1], core_bit, devices))
                out_far = scatter_end((out_part[2], swap(out_part[3], core_bit, devices)))
                ready.append(out_far)
            for which in steps.pop(0):
                order = wide_orders[which]
                parts, query_grads[-1] = lax.optimization_barrier(
                    (wide_parts[which], query_grads[-1])
                )
                order.pop(0)
                sent, kept = scatter_split(scatter_end(parts), order, order[0], me)
                ready.append(sent)
                wide_parts[which] = (kept, swap(sent, order[0], devices))
        kv_parts.append(
            scatter_sum(kv_grad.reshape(2, 2, 2 * HD, span), ctx_bits, me, devices)
        )
    kv_grads = [part.astype(F32).reshape(2, HD, span) for part in kv_parts]
    qk_grad = jnp.concatenate(query_grads + [grad[:1] for grad in kv_grads], axis=0)
    qk_back = rotate_back(qk_grad, cosine, sine_part).reshape(QD + KVD, tokens)
    qkv_back = jnp.concatenate(
        [qk_back] + [grad[1] for grad in kv_grads], axis=0
    ).astype(BF16)
    grad_qkv = mm(back_one, qkv_back, ((1,), (1,)))
    here_core = jnp.where((me & core_bit) != 0, 1, 0)
    here_x = jnp.where((me & x_bit) != 0, 1, 0)
    left = list(all_bits)
    qkv_order = [core_bit, dp_bits[0], x_bit] + dp_bits[1:]
    sent, kept = scatter_split(
        grad_qkv.astype(BF16).reshape(many + (padded, qkv)), left, core_bit, me
    )
    wide_parts, sent = lax.optimization_barrier((wide_parts, sent))
    qkv_parts = (kept, swap(sent, core_bit, devices))
    left.remove(core_bit)
    gate_sum, up_sum, down_sum, out_sum_rows = [
        scatter_sum(scatter_end(parts), order[1:], me, devices)
        for parts, order in zip(wide_parts, wide_orders)
    ]
    mats = combine(old_pair, gate_sum, up_sum, old_down, down_sum, old_out, out_sum_rows)
    mats = mats.reshape(2, 2, frows, D)
    row_parts = (choose(mats, here_core, 1), swap(choose(mats, 1 - here_core, 1), core_bit, devices))
    count = len(block_pairs(D // BLOCK))
    places = (count + n_dp - 1) // n_dp * n_dp
    dp_many = tuple([2] * len(dp_bits))
    gram_left = list(dp_bits)
    for step, bit in enumerate(qkv_order[1:]):
        qkv_parts, row_parts = lax.optimization_barrier((qkv_parts, row_parts))
        sent, kept = scatter_split(scatter_end(qkv_parts), left, bit, me)
        left.remove(bit)
        qkv_parts = (kept, swap(sent, bit, devices))
        if step == 0:
            mats = jnp.stack(row_parts, axis=1)
            row_parts = (choose(mats, here_x, 0), swap(choose(mats, 1 - here_x, 0), x_bit, devices))
            continue
        if step == 1:
            owned = jnp.stack(row_parts).reshape(n_ctx * frows, D)
            gram = gram_blocks(owned, places).reshape(dp_many + (places // n_dp, BLOCK, BLOCK))
        else:
            gram = scatter_end(row_parts)
        sent, kept = scatter_split(gram, gram_left, gram_left[0], me)
        row_parts = (kept, swap(sent, gram_left.pop(0), devices))
    qkv_parts, row_parts, out_far = lax.optimization_barrier((qkv_parts, row_parts, out_far))
    out_far = swap(out_far, x_bit, devices)
    qkv_sum_rows = scatter_end(qkv_parts)
    moved_qkv = MOMENTUM_DECAY * old_qkv + qkv_sum_rows.astype(F32)
    moved_low = moved_qkv.astype(BF16)
    qkv_all = lax.all_gather(moved_low, BOTH, axis=0, tiled=True)
    gram = gather_bits(scatter_end(row_parts), dp_bits[::-1], me, devices)
    gram = gram.reshape(places, BLOCK, BLOCK)

    (gate_sum, up_sum), out_far, gram = lax.optimization_barrier(
        ((gate_sum, up_sum), out_far, gram)
    )
    out_sum = out_near[0].astype(F32) + out_near[1].astype(F32) + out_far.astype(F32)
    layer_out = jnp.where(live, hidden + out_sum, 0.0).astype(BF16)
    pair_rows = to_rows(gate_sum, up_sum)
    ortho = orthogonal_wide(gram, owned).reshape(2, 2, frows, D)
    ortho, pair_rows = lax.optimization_barrier((ortho, pair_rows))
    got = swap(ortho[1], x_bit, devices)
    qkv_back, own = lax.optimization_barrier((qkv_back, ortho[0]))
    grad_bias = jnp.sum(qkv_back.astype(F32), axis=1)
    normed_one_grad = mm(qkv_back, w_qkv, ((0,), (1,)))
    input_norm_grad, grad_gain_first = norm_backward(inputs, scale_one, gain_first, normed_one_grad)
    input_grad = (hidden_grad + input_norm_grad).astype(BF16).reshape(slots, span, width)

    vector_part = join_small(
        [
            grad_gain_first,
            grad_gain_second,
            grad_bias[:QD],
            grad_bias[QD : QD + KVD],
            grad_bias[QD + KVD :],
        ],
        devices,
    )
    vector_rows = lax.all_to_all(vector_part, BOTH, split_axis=0, concat_axis=0, tiled=True)
    own, vector_part = lax.optimization_barrier((own, vector_part))
    ortho = jnp.where((me & x_bit) != 0, jnp.stack([got, own]), jnp.stack([own, got]))
    got = swap(ortho[:, 1], core_bit, devices)
    ortho = jnp.where(
        (me & core_bit) != 0,
        jnp.stack([got, ortho[:, 0]], axis=1),
        jnp.stack([ortho[:, 0], got], axis=1),
    ).reshape(n_ctx, frows, D)
    turned = turn(ortho[0], ortho[1], devices)
    momentum_flat, turned = lax.optimization_barrier((momentum_flat, turned))
    ortho_pair = lax.all_to_all(turned, BOTH, split_axis=0, concat_axis=0, tiled=True)
    ortho_qkv = orthogonal_whole(qkv_all, moved_qkv, (QD, KVD, KVD))
    vector_rows, ortho_qkv = lax.optimization_barrier((vector_rows, ortho_qkv))
    new_momentum = update(
        momentum_flat,
        qkv_sum_rows,
        out_sum_rows,
        pair_rows,
        down_sum,
        devices,
        MOMENTUM_DECAY,
        [1.0] * 7,
    ).reshape(momentum.shape)

    factors = [
        -MUON_RATE * math.sqrt(max(1.0, breadth / height)) for height, breadth in matrix_shapes()
    ]
    new_master = update(
        master_flat,
        ortho_qkv,
        ortho[3, :padded],
        ortho_pair,
        ortho[2],
        devices,
        1.0 - MUON_RATE * MUON_DECAY,
        factors,
    ).reshape(master.shape)
    vector_grad = jnp.sum(vector_rows, axis=0, keepdims=True)
    first_new = BETA_FIRST * vector_first + (1.0 - BETA_FIRST) * vector_grad
    second_new = BETA_SECOND * vector_second + (1.0 - BETA_SECOND) * vector_grad * vector_grad
    adjusted = (
        first_new
        / (1.0 - BETA_FIRST**STEP)
        / (jnp.sqrt(second_new / (1.0 - BETA_SECOND**STEP)) + ADAM_EPS)
    )
    new_vectors = vectors - ADAM_RATE * adjusted
    return (
        layer_out.reshape(slots, span, width),
        input_grad,
        new_master,
        new_momentum,
        new_master.astype(BF16),
        new_vectors,
        first_new,
        second_new,
    )


def solution(mesh):
    return jax.shard_map(
        on_device,
        mesh=mesh,
        in_specs=(
            P("dp", "ctx", None),
            P("dp", "ctx", None),
            P("dp"),
            P("dp"),
            P(BOTH, None),
            P(BOTH, None),
            P(BOTH, None),
            P(BOTH, None),
            P(BOTH, None),
        ),
        out_specs=(
            P("dp", "ctx", None),
            P("dp", "ctx", None),
            P(BOTH, None),
            P(BOTH, None),
            P(BOTH, None),
            P(BOTH, None),
            P(BOTH, None),
            P(BOTH, None),
        ),
        check_vma=False,
    )
```

```python
import math

import jax
import jax.numpy as jnp
from jax import lax
from jax.experimental import pallas as pl
from jax.experimental.pallas import tpu as pltpu
from jax.sharding import PartitionSpec as P

D = 896
HEADS = 14
KVH = 2
HD = 64
FF = 4864
SLOT = 2048
NS_STEPS = 3
STEP = 10
QD = 896
KVD = 128

NORM_EPS = 1e-06
ROPE_BASE = 1000000.0
NS_LINEAR = 3.4445
NS_SQUARE = -4.775
NS_CUBIC = 2.0315
MOMENTUM_DECAY = 0.5
MUON_RATE = 0.6
MUON_DECAY = 0.1
ADAM_RATE = 0.2
BETA_FIRST = 0.9
BETA_SECOND = 0.95
ADAM_EPS = 1e-08
MASK_FLOOR = -1e30

F32 = jnp.float32
BF16 = jnp.bfloat16
BOTH = ("dp", "ctx")
LANES = 128


def matrix_shapes():
    return [(D, QD), (D, KVD), (D, KVD), (QD, D), (D, FF), (D, FF), (FF, D)]


def vector_sizes():
    return [D, D, QD, KVD, KVD]


def mm(left, right, contract=((1,), (0,))):
    return lax.dot_general(left, right, (contract, ((), ())), preferred_element_type=F32)


def split_small(flat, devices):
    result = []
    offset = 0
    for extent_all in vector_sizes():
        extent = extent_all // devices
        result.append(flat[:, offset : offset + extent].reshape(extent_all))
        offset += extent
    return result


def join_small(pieces, devices):
    return jnp.concatenate([piece.reshape(devices, -1) for piece in pieces], axis=1)


def swap(value, mask, devices):
    return lax.ppermute(value, BOTH, [(index, index ^ mask) for index in range(devices)])


def gather_bits(value, bits, me, devices, before=()):
    held = value
    done = list(before)
    for bit in bits:
        place = sum(1 for other in done if other > bit)
        got = swap(held, bit, devices)
        mine = (me & bit) != 0
        held = jnp.where(
            mine, jnp.stack([got, held], axis=place), jnp.stack([held, got], axis=place)
        )
        done.append(bit)
    return held


def scatter_split(held, left, bit, me, lead=0):
    axis = sorted(left, reverse=True).index(bit) + lead
    mine = jnp.where((me & bit) != 0, 1, 0)
    return choose(held, 1 - mine, axis).astype(BF16), choose(held, mine, axis)


def scatter_start(held, left, bit, me, devices):
    sent, kept = scatter_split(held, left, bit, me)
    return kept, swap(sent, bit, devices)


def scatter_end(parts):
    return (parts[0].astype(F32) + parts[1].astype(F32)).astype(BF16)


def scatter_sum(value, bits, me, devices):
    left = list(bits)
    held = value
    for bit in bits:
        held = scatter_end(scatter_start(held, left, bit, me, devices))
        left.remove(bit)
    return held


def choose(value, mine, axis):
    return lax.dynamic_index_in_dim(value, mine, axis, keepdims=False)


def rotate(values, cosine, sine_part):
    midpoint = HD // 2
    turned = jnp.concatenate([-values[:, midpoint:], values[:, :midpoint]], axis=1)
    return values * cosine + turned * sine_part


def rotate_back(gradient, cosine, sine_part):
    midpoint = HD // 2
    scaled = gradient * sine_part
    turned = jnp.concatenate([scaled[:, midpoint:], -scaled[:, :midpoint]], axis=1)
    return gradient * cosine + turned


def norm_backward(source, scale_row, gain, incoming):
    gain_grad = jnp.sum(incoming * source * scale_row, axis=0)
    weighted = incoming * gain
    result = scale_row * weighted - source * scale_row**3 * jnp.mean(
        weighted * source, axis=-1, keepdims=True
    )
    return (result, gain_grad)


def halves_of(span):
    return [slice(0, span // 2), slice(span // 2, span)]


def fill_mask(info, mask, chunk, span):
    key = chunk * span + lax.broadcasted_iota(jnp.int32, (span, span), 0)
    query = info[0] * span + lax.broadcasted_iota(jnp.int32, (span, span), 1)
    key_doc = (key >= info[2]).astype(jnp.int32) + (key >= info[1]).astype(jnp.int32)
    query_doc = (query >= info[2]).astype(jnp.int32) + (query >= info[1]).astype(jnp.int32)
    allowed = jnp.logical_and(key_doc == query_doc, key <= query)
    mask[chunk] = jnp.where(allowed, 0.0, MASK_FLOOR).astype(F32)


def attend_kernel(info, kv, q, out, lse, keys, mask, best, total, acc):
    head = pl.program_id(0)
    span = q.shape[-1]
    mine = info[0]
    chunks = mine + 1

    @pl.when(head == 0)
    def _():
        def fill(chunk, carry):
            slot = jnp.bitwise_xor(chunk, mine)
            keys[chunk] = kv[slot, :HD, :].astype(F32).T.astype(BF16)
            fill_mask(info, mask, chunk, span)
            return carry

        lax.fori_loop(0, chunks, fill, 0)

    best[...] = jnp.full(best.shape, MASK_FLOOR, F32)
    total[...] = jnp.zeros(total.shape, F32)
    acc[...] = jnp.zeros(acc.shape, F32)
    queries = q[0]

    def step(index, carry):
        chunk = mine - index
        slot = jnp.bitwise_xor(chunk, mine)
        scores = jnp.dot(keys[chunk], queries, preferred_element_type=F32) + mask[chunk]
        old = best[...]
        new = jnp.maximum(old, jnp.max(scores, axis=0, keepdims=True))
        present = jnp.exp(scores - new)
        shrink = jnp.exp(old - new)
        best[...] = new
        total[...] = total[...] * shrink + jnp.sum(present, axis=0, keepdims=True)
        acc[...] = acc[...] * shrink + jnp.dot(
            kv[slot, HD:, :], present.astype(BF16), preferred_element_type=F32
        )
        return carry

    lax.fori_loop(0, chunks, step, 0)
    out[0] = acc[...] / total[...]
    lse[0] = best[...] + jnp.log(total[...])


def attend_back_kernel(
    info, kv, q, dout, lse, delta, before, dq, dkv, keys, values, mask, dk, dv, acc
):
    head = pl.program_id(0)
    span = q.shape[-1]
    mine = info[0]
    chunks = mine + 1
    n_ctx = kv.shape[0]

    @pl.when(head == 0)
    def _():
        dk[...] = jnp.zeros(dk.shape, F32)
        dv[...] = jnp.zeros(dv.shape, F32)

        def fill(chunk, carry):
            slot = jnp.bitwise_xor(chunk, mine)
            keys[chunk] = kv[slot, :HD, :].astype(F32).T.astype(BF16)
            values[chunk] = kv[slot, HD:, :].astype(F32).T.astype(BF16)
            fill_mask(info, mask, chunk, span)
            return carry

        lax.fori_loop(0, chunks, fill, 0)

    acc[...] = jnp.zeros(acc.shape, F32)
    queries = q[0]
    douts = dout[0]
    query_rows = queries.astype(F32).T.astype(BF16)
    dout_rows = douts.astype(F32).T.astype(BF16)

    def step(chunk, carry):
        slot = jnp.bitwise_xor(chunk, mine)
        value_sum, key_sum = dv[chunk], dk[chunk]
        for lanes in halves_of(span):
            scores = (
                jnp.dot(keys[chunk], queries[:, lanes], preferred_element_type=F32)
                + mask[chunk, :, lanes]
            )
            shares = jnp.exp(scores - lse[0, :, lanes])
            share_grad = jnp.dot(values[chunk], douts[:, lanes], preferred_element_type=F32)
            score_grad = (shares * (share_grad - delta[0, :, lanes])).astype(BF16)
            value_sum += jnp.dot(
                shares.astype(BF16), dout_rows[lanes, :], preferred_element_type=F32
            )
            key_sum += jnp.dot(score_grad, query_rows[lanes, :], preferred_element_type=F32)
            acc[:, lanes] += jnp.dot(kv[slot, :HD, :], score_grad, preferred_element_type=F32)
        dv[chunk], dk[chunk] = value_sum, key_sum
        return carry

    lax.fori_loop(0, chunks, step, 0)
    dq[0] = acc[...] * HD ** (-0.5)

    @pl.when(head == pl.num_programs(0) - 1)
    def _():
        for chunk in range(n_ctx):
            sums = jnp.concatenate([dk[chunk].T, dv[chunk].T], axis=0)
            if before is not None:
                sums += before[chunk].astype(F32)
            dkv[chunk] = sums.astype(BF16)


def attend(info, kv, q):
    heads, _, span = q.shape
    n_ctx = kv.shape[0]
    per_head = lambda rows: pl.BlockSpec((1, rows, span), lambda head: (head, 0, 0))
    return pl.pallas_call(
        attend_kernel,
        grid=(heads,),
        in_specs=[
            pl.BlockSpec(memory_space=pltpu.SMEM),
            pl.BlockSpec(kv.shape, lambda head: (0, 0, 0)),
            per_head(HD),
        ],
        out_specs=[per_head(HD), per_head(1)],
        out_shape=[
            jax.ShapeDtypeStruct((heads, HD, span), F32),
            jax.ShapeDtypeStruct((heads, 1, span), F32),
        ],
        scratch_shapes=[
            pltpu.VMEM((n_ctx, span, HD), BF16),
            pltpu.VMEM((n_ctx, span, span), F32),
            pltpu.VMEM((1, span), F32),
            pltpu.VMEM((1, span), F32),
            pltpu.VMEM((HD, span), F32),
        ],
        compiler_params=pltpu.CompilerParams(vmem_limit_bytes=40 * 1024 * 1024),
        cost_estimate=pl.CostEstimate(
            flops=4 * heads * span * span * n_ctx * HD * 4,
            bytes_accessed=4 * heads * span * HD * 2,
            transcendentals=heads * span * span * n_ctx,
        ),
        name="attend",
    )(info, kv, q)


def attend_back(info, kv, q, dout, lse, delta, before):
    heads, _, span = q.shape
    n_ctx = kv.shape[0]
    per_head = lambda rows: pl.BlockSpec((1, rows, span), lambda head: (head, 0, 0))
    whole = pl.BlockSpec(kv.shape, lambda head: (0, 0, 0))
    if before is None:
        body = lambda *refs: attend_back_kernel(*refs[:6], None, *refs[6:])
    else:
        body = attend_back_kernel
    return pl.pallas_call(
        body,
        grid=(heads,),
        in_specs=[
            pl.BlockSpec(memory_space=pltpu.SMEM),
            whole,
            per_head(HD),
            per_head(HD),
            per_head(1),
            per_head(1),
        ]
        + [whole] * (before is not None),
        out_specs=[per_head(HD), whole],
        out_shape=[
            jax.ShapeDtypeStruct((heads, HD, span), F32),
            jax.ShapeDtypeStruct(kv.shape, BF16),
        ],
        scratch_shapes=[
            pltpu.VMEM((n_ctx, span, HD), BF16),
            pltpu.VMEM((n_ctx, span, HD), BF16),
            pltpu.VMEM((n_ctx, span, span), F32),
            pltpu.VMEM((n_ctx, span, HD), F32),
            pltpu.VMEM((n_ctx, span, HD), F32),
            pltpu.VMEM((HD, span), F32),
        ],
        compiler_params=pltpu.CompilerParams(vmem_limit_bytes=40 * 1024 * 1024),
        cost_estimate=pl.CostEstimate(
            flops=10 * heads * span * span * n_ctx * HD * 4,
            bytes_accessed=8 * heads * span * HD * 2,
            transcendentals=heads * span * span * n_ctx,
        ),
        name="attend_back",
    )(*[info, kv, q, dout, lse, delta] + [before] * (before is not None))


def forward_backward_kernel(
    x0, x1, dy0, dy1, wide, down, act_out, both_out, x_out, dy_out, back0, back1
):
    first = pl.program_id(0) == 0
    units = down.shape[0]
    x = jnp.where(first, x0[...], x1[...])
    dy = jnp.where(first, dy0[...], dy1[...])
    x_out[...] = x
    dy_out[...] = dy
    both = jnp.dot(x, wide[...], preferred_element_type=F32)
    gate_pre = both[:, :units]
    up_pre = both[:, units:]
    grad_act = mm(dy, down[...], ((1,), (1,)))
    sigmoid_gate = jax.nn.sigmoid(gate_pre)
    swish = gate_pre * sigmoid_gate
    slope = sigmoid_gate * (1.0 + gate_pre * (1.0 - sigmoid_gate))
    act_out[...] = (swish * up_pre).astype(BF16)
    both_back = jnp.concatenate([grad_act * up_pre * slope, grad_act * swish], axis=1).astype(BF16)
    both_out[...] = both_back
    back = mm(both_back, wide[...], ((1,), (1,))).astype(BF16)

    @pl.when(first)
    def _():
        back0[...] = back

    @pl.when(jnp.logical_not(first))
    def _():
        back1[...] = back


def feed_forward(x, dy, wide, down, blocks, earlier):
    span, width = x[0].shape
    units = down.shape[0]
    first = 0 if earlier is None else 2
    whole = lambda shape: pl.BlockSpec(
        shape, lambda block: (0, 0), pipeline_mode=pl.Buffered(1)
    )
    line = lambda columns: pl.BlockSpec((span, columns), lambda block: (block + first, 0))
    columns = [units, 2 * units, width, width]
    shapes = [jax.ShapeDtypeStruct((blocks * span, count), BF16) for count in columns]
    in_specs = [whole((span, width))] * 4 + [whole((width, 2 * units)), whole((units, width))]
    operands = [*x, *dy, wide, down]
    aliases = {}
    body = forward_backward_kernel
    if earlier is not None:
        in_specs += [pl.BlockSpec(memory_space=pl.ANY)] * 4
        operands += list(earlier)
        aliases = {6 + index: index for index in range(4)}
        body = lambda *refs: forward_backward_kernel(*refs[:6], *refs[10:])
    back = pl.BlockSpec((span, width), lambda block: (0, 0))
    results = pl.pallas_call(
        body,
        grid=(2,),
        in_specs=in_specs,
        out_specs=[line(count) for count in columns] + [back, back],
        out_shape=shapes + [jax.ShapeDtypeStruct((span, width), BF16)] * 2,
        input_output_aliases=aliases,
        compiler_params=pltpu.CompilerParams(vmem_limit_bytes=60 * 1024 * 1024),
        cost_estimate=pl.CostEstimate(
            flops=20 * span * width * units,
            bytes_accessed=6 * width * units + 2 * span * 10 * width,
            transcendentals=2 * span * units,
        ),
        name="feed_forward",
    )(*operands)
    return results[:4], results[4:]


BLOCK = 128


def block_pairs(count):
    return [(low, high) for low in range(count) for high in range(low, count)]


def gram_kernel(rows, out):
    count = rows.shape[1] // BLOCK
    place = 0
    for low in range(count):
        line = lax.dot_general(
            rows[:, low * BLOCK : (low + 1) * BLOCK],
            rows[:, low * BLOCK :],
            (((0,), (0,)), ((), ())),
            preferred_element_type=F32,
        ).astype(BF16)
        for high in range(low, count):
            out[place] = line[:, (high - low) * BLOCK : (high - low + 1) * BLOCK]
            place += 1
    for extra in range(place, out.shape[0]):
        out[extra] = jnp.zeros((BLOCK, BLOCK), BF16)


def gram_blocks(rows, places):
    return pl.pallas_call(
        gram_kernel,
        out_shape=jax.ShapeDtypeStruct((places, BLOCK, BLOCK), BF16),
        compiler_params=pltpu.CompilerParams(vmem_limit_bytes=32 * 1024 * 1024),
        name="gram",
    )(rows)


def newton_schulz(gram, low, poly, mixed, rows):
    size = gram.shape[0]
    part = size // 2 if size % 16 == 0 and size > BLOCK else size
    parts = [pl.ds(begin, part) for begin in range(0, size, part)]
    row_id = lax.broadcasted_iota(jnp.int32, (size, size), 0)
    column_id = lax.broadcasted_iota(jnp.int32, (size, size), 1)
    square = jnp.where(row_id == column_id, gram[...], 0.0)
    square = jnp.sum(jnp.sum(square, axis=0, keepdims=True), axis=1, keepdims=True)
    scale = 1.0 / (jnp.sqrt(square) + 1e-07)
    for place in parts:
        scaled = gram[place, :] * (scale * scale)
        gram[place, :] = scaled
        low[place, :] = scaled.astype(BF16)
    work = (rows * scale).astype(BF16)
    for step in range(NS_STEPS):
        for place in parts:
            second = jnp.dot(low[place, :], low[...], preferred_element_type=F32)
            poly[place, :] = (NS_SQUARE * gram[place, :] + NS_CUBIC * second).astype(BF16)
        moved = jnp.dot(work, poly[...], preferred_element_type=F32)
        work = (NS_LINEAR * work.astype(F32) + moved).astype(BF16)
        if step + 1 < NS_STEPS:
            for place in parts:
                first = jnp.dot(poly[place, :], low[...], preferred_element_type=F32)
                mixed[place, :] = first.astype(BF16)
                gram[place, :] = (
                    NS_LINEAR * NS_LINEAR * gram[place, :] + (2.0 * NS_LINEAR) * first
                )
            for place in parts:
                second = jnp.dot(poly[place, :], mixed[...], preferred_element_type=F32)
                renewed = gram[place, :] + second
                gram[place, :] = renewed
                low[place, :] = renewed.astype(BF16)
    return work


def wide_kernel(blocks, rows, out, gram, low, poly, mixed):
    for place, (first, second) in enumerate(block_pairs(gram.shape[0] // BLOCK)):
        tile = blocks[place].astype(F32)
        gram[first * BLOCK : (first + 1) * BLOCK, second * BLOCK : (second + 1) * BLOCK] = tile
        if first != second:
            gram[second * BLOCK : (second + 1) * BLOCK, first * BLOCK : (first + 1) * BLOCK] = tile.T
    out[...] = newton_schulz(gram, low, poly, mixed, rows[...].astype(F32))


def square_scratch(size):
    return [
        pltpu.VMEM((size, size), F32),
        pltpu.VMEM((size, size), BF16),
        pltpu.VMEM((size, size), BF16),
        pltpu.VMEM((size, size), BF16),
    ]


def orthogonal_wide(blocks, rows):
    return pl.pallas_call(
        wide_kernel,
        out_shape=jax.ShapeDtypeStruct(rows.shape, BF16),
        scratch_shapes=square_scratch(rows.shape[1]),
        compiler_params=pltpu.CompilerParams(vmem_limit_bytes=40 * 1024 * 1024),
        cost_estimate=pl.CostEstimate(
            flops=14 * rows.shape[1] ** 3, bytes_accessed=4 * rows.size, transcendentals=0
        ),
        name="newton_wide",
    )(blocks, rows)


def whole_kernel(widths, whole, rows, out, *scratch):
    begin = 0
    for index, width in enumerate(widths):
        gram, low, poly, mixed = scratch[4 * index : 4 * index + 4]
        for first in range(0, width, BLOCK):
            gram[first : first + BLOCK, :] = lax.dot_general(
                whole[:, begin + first : begin + first + BLOCK],
                whole[:, begin : begin + width],
                (((0,), (0,)), ((), ())),
                preferred_element_type=F32,
            )
        out[:, begin : begin + width] = newton_schulz(
            gram, low, poly, mixed, rows[:, begin : begin + width]
        )
        begin += width


def orthogonal_whole(whole, rows, widths):
    scratch = []
    for width in widths:
        scratch += square_scratch(width)
    return pl.pallas_call(
        lambda *refs: whole_kernel(widths, *refs),
        out_shape=jax.ShapeDtypeStruct(rows.shape, BF16),
        scratch_shapes=scratch,
        compiler_params=pltpu.CompilerParams(vmem_limit_bytes=48 * 1024 * 1024),
        cost_estimate=pl.CostEstimate(
            flops=16 * sum(width**3 for width in widths),
            bytes_accessed=2 * whole.size,
            transcendentals=0,
        ),
        name="newton_whole",
    )(whole, rows)


def from_flat(flat, base, target, height, breadth):
    lines = breadth // LANES
    for begin in range(0, height, 8):
        count = min(8, height - begin)
        for index in range(lines):
            start = base + begin * lines + index
            if lines == 1:
                tile = flat[start : start + count, :]
            else:
                tile = flat[pl.ds(start, count, stride=lines), :]
            target[begin : begin + count, index * LANES : (index + 1) * LANES] = tile


def to_flat(flat, base, value, height, breadth):
    lines = breadth // LANES
    for begin in range(0, height, 8):
        count = min(8, height - begin)
        for index in range(lines):
            start = base + begin * lines + index
            tile = value(slice(begin, begin + count), slice(index * LANES, (index + 1) * LANES))
            if lines == 1:
                flat[start : start + count, :] = tile
            else:
                flat[pl.ds(start, count, stride=lines), :] = tile


def section_bases(devices):
    bases = []
    base = 0
    for height, breadth in matrix_shapes():
        bases.append(base)
        base += height // devices * breadth // LANES
    return bases


def pack_kernel(devices, group, flat, extra, qkv_out, out_out, wide_out, down_out, qkv, out, wide, down):
    rows = D // devices
    frows = FF // devices
    bases = section_bases(devices)
    qkv[...] = jnp.zeros(qkv.shape, F32)
    out[...] = jnp.zeros(out.shape, F32)
    from_flat(flat, bases[0], qkv.at[:, :QD], rows, QD)
    from_flat(flat, bases[1], qkv.at[:, QD : QD + KVD], rows, KVD)
    from_flat(flat, bases[2], qkv.at[:, QD + KVD :], rows, KVD)
    if extra is not None:
        qkv[rows : rows + 1, :LANES] = extra[...]
    from_flat(flat, bases[3], out, rows, D)
    from_flat(flat, bases[6], down, FF // devices, D)
    qkv_out[...] = qkv[...].astype(qkv_out.dtype)
    out_out[...] = out[...].astype(out_out.dtype)
    down_out[...] = down[...].astype(down_out.dtype)
    for which in range(2):
        from_flat(flat, bases[4 + which], wide, rows, FF)
        targets = devices // group
        for target in range(targets):
            piece = jnp.concatenate(
                [
                    wide[:, (turn * targets + target) * frows : (turn * targets + target + 1) * frows]
                    for turn in range(group)
                ],
                axis=1,
            )
            width = group * frows
            wide_out[target, :, which * width : (which + 1) * width] = piece.astype(wide_out.dtype)


def pack(flat, extra, devices, group, dtype):
    rows = D // devices
    frows = FF // devices
    padded = (rows // 16 + 1) * 16
    targets = devices // group
    wide = (targets, rows, 2 * group * frows)
    shapes = [(padded, QD + 2 * KVD), (padded, D), wide, (frows, D)]
    types = [dtype, dtype, BF16, dtype]
    if extra is None:
        body = lambda flat_ref, *refs: pack_kernel(devices, group, flat_ref, None, *refs)
        operands = [flat]
    else:
        body = lambda *refs: pack_kernel(devices, group, *refs)
        operands = [flat, extra]
    return pl.pallas_call(
        body,
        out_shape=[jax.ShapeDtypeStruct(shape, kind) for shape, kind in zip(shapes, types)],
        scratch_shapes=[
            pltpu.VMEM((padded, QD + 2 * KVD), F32),
            pltpu.VMEM((padded, D), F32),
            pltpu.VMEM((rows, FF), F32),
            pltpu.VMEM((frows, D), F32),
        ],
        compiler_params=pltpu.CompilerParams(vmem_limit_bytes=32 * 1024 * 1024),
        cost_estimate=pl.CostEstimate(flops=0, bytes_accessed=6 * flat.size, transcendentals=0),
        name="pack",
    )(*operands)


def update_kernel(devices, decay, factors, flat, qkv, out, wide, down, result, moved, rows_wide):
    rows = D // devices
    frows = FF // devices
    bases = section_bases(devices)
    whole = qkv[...].astype(F32)
    out_whole = out[...].astype(F32)
    down_whole = down[...].astype(F32)
    parts = [
        lambda r, c: whole[r, c],
        lambda r, c: whole[r, slice(QD + c.start, QD + c.stop)],
        lambda r, c: whole[r, slice(QD + KVD + c.start, QD + KVD + c.stop)],
        lambda r, c: out_whole[r, c],
    ]
    shapes = matrix_shapes()
    for index, part in enumerate(parts):
        to_flat(
            moved, bases[index], lambda r, c: part(r, c) * factors[index], rows, shapes[index][1]
        )
    to_flat(moved, bases[6], lambda r, c: down_whole[r, c] * factors[6], frows, D)
    for which in range(2):
        for source in range(devices):
            rows_wide[:, source * frows : (source + 1) * frows] = wide[
                source, :, which * frows : (which + 1) * frows
            ].astype(F32)
        to_flat(
            moved, bases[4 + which], lambda r, c: rows_wide[r, c] * factors[4 + which], rows, FF
        )
    result[...] = decay * flat[...] + moved[...]


def update(flat, qkv, out, wide, down, devices, decay, factors):
    return pl.pallas_call(
        lambda *refs: update_kernel(devices, decay, factors, *refs),
        out_shape=jax.ShapeDtypeStruct(flat.shape, F32),
        scratch_shapes=[
            pltpu.VMEM(flat.shape, F32),
            pltpu.VMEM((D // devices, FF), F32),
        ],
        compiler_params=pltpu.CompilerParams(vmem_limit_bytes=32 * 1024 * 1024),
        cost_estimate=pl.CostEstimate(flops=0, bytes_accessed=10 * flat.size, transcendentals=0),
        name="update",
    )(flat, qkv, out, wide, down)


def combine_kernel(old_pair, gate, up, old_down, down, old_out, out, mats, lines):
    devices, rows, _ = old_pair.shape
    frows = gate.shape[0]
    padded = out.shape[0]
    lines[...] = jnp.zeros(lines.shape, F32)
    for source in range(devices):
        lines[source * rows : (source + 1) * rows, : 2 * frows] = old_pair[source].astype(F32)
    old = lines[...].T
    mats[0] = (MOMENTUM_DECAY * old[:frows] + gate[...].astype(F32)).astype(BF16)
    mats[1] = (MOMENTUM_DECAY * old[frows : 2 * frows] + up[...].astype(F32)).astype(BF16)
    mats[2] = (MOMENTUM_DECAY * old_down[...] + down[...].astype(F32)).astype(BF16)
    last = MOMENTUM_DECAY * old_out[...] + out[...].astype(F32)
    mats[3] = jnp.concatenate(
        [last, jnp.zeros((frows - padded, last.shape[1]), F32)], axis=0
    ).astype(BF16)


def combine(old_pair, gate, up, old_down, down, old_out, out):
    frows, width = gate.shape
    return pl.pallas_call(
        combine_kernel,
        out_shape=jax.ShapeDtypeStruct((4, frows, width), BF16),
        scratch_shapes=[pltpu.VMEM((width, -(-2 * frows // LANES) * LANES), F32)],
        compiler_params=pltpu.CompilerParams(vmem_limit_bytes=32 * 1024 * 1024),
        name="combine",
    )(old_pair, gate, up, old_down, down, old_out, out)


def turn_kernel(gate, up, out, columns):
    devices, rows, _ = out.shape
    frows = gate.shape[0]
    columns[...] = jnp.zeros(columns.shape, F32)
    columns[:frows] = gate[...].astype(F32)
    columns[frows : 2 * frows] = up[...].astype(F32)
    lines = columns[...].T
    for target in range(devices):
        out[target] = lines[target * rows : (target + 1) * rows, : 2 * frows].astype(BF16)


def turn(gate, up, devices):
    frows, width = gate.shape
    return pl.pallas_call(
        turn_kernel,
        out_shape=jax.ShapeDtypeStruct((devices, width // devices, 2 * frows), BF16),
        scratch_shapes=[pltpu.VMEM((-(-2 * frows // LANES) * LANES, width), F32)],
        compiler_params=pltpu.CompilerParams(vmem_limit_bytes=32 * 1024 * 1024),
        name="turn",
    )(gate, up)


def on_device(
    block_input,
    cotangent,
    lengths,
    doc_starts,
    master,
    momentum,
    vectors,
    vector_first,
    vector_second,
):
    n_dp = lax.axis_size("dp")
    n_ctx = lax.axis_size("ctx")
    devices = n_dp * n_ctx
    rows = D // devices
    frows = FF // devices
    fblock = FF // n_ctx
    slots, span, width = block_input.shape
    tokens = slots * span
    group = HEADS // KVH
    qkv = QD + 2 * KVD
    my_ctx = lax.axis_index("ctx")
    me = lax.axis_index("dp") * n_ctx + my_ctx
    core_bit, x_bit = 1, 2
    ctx_bits = [core_bit, x_bit]
    dp_bits = [n_ctx << index for index in range(n_dp.bit_length() - 1)]
    all_bits = ctx_bits + dp_bits
    many = tuple([2] * len(all_bits))
    padded = (rows // 16 + 1) * 16

    master_flat = master.reshape(-1, LANES)
    momentum_flat = momentum.reshape(-1, LANES)
    small = jnp.pad(vectors, ((0, 0), (0, LANES - vectors.shape[1])))
    qkv_local, out_local, gate_up, down_local = pack(master_flat, small, devices, n_dp, BF16)

    attn_full = gather_bits(
        jnp.concatenate([qkv_local, out_local], axis=1), dp_bits[::-1], me, devices
    )
    down_bits = dp_bits[::-1]
    down_part, attn_full = lax.optimization_barrier((down_local, attn_full))
    high, low = down_bits[:2]
    down_came = [swap(down_part, mask, devices) for mask in (low, high, high + low)]
    qkv_full = gather_bits(attn_full[..., :qkv], ctx_bits[::-1], me, devices, dp_bits)
    qkv_full = qkv_full.reshape(devices, padded, qkv)
    gain_first, gain_second, bias_query, bias_key, bias_value = [
        piece.astype(F32) for piece in split_small(qkv_full[:, rows], devices)
    ]
    w_qkv = qkv_full[:, :rows].reshape(D, qkv)

    came = [choose(gate_up, my_ctx, 0)] + [
        swap(choose(gate_up, my_ctx ^ mask, 0), mask, devices) for mask in range(1, n_ctx)
    ]
    came, attn_full = lax.optimization_barrier((came, attn_full))
    ordered = []
    for source in range(n_ctx):
        piece = came[0]
        for mask in range(1, n_ctx):
            piece = jnp.where(my_ctx ^ mask == source, came[mask], piece)
        ordered.append(piece)
    w_wide = lax.all_gather(jnp.concatenate(ordered, axis=0), "dp", axis=0, tiled=True)

    def to_rows(gate, up):
        return lax.all_to_all(
            turn(gate, up, devices), BOTH, split_axis=0, concat_axis=0, tiled=True
        )

    length, second = lengths[0], doc_starts[0]
    places = my_ctx * span + jnp.arange(span, dtype=jnp.int32)
    doc_begin = jnp.where(places >= length, length, jnp.where(places >= second, second, 0))
    position = (places - doc_begin).astype(F32)
    live = (places < length)[:, None]
    info = jnp.stack([my_ctx, length, second]).astype(jnp.int32)
    inverse = ROPE_BASE ** (-2.0 * jnp.arange(HD // 2, dtype=F32) / HD)
    angles = inverse[:, None] * position[None, :]
    cosine, sine_part = jnp.cos(angles), jnp.sin(angles)
    cosine = jnp.concatenate([cosine, cosine], axis=0)[None]
    sine_part = jnp.concatenate([sine_part, sine_part], axis=0)[None]

    def from_ctx(value, other_x=None):
        other_core = swap(value, core_bit, devices)
        if other_x is None:
            other_x = swap(value, x_bit, devices)
        return value, other_core, other_x

    cot_here = jnp.where(live, cotangent.reshape(tokens, width), jnp.zeros((), BF16))

    def pair_of_heads(kv, index):
        begin = index * HD
        return jnp.concatenate(
            [kv[:, begin : begin + HD], kv[:, KVD + begin : KVD + begin + HD]], axis=1
        )

    inputs = block_input.astype(F32).reshape(tokens, width)
    scale_one = lax.rsqrt(jnp.mean(inputs * inputs, axis=-1, keepdims=True) + NORM_EPS)
    normed_one = (inputs * scale_one * gain_first).astype(BF16)
    bias = jnp.concatenate([bias_query, bias_key, bias_value])
    pre = mm(w_qkv, normed_one, ((0,), (1,))) + bias[:, None]
    turned = rotate(
        pre[: QD + KVD].reshape(HEADS + KVH, HD, tokens), cosine, sine_part
    )
    queries = (turned[:HEADS].astype(BF16).astype(F32) * HD ** (-0.5)).astype(BF16)
    kv_here = jnp.concatenate(
        [turned[HEADS:].astype(BF16).reshape(KVD, tokens), pre[QD + KVD :].astype(BF16)], axis=0
    )
    kv = from_ctx(kv_here)
    kv = jnp.stack(kv + (swap(kv[2], core_bit, devices),))
    back_one = jnp.pad(
        normed_one.T.reshape(devices, rows, tokens), ((0, 0), (0, padded - rows), (0, 0))
    ).reshape(devices * padded, tokens)
    back_one, kv = lax.optimization_barrier((back_one, kv))
    down_came = [down_part] + down_came
    at_z = jnp.where((me & high) != 0, 2, 0) + jnp.where((me & low) != 0, 1, 0)
    ordered = []
    for source in range(4):
        piece = down_came[0]
        for mask in range(1, 4):
            piece = jnp.where(at_z ^ mask == source, down_came[mask], piece)
        ordered.append(piece)
    down_part = jnp.stack(ordered).reshape(2, 2, frows, D)
    kv, down_part = lax.optimization_barrier((kv, down_part))
    down_came = swap(down_part, down_bits[2], devices)
    out_full, kv = lax.optimization_barrier((attn_full[..., qkv:], kv))
    halves = []
    for index in range(KVH):
        if index == 1:
            out_full, cot_here, halves = lax.optimization_barrier((out_full, cot_here, halves))
            cot_far = swap(cot_here, x_bit, devices)
        out_full = gather_bits(
            out_full, ctx_bits[::-1][index : index + 1], me, devices, dp_bits + ctx_bits[::-1][:index]
        )
        kv_one = pair_of_heads(kv, index)
        halves.append(attend(info, kv_one, queries[index * group : (index + 1) * group]))
    halves, cot_far, down_came = lax.optimization_barrier((halves, cot_far, down_came))
    down_part = jnp.where(
        (me & down_bits[2]) != 0,
        jnp.stack([down_came, down_part], axis=2),
        jnp.stack([down_part, down_came], axis=2),
    )
    down_part = gather_bits(down_part, down_bits[3:], me, devices, down_bits[:3])
    attended = jnp.concatenate([half[0] for half in halves], axis=0)
    log_total = jnp.concatenate([half[1] for half in halves], axis=0)
    out_pieces = out_full.reshape(devices * padded, D)

    mixed_pieces = jnp.pad(
        attended.reshape(devices, rows, tokens).astype(BF16), ((0, 0), (0, padded - rows), (0, 0))
    ).reshape(devices * padded, tokens)
    hidden = inputs + mm(mixed_pieces, out_pieces, ((0,), (0,)))
    scale_two = lax.rsqrt(jnp.mean(hidden * hidden, axis=-1, keepdims=True) + NORM_EPS)
    normed_two = (hidden * scale_two * gain_second).astype(BF16)

    normed_two, down_part = lax.optimization_barrier((normed_two, down_part))
    w_down = down_part.reshape(fblock, D)
    normed = from_ctx(normed_two)
    out_pieces, own = lax.optimization_barrier((out_pieces, normed[0]))
    normed = (own,) + normed[1:]
    w_out = out_pieces.reshape(devices, padded, D)[:, :rows].reshape(QD, D)
    cot = from_ctx(cot_here, cot_far)
    kept, near_parts = feed_forward(normed[:2], cot[:2], w_wide, w_down, n_ctx, None)
    (far_x, far_dy), momentum_flat, kept = lax.optimization_barrier(
        ((normed[2], cot[2]), momentum_flat, kept)
    )
    old_qkv, old_out, old_pair, old_down = pack(momentum_flat, None, devices, 1, F32)
    old_pair, far_x = lax.optimization_barrier((old_pair, far_x))
    old_pair = lax.all_to_all(old_pair, BOTH, split_axis=0, concat_axis=0, tiled=True)
    kept, far_parts = feed_forward(
        (far_x, swap(far_x, core_bit, devices)),
        (far_dy, swap(far_dy, core_bit, devices)),
        w_wide,
        w_down,
        n_ctx,
        kept,
    )
    kept, far_parts, old_pair = lax.optimization_barrier((kept, far_parts, old_pair))
    acts, both_backs, normed_all, cot_all = kept

    def to_ctx(near, far):
        crossed = swap(far[1], core_bit, devices)
        far = (far[0].astype(F32) + crossed.astype(F32)).astype(BF16)
        crossed = swap(near[1], core_bit, devices)
        near = near[0].astype(F32) + crossed.astype(F32)
        return near + swap(far, x_bit, devices).astype(F32), far

    normed_two_grad, ready = to_ctx(near_parts, far_parts)
    (acts, both_backs), ready = lax.optimization_barrier(((acts, both_backs), ready))

    dp_shape = tuple([2] * len(dp_bits)) + (frows, D)
    dp_order = dp_bits[1:] + dp_bits[:1]
    down_value = mm(acts, cot_all, ((0,), (0,))).astype(BF16)
    both_value = mm(both_backs, normed_all, ((0,), (0,))).astype(BF16)
    values = [both_value[:fblock], both_value[fblock:], down_value]
    orders = [dp_bits, dp_order, dp_bits]
    started = []
    for index in (2, 1, 0):
        sent, kept = scatter_split(values[index].reshape(dp_shape), dp_bits, orders[index][0], me)
        started.insert(0, (kept, swap(sent, orders[index][0], devices)))

    out_grad = cot_here.astype(F32)
    hidden_norm_grad, grad_gain_second = norm_backward(
        hidden, scale_two, gain_second, normed_two_grad
    )
    hidden_grad = out_grad + hidden_norm_grad
    hidden_low = hidden_grad.astype(BF16)
    heads_grad = mm(w_out, hidden_low, ((1,), (1,))).astype(BF16).reshape(HEADS, HD, tokens)
    delta = jnp.sum(heads_grad.astype(F32) * attended, axis=1, keepdims=True)
    grad_output = mm(mixed_pieces, hidden_low)
    query_grads, kv_parts = [], []
    sent, kept = scatter_split(
        grad_output.astype(BF16).reshape(many + (padded, D)), all_bits, all_bits[0], me
    )
    wide_parts = started + [(kept, swap(sent, all_bits[0], devices))]
    wide_orders = [list(order) for order in orders] + [list(all_bits)]
    steps = [[1, 0, 3], [2, 3], [1, 0, 3], [2, 3]]
    shares = [4, 3]
    ready = [sent]
    for index in range(KVH):
        kv_one = pair_of_heads(kv, index)
        kv_grad = None
        begin = index * group
        for count in shares:
            chosen = slice(begin, begin + count)
            begin += count
            query_part, ready = lax.optimization_barrier((queries[chosen], ready))
            query_grad, kv_grad = attend_back(
                info, kv_one, query_part, heads_grad[chosen], log_total[chosen], delta[chosen], kv_grad
            )
            query_grads.append(query_grad)
            ready = []
            if len(steps) == 3:
                acts, query_grads[-1] = lax.optimization_barrier((acts, query_grad))
                out_part = mm(acts, w_down).astype(BF16).reshape(n_ctx, span, D)
                out_near = (out_part[0], swap(out_part[1], core_bit, devices))
                out_far = scatter_end((out_part[2], swap(out_part[3], core_bit, devices)))
                ready.append(out_far)
            for which in steps.pop(0):
                order = wide_orders[which]
                parts, query_grads[-1] = lax.optimization_barrier(
                    (wide_parts[which], query_grads[-1])
                )
                order.pop(0)
                sent, kept = scatter_split(scatter_end(parts), order, order[0], me)
                ready.append(sent)
                wide_parts[which] = (kept, swap(sent, order[0], devices))
        kv_parts.append(
            scatter_sum(kv_grad.reshape(2, 2, 2 * HD, span), ctx_bits, me, devices)
        )
    kv_grads = [part.astype(F32).reshape(2, HD, span) for part in kv_parts]
    qk_grad = jnp.concatenate(query_grads + [grad[:1] for grad in kv_grads], axis=0)
    qk_back = rotate_back(qk_grad, cosine, sine_part).reshape(QD + KVD, tokens)
    qkv_back = jnp.concatenate(
        [qk_back] + [grad[1] for grad in kv_grads], axis=0
    ).astype(BF16)
    grad_qkv = mm(back_one, qkv_back, ((1,), (1,)))
    here_core = jnp.where((me & core_bit) != 0, 1, 0)
    here_x = jnp.where((me & x_bit) != 0, 1, 0)
    left = list(all_bits)
    qkv_order = [core_bit, dp_bits[0], x_bit] + dp_bits[1:]
    sent, kept = scatter_split(
        grad_qkv.astype(BF16).reshape(many + (padded, qkv)), left, core_bit, me
    )
    wide_parts, sent = lax.optimization_barrier((wide_parts, sent))
    qkv_parts = (kept, swap(sent, core_bit, devices))
    left.remove(core_bit)
    gate_sum, up_sum, down_sum, out_sum_rows = [
        scatter_sum(scatter_end(parts), order[1:], me, devices)
        for parts, order in zip(wide_parts, wide_orders)
    ]
    mats = combine(old_pair, gate_sum, up_sum, old_down, down_sum, old_out, out_sum_rows)
    mats = mats.reshape(2, 2, frows, D)
    row_parts = (choose(mats, here_core, 1), swap(choose(mats, 1 - here_core, 1), core_bit, devices))
    count = len(block_pairs(D // BLOCK))
    places = (count + n_dp - 1) // n_dp * n_dp
    dp_many = tuple([2] * len(dp_bits))
    gram_left = list(dp_bits)
    for step, bit in enumerate(qkv_order[1:]):
        qkv_parts, row_parts = lax.optimization_barrier((qkv_parts, row_parts))
        sent, kept = scatter_split(scatter_end(qkv_parts), left, bit, me)
        left.remove(bit)
        qkv_parts = (kept, swap(sent, bit, devices))
        if step == 0:
            mats = jnp.stack(row_parts, axis=1)
            row_parts = (choose(mats, here_x, 0), swap(choose(mats, 1 - here_x, 0), x_bit, devices))
            continue
        if step == 1:
            owned = jnp.stack(row_parts).reshape(n_ctx * frows, D)
            gram = gram_blocks(owned, places).reshape(dp_many + (places // n_dp, BLOCK, BLOCK))
        else:
            gram = scatter_end(row_parts)
        sent, kept = scatter_split(gram, gram_left, gram_left[0], me)
        row_parts = (kept, swap(sent, gram_left.pop(0), devices))
    qkv_parts, row_parts, out_far = lax.optimization_barrier((qkv_parts, row_parts, out_far))
    out_far = swap(out_far, x_bit, devices)
    qkv_sum_rows = scatter_end(qkv_parts)
    moved_qkv = MOMENTUM_DECAY * old_qkv + qkv_sum_rows.astype(F32)
    moved_low = moved_qkv.astype(BF16)
    qkv_all = lax.all_gather(moved_low, BOTH, axis=0, tiled=True)
    gram = gather_bits(scatter_end(row_parts), dp_bits[::-1], me, devices)
    gram = gram.reshape(places, BLOCK, BLOCK)

    (gate_sum, up_sum), gram = lax.optimization_barrier(((gate_sum, up_sum), gram))
    pair_rows = to_rows(gate_sum, up_sum)
    ortho = orthogonal_wide(gram, owned).reshape(2, 2, frows, D)
    ortho, pair_rows = lax.optimization_barrier((ortho, pair_rows))
    got = swap(ortho[1], x_bit, devices)
    qkv_back, out_far, own = lax.optimization_barrier((qkv_back, out_far, ortho[0]))
    out_sum = out_near[0].astype(F32) + out_near[1].astype(F32) + out_far.astype(F32)
    layer_out = jnp.where(live, hidden + out_sum, 0.0).astype(BF16)
    grad_bias = jnp.sum(qkv_back.astype(F32), axis=1)
    normed_one_grad = mm(qkv_back, w_qkv, ((0,), (1,)))
    input_norm_grad, grad_gain_first = norm_backward(inputs, scale_one, gain_first, normed_one_grad)
    input_grad = (hidden_grad + input_norm_grad).astype(BF16).reshape(slots, span, width)

    vector_part = join_small(
        [
            grad_gain_first,
            grad_gain_second,
            grad_bias[:QD],
            grad_bias[QD : QD + KVD],
            grad_bias[QD + KVD :],
        ],
        devices,
    )
    vector_rows = lax.all_to_all(vector_part, BOTH, split_axis=0, concat_axis=0, tiled=True)
    own, vector_part = lax.optimization_barrier((own, vector_part))
    ortho = jnp.where((me & x_bit) != 0, jnp.stack([got, own]), jnp.stack([own, got]))
    got = swap(ortho[:, 1], core_bit, devices)
    ortho = jnp.where(
        (me & core_bit) != 0,
        jnp.stack([got, ortho[:, 0]], axis=1),
        jnp.stack([ortho[:, 0], got], axis=1),
    ).reshape(n_ctx, frows, D)
    turned = turn(ortho[0], ortho[1], devices)
    momentum_flat, turned = lax.optimization_barrier((momentum_flat, turned))
    ortho_pair = lax.all_to_all(turned, BOTH, split_axis=0, concat_axis=0, tiled=True)
    ortho_qkv = orthogonal_whole(qkv_all, moved_qkv, (QD, KVD, KVD))
    vector_rows, ortho_qkv = lax.optimization_barrier((vector_rows, ortho_qkv))
    new_momentum = update(
        momentum_flat,
        qkv_sum_rows,
        out_sum_rows,
        pair_rows,
        down_sum,
        devices,
        MOMENTUM_DECAY,
        [1.0] * 7,
    ).reshape(momentum.shape)

    factors = [
        -MUON_RATE * math.sqrt(max(1.0, breadth / height)) for height, breadth in matrix_shapes()
    ]
    new_master = update(
        master_flat,
        ortho_qkv,
        ortho[3, :padded],
        ortho_pair,
        ortho[2],
        devices,
        1.0 - MUON_RATE * MUON_DECAY,
        factors,
    ).reshape(master.shape)
    vector_grad = jnp.sum(vector_rows, axis=0, keepdims=True)
    first_new = BETA_FIRST * vector_first + (1.0 - BETA_FIRST) * vector_grad
    second_new = BETA_SECOND * vector_second + (1.0 - BETA_SECOND) * vector_grad * vector_grad
    adjusted = (
        first_new
        / (1.0 - BETA_FIRST**STEP)
        / (jnp.sqrt(second_new / (1.0 - BETA_SECOND**STEP)) + ADAM_EPS)
    )
    new_vectors = vectors - ADAM_RATE * adjusted
    return (
        layer_out.reshape(slots, span, width),
        input_grad,
        new_master,
        new_momentum,
        new_master.astype(BF16),
        new_vectors,
        first_new,
        second_new,
    )


def solution(mesh):
    return jax.shard_map(
        on_device,
        mesh=mesh,
        in_specs=(
            P("dp", "ctx", None),
            P("dp", "ctx", None),
            P("dp"),
            P("dp"),
            P(BOTH, None),
            P(BOTH, None),
            P(BOTH, None),
            P(BOTH, None),
            P(BOTH, None),
        ),
        out_specs=(
            P("dp", "ctx", None),
            P("dp", "ctx", None),
            P(BOTH, None),
            P(BOTH, None),
            P(BOTH, None),
            P(BOTH, None),
            P(BOTH, None),
            P(BOTH, None),
        ),
        check_vma=False,
    )
```
